32 devices in a mesh: group: 4 (over x, core), frame: 2 (over y), tensor: 4 (over z).
Axes of the slice: x: 2, y: 2, z: 4, core: 2. Of those that a mesh axis runs over, the one named last changes fastest.
Arguments:
- latent: bfloat16 [4, 4, 256, 1152], P('group', 'frame', 'tensor'), may hold values from -6 to 6
- captions: bfloat16 [4, 2, 120, 4096], P('group'), may hold values from -6 to 6
- bucket: int32 [4], P('group'), may hold values from 0 to 7
- clip_ids: int32 [4, 4], P('group'), may hold values from 0 to 1, as said below
- window_mask: int32 [4, 4, 4], P('group', 'frame'), may hold values 0 or 1
- text_counts: int32 [4, 2], P('group'), may hold values from 1 to 120, as said below
- time_table: bfloat16 [8, 1152], P(None, 'tensor'), may hold values from -6 to 6
- ada_weight: bfloat16 [1152, 9, 1152], P('tensor'), may hold values from -0.1875 to 0.1875
- spatial_inproj: bfloat16 [1152, 3, 1152], P(None, None, 'tensor'), may hold values from -0.1875 to 0.1875
- spatial_outproj: bfloat16 [1152, 1152], P('tensor'), may hold values from -1.5 to 1.5
- temporal_inproj: bfloat16 [1152, 3, 1152], P(None, None, 'tensor'), may hold values from -0.1875 to 0.1875
- temporal_outproj: bfloat16 [1152, 1152], P('tensor'), may hold values from -0.25 to 0.25
- caption_proj: bfloat16 [4096, 1152], P(None, 'tensor'), may hold values from -0.09375 to 0.09375
- cross_gain: bfloat16 [1152], replicated, may hold values from 0.5 to 1.5
- cross_query: bfloat16 [1152, 1152], P(None, 'tensor'), may hold values from -0.1875 to 0.1875
- cross_keyval: bfloat16 [1152, 2, 1152], P(None, None, 'tensor'), may hold values from -0.1875 to 0.1875
- cross_outproj: bfloat16 [1152, 1152], P('tensor'), may hold values from -1 to 1
- mlp_up: bfloat16 [1152, 4608], P(None, 'tensor'), may hold values from -0.1875 to 0.1875
- mlp_down: bfloat16 [4608, 1152], P('tensor'), may hold values from -0.09375 to 0.09375
- cotangent: bfloat16 [4, 4, 256, 1152], P('group', 'frame', 'tensor'), may hold values from -6 to 6
Outputs:
- output: bfloat16 [4, 4, 256, 1152], P('group', 'frame', 'tensor')
- grad_latent: bfloat16 [4, 4, 256, 1152], P('group', 'frame', 'tensor')
- grad_time_table: float32 [8, 1152], P(None, 'tensor')
- grad_ada_weight: float32 [1152, 9, 1152], P('tensor', None, ('group', 'frame'))
- grad_spatial_inproj: float32 [1152, 3, 1152], P(('group', 'frame'), None, 'tensor')
- grad_spatial_outproj: float32 [1152, 1152], P('tensor', ('group', 'frame'))
- grad_temporal_inproj: float32 [1152, 3, 1152], P(('group', 'frame'), None, 'tensor')
- grad_temporal_outproj: float32 [1152, 1152], P('tensor', ('group', 'frame'))
- grad_caption_proj: float32 [4096, 1152], P(('group', 'frame'), 'tensor')
- grad_cross_gain: float32 [1152], replicated
- grad_cross_query: float32 [1152, 1152], P(('group', 'frame'), 'tensor')
- grad_cross_keyval: float32 [1152, 2, 1152], P(('group', 'frame'), None, 'tensor')
- grad_cross_outproj: float32 [1152, 1152], P('tensor', ('group', 'frame'))
- grad_mlp_up: float32 [1152, 4608], P(('group', 'frame'), 'tensor')
- grad_mlp_down: float32 [4608, 1152], P('tensor', ('group', 'frame'))
The draws below stay inside these ranges and needn't reach their ends.
Inputs may be any that keep to these rules, and one draw needn't show every extreme that they name: `clip_ids`: along each group's frames the clip numbers start at 0 and rise by one at each clip boundary; clips hold 8 consecutive frames except the first and the last, which may be shorter; in one group all frames form a single clip. `text_counts`: the first caption of every group has all 120 tokens valid.
All inputs are finite; a program needn't handle non-finite values. No bound on the sum of `window_mask` on one device may be relied on, other than what follows from the above.
Results may differ from the reference program's by a relative error of at most 0.03.
Values may be sent and summed in bfloat16 or wider, within the bound.
A program may use at most 256 MiB of HBM per device.

```python
import jax
import jax.numpy as jnp
from jax import lax

D = 1152
HEADS = 16
HD = 72
FF = 4608
TD = 4096
TXT = 120
P_SIZE = 256
CLIP = 8
WIN = 4
NB = 8
G = 4
NF = 4
NCLIP = 2


def draw_clip_ids(key, part):
    key = jax.random.fold_in(key, 11)
    whole_group = jax.random.randint(jax.random.fold_in(key, 1), (), 0, G)
    offsets = jax.random.randint(jax.random.fold_in(key, 2), (G,), 1, CLIP)
    groups = jnp.arange(G)
    offsets = jnp.where(groups == (whole_group + 1) % G, CLIP - 1, offsets)
    clip_number = (jnp.arange(NF)[None, :] + offsets[:, None]) // CLIP
    return jnp.where(groups[:, None] == whole_group, 0, clip_number).astype(jnp.int32)


def draw_text_counts(key, part):
    key = jax.random.fold_in(key, 23)
    token_counts = jax.random.randint(key, (G, NCLIP), 1, TXT + 1)
    return token_counts.at[:, 0].set(TXT).astype(jnp.int32)


def place_ends(drawn, stream_key, smallest, high):
    longest = drawn.shape.index(max(drawn.shape))
    spots = []
    for shift in (0, 1):
        where = [jax.random.randint(jax.random.fold_in(stream_key, axis), (), 0, length) for axis, length in enumerate(drawn.shape)]
        where[longest] = (where[longest] + shift) % drawn.shape[longest]
        spots.append(tuple(where))
    return drawn.at[spots[0]].set(smallest).at[spots[1]].set(high)


def steps_of(stream_key, dims, split, smallest, largest):
    def one(dim, parts):
        draws = jax.random.uniform(jax.random.fold_in(jax.random.fold_in(stream_key, 6), dim), (parts,), jnp.float32, smallest / len(split), largest / len(split))
        return jnp.repeat(jnp.exp(draws), dims[dim] // parts).reshape((-1,) + (1,) * (len(dims) - dim - 1))

    level = one(*split[0])
    for cut in split[1:]:
        level = level * one(*cut)
    return level


def scatter_about(key, dims, deviation, limit, shards=(), held_as=jnp.bfloat16):
    values = deviation * jax.random.normal(key, dims, jnp.float32)
    if shards:
        values = values * steps_of(key, dims, shards, -0.22, 0.18)
    return jnp.clip(values, -limit, limit).astype(held_as)


def setup_inputs(seed: int = 0) -> dict:
    key_of = jax.random.split(jax.random.key(seed), 21)
    return {
        "latent": scatter_about(key_of[0], (G, NF, P_SIZE, D), 1.0, 6.0, ((0, 4), (1, 2), (2, 4))),
        "captions": scatter_about(key_of[1], (G, NCLIP, TXT, TD), 1.0, 6.0, ((0, 4),)),
        "bucket": place_ends(jax.random.randint(key_of[2], (G,), 0, NB), jax.random.fold_in(key_of[2], 1), 0, NB - 1).astype(jnp.int32),
        "clip_ids": draw_clip_ids(jax.random.fold_in(key_of[20], 71), 0),
        "window_mask": place_ends((jax.random.randint(key_of[4], (G, NF, WIN), 0, 4) < 3).astype(jnp.int32), jax.random.fold_in(key_of[4], 1), 0, 1),
        "text_counts": draw_text_counts(jax.random.fold_in(key_of[20], 71), 0),
        "time_table": scatter_about(key_of[6], (NB, D), 1.0, 6.0, ((1, 4),)),
        "ada_weight": scatter_about(key_of[7], (D, 9, D), D ** -0.5, 0.1875, ((0, 4),)),
        "spatial_inproj": scatter_about(key_of[8], (D, 3, D), D ** -0.5, 0.1875, ((2, 4),)),
        "spatial_outproj": scatter_about(key_of[9], (D, D), (D // 64) ** -0.5, 1.5, ((0, 4),)),
        "temporal_inproj": scatter_about(key_of[10], (D, 3, D), D ** -0.5, 0.1875, ((2, 4),)),
        "temporal_outproj": scatter_about(key_of[11], (D, D), (D // 2) ** -0.5, 0.25, ((0, 4),)),
        "caption_proj": scatter_about(key_of[12], (TD, D), TD ** -0.5, 0.09375, ((1, 4),)),
        "cross_gain": jnp.clip(1.0 + 0.1 * jax.random.normal(key_of[13], (D,), jnp.float32), 0.5, 1.5).astype(jnp.bfloat16),
        "cross_query": scatter_about(key_of[14], (D, D), D ** -0.5, 0.1875, ((1, 4),)),
        "cross_keyval": scatter_about(key_of[15], (D, 2, D), D ** -0.5, 0.1875, ((2, 4),)),
        "cross_outproj": scatter_about(key_of[16], (D, D), (D // 32) ** -0.5, 1.0, ((0, 4),)),
        "mlp_up": scatter_about(key_of[17], (D, FF), D ** -0.5, 0.1875, ((1, 4),)),
        "mlp_down": scatter_about(key_of[18], (FF, D), FF ** -0.5, 0.09375, ((0, 4),)),
        "cotangent": scatter_about(key_of[19], (G, NF, P_SIZE, D), 1.0, 6.0, ((0, 4), (1, 2), (2, 4))),
    }


@jax.custom_vjp
def low(v):
    return lax.optimization_barrier(v.astype(jnp.bfloat16)).astype(jnp.float32)

@jax.custom_vjp
def low_back(v):
    return v

def low_keep(v):
    return (low(v), None)

def low_pass(kept, grad):
    return (grad,)

def back_keep(v):
    return (v, None)

def back_low(kept, grad):
    return (low(grad),)
low.defvjp(low_keep, low_pass)
low_back.defvjp(back_keep, back_low)
EPSILON = 1e-06
HIGHEST = lax.Precision.HIGHEST
NEGATIVE = -1e+30

def layer_norm(values):
    centred = values - lax.optimization_barrier(jnp.mean(values, axis=-1, keepdims=True))
    return centred * lax.rsqrt(lax.optimization_barrier(jnp.mean(centred * centred, axis=-1, keepdims=True)) + EPSILON)

def swish_act(values):
    return values / (1.0 + jnp.exp(-values))

def gelu_tanh(values):
    return 0.5 * values * (1.0 + jnp.tanh(0.7978845608028654 * (values + 0.044715 * values * values * values)))

def softmax_last(scores):
    shifted = jnp.exp(scores - lax.optimization_barrier(jnp.max(scores, axis=-1, keepdims=True)))
    return shifted / lax.optimization_barrier(jnp.sum(shifted, axis=-1, keepdims=True))

def split_heads(values):
    return values.reshape(values.shape[:-1] + (HEADS, HD))

def forward(residual, weights, caption_rows, bucket_one, clip_row, window_row, counts_row):
    time_table, ada_weight, spatial_inproj, spatial_outproj, temporal_inproj, temporal_outproj, caption_proj, cross_gain, cross_query, cross_keyval, cross_outproj, mlp_up, mlp_down = weights
    score_scale = HD ** (-0.5)
    activated = low(swish_act(time_table[bucket_one]))
    modulation = jnp.einsum('c,ckd->kd', activated, ada_weight, precision=HIGHEST)

    def modulate(values, which):
        return layer_norm(values) * (1.0 + modulation[3 * which + 1]) + modulation[3 * which]
    spatial_normed = low(modulate(residual, 0))
    spatial_packed = low(low_back(jnp.einsum('fpd,dkc->fpkc', spatial_normed, spatial_inproj, precision=HIGHEST)))
    spatial_query = split_heads(spatial_packed[:, :, 0])
    spatial_keys = split_heads(spatial_packed[:, :, 1])
    spatial_values = split_heads(spatial_packed[:, :, 2])
    spatial_scores = low_back(score_scale * jnp.einsum('fphe,fqhe->fhpq', spatial_query, spatial_keys, precision=HIGHEST))
    spatial_probs = low(softmax_last(spatial_scores))
    spatial_heads = low(low_back(jnp.einsum('fhpq,fqhe->fphe', spatial_probs, spatial_values, precision=HIGHEST)))
    spatial_out = low_back(jnp.einsum('fpc,cd->fpd', spatial_heads.reshape(NF, P_SIZE, D), spatial_outproj, precision=HIGHEST))
    after_spatial = residual + modulation[2] * spatial_out
    temporal_normed = low(modulate(after_spatial, 1))
    temporal_packed = low(low_back(jnp.einsum('fpd,dkc->fpkc', temporal_normed, temporal_inproj, precision=HIGHEST)))
    temporal_query = split_heads(temporal_packed[:, :, 0])
    temporal_keys = split_heads(jnp.pad(temporal_packed[:, :, 1], ((2, 1), (0, 0), (0, 0))))
    temporal_values = split_heads(jnp.pad(temporal_packed[:, :, 2], ((2, 1), (0, 0), (0, 0))))
    clip_padded = jnp.pad(clip_row, (2, 1), constant_values=-1)
    score_list = []
    for offset in range(WIN):
        allowed = (clip_padded[offset:offset + NF] == clip_row) & ((window_row[:, offset] == 1) | (offset == 2))
        raw_scores = score_scale * lax.optimization_barrier(jnp.sum(temporal_query * temporal_keys[offset:offset + NF], axis=-1))
        score_list.append(jnp.where(allowed[:, None, None], raw_scores, NEGATIVE))
    temporal_probs = softmax_last(jnp.stack(score_list, axis=-1))
    temporal_mixed = temporal_probs[..., 0, None] * temporal_values[0:NF]
    for offset in range(1, WIN):
        temporal_mixed = temporal_mixed + temporal_probs[..., offset, None] * temporal_values[offset:offset + NF]
    temporal_heads = low(low_back(temporal_mixed))
    temporal_out = low_back(jnp.einsum('fpc,cd->fpd', temporal_heads.reshape(NF, P_SIZE, D), temporal_outproj, precision=HIGHEST))
    after_temporal = after_spatial + modulation[5] * temporal_out
    text_rows = low(jnp.einsum('ntc,cd->ntd', caption_rows, caption_proj, precision=HIGHEST))
    cross_normed = low(layer_norm(after_temporal) * cross_gain)
    cross_packed = low(low_back(jnp.einsum('fpd,dc->fpc', cross_normed, cross_query, precision=HIGHEST)))
    text_packed = low(jnp.einsum('ntd,dkc->ntkc', text_rows, cross_keyval, precision=HIGHEST))
    text_keys = split_heads(text_packed[:, :, 0].reshape(NCLIP * TXT, D))
    text_values = split_heads(text_packed[:, :, 1].reshape(NCLIP * TXT, D))
    slot_index = jnp.arange(NCLIP * TXT)
    key_valid = (clip_row[:, None] == (slot_index // TXT)[None, :]) & (slot_index % TXT < jnp.repeat(counts_row, TXT))[None, :]
    cross_scores = low_back(score_scale * jnp.einsum('fphe,mhe->fhpm', split_heads(cross_packed), text_keys, precision=HIGHEST))
    cross_scores = jnp.where(key_valid[:, None, None, :], cross_scores, NEGATIVE)
    cross_probs = low(softmax_last(cross_scores))
    cross_heads = low(low_back(jnp.einsum('fhpm,mhe->fphe', cross_probs, text_values, precision=HIGHEST)))
    cross_out = low_back(jnp.einsum('fpc,cd->fpd', cross_heads.reshape(NF, P_SIZE, D), cross_outproj, precision=HIGHEST))
    after_cross = after_temporal + cross_out
    mlp_normed = low(modulate(after_cross, 2))
    mlp_inner = low_back(jnp.einsum('fpd,dh->fph', mlp_normed, mlp_up, precision=HIGHEST))
    mlp_active = low(gelu_tanh(mlp_inner))
    mlp_out = low_back(jnp.einsum('fph,hd->fpd', mlp_active, mlp_down, precision=HIGHEST))
    return after_cross + modulation[8] * mlp_out

def reference(latent, captions, bucket, clip_ids, window_mask, text_counts, time_table, ada_weight, spatial_inproj, spatial_outproj, temporal_inproj, temporal_outproj, caption_proj, cross_gain, cross_query, cross_keyval, cross_outproj, mlp_up, mlp_down, cotangent):
    weights = tuple((item.astype(jnp.float32) for item in (time_table, ada_weight, spatial_inproj, spatial_outproj, temporal_inproj, temporal_outproj, caption_proj, cross_gain, cross_query, cross_keyval, cross_outproj, mlp_up, mlp_down)))

    def one_group(totals, items):
        residual, caption_rows, bucket_one, clip_row, window_row, counts_row, cotangent_one = items
        caption_wide = caption_rows.astype(jnp.float32)

        def run(residual_in, params):
            return forward(residual_in, params, caption_wide, bucket_one, clip_row, window_row, counts_row)
        result, pull = jax.vjp(run, residual.astype(jnp.float32), weights)
        grad_residual, grad_weights = pull(cotangent_one.astype(jnp.float32))
        totals = tuple((first + second for first, second in zip(totals, grad_weights)))
        return (totals, (result.astype(jnp.bfloat16), grad_residual.astype(jnp.bfloat16)))
    start_totals = tuple((jnp.zeros_like(item) for item in weights))
    totals, (output, grad_latent) = lax.scan(one_group, start_totals, (latent, captions, bucket, clip_ids, window_mask, text_counts, cotangent))
    return (output, grad_latent, totals[0], totals[1], totals[2], totals[3], totals[4], totals[5], totals[6], totals[7], totals[8], totals[9], totals[10], totals[11], totals[12])
```

```python
import functools

import jax
import jax.numpy as jnp
from jax import lax
from jax.experimental import pallas as pl
from jax.experimental.pallas import tpu as pltpu
from jax.sharding import PartitionSpec as P

HD = 72
WIN = 4
EPSILON = 1e-06
HIGHEST = lax.Precision.HIGHEST
NEGATIVE = -1e30
WIDE = jnp.float32
NARROW = jnp.bfloat16
GROUP, FRAME, LINE = "group", "frame", "tensor"
BOTH = (GROUP, FRAME)
MESH = pl.DeviceIdType.MESH
CHUNKS = 16
LAG = 2
VMEM_LIMIT = 48 * 2**20


def swish_act(values):
    return values / (1.0 + jnp.exp(-values))


def gelu_tanh(values):
    return (
        0.5
        * values
        * (1.0 + jnp.tanh(0.7978845608028654 * (values + 0.044715 * values * values * values)))
    )


def dot(first, second, contract_first, contract_second):
    return lax.dot_general(
        first, second, (((contract_first,), (contract_second,)), ((), ())), preferred_element_type=WIDE
    )


def split_heads(values):
    return values.reshape(values.shape[:-1] + (values.shape[-1] // HD, HD))


def split_pair(values):
    high_part = values.astype(NARROW)
    rest_part = (values - high_part.astype(WIDE)).astype(NARROW)
    return (high_part, rest_part)


def norm_parts(values):
    centred = values - jnp.mean(values, axis=-1, keepdims=True)
    spread = lax.rsqrt(jnp.mean(centred * centred, axis=-1, keepdims=True) + EPSILON)
    return centred * spread, spread


def remote(source, target, send_sem, recv_sem, where):
    return pltpu.make_async_remote_copy(
        src_ref=source,
        dst_ref=target,
        send_sem=send_sem,
        recv_sem=recv_sem,
        device_id=where,
        device_id_type=MESH,
    )


def greet_line(place, count):
    barrier = pltpu.get_barrier_semaphore()

    @pl.when(place > 0)
    def _():
        pl.semaphore_signal(barrier, inc=1, device_id={LINE: place - 1}, device_id_type=MESH)

    @pl.when(place < count - 1)
    def _():
        pl.semaphore_signal(barrier, inc=1, device_id={LINE: place + 1}, device_id_type=MESH)

    pl.semaphore_wait(
        barrier, (place > 0).astype(jnp.int32) + (place < count - 1).astype(jnp.int32)
    )


def line_sum(count, place, part_ref, land, cross, stage, total, sems, consume):
    in_send, land_recv, cross_recv, out_send, out_recv = sems
    depth = part_ref.shape[0] // CHUNKS
    half = count // 2
    left = place < half
    level = jnp.where(left, place, count - 1 - place)
    inner = jnp.where(left, place + 1, place - 1)
    outer = jnp.where(left, place - 1, place + 1)
    is_end, is_middle = level == 0, level == half - 1

    def rows_of(chunk):
        return pl.ds(pl.multiple_of(chunk * depth, depth), depth)

    def inward(chunk):
        rows = rows_of(chunk)
        return remote(stage.at[rows], land.at[rows], in_send.at[chunk], land_recv.at[chunk], {LINE: inner})

    def across(chunk):
        rows = rows_of(chunk)
        return remote(stage.at[rows], cross.at[rows], in_send.at[chunk], cross_recv.at[chunk], {LINE: inner})

    def outward(chunk):
        rows = rows_of(chunk)
        return remote(total.at[rows], total.at[rows], out_send.at[chunk], out_recv.at[chunk], {LINE: outer})

    def send_in(chunk):
        @pl.when(is_middle)
        def _():
            across(chunk).start()

        @pl.when(jnp.logical_not(is_middle))
        def _():
            inward(chunk).start()

    def gather_in(chunk):
        rows = rows_of(chunk)
        inward(chunk).wait_recv()
        stage[rows] = (part_ref[rows].astype(WIDE) + land[rows].astype(WIDE)).astype(NARROW)
        send_in(chunk)

    def finish(chunk):
        rows = rows_of(chunk)

        @pl.when(is_middle)
        def _():
            across(chunk).wait_recv()
            total[rows] = (stage[rows].astype(WIDE) + cross[rows].astype(WIDE)).astype(NARROW)

        @pl.when(jnp.logical_not(is_middle))
        def _():
            outward(chunk).wait_recv()

        @pl.when(jnp.logical_not(is_end))
        def _():
            outward(chunk).start()

        consume(rows)

    def begin(chunk, carry):
        rows = rows_of(chunk)
        stage[rows] = part_ref[rows]
        send_in(chunk)
        return carry

    def step(number, carry):
        @pl.when(jnp.logical_not(is_end) & (number < CHUNKS))
        def _():
            gather_in(number)

        @pl.when(number >= LAG)
        def _():
            finish(number - LAG)

        return carry

    @pl.when(is_end)
    def _():
        lax.fori_loop(0, CHUNKS, begin, 0)

    lax.fori_loop(0, CHUNKS + LAG, step, 0)

    def settle(chunk, carry):
        @pl.when(is_middle)
        def _():
            across(chunk).wait_send()

        @pl.when(jnp.logical_not(is_middle))
        def _():
            inward(chunk).wait_send()

        @pl.when(jnp.logical_not(is_end))
        def _():
            outward(chunk).wait_send()

        return carry

    lax.fori_loop(0, CHUNKS, settle, 0)


def forward_kernel(
    count, part_ref, base_ref, rows_ref, out_ref, next_ref, normed_ref, land, cross, stage, *sems
):
    place = lax.axis_index(LINE)
    greet_line(place, count)
    gate, gain, shift = (rows_ref[i : i + 1] for i in range(3))

    def consume(rows):
        moved = base_ref[rows] + gate * out_ref[rows].astype(WIDE)
        next_ref[rows] = moved
        normed_ref[rows] = (norm_parts(moved)[0] * gain + shift).astype(NARROW)

    line_sum(count, place, part_ref, land, cross, stage, out_ref, sems, consume)


def backward_kernel(
    count, part_ref, base_ref, grad_ref, below_ref, rows_ref,
    moved_ref, low_ref, sums_ref, total, land, cross, stage, tally, *sems
):
    place = lax.axis_index(LINE)
    greet_line(place, count)
    gain, gate = (rows_ref[i : i + 1] for i in range(2))
    tally[...] = jnp.zeros_like(tally)

    def consume(rows):
        grads = total[rows].astype(WIDE)
        normal, spread = norm_parts(base_ref[rows])
        scaled = grads * gain
        moved = grad_ref[rows] + spread * (
            scaled
            - jnp.mean(scaled, axis=-1, keepdims=True)
            - normal * jnp.mean(scaled * normal, axis=-1, keepdims=True)
        )
        moved_ref[rows] = moved
        low_ref[rows] = (gate * moved).astype(NARROW)
        for i, terms in enumerate((grads, grads * normal, moved * below_ref[rows].astype(WIDE))):
            tally[i] += jnp.sum(terms.reshape(-1, 8, terms.shape[-1]), axis=0)

    line_sum(count, place, part_ref, land, cross, stage, total, sems, consume)
    sums_ref[...] = jnp.zeros_like(sums_ref)
    for i in range(3):
        sums_ref[i : i + 1] = jnp.sum(tally[i], axis=0, keepdims=True)


def vmem(count):
    return [pl.BlockSpec(memory_space=pltpu.VMEM)] * count


def line_sems():
    return [pltpu.SemaphoreType.DMA((CHUNKS,))] * 5


def call_forward(count, part, base, rows):
    shape = part.shape
    return pl.pallas_call(
        functools.partial(forward_kernel, count),
        out_shape=(
            jax.ShapeDtypeStruct(shape, NARROW),
            jax.ShapeDtypeStruct(shape, WIDE),
            jax.ShapeDtypeStruct(shape, NARROW),
        ),
        in_specs=vmem(3),
        out_specs=tuple(vmem(3)),
        scratch_shapes=[pltpu.VMEM(shape, NARROW)] * 3 + line_sems(),
        compiler_params=pltpu.CompilerParams(
            collective_id=1, has_side_effects=True, vmem_limit_bytes=VMEM_LIMIT
        ),
        name="forward_sum",
    )(part, base, rows)


def call_backward(count, part, base, grad, below, rows):
    shape = part.shape
    return pl.pallas_call(
        functools.partial(backward_kernel, count),
        out_shape=(
            jax.ShapeDtypeStruct(shape, WIDE),
            jax.ShapeDtypeStruct(shape, NARROW),
            jax.ShapeDtypeStruct((8, shape[1]), WIDE),
        ),
        in_specs=vmem(5),
        out_specs=tuple(vmem(3)),
        scratch_shapes=[pltpu.VMEM(shape, NARROW)] * 4
        + [pltpu.VMEM((3, 8, shape[1]), WIDE)]
        + line_sems(),
        compiler_params=pltpu.CompilerParams(
            collective_id=2, has_side_effects=True, vmem_limit_bytes=VMEM_LIMIT
        ),
        name="backward_sum",
    )(part, base, grad, below, rows)


def opening_kernel(
    count, groups, frames_axis, latent_ref, act_ref, ada_ref, captions_ref,
    base_ref, normed_ref, mods_ref, spread_ref,
    land, ada, mine, others,
    up_send, down_send, land_recv, ada_sem, mods_send, mods_recv, cap_send, cap_recv, cap_local,
):
    place = lax.axis_index(LINE)
    group = lax.axis_index(GROUP)
    here = lax.axis_index(FRAME)
    last = count - 1
    width = spread_ref.shape[2]
    parts = ada_ref.shape[0]
    share = latent_ref.shape[1]

    loads = [pltpu.make_async_copy(ada_ref.at[k], ada.at[k], ada_sem.at[k]) for k in range(parts)]
    for load in loads:
        load.start()

    barrier = pltpu.get_barrier_semaphore()
    for ahead in range(1, count):
        pl.semaphore_signal(
            barrier, inc=1, device_id={LINE: lax.rem(place + ahead, count)}, device_id_type=MESH
        )
    for ahead in range(1, groups):
        pl.semaphore_signal(
            barrier, inc=1, device_id={GROUP: lax.rem(group + ahead, groups)}, device_id_type=MESH
        )
    pl.semaphore_wait(barrier, count - 1 + groups - 1)

    def shift(owner, up):
        to = place + 1 if up else place - 1
        return remote(
            land.at[owner], land.at[owner], (up_send if up else down_send).at[owner], land_recv.at[owner], {LINE: to}
        )

    land[place] = latent_ref[...]

    @pl.when(place < last)
    def _():
        shift(place, True).start()

    @pl.when(place > 0)
    def _():
        shift(place, False).start()

    def caption_block(to):
        if len(captions_ref.shape) == 3:
            return captions_ref.at[to]
        first = pl.multiple_of((to * frames_axis + here) * width, width)
        return captions_ref.at[:, pl.ds(first, width)]

    def caption_copy(ahead):
        to = lax.rem(group + ahead, groups)
        return remote(
            caption_block(to),
            spread_ref.at[group],
            cap_send.at[ahead],
            cap_recv.at[ahead],
            {GROUP: to},
        )

    own_caption = pltpu.make_async_copy(caption_block(group), spread_ref.at[group], cap_local)
    own_caption.start()
    for ahead in range(1, groups):
        caption_copy(ahead).start()

    def arrive(distance):
        @pl.when(place >= distance)
        def _():
            shift(place - distance, True).wait_recv()

            @pl.when(place < last)
            def _():
                shift(place - distance, True).start()

        @pl.when(place + distance <= last)
        def _():
            shift(place + distance, False).wait_recv()

            @pl.when(place > 0)
            def _():
                shift(place + distance, False).start()

    def weigh(k):
        loads[k].wait()
        product = dot(act_ref[...], ada[k], 1, 0)
        mine[k : k + 1] = product[0:1]

    def mods_copy(ahead):
        return remote(
            mine, others.at[place], mods_send.at[ahead], mods_recv.at[ahead], {LINE: lax.rem(place + ahead, count)}
        )

    mine[...] = jnp.zeros_like(mine)
    cut = parts // 2 + 1
    for k in range(cut):
        weigh(k)
    arrive(1)
    for k in range(cut, parts):
        weigh(k)
    for ahead in range(1, count):
        mods_copy(ahead).start()
    others[place] = mine[...]
    for distance in range(2, count - 1):
        arrive(distance)
    for ahead in range(1, count):
        mods_copy(ahead).wait_recv()
    mods = others[0]
    for i in range(1, count):
        mods = mods + others[i]
    mods_ref[...] = mods
    gain = 1.0 + mods[1:2]
    shift_row = mods[0:1]

    def norm_owner(owner):
        for f in range(latent_ref.shape[0]):
            values = land[owner, f].astype(WIDE)
            rows = pl.ds(pl.multiple_of(owner * share, share), share)
            base_ref[f, rows] = values
            normed_ref[f, rows] = (norm_parts(values)[0] * gain + shift_row).astype(NARROW)

    def near(distance):
        @pl.when(place >= distance)
        def _():
            norm_owner(place - distance)

        @pl.when(place + distance <= last)
        def _():
            norm_owner(place + distance)

    norm_owner(place)
    for distance in range(1, count - 1):
        near(distance)
    if count > 2:
        arrive(count - 1)
    near(count - 1)

    for owner in range(count):

        @pl.when((place < last) & (owner <= place))
        def _():
            shift(owner, True).wait_send()

        @pl.when((place > 0) & (owner >= place))
        def _():
            shift(owner, False).wait_send()

    for ahead in range(1, count):
        mods_copy(ahead).wait_send()
    for ahead in range(1, groups):
        caption_copy(ahead).wait_send()
        caption_copy(ahead).wait_recv()
    own_caption.wait()


def call_opening(count, groups, frames_axis, latent, act, ada, captions):
    frames, share, features = latent.shape
    parts = ada.shape[0]
    length, text_width = captions.shape
    width = text_width // (groups * frames_axis)
    if width % 128:
        blocks = captions.reshape(length, groups, frames_axis, width)
        captions = jnp.transpose(
            lax.dynamic_index_in_dim(blocks, lax.axis_index(FRAME), 2, keepdims=False), (1, 0, 2)
        )
    full = (frames, share * count, features)
    dma = pltpu.SemaphoreType.DMA
    anywhere = pl.BlockSpec(memory_space=pl.ANY)
    return pl.pallas_call(
        functools.partial(opening_kernel, count, groups, frames_axis),
        out_shape=(
            jax.ShapeDtypeStruct(full, WIDE),
            jax.ShapeDtypeStruct(full, NARROW),
            jax.ShapeDtypeStruct((16, features), WIDE),
            jax.ShapeDtypeStruct((groups, length, width), NARROW),
        ),
        in_specs=vmem(2) + [anywhere] * 2,
        out_specs=tuple(vmem(3) + [anywhere]),
        scratch_shapes=[
            pltpu.VMEM((count, frames, share, features), NARROW),
            pltpu.VMEM(ada.shape, NARROW),
            pltpu.VMEM((16, features), WIDE),
            pltpu.VMEM((count, 16, features), WIDE),
            dma((count,)),
            dma((count,)),
            dma((count,)),
            dma((parts,)),
            dma((count,)),
            dma((count,)),
            dma((groups,)),
            dma((groups,)),
            dma,
        ],
        compiler_params=pltpu.CompilerParams(
            collective_id=3, has_side_effects=True, vmem_limit_bytes=VMEM_LIMIT
        ),
        name="opening",
    )(latent, act, ada, captions)


def attend_scores(query, keys, key_valid):
    raw_scores = HD ** (-0.5) * jnp.einsum("fphe,fqhe->fhpq", query, keys, preferred_element_type=WIDE)
    if key_valid is None:
        return raw_scores
    return jnp.where(key_valid[:, None, None, :], raw_scores, NEGATIVE)


def attend_forward(query, keys, values, key_valid):
    scores = attend_scores(query, keys, key_valid)
    row_max = jnp.max(scores, axis=-1, keepdims=True)
    shifted = jnp.exp(scores - row_max)
    row_total = jnp.sum(shifted, axis=-1, keepdims=True)
    probs_low = (shifted / row_total).astype(NARROW)
    heads_out = jnp.einsum("fhpq,fqhe->fphe", probs_low, values, preferred_element_type=WIDE)
    return (heads_out.astype(NARROW), row_max + jnp.log(row_total))


def attend_backward(query, keys, values, key_valid, log_total, grad_out):
    probs = jnp.exp(attend_scores(query, keys, key_valid) - log_total)
    grad_probs = jnp.einsum("fphe,fqhe->fhpq", grad_out, values, preferred_element_type=WIDE)
    grad_values = jnp.einsum("fhpq,fphe->fqhe", probs.astype(NARROW), grad_out, preferred_element_type=WIDE)
    grad_scores = probs * (grad_probs - jnp.sum(grad_probs * probs, axis=-1, keepdims=True))
    grad_scores = grad_scores.astype(NARROW)
    grad_query = HD ** (-0.5) * jnp.einsum("fhpq,fqhe->fphe", grad_scores, keys, preferred_element_type=WIDE)
    grad_keys = HD ** (-0.5) * jnp.einsum("fhpq,fphe->fqhe", grad_scores, query, preferred_element_type=WIDE)
    return (grad_query, grad_keys, grad_values)


def over_heads(first, second):
    return jnp.einsum("fphe,fphe->fhp", first, second, precision=HIGHEST, preferred_element_type=WIDE)


def by_heads(weights, values):
    return jnp.einsum("fhp,fphe->fphe", weights, values, precision=HIGHEST)


def temporal_weights(query, keys, allowed, frames):
    score_list = []
    for offset in range(WIN):
        raw_scores = HD ** (-0.5) * jnp.einsum(
            "fphe,fphe->fhp", query, keys[offset : offset + frames], preferred_element_type=WIDE
        )
        score_list.append(jnp.where(allowed[offset][:, None, None], raw_scores, NEGATIVE))
    scores = jnp.stack(score_list)
    shifted = jnp.exp(scores - jnp.max(scores, axis=0, keepdims=True))
    return shifted / jnp.sum(shifted, axis=0, keepdims=True)


def temporal_mix(probs, values, frames):
    values_wide = values.astype(WIDE)
    mixed = by_heads(probs[0], values_wide[0:frames])
    for offset in range(1, WIN):
        mixed = mixed + by_heads(probs[offset], values_wide[offset : offset + frames])
    return mixed


def temporal_backward(query, keys, values, probs, grad_out, frames):
    query_wide, keys_wide = query.astype(WIDE), keys.astype(WIDE)
    values_wide, grad_wide = values.astype(WIDE), grad_out.astype(WIDE)
    grad_probs = jnp.stack(
        [over_heads(grad_wide, values_wide[offset : offset + frames]) for offset in range(WIN)]
    )
    grad_scores = probs * (grad_probs - jnp.sum(grad_probs * probs, axis=0, keepdims=True))
    grad_query = jnp.zeros(query.shape, WIDE)
    for offset in range(WIN):
        grad_query = grad_query + HD ** (-0.5) * by_heads(
            grad_scores[offset], keys_wide[offset : offset + frames]
        )

    def near_sums(weights, sources):
        found = []
        for cell in range(frames + WIN - 1):
            terms = [
                by_heads(weights[offset][cell - offset : cell - offset + 1], sources[cell - offset : cell - offset + 1])
                for offset in range(WIN)
                if 0 <= cell - offset < frames
            ]
            found.append(sum(terms[1:], terms[0]))
        return found

    grad_keys = near_sums(HD ** (-0.5) * grad_scores, query_wide)
    return (grad_query, grad_keys, near_sums(probs, grad_wide))


def to_next(cells):
    ends = lax.axis_size(FRAME) - 1
    return lax.ppermute(cells, FRAME, [(i, i + 1) for i in range(ends)])


def to_previous(cells):
    ends = lax.axis_size(FRAME) - 1
    return lax.ppermute(cells, FRAME, [(i + 1, i) for i in range(ends)])


def sum_matrix_grads(pieces):
    packed = jnp.concatenate([piece.astype(NARROW) for piece in pieces], axis=1)
    summed = lax.psum_scatter(packed, BOTH, scatter_dimension=0, tiled=True).astype(WIDE)
    found, start = [], 0
    for piece in pieces:
        found.append(summed[:, start : start + piece.shape[1]])
        start += piece.shape[1]
    return found


def per_device(
    latent, captions, bucket, clip_ids, window_mask, text_counts, time_table, ada_weight,
    spatial_inproj, spatial_outproj, temporal_inproj, temporal_outproj, caption_proj, cross_gain,
    cross_query, cross_keyval, cross_outproj, mlp_up, mlp_down, cotangent,
):
    count, groups, frames_axis = (lax.axis_size(axis) for axis in (LINE, GROUP, FRAME))
    place = lax.axis_index(LINE)
    frames, share, features = latent.shape[1:]
    patches = share * count
    tokens = frames * patches
    local = spatial_outproj.shape[0]
    clip_count, text_length, text_width = captions.shape[1:]
    slots = clip_count * text_length

    def flat(values):
        return values.reshape(tokens, -1)

    def grid(values):
        return values.reshape(frames, patches, -1)

    def heads(values):
        return split_heads(grid(values))

    def own(values):
        return lax.dynamic_slice_in_dim(grid(values), place * share, share, axis=1)

    spatial_in, temporal_in, keyval_in = (
        jnp.transpose(w, (1, 2, 0)).reshape(-1, features)
        for w in (spatial_inproj, temporal_inproj, cross_keyval)
    )
    query_in = cross_query.T

    chosen = (jnp.arange(time_table.shape[0]) == bucket[0]).astype(WIDE)
    cond_row = jnp.sum(chosen[:, None] * time_table.astype(WIDE), axis=0)
    act_low = swish_act(cond_row).astype(NARROW)
    caption_here = captions[0].reshape(slots, text_width)
    base_grid, normed_grid, mods, caption_share = call_opening(
        count, groups, frames_axis, latent[0], jnp.broadcast_to(act_low[None], (16, local)),
        jnp.transpose(ada_weight, (1, 0, 2)), caption_here,
    )
    base_zero, spatial_hidden = flat(base_grid), flat(normed_grid)
    cotangent_full = flat(lax.all_gather(cotangent[0], LINE, axis=1, tiled=True))

    text_part = dot(caption_here, caption_proj, 1, 0).astype(NARROW)
    text_rows = lax.all_gather(text_part, LINE, axis=1, tiled=True)

    def rows_of(*rows):
        filled = [jnp.zeros((features,), WIDE)] * (8 - len(rows))
        return jnp.stack(list(rows) + filled)

    spatial_packed = dot(spatial_hidden, spatial_in, 1, 1).astype(NARROW)
    spatial_query, spatial_keys, spatial_values = (
        heads(spatial_packed[:, i * local : (i + 1) * local]) for i in range(3)
    )
    spatial_heads, spatial_logs = attend_forward(spatial_query, spatial_keys, spatial_values, None)
    spatial_flat = flat(spatial_heads)
    spatial_out, base_one, temporal_hidden = call_forward(
        count,
        dot(spatial_flat, spatial_outproj, 1, 0).astype(NARROW),
        base_zero,
        rows_of(mods[2], 1.0 + mods[4], mods[3]),
    )

    temporal_packed = dot(temporal_hidden, temporal_in, 1, 1).astype(NARROW)
    temporal_query = heads(temporal_packed[:, 0:local])
    own_pair = grid(temporal_packed[:, local:])
    near = jnp.concatenate(
        [to_next(own_pair[frames - 2 :]), own_pair, to_previous(own_pair[0:1])], axis=0
    )
    temporal_keys = split_heads(near[:, :, 0:local])
    temporal_values = split_heads(near[:, :, local:])
    first_frame = lax.axis_index(FRAME) * frames
    clip_near = lax.dynamic_slice_in_dim(
        jnp.pad(clip_ids[0], (2, 2), constant_values=-1), first_frame, frames + 4
    )
    own_clip = clip_near[2 : 2 + frames]
    allowed = jnp.stack(
        [
            (clip_near[offset : offset + frames] == own_clip)
            & ((window_mask[0][:, offset] == 1) | (offset == 2))
            for offset in range(WIN)
        ]
    )
    temporal_probs = temporal_weights(temporal_query, temporal_keys, allowed, frames)
    temporal_flat = flat(temporal_mix(temporal_probs, temporal_values, frames).astype(NARROW))
    temporal_out, base_two, cross_hidden = call_forward(
        count,
        dot(temporal_flat, temporal_outproj, 1, 0).astype(NARROW),
        base_one,
        rows_of(mods[5], cross_gain.astype(WIDE), jnp.zeros((features,), WIDE)),
    )

    cross_packed = dot(cross_hidden, query_in, 1, 1).astype(NARROW)
    text_packed = dot(text_rows, keyval_in, 1, 1).astype(NARROW)

    def each_frame(values):
        return jnp.broadcast_to(split_heads(values)[None], (frames, slots, local // HD, HD))

    text_keys, text_values = (each_frame(text_packed[:, i * local : (i + 1) * local]) for i in range(2))
    slot_index = jnp.arange(slots)
    key_valid = (own_clip[:, None] == (slot_index // text_length)[None, :]) & (
        slot_index % text_length < jnp.repeat(text_counts[0], text_length)
    )[None, :]
    cross_queries = heads(cross_packed)
    cross_heads, cross_logs = attend_forward(cross_queries, text_keys, text_values, key_valid)
    cross_flat = flat(cross_heads)
    cross_out, base_three, mlp_hidden = call_forward(
        count,
        dot(cross_flat, cross_outproj, 1, 0).astype(NARROW),
        base_two,
        rows_of(jnp.ones((features,), WIDE), 1.0 + mods[7], mods[6]),
    )

    mlp_inner = dot(mlp_hidden, mlp_up, 1, 0)
    mlp_active, gelu_pull = jax.vjp(gelu_tanh, mlp_inner)
    mlp_low = mlp_active.astype(NARROW)
    grad_four = cotangent_full.astype(WIDE)
    grad_mlp_low = (mods[8] * grad_four).astype(NARROW)
    grad_active = dot(grad_mlp_low, mlp_down, 1, 1)
    grad_inner = gelu_pull(grad_active)[0].astype(NARROW)
    grad_three, grad_cross_low, sums_mlp = call_backward(
        count,
        dot(grad_inner, mlp_up, 1, 1).astype(NARROW),
        base_three,
        grad_four,
        cross_out,
        rows_of(1.0 + mods[7], jnp.ones((features,), WIDE)),
    )
    mlp_out = lax.psum_scatter(
        grid(dot(mlp_low, mlp_down, 1, 0).astype(NARROW)), LINE, scatter_dimension=1, tiled=True
    ).astype(WIDE)
    output = (own(base_three) + mods[8] * mlp_out).astype(NARROW)[None]
    gate_mlp_part = jnp.sum(cotangent[0].astype(WIDE) * mlp_out, axis=(0, 1))
    grad_up, grad_down = sum_matrix_grads(
        [dot(mlp_hidden, grad_inner, 0, 0), dot(grad_mlp_low, mlp_low, 0, 0)]
    )

    grad_cross_heads = dot(grad_cross_low, cross_outproj, 1, 1).astype(NARROW)
    cross_grad_query, text_grad_keys, text_grad_values = attend_backward(
        cross_queries, text_keys, text_values, key_valid, cross_logs, heads(grad_cross_heads)
    )
    grad_cross_packed = flat(cross_grad_query).astype(NARROW)
    grad_two, grad_temporal_low, sums_cross = call_backward(
        count,
        dot(grad_cross_packed, query_in, 1, 0).astype(NARROW),
        base_two,
        grad_three,
        temporal_out,
        rows_of(cross_gain.astype(WIDE), mods[5]),
    )
    grad_text_packed = jnp.concatenate(
        [jnp.sum(part, axis=0).reshape(slots, local) for part in (text_grad_keys, text_grad_values)],
        axis=1,
    )
    text_high, text_rest = split_pair(grad_text_packed)
    grad_keyval_part = dot(text_rows, text_high, 0, 0) + dot(text_rows, text_rest, 0, 0)
    text_grad_part = dot(text_high, keyval_in, 1, 0) + dot(text_rest, keyval_in, 1, 0)
    text_grad = lax.psum_scatter(text_grad_part.astype(NARROW), LINE, scatter_dimension=1, tiled=True)
    text_grad_all = lax.all_gather(text_grad, BOTH).reshape(groups, frames_axis, slots, local)
    text_grad_wide = jnp.sum(text_grad_all.astype(WIDE), axis=1).reshape(groups * slots, local)
    text_all_high, text_all_rest = split_pair(text_grad_wide)
    caption_rows = caption_share.reshape(groups * slots, -1)
    grad_caption = dot(caption_rows, text_all_high, 0, 0) + dot(caption_rows, text_all_rest, 0, 0)
    grad_query_cross, grad_outproj_cross, grad_keyval_cross = sum_matrix_grads(
        [
            dot(cross_hidden, grad_cross_packed, 0, 0),
            dot(grad_cross_low, cross_flat, 0, 0),
            grad_keyval_part,
        ]
    )

    grad_temporal_heads = dot(grad_temporal_low, temporal_outproj, 1, 1).astype(NARROW)
    temporal_grad_query, near_grad_keys, near_grad_values = temporal_backward(
        temporal_query, temporal_keys, temporal_values, temporal_probs, heads(grad_temporal_heads), frames
    )

    def joined(first, last):
        return jnp.concatenate(
            [
                jnp.concatenate([part[cell].reshape(1, patches, local) for cell in range(first, last)], axis=0)
                for part in (near_grad_keys, near_grad_values)
            ],
            axis=2,
        )

    from_next = to_previous(joined(0, 2).astype(NARROW)).astype(WIDE)
    from_previous = to_next(joined(frames + 2, frames + 3).astype(NARROW)).astype(WIDE)
    own_grads = joined(2, 2 + frames)
    own_grads = (
        own_grads
        + jnp.pad(from_next, ((frames - 2, 0), (0, 0), (0, 0)))
        + jnp.pad(from_previous, ((0, frames - 1), (0, 0), (0, 0)))
    )
    grad_temporal_packed = jnp.concatenate(
        [flat(temporal_grad_query).astype(NARROW), flat(own_grads).astype(NARROW)], axis=1
    )
    grad_one, grad_spatial_low, sums_temporal = call_backward(
        count,
        dot(grad_temporal_packed, temporal_in, 1, 0).astype(NARROW),
        base_one,
        grad_two,
        spatial_out,
        rows_of(1.0 + mods[4], mods[2]),
    )
    grad_inproj_temporal, grad_outproj_temporal = sum_matrix_grads(
        [dot(temporal_hidden, grad_temporal_packed, 0, 0), dot(grad_temporal_low, temporal_flat, 0, 0)]
    )

    grad_spatial_heads = dot(grad_spatial_low, spatial_outproj, 1, 1).astype(NARROW)
    spatial_grads = attend_backward(
        spatial_query, spatial_keys, spatial_values, None, spatial_logs, heads(grad_spatial_heads)
    )
    grad_spatial_packed = jnp.concatenate([flat(part) for part in spatial_grads], axis=1).astype(NARROW)
    grad_spatial_part = dot(grad_spatial_packed, spatial_in, 1, 0).astype(NARROW)
    grad_spatial_normed = lax.psum_scatter(
        grid(grad_spatial_part), LINE, scatter_dimension=1, tiled=True
    ).astype(WIDE)
    normal, spread = norm_parts(own(base_zero))
    scaled = grad_spatial_normed * (1.0 + mods[1])
    grad_latent = own(grad_one) + spread * (
        scaled
        - jnp.mean(scaled, axis=-1, keepdims=True)
        - normal * jnp.mean(scaled * normal, axis=-1, keepdims=True)
    )
    shift_part = jnp.sum(grad_spatial_normed, axis=(0, 1))
    scale_part = jnp.sum(grad_spatial_normed * normal, axis=(0, 1))
    grad_inproj_spatial, grad_outproj_spatial = sum_matrix_grads(
        [dot(spatial_hidden, grad_spatial_packed, 0, 0), dot(grad_spatial_low, spatial_flat, 0, 0)]
    )

    shift_spatial, scale_spatial, gate_mlp = lax.psum(
        jnp.stack([shift_part, scale_part, gate_mlp_part]), LINE
    )
    side_row = jnp.pad(jnp.concatenate([cond_row, chosen]), (0, features - local - chosen.shape[0]))
    small = jnp.stack(
        [
            shift_spatial, scale_spatial, sums_temporal[2], sums_temporal[0], sums_temporal[1],
            sums_cross[2], sums_mlp[0], sums_mlp[1], gate_mlp, sums_cross[1], side_row,
        ]
    )
    small_all = lax.all_gather(small, BOTH).reshape(groups, frames_axis, 11, features)
    modulation_grad = jnp.sum(small_all[:, :, 0:9], axis=1)
    grad_gain = jnp.sum(small_all[:, :, 9], axis=(0, 1))
    cond_all = small_all[:, 0, 10, 0:local]
    chosen_all = small_all[:, 0, 10, local : local + chosen.shape[0]]
    act_all, swish_pull = jax.vjp(swish_act, cond_all)
    act_all = act_all.astype(NARROW).astype(WIDE)
    column = features // (groups * frames_axis)
    rank = lax.axis_index(BOTH)
    column_grads = lax.dynamic_slice_in_dim(modulation_grad, rank * column, column, axis=2)
    grad_ada = jnp.einsum("gc,gkd->ckd", act_all, column_grads, precision=HIGHEST)
    grad_act = jnp.einsum("ckd,gkd->gc", ada_weight.astype(WIDE), modulation_grad, precision=HIGHEST)
    grad_cond = swish_pull(grad_act)[0]
    grad_table = jnp.einsum("gn,gc->nc", chosen_all, grad_cond, precision=HIGHEST)

    def unpack(values, parts):
        return values.reshape(values.shape[0], parts, -1)

    return (
        output,
        grad_latent.astype(NARROW)[None],
        grad_table,
        grad_ada,
        unpack(grad_inproj_spatial, 3),
        grad_outproj_spatial.T,
        unpack(grad_inproj_temporal, 3),
        grad_outproj_temporal.T,
        grad_caption,
        grad_gain,
        grad_query_cross,
        unpack(grad_keyval_cross, 2),
        grad_outproj_cross.T,
        grad_up,
        grad_down.T,
    )


def solution(mesh):
    tokens = P(GROUP, FRAME, LINE, None)
    packed_in, rows_in, columns_in = P(None, None, LINE), P(LINE, None), P(None, LINE)
    in_specs = (
        tokens, P(GROUP, None, None, None), P(GROUP), P(GROUP, None), P(GROUP, FRAME, None),
        P(GROUP, None), columns_in, P(LINE, None, None), packed_in, rows_in, packed_in, rows_in,
        columns_in, P(), columns_in, packed_in, rows_in, columns_in, rows_in, tokens,
    )
    packed_out, rows_out, columns_out = P(BOTH, None, LINE), P(LINE, BOTH), P(BOTH, LINE)
    out_specs = (
        tokens, tokens, columns_in, P(LINE, None, BOTH), packed_out, rows_out, packed_out, rows_out,
        columns_out, P(), columns_out, packed_out, rows_out, columns_out, rows_out,
    )
    return jax.shard_map(
        per_device, mesh=mesh, in_specs=in_specs, out_specs=out_specs, check_vma=False
    )
```

```python
import functools

import jax
import jax.numpy as jnp
from jax import lax
from jax.experimental import pallas as pl
from jax.experimental.pallas import tpu as pltpu
from jax.sharding import PartitionSpec as P

HD = 72
WIN = 4
EPSILON = 1e-06
HIGHEST = lax.Precision.HIGHEST
NEGATIVE = -1e30
WIDE = jnp.float32
NARROW = jnp.bfloat16
GROUP, FRAME, LINE = "group", "frame", "tensor"
BOTH = (GROUP, FRAME)
MESH = pl.DeviceIdType.MESH
CHUNKS = 16
LAG = 2
FIRST_FOLD = 3
VMEM_LIMIT = 48 * 2**20


def swish_act(values):
    return values / (1.0 + jnp.exp(-values))


def gelu_tanh(values):
    return (
        0.5
        * values
        * (1.0 + jnp.tanh(0.7978845608028654 * (values + 0.044715 * values * values * values)))
    )


def dot(first, second, contract_first, contract_second):
    return lax.dot_general(
        first, second, (((contract_first,), (contract_second,)), ((), ())), preferred_element_type=WIDE
    )


def split_heads(values):
    return values.reshape(values.shape[:-1] + (values.shape[-1] // HD, HD))


def split_pair(values):
    high_part = values.astype(NARROW)
    rest_part = (values - high_part.astype(WIDE)).astype(NARROW)
    return (high_part, rest_part)


def norm_parts(values):
    centred = values - jnp.mean(values, axis=-1, keepdims=True)
    spread = lax.rsqrt(jnp.mean(centred * centred, axis=-1, keepdims=True) + EPSILON)
    return centred * spread, spread


def norm_pull(scaled, normal, spread):
    return spread * (
        scaled
        - jnp.mean(scaled, axis=-1, keepdims=True)
        - normal * jnp.mean(scaled * normal, axis=-1, keepdims=True)
    )


def remote(source, target, send_sem, recv_sem, where):
    return pltpu.make_async_remote_copy(
        src_ref=source,
        dst_ref=target,
        send_sem=send_sem,
        recv_sem=recv_sem,
        device_id=where,
        device_id_type=MESH,
    )


def greet_line(place, count, others=()):
    barrier = pltpu.get_barrier_semaphore()
    for where in others:
        pl.semaphore_signal(barrier, inc=1, device_id=where, device_id_type=MESH)

    @pl.when(place > 0)
    def _():
        pl.semaphore_signal(barrier, inc=1, device_id={LINE: place - 1}, device_id_type=MESH)

    @pl.when(place < count - 1)
    def _():
        pl.semaphore_signal(barrier, inc=1, device_id={LINE: place + 1}, device_id_type=MESH)

    pl.semaphore_wait(
        barrier, (place > 0).astype(jnp.int32) + (place < count - 1).astype(jnp.int32) + len(others)
    )


class Scatter:
    def __init__(self, groups, frames_axis, sources, results, scratch):
        pieces = len(sources)
        self.pieces = range(pieces)
        self.sources, self.results = sources, results
        self.inbox, self.stage, self.kept, self.found = (scratch[i * pieces : (i + 1) * pieces] for i in range(4))
        self.twin_send, self.twin_recv, self.peer_send, self.peer_recv = scratch[4 * pieces :]
        self.groups, self.frames_axis = groups, frames_axis
        self.total = groups // 2 * frames_axis
        group = lax.axis_index(GROUP)
        self.core = lax.rem(group, 2)
        self.me = lax.div(group, 2) * frames_axis + lax.axis_index(FRAME)
        self.twin = {GROUP: group + 1 - 2 * self.core}

    def peer(self, step):
        to = lax.rem(self.me + step, self.total)
        return to, {GROUP: lax.div(to, self.frames_axis) * 2 + self.core, FRAME: lax.rem(to, self.frames_axis)}

    def partners(self):
        return [self.twin] + [self.peer(step)[1] for step in range(1, self.total)]

    def block(self, piece):
        return self.sources[piece].shape[0] // (self.groups * self.frames_axis)

    def twin_copy(self, piece, high):
        rows = self.block(piece) * self.frames_axis
        first = pl.multiple_of((high * 2 + 1 - self.core) * rows, 16)
        return remote(
            self.sources[piece].at[pl.ds(first, rows)],
            self.inbox[piece].at[pl.ds(high * rows, rows)],
            self.twin_send.at[piece, high],
            self.twin_recv.at[piece, high],
            self.twin,
        )

    def peer_copy(self, piece, step):
        return remote(
            self.stage[piece].at[step],
            self.found[piece].at[step],
            self.peer_send.at[piece, step],
            self.peer_recv.at[piece, step],
            self.peer(step)[1],
        )

    def start(self):
        for piece in self.pieces:
            for high in range(self.groups // 2):
                self.twin_copy(piece, high).start()

    def fold(self, step):
        if step == self.total - 1:
            for piece in self.pieces:
                for high in range(self.groups // 2):
                    self.twin_copy(piece, high).wait_recv()
        to = self.peer(step)[0]
        for piece in self.pieces:
            block = self.block(piece)
            high, frame = lax.div(to, self.frames_axis), lax.rem(to, self.frames_axis)
            first = ((high * 2 + self.core) * self.frames_axis + frame) * block
            mine = self.sources[piece][pl.ds(pl.multiple_of(first, 16), block)]
            other = self.inbox[piece][pl.ds(pl.multiple_of(to * block, 16), block)]
            summed = mine.astype(WIDE) + other.astype(WIDE)
            if step == 0:
                self.kept[piece][...] = summed
            else:
                self.stage[piece][step] = summed.astype(NARROW)
                self.peer_copy(piece, step).start()

    def finish(self):
        for piece in self.pieces:
            for step in range(1, self.total):
                self.peer_copy(piece, step).wait_recv()
            summed = self.kept[piece][...]
            for step in range(1, self.total):
                summed = summed + self.found[piece][step].astype(WIDE)
            self.results[piece][...] = summed
        for piece in self.pieces:
            for high in range(self.groups // 2):
                self.twin_copy(piece, high).wait_send()
            for step in range(1, self.total):
                self.peer_copy(piece, step).wait_send()

    @staticmethod
    def shapes(groups, frames_axis, sources):
        total, many = groups // 2 * frames_axis, len(sources)
        kept = [(item.shape[0] // (groups * frames_axis), item.shape[1]) for item in sources]
        results = [jax.ShapeDtypeStruct(shape, WIDE) for shape in kept]
        scratch = [pltpu.VMEM((item.shape[0] // 2, item.shape[1]), NARROW) for item in sources]
        scratch += [pltpu.VMEM((total,) + shape, NARROW) for shape in kept]
        scratch += [pltpu.VMEM(shape, WIDE) for shape in kept]
        scratch += [pltpu.VMEM((total,) + shape, NARROW) for shape in kept]
        dma = pltpu.SemaphoreType.DMA
        scratch += [dma((many, groups // 2))] * 2 + [dma((many, total))] * 2
        return results, scratch


def can_scatter(groups, frames_axis, width):
    return groups % 2 == 0 and width % (16 * groups * frames_axis) == 0


def line_sum(count, place, part_ref, land, cross, stage, total, sems, consume, aside=None):
    in_send, land_recv, cross_recv, out_send, out_recv = sems
    depth = part_ref.shape[0] // CHUNKS
    half = count // 2
    left = place < half
    level = jnp.where(left, place, count - 1 - place)
    inner = jnp.where(left, place + 1, place - 1)
    outer = jnp.where(left, place - 1, place + 1)
    is_end, is_middle = level == 0, level == half - 1

    def rows_of(chunk):
        return pl.ds(pl.multiple_of(chunk * depth, depth), depth)

    def inward(chunk):
        rows = rows_of(chunk)
        return remote(stage.at[rows], land.at[rows], in_send.at[chunk], land_recv.at[chunk], {LINE: inner})

    def across(chunk):
        rows = rows_of(chunk)
        return remote(stage.at[rows], cross.at[rows], in_send.at[chunk], cross_recv.at[chunk], {LINE: inner})

    def outward(chunk):
        rows = rows_of(chunk)
        return remote(total.at[rows], total.at[rows], out_send.at[chunk], out_recv.at[chunk], {LINE: outer})

    def send_in(chunk):
        @pl.when(is_middle)
        def _():
            across(chunk).start()

        @pl.when(jnp.logical_not(is_middle))
        def _():
            inward(chunk).start()

    def gather_in(chunk):
        rows = rows_of(chunk)
        inward(chunk).wait_recv()
        stage[rows] = (part_ref[rows].astype(WIDE) + land[rows].astype(WIDE)).astype(NARROW)
        send_in(chunk)

    def finish(chunk):
        rows = rows_of(chunk)

        @pl.when(is_middle)
        def _():
            across(chunk).wait_recv()
            total[rows] = (stage[rows].astype(WIDE) + cross[rows].astype(WIDE)).astype(NARROW)

        @pl.when(jnp.logical_not(is_middle))
        def _():
            outward(chunk).wait_recv()

        @pl.when(jnp.logical_not(is_end))
        def _():
            outward(chunk).start()

        consume(rows)

    def begin(chunk, carry):
        rows = rows_of(chunk)
        stage[rows] = part_ref[rows]
        send_in(chunk)
        return carry

    def step(number, carry):
        @pl.when(jnp.logical_not(is_end) & (number < CHUNKS))
        def _():
            gather_in(number)

        @pl.when(number >= LAG)
        def _():
            finish(number - LAG)

        if aside is not None:
            for fold in range(aside.total):

                @pl.when(number == FIRST_FOLD + fold)
                def _():
                    aside.fold(aside.total - 1 - fold)

        return carry

    @pl.when(is_end)
    def _():
        lax.fori_loop(0, CHUNKS, begin, 0)

    lax.fori_loop(0, CHUNKS + LAG, step, 0)

    def settle(chunk, carry):
        @pl.when(is_middle)
        def _():
            across(chunk).wait_send()

        @pl.when(jnp.logical_not(is_middle))
        def _():
            inward(chunk).wait_send()

        @pl.when(jnp.logical_not(is_end))
        def _():
            outward(chunk).wait_send()

        return carry

    lax.fori_loop(0, CHUNKS, settle, 0)


def forward_kernel(
    count, part_ref, base_ref, rows_ref, out_ref, next_ref, normed_ref, land, cross, stage, *sems
):
    place = lax.axis_index(LINE)
    greet_line(place, count)
    gate, gain, shift = (rows_ref[i : i + 1] for i in range(3))

    def consume(rows):
        moved = base_ref[rows] + gate * out_ref[rows].astype(WIDE)
        next_ref[rows] = moved
        normed_ref[rows] = (norm_parts(moved)[0] * gain + shift).astype(NARROW)

    line_sum(count, place, part_ref, land, cross, stage, out_ref, sems, consume)


def backward_kernel(count, groups, frames_axis, pieces, *refs):
    part_ref, base_ref, grad_ref, below_ref, rows_ref = refs[:5]
    sources, refs = refs[5 : 5 + pieces], refs[5 + pieces :]
    moved_ref, low_ref, sums_ref = refs[:3]
    results, refs = refs[3 : 3 + pieces], refs[3 + pieces :]
    total, land, cross, stage, tally = refs[:5]
    sems, scratch = refs[5:10], refs[10:]
    place = lax.axis_index(LINE)
    aside = Scatter(groups, frames_axis, sources, results, scratch) if pieces else None
    greet_line(place, count, aside.partners() if pieces else ())
    if pieces:
        aside.start()
    gain, gate = (rows_ref[i : i + 1] for i in range(2))
    tally[...] = jnp.zeros_like(tally)

    def consume(rows):
        grads = total[rows].astype(WIDE)
        normal, spread = norm_parts(base_ref[rows])
        moved = grad_ref[rows] + norm_pull(grads * gain, normal, spread)
        moved_ref[rows] = moved
        low_ref[rows] = (gate * moved).astype(NARROW)
        for i, terms in enumerate((grads, grads * normal, moved * below_ref[rows].astype(WIDE))):
            tally[i] += jnp.sum(terms.reshape(-1, 8, terms.shape[-1]), axis=0)

    line_sum(count, place, part_ref, land, cross, stage, total, sems, consume, aside)
    sums_ref[...] = jnp.zeros_like(sums_ref)
    for i in range(3):
        sums_ref[i : i + 1] = jnp.sum(tally[i], axis=0, keepdims=True)
    if pieces:
        aside.finish()


def vmem(count):
    return [pl.BlockSpec(memory_space=pltpu.VMEM)] * count


def line_sems():
    return [pltpu.SemaphoreType.DMA((CHUNKS,))] * 5


def call_forward(count, part, base, rows):
    shape = part.shape
    return pl.pallas_call(
        functools.partial(forward_kernel, count),
        out_shape=(
            jax.ShapeDtypeStruct(shape, NARROW),
            jax.ShapeDtypeStruct(shape, WIDE),
            jax.ShapeDtypeStruct(shape, NARROW),
        ),
        in_specs=vmem(3),
        out_specs=tuple(vmem(3)),
        scratch_shapes=[pltpu.VMEM(shape, NARROW)] * 3 + line_sems(),
        compiler_params=pltpu.CompilerParams(
            collective_id=1, has_side_effects=True, vmem_limit_bytes=VMEM_LIMIT
        ),
        name="forward_sum",
    )(part, base, rows)


def call_backward(count, groups, frames_axis, part, base, grad, below, rows, sources, kernel_id):
    shape = part.shape
    results, scratch = Scatter.shapes(groups, frames_axis, sources) if sources else ([], [])
    return pl.pallas_call(
        functools.partial(backward_kernel, count, groups, frames_axis, len(sources)),
        out_shape=(
            jax.ShapeDtypeStruct(shape, WIDE),
            jax.ShapeDtypeStruct(shape, NARROW),
            jax.ShapeDtypeStruct((8, shape[1]), WIDE),
            *results,
        ),
        in_specs=vmem(5 + len(sources)),
        out_specs=tuple(vmem(3 + len(sources))),
        scratch_shapes=[pltpu.VMEM(shape, NARROW)] * 4
        + [pltpu.VMEM((3, 8, shape[1]), WIDE)]
        + line_sems()
        + scratch,
        compiler_params=pltpu.CompilerParams(
            collective_id=kernel_id, has_side_effects=True, vmem_limit_bytes=VMEM_LIMIT
        ),
        name="backward_sum",
    )(part, base, grad, below, rows, *sources)


def closing_kernel(count, groups, frames_axis, pieces, *refs):
    part_ref, base_ref, grad_ref, small_ref, rows_ref = refs[:5]
    sources, refs = refs[5 : 5 + pieces], refs[5 + pieces :]
    latent_ref, every_ref = refs[:2]
    results, refs = refs[2 : 2 + pieces], refs[2 + pieces :]
    land, stage, line_rows, own_rows, tally = refs[:5]
    from_left, from_right, to_left, to_right, line_send, line_recv, all_send, all_recv = refs[5:13]
    place, group, here = (lax.axis_index(axis) for axis in (LINE, GROUP, FRAME))
    last = count - 1
    frames, share = latent_ref.shape[0], latent_ref.shape[1]
    everyone = groups * frames_axis
    rank = group * frames_axis + here
    aside = Scatter(groups, frames_axis, sources, results, refs[13:]) if pieces else None

    def member(ahead):
        to = lax.rem(rank + ahead, everyone)
        return {GROUP: lax.div(to, frames_axis), FRAME: lax.rem(to, frames_axis)}

    def neighbour(ahead):
        return {LINE: lax.rem(place + ahead, count)}

    barrier = pltpu.get_barrier_semaphore()

    def greet(ahead, carry):
        pl.semaphore_signal(barrier, inc=1, device_id=member(ahead), device_id_type=MESH)
        return carry

    for ahead in range(1, count):
        pl.semaphore_signal(barrier, inc=1, device_id=neighbour(ahead), device_id_type=MESH)
    lax.fori_loop(1, everyone, greet, 0)
    pl.semaphore_wait(barrier, last + everyone - 1)

    def rows_of(owner):
        return pl.ds(pl.multiple_of(owner * share, share), share)

    def pass_on(owner, frame, right):
        side = 0 if right else 1
        return remote(
            stage.at[side, owner, frame],
            land.at[side, owner, frame],
            (to_right if right else to_left).at[owner, frame],
            (from_left if right else from_right).at[owner, frame],
            {LINE: place + 1 if right else place - 1},
        )

    def relay(distance, right):
        owner = place + distance if right else place - distance
        source = (place == 0) if right else (place == last)

        @pl.when((owner <= last) if right else (owner >= 0))
        def _():
            for frame in range(frames):
                side = 0 if right else 1

                @pl.when(source)
                def _():
                    stage[side, owner, frame] = part_ref[frame, rows_of(owner)]

                @pl.when(jnp.logical_not(source))
                def _():
                    pass_on(owner, frame, right).wait_recv()
                    stage[side, owner, frame] = (
                        part_ref[frame, rows_of(owner)].astype(WIDE) + land[side, owner, frame].astype(WIDE)
                    ).astype(NARROW)

                pass_on(owner, frame, right).start()

    def relay_both(distance):
        relay(distance, True)
        relay(distance, False)

    if pieces:
        aside.start()
    relay_both(last)

    tally[...] = jnp.zeros_like(tally)
    depth = 32
    blocks = base_ref.shape[1] // depth

    def add_rows(number, carry):
        frame, rows = lax.div(number, blocks), pl.ds(pl.multiple_of(lax.rem(number, blocks) * depth, depth), depth)
        normal = norm_parts(base_ref[frame, rows])[0]
        grads = part_ref[frame, rows].astype(WIDE)
        for i, terms in enumerate((grads, grads * normal)):
            tally[i] += jnp.sum(terms.reshape(-1, 8, terms.shape[-1]), axis=0)
        return carry

    lax.fori_loop(0, frames * blocks, add_rows, 0)
    line_rows[place] = small_ref[0:8]
    for i in range(2):
        line_rows[place, i : i + 1] = jnp.sum(tally[i], axis=0, keepdims=True)

    def line_copy(ahead):
        return remote(
            line_rows.at[place], line_rows.at[place], line_send.at[ahead], line_recv.at[ahead], neighbour(ahead)
        )

    def all_copy(ahead):
        return remote(
            own_rows, every_ref.at[rank], all_send.at[ahead], all_recv.at[ahead], member(ahead)
        )

    for ahead in range(1, count):
        line_copy(ahead).start()
    for distance in range(last - 1, 0, -1):
        relay_both(distance)
        if pieces and distance == last - 1:
            for fold in range(aside.total):
                aside.fold(aside.total - 1 - fold)
    for ahead in range(1, count):
        line_copy(ahead).wait_recv()
    summed = line_rows[0]
    for i in range(1, count):
        summed = summed + line_rows[i]
    own_rows[0:8] = summed
    own_rows[8:16] = small_ref[8:16]
    every_ref[rank] = own_rows[...]

    def send_rows(ahead, carry):
        all_copy(ahead).start()
        return carry

    lax.fori_loop(1, everyone, send_rows, 0)

    own = rows_of(place)
    for frame in range(frames):
        for right in (True, False):
            @pl.when((place > 0) if right else (place < last))
            def _():
                pass_on(place, frame, right).wait_recv()

        left_part = jnp.where(place > 0, land[0, place, frame].astype(WIDE), 0.0)
        right_part = jnp.where(place < last, land[1, place, frame].astype(WIDE), 0.0)
        grads = part_ref[frame, own].astype(WIDE) + left_part + right_part
        normal, spread = norm_parts(base_ref[frame, own])
        latent_ref[frame] = (
            grad_ref[frame, own] + norm_pull(grads * rows_ref[0:1], normal, spread)
        ).astype(NARROW)

    for owner in range(count):
        for frame in range(frames):

            @pl.when(owner > place)
            def _():
                pass_on(owner, frame, True).wait_send()

            @pl.when(owner < place)
            def _():
                pass_on(owner, frame, False).wait_send()

    for ahead in range(1, count):
        line_copy(ahead).wait_send()

    def settle(ahead, carry):
        all_copy(ahead).wait_recv()
        all_copy(ahead).wait_send()
        return carry

    lax.fori_loop(1, everyone, settle, 0)
    if pieces:
        aside.finish()


def call_closing(count, groups, frames_axis, part, base, grad, small, rows, sources):
    frames, patches, features = part.shape
    everyone = groups * frames_axis
    share = patches // count
    results, scratch = Scatter.shapes(groups, frames_axis, sources) if sources else ([], [])
    dma = pltpu.SemaphoreType.DMA
    return pl.pallas_call(
        functools.partial(closing_kernel, count, groups, frames_axis, len(sources)),
        out_shape=(
            jax.ShapeDtypeStruct((frames, share, features), NARROW),
            jax.ShapeDtypeStruct((everyone, 16, features), WIDE),
            *results,
        ),
        in_specs=vmem(5 + len(sources)),
        out_specs=tuple(vmem(2 + len(sources))),
        scratch_shapes=[
            pltpu.VMEM((2, count, frames, share, features), NARROW),
            pltpu.VMEM((2, count, frames, share, features), NARROW),
            pltpu.VMEM((count, 8, features), WIDE),
            pltpu.VMEM((16, features), WIDE),
            pltpu.VMEM((2, 8, features), WIDE),
        ]
        + [dma((count, frames))] * 4
        + [dma((count,))] * 2
        + [dma((everyone,))] * 2
        + scratch,
        compiler_params=pltpu.CompilerParams(
            collective_id=4, has_side_effects=True, vmem_limit_bytes=VMEM_LIMIT
        ),
        name="closing",
    )(part, base, grad, small, rows, *sources)


def opening_kernel(
    count, groups, frames_axis, latent_ref, act_ref, ada_ref, captions_ref,
    base_ref, normed_ref, mods_ref, spread_ref,
    land, ada, mine, others,
    up_send, down_send, land_recv, ada_sem, mods_send, mods_recv, cap_send, cap_recv, cap_local,
):
    place = lax.axis_index(LINE)
    group = lax.axis_index(GROUP)
    here = lax.axis_index(FRAME)
    last = count - 1
    width = spread_ref.shape[2]
    parts = ada_ref.shape[0]
    share = latent_ref.shape[1]

    loads = [pltpu.make_async_copy(ada_ref.at[k], ada.at[k], ada_sem.at[k]) for k in range(parts)]
    for load in loads:
        load.start()

    barrier = pltpu.get_barrier_semaphore()
    for ahead in range(1, count):
        pl.semaphore_signal(
            barrier, inc=1, device_id={LINE: lax.rem(place + ahead, count)}, device_id_type=MESH
        )
    for ahead in range(1, groups):
        pl.semaphore_signal(
            barrier, inc=1, device_id={GROUP: lax.rem(group + ahead, groups)}, device_id_type=MESH
        )
    pl.semaphore_wait(barrier, count - 1 + groups - 1)

    def shift(owner, up):
        to = place + 1 if up else place - 1
        return remote(
            land.at[owner], land.at[owner], (up_send if up else down_send).at[owner], land_recv.at[owner], {LINE: to}
        )

    land[place] = latent_ref[...]

    @pl.when(place < last)
    def _():
        shift(place, True).start()

    @pl.when(place > 0)
    def _():
        shift(place, False).start()

    def caption_block(to):
        if len(captions_ref.shape) == 3:
            return captions_ref.at[to]
        first = pl.multiple_of((to * frames_axis + here) * width, width)
        return captions_ref.at[:, pl.ds(first, width)]

    def caption_copy(ahead):
        to = lax.rem(group + ahead, groups)
        return remote(
            caption_block(to),
            spread_ref.at[group],
            cap_send.at[ahead],
            cap_recv.at[ahead],
            {GROUP: to},
        )

    own_caption = pltpu.make_async_copy(caption_block(group), spread_ref.at[group], cap_local)
    own_caption.start()
    for ahead in range(1, groups):
        caption_copy(ahead).start()

    def arrive(distance):
        @pl.when(place >= distance)
        def _():
            shift(place - distance, True).wait_recv()

            @pl.when(place < last)
            def _():
                shift(place - distance, True).start()

        @pl.when(place + distance <= last)
        def _():
            shift(place + distance, False).wait_recv()

            @pl.when(place > 0)
            def _():
                shift(place + distance, False).start()

    def weigh(k):
        loads[k].wait()
        product = dot(act_ref[...], ada[k], 1, 0)
        mine[k : k + 1] = product[0:1]

    def mods_copy(ahead):
        return remote(
            mine, others.at[place], mods_send.at[ahead], mods_recv.at[ahead], {LINE: lax.rem(place + ahead, count)}
        )

    mine[...] = jnp.zeros_like(mine)
    cut = parts // 2 + 1
    for k in range(cut):
        weigh(k)
    arrive(1)
    for k in range(cut, parts):
        weigh(k)
    for ahead in range(1, count):
        mods_copy(ahead).start()
    others[place] = mine[...]
    for distance in range(2, count - 1):
        arrive(distance)
    for ahead in range(1, count):
        mods_copy(ahead).wait_recv()
    mods = others[0]
    for i in range(1, count):
        mods = mods + others[i]
    mods_ref[...] = mods
    gain = 1.0 + mods[1:2]
    shift_row = mods[0:1]

    def norm_owner(owner):
        for f in range(latent_ref.shape[0]):
            values = land[owner, f].astype(WIDE)
            rows = pl.ds(pl.multiple_of(owner * share, share), share)
            base_ref[f, rows] = values
            normed_ref[f, rows] = (norm_parts(values)[0] * gain + shift_row).astype(NARROW)

    def near(distance):
        @pl.when(place >= distance)
        def _():
            norm_owner(place - distance)

        @pl.when(place + distance <= last)
        def _():
            norm_owner(place + distance)

    norm_owner(place)
    for distance in range(1, count - 1):
        near(distance)
    if count > 2:
        arrive(count - 1)
    near(count - 1)

    for owner in range(count):

        @pl.when((place < last) & (owner <= place))
        def _():
            shift(owner, True).wait_send()

        @pl.when((place > 0) & (owner >= place))
        def _():
            shift(owner, False).wait_send()

    for ahead in range(1, count):
        mods_copy(ahead).wait_send()
    for ahead in range(1, groups):
        caption_copy(ahead).wait_send()
        caption_copy(ahead).wait_recv()
    own_caption.wait()


def call_opening(count, groups, frames_axis, latent, act, ada, captions):
    frames, share, features = latent.shape
    parts = ada.shape[0]
    length, text_width = captions.shape
    width = text_width // (groups * frames_axis)
    if width % 128:
        blocks = captions.reshape(length, groups, frames_axis, width)
        captions = jnp.transpose(
            lax.dynamic_index_in_dim(blocks, lax.axis_index(FRAME), 2, keepdims=False), (1, 0, 2)
        )
    full = (frames, share * count, features)
    dma = pltpu.SemaphoreType.DMA
    anywhere = pl.BlockSpec(memory_space=pl.ANY)
    return pl.pallas_call(
        functools.partial(opening_kernel, count, groups, frames_axis),
        out_shape=(
            jax.ShapeDtypeStruct(full, WIDE),
            jax.ShapeDtypeStruct(full, NARROW),
            jax.ShapeDtypeStruct((16, features), WIDE),
            jax.ShapeDtypeStruct((groups, length, width), NARROW),
        ),
        in_specs=vmem(2) + [anywhere] * 2,
        out_specs=tuple(vmem(3) + [anywhere]),
        scratch_shapes=[
            pltpu.VMEM((count, frames, share, features), NARROW),
            pltpu.VMEM(ada.shape, NARROW),
            pltpu.VMEM((16, features), WIDE),
            pltpu.VMEM((count, 16, features), WIDE),
            dma((count,)),
            dma((count,)),
            dma((count,)),
            dma((parts,)),
            dma((count,)),
            dma((count,)),
            dma((groups,)),
            dma((groups,)),
            dma,
        ],
        compiler_params=pltpu.CompilerParams(
            collective_id=3, has_side_effects=True, vmem_limit_bytes=VMEM_LIMIT
        ),
        name="opening",
    )(latent, act, ada, captions)


STAGES = 4
MIDDLE_ROWS = 32
MIDDLE_LAG = 2


def gelu_both(values):
    square = values * values
    bent = jnp.tanh(0.7978845608028654 * (values + 0.044715 * values * square))
    slope = 0.5 * (1.0 + bent) + 0.5 * values * (1.0 - bent * bent) * (
        0.7978845608028654 * (1.0 + 3.0 * 0.044715 * square)
    )
    return 0.5 * values * (1.0 + bent), slope


def middle_kernel(
    count, frames, first_ref, base_ref, cotangent_ref, rows_ref, bias_ref,
    keys_ref, values_ref, query_w, out_w, up_w, down_w,
    base_three, grad_two, low_two, low_three, low_four, normed_three, normed_four,
    active, grad_inner, heads_out, grad_query, grad_keys, grad_values, sums_ref,
    base_two, grad_three, branch_two, query, grad_heads, part, mixed, tally,
    land, cross, stage, total, in_send, land_recv, cross_recv, out_send, out_recv,
):
    place = lax.axis_index(LINE)
    greet_line(place, count)
    half = count // 2
    left = place < half
    level = jnp.where(left, place, count - 1 - place)
    inner = jnp.where(left, place + 1, place - 1)
    outer = jnp.where(left, place - 1, place + 1)
    is_end, is_middle = level == 0, level == half - 1
    inside = jnp.logical_not(is_end)
    patches = base_ref.shape[0] // frames
    chunks = patches // MIDDLE_ROWS
    slots = STAGES * frames
    scale = HD ** (-0.5)
    width = bias_ref.shape[2]
    local = query_w.shape[0]
    half_heads = local // HD // 2
    tile = up_w.shape[1] // 3
    gate_two, cross_gain, gain_three, shift_three, gate_three = (rows_ref[i : i + 1] for i in range(5))

    def where_of(slot, chunk):
        rows = pl.ds(pl.multiple_of(lax.rem(slot, frames) * patches + chunk * MIDDLE_ROWS, MIDDLE_ROWS), MIDDLE_ROWS)
        return lax.rem(lax.div(slot, frames), 2), rows

    def inward(slot, chunk):
        side, rows = where_of(slot, chunk)
        return remote(
            stage.at[side, rows], land.at[side, rows], in_send.at[slot, chunk], land_recv.at[slot, chunk], {LINE: inner}
        )

    def across(slot, chunk):
        side, rows = where_of(slot, chunk)
        return remote(
            stage.at[side, rows], cross.at[side, rows], in_send.at[slot, chunk], cross_recv.at[slot, chunk], {LINE: inner}
        )

    def outward(slot, chunk):
        side, rows = where_of(slot, chunk)
        return remote(
            total.at[side, rows], total.at[side, rows], out_send.at[slot, chunk], out_recv.at[slot, chunk], {LINE: outer}
        )

    def own_part(slot, rows):
        return jnp.where(slot < frames, first_ref[rows], part[rows])

    def send_in(slot, chunk):
        @pl.when(is_middle)
        def _():
            across(slot, chunk).start()

        @pl.when(jnp.logical_not(is_middle))
        def _():
            inward(slot, chunk).start()

    def sent(slot, chunk):
        @pl.when(is_middle)
        def _():
            across(slot, chunk).wait_send()

        @pl.when(jnp.logical_not(is_middle))
        def _():
            inward(slot, chunk).wait_send()

        @pl.when(inside)
        def _():
            outward(slot, chunk).wait_send()

    def free(slot, chunk):
        @pl.when(slot >= 2 * frames)
        def _():
            sent(slot - 2 * frames, chunk)

    def gather_in(slot, chunk):
        side, rows = where_of(slot, chunk)
        free(slot, chunk)
        inward(slot, chunk).wait_recv()
        stage[side, rows] = (own_part(slot, rows).astype(WIDE) + land[side, rows].astype(WIDE)).astype(NARROW)
        send_in(slot, chunk)

    def add_rows(which, terms):
        tally[which] += jnp.sum(terms.reshape(-1, 8, terms.shape[-1]), axis=0)

    def consume(slot, rows, summed):
        number = lax.div(slot, frames)

        @pl.when(number == 0)
        def _():
            branch_two[rows] = summed
            moved = base_ref[rows] + gate_two * summed.astype(WIDE)
            base_two[rows] = moved
            normed_three[rows] = (norm_parts(moved)[0] * cross_gain).astype(NARROW)

        @pl.when(number == 1)
        def _():
            moved = base_two[rows] + summed.astype(WIDE)
            base_three[rows] = moved
            normed_four[rows] = (norm_parts(moved)[0] * gain_three + shift_three).astype(NARROW)
            low_four[rows] = (gate_three * cotangent_ref[rows].astype(WIDE)).astype(NARROW)

        @pl.when(number == 2)
        def _():
            grads = summed.astype(WIDE)
            normal, spread = norm_parts(base_three[rows])
            moved = cotangent_ref[rows].astype(WIDE) + norm_pull(grads * gain_three, normal, spread)
            grad_three[rows] = moved
            low_three[rows] = moved.astype(NARROW)
            add_rows(0, grads)
            add_rows(1, grads * normal)

        @pl.when(number == 3)
        def _():
            grads = summed.astype(WIDE)
            normal, spread = norm_parts(base_two[rows])
            moved = grad_three[rows] + norm_pull(grads * cross_gain, normal, spread)
            grad_two[rows] = moved
            low_two[rows] = (gate_two * moved).astype(NARROW)
            add_rows(2, grads * normal)
            add_rows(3, moved * branch_two[rows].astype(WIDE))

    def finish(slot, chunk):
        side, rows = where_of(slot, chunk)

        @pl.when(is_middle)
        def _():
            across(slot, chunk).wait_recv()
            total[side, rows] = (stage[side, rows].astype(WIDE) + cross[side, rows].astype(WIDE)).astype(NARROW)

        @pl.when(jnp.logical_not(is_middle))
        def _():
            outward(slot, chunk).wait_recv()

        @pl.when(inside)
        def _():
            outward(slot, chunk).start()

        consume(slot, rows, total[side, rows])

    def head_rows(head):
        return pl.ds(head * width, width)

    def probs_of(stream, asked, head):
        scores = scale * dot(asked, keys_ref[head_rows(head)], 1, 1) + bias_ref[stream, 0:1]
        raised = jnp.exp(scores - jnp.max(scores, axis=-1, keepdims=True))
        return raised / jnp.sum(raised, axis=-1, keepdims=True)

    def cross_forward(piece, stream, rows):
        if piece == 0:
            query[rows] = dot(normed_three[rows], query_w[...], 1, 1).astype(NARROW)
        elif piece in (1, 2):
            asked = query[rows]
            found = jnp.zeros((patches, local), WIDE) if piece == 1 else mixed[...]
            for head in range((piece - 1) * half_heads, piece * half_heads):
                probs = probs_of(stream, asked, head).astype(NARROW)
                found = found + dot(probs, values_ref[head_rows(head)], 1, 0)
            if piece == 1:
                mixed[...] = found
            else:
                heads_out[rows] = found.astype(NARROW)
        elif piece == 3:
            part[rows] = dot(heads_out[rows], out_w[...], 1, 0).astype(NARROW)

    def feed_forward(piece, stream, rows):
        if piece < 3:
            span = slice(piece * tile, (piece + 1) * tile)
            inner_values = dot(normed_four[rows], up_w[:, span], 1, 0)
            pulled = dot(low_four[rows], down_w[span], 1, 1)
            raised, slope = gelu_both(inner_values)
            active[rows, span] = raised.astype(NARROW)
            grad_inner[rows, span] = (pulled * slope).astype(NARROW)
        else:
            third = up_w.shape[0] // 3
            span = slice((piece - 3) * third, (piece - 2) * third)
            part[rows, span] = dot(grad_inner[rows], up_w[span], 1, 1).astype(NARROW)

    def cross_backward(piece, stream, rows):
        if piece == 0:
            grad_heads[rows] = dot(low_three[rows], out_w[...], 1, 1).astype(NARROW)
        elif piece in (1, 2):
            asked, given = query[rows], grad_heads[rows]
            found = jnp.zeros((patches, local), WIDE) if piece == 1 else mixed[...]
            for head in range((piece - 1) * half_heads, piece * half_heads):
                spot = head_rows(head)
                probs = probs_of(stream, asked, head)
                pulled = dot(given, values_ref[spot], 1, 1)
                grad_scores = probs * (pulled - jnp.sum(pulled * probs, axis=-1, keepdims=True))
                grad_scores = grad_scores.astype(NARROW)
                found = found + dot(grad_scores, keys_ref[spot], 1, 0)
                grad_keys[spot] += dot(grad_scores, asked, 0, 0)
                grad_values[spot] += dot(probs.astype(NARROW), given, 0, 0)
            if piece == 1:
                mixed[...] = found
            else:
                grad_query[rows] = (scale * found).astype(NARROW)
        elif piece == 3:
            part[rows] = dot(grad_query[rows], query_w[...], 1, 0).astype(NARROW)

    tally[...] = jnp.zeros_like(tally)
    grad_keys[...] = jnp.zeros_like(grad_keys)
    grad_values[...] = jnp.zeros_like(grad_values)

    def step(number, carry):
        slot, chunk = lax.div(number, chunks), lax.rem(number, chunks)
        before = slot - 1

        @pl.when(is_end & (chunk == 0))
        def _():
            @pl.when(slot < slots)
            def _():
                def begin(item, inner_carry):
                    side, rows = where_of(slot, item)
                    free(slot, item)
                    stage[side, rows] = own_part(slot, rows)
                    send_in(slot, item)
                    return inner_carry

                lax.fori_loop(0, chunks, begin, 0)

            @pl.when(slot > 0)
            def _():
                def end(item, inner_carry):
                    finish(before, item)
                    return inner_carry

                lax.fori_loop(0, chunks, end, 0)

        @pl.when(inside & (slot < slots))
        def _():
            gather_in(slot, chunk)

            @pl.when(chunk >= MIDDLE_LAG)
            def _():
                finish(slot, chunk - MIDDLE_LAG)

        @pl.when(inside & (slot > 0) & (chunk < MIDDLE_LAG))
        def _():
            finish(before, chunks - MIDDLE_LAG + chunk)

        stream = lax.rem(jnp.maximum(before, 0), frames)
        rows = pl.ds(pl.multiple_of(stream * patches, patches), patches)
        for which, work in enumerate((cross_forward, feed_forward, cross_backward)):

            @pl.when((slot > 0) & (lax.div(jnp.maximum(before, 0), frames) == which))
            def _():
                for piece in range(6 if which == 1 else 4):

                    @pl.when(chunk == MIDDLE_LAG + piece)
                    def _():
                        work(piece, stream, rows)

        return carry

    lax.fori_loop(0, slots * chunks + MIDDLE_LAG, step, 0)

    def settle(number, carry):
        sent(lax.div(number, chunks), lax.rem(number, chunks))
        return carry

    lax.fori_loop((slots - 2 * frames) * chunks, slots * chunks, settle, 0)
    sums_ref[...] = jnp.zeros_like(sums_ref)
    for i in range(4):
        sums_ref[i : i + 1] = jnp.sum(tally[i], axis=0, keepdims=True)


def call_middle(count, frames, first, base, cotangent, rows, bias, keys, values, query_w, out_w, up_w, down_w):
    tokens, features = first.shape
    local, hidden = query_w.shape[0], up_w.shape[1]
    chunks = tokens // frames // MIDDLE_ROWS

    def wide(*shape):
        return jax.ShapeDtypeStruct(shape, WIDE)

    def narrow(*shape):
        return jax.ShapeDtypeStruct(shape, NARROW)

    results = (
        [wide(tokens, features)] * 2
        + [narrow(tokens, features)] * 5
        + [narrow(tokens, hidden)] * 2
        + [narrow(tokens, local)] * 2
        + [wide(*keys.shape)] * 2
        + [wide(8, features)]
    )
    sem = pltpu.SemaphoreType.DMA((STAGES * frames, chunks))
    return pl.pallas_call(
        functools.partial(middle_kernel, count, frames),
        out_shape=tuple(results),
        in_specs=vmem(11),
        out_specs=tuple(vmem(len(results))),
        scratch_shapes=[
            pltpu.VMEM((tokens, features), WIDE),
            pltpu.VMEM((tokens, features), WIDE),
            pltpu.VMEM((tokens, features), NARROW),
            pltpu.VMEM((tokens, local), NARROW),
            pltpu.VMEM((tokens, local), NARROW),
            pltpu.VMEM((tokens, features), NARROW),
            pltpu.VMEM((tokens // frames, local), WIDE),
            pltpu.VMEM((4, 8, features), WIDE),
        ]
        + [pltpu.VMEM((2, tokens, features), NARROW)] * 4
        + [sem] * 5,
        compiler_params=pltpu.CompilerParams(
            collective_id=7, has_side_effects=True, vmem_limit_bytes=60 * 2**20
        ),
        name="middle",
    )(first, base, cotangent, rows, bias, keys, values, query_w, out_w, up_w, down_w)


def attend_scores(query, keys, key_valid):
    raw_scores = HD ** (-0.5) * jnp.einsum("fphe,fqhe->fhpq", query, keys, preferred_element_type=WIDE)
    if key_valid is None:
        return raw_scores
    return jnp.where(key_valid[:, None, None, :], raw_scores, NEGATIVE)


def attend_forward(query, keys, values, key_valid):
    scores = attend_scores(query, keys, key_valid)
    row_max = jnp.max(scores, axis=-1, keepdims=True)
    shifted = jnp.exp(scores - row_max)
    row_total = jnp.sum(shifted, axis=-1, keepdims=True)
    probs_low = (shifted / row_total).astype(NARROW)
    heads_out = jnp.einsum("fhpq,fqhe->fphe", probs_low, values, preferred_element_type=WIDE)
    return (heads_out.astype(NARROW), row_max + jnp.log(row_total))


def attend_backward(query, keys, values, key_valid, log_total, grad_out):
    probs = jnp.exp(attend_scores(query, keys, key_valid) - log_total)
    grad_probs = jnp.einsum("fphe,fqhe->fhpq", grad_out, values, preferred_element_type=WIDE)
    grad_values = jnp.einsum("fhpq,fphe->fqhe", probs.astype(NARROW), grad_out, preferred_element_type=WIDE)
    grad_scores = probs * (grad_probs - jnp.sum(grad_probs * probs, axis=-1, keepdims=True))
    grad_scores = grad_scores.astype(NARROW)
    grad_query = HD ** (-0.5) * jnp.einsum("fhpq,fqhe->fphe", grad_scores, keys, preferred_element_type=WIDE)
    grad_keys = HD ** (-0.5) * jnp.einsum("fhpq,fphe->fqhe", grad_scores, query, preferred_element_type=WIDE)
    return (grad_query, grad_keys, grad_values)


def over_heads(first, second):
    return jnp.einsum("fphe,fphe->fhp", first, second, precision=HIGHEST, preferred_element_type=WIDE)


def by_heads(weights, values):
    return jnp.einsum("fhp,fphe->fphe", weights, values, precision=HIGHEST)


def temporal_weights(query, keys, allowed, frames):
    score_list = []
    for offset in range(WIN):
        raw_scores = HD ** (-0.5) * jnp.einsum(
            "fphe,fphe->fhp", query, keys[offset : offset + frames], preferred_element_type=WIDE
        )
        score_list.append(jnp.where(allowed[offset][:, None, None], raw_scores, NEGATIVE))
    scores = jnp.stack(score_list)
    shifted = jnp.exp(scores - jnp.max(scores, axis=0, keepdims=True))
    return shifted / jnp.sum(shifted, axis=0, keepdims=True)


def temporal_mix(probs, values, frames):
    values_wide = values.astype(WIDE)
    mixed = by_heads(probs[0], values_wide[0:frames])
    for offset in range(1, WIN):
        mixed = mixed + by_heads(probs[offset], values_wide[offset : offset + frames])
    return mixed


def temporal_backward(query, keys, values, probs, grad_out, frames):
    query_wide, keys_wide = query.astype(WIDE), keys.astype(WIDE)
    values_wide, grad_wide = values.astype(WIDE), grad_out.astype(WIDE)
    grad_probs = jnp.stack(
        [over_heads(grad_wide, values_wide[offset : offset + frames]) for offset in range(WIN)]
    )
    grad_scores = probs * (grad_probs - jnp.sum(grad_probs * probs, axis=0, keepdims=True))
    grad_query = jnp.zeros(query.shape, WIDE)
    for offset in range(WIN):
        grad_query = grad_query + HD ** (-0.5) * by_heads(
            grad_scores[offset], keys_wide[offset : offset + frames]
        )

    def near_sums(weights, sources):
        found = []
        for cell in range(frames + WIN - 1):
            terms = [
                by_heads(weights[offset][cell - offset : cell - offset + 1], sources[cell - offset : cell - offset + 1])
                for offset in range(WIN)
                if 0 <= cell - offset < frames
            ]
            found.append(sum(terms[1:], terms[0]))
        return found

    grad_keys = near_sums(HD ** (-0.5) * grad_scores, query_wide)
    return (grad_query, grad_keys, near_sums(probs, grad_wide))


def to_next(cells):
    ends = lax.axis_size(FRAME) - 1
    return lax.ppermute(cells, FRAME, [(i, i + 1) for i in range(ends)])


def to_previous(cells):
    ends = lax.axis_size(FRAME) - 1
    return lax.ppermute(cells, FRAME, [(i + 1, i) for i in range(ends)])


def sum_matrix_grads(pieces):
    if not pieces:
        return []
    packed = jnp.concatenate([piece.astype(NARROW) for piece in pieces], axis=1)
    summed = lax.psum_scatter(packed, BOTH, scatter_dimension=0, tiled=True).astype(WIDE)
    found, start = [], 0
    for piece in pieces:
        found.append(summed[:, start : start + piece.shape[1]])
        start += piece.shape[1]
    return found


def per_device(
    latent, captions, bucket, clip_ids, window_mask, text_counts, time_table, ada_weight,
    spatial_inproj, spatial_outproj, temporal_inproj, temporal_outproj, caption_proj, cross_gain,
    cross_query, cross_keyval, cross_outproj, mlp_up, mlp_down, cotangent,
):
    count, groups, frames_axis = (lax.axis_size(axis) for axis in (LINE, GROUP, FRAME))
    place = lax.axis_index(LINE)
    frames, share, features = latent.shape[1:]
    patches = share * count
    tokens = frames * patches
    local = spatial_outproj.shape[0]
    clip_count, text_length, text_width = captions.shape[1:]
    slots = clip_count * text_length

    def flat(values):
        return values.reshape(tokens, -1)

    def grid(values):
        return values.reshape(frames, patches, -1)

    def heads(values):
        return split_heads(grid(values))

    def own(values):
        return lax.dynamic_slice_in_dim(grid(values), place * share, share, axis=1)

    spatial_in, temporal_in, keyval_in = (
        jnp.transpose(w, (1, 2, 0)).reshape(-1, features)
        for w in (spatial_inproj, temporal_inproj, cross_keyval)
    )
    query_in = cross_query.T

    chosen = (jnp.arange(time_table.shape[0]) == bucket[0]).astype(WIDE)
    cond_row = jnp.sum(chosen[:, None] * time_table.astype(WIDE), axis=0)
    act_low = swish_act(cond_row).astype(NARROW)
    caption_here = captions[0].reshape(slots, text_width)
    base_grid, normed_grid, mods, caption_share = call_opening(
        count, groups, frames_axis, latent[0], jnp.broadcast_to(act_low[None], (16, local)),
        jnp.transpose(ada_weight, (1, 0, 2)), caption_here,
    )
    base_zero, spatial_hidden = flat(base_grid), flat(normed_grid)
    text_part = dot(caption_here, caption_proj, 1, 0).astype(NARROW)
    text_rows = lax.all_gather(text_part, LINE, axis=1, tiled=True)

    def rows_of(*rows):
        filled = [jnp.zeros((features,), WIDE)] * (8 - len(rows))
        return jnp.stack(list(rows) + filled)

    spatial_packed = dot(spatial_hidden, spatial_in, 1, 1).astype(NARROW)
    spatial_query, spatial_keys, spatial_values = (
        heads(spatial_packed[:, i * local : (i + 1) * local]) for i in range(3)
    )
    spatial_heads, spatial_logs = attend_forward(spatial_query, spatial_keys, spatial_values, None)
    spatial_flat = flat(spatial_heads)
    spatial_out, base_one, temporal_hidden = call_forward(
        count,
        dot(spatial_flat, spatial_outproj, 1, 0).astype(NARROW),
        base_zero,
        rows_of(mods[2], 1.0 + mods[4], mods[3]),
    )

    cotangent_here, temporal_hidden = lax.optimization_barrier((cotangent[0], temporal_hidden))
    cotangent_full = flat(lax.all_gather(cotangent_here, LINE, axis=1, tiled=True))

    temporal_packed = dot(temporal_hidden, temporal_in, 1, 1).astype(NARROW)
    temporal_query = heads(temporal_packed[:, 0:local])
    own_pair = grid(temporal_packed[:, local:])
    near = jnp.concatenate(
        [to_next(own_pair[frames - 2 :]), own_pair, to_previous(own_pair[0:1])], axis=0
    )
    temporal_keys = split_heads(near[:, :, 0:local])
    temporal_values = split_heads(near[:, :, local:])
    first_frame = lax.axis_index(FRAME) * frames
    clip_near = lax.dynamic_slice_in_dim(
        jnp.pad(clip_ids[0], (2, 2), constant_values=-1), first_frame, frames + 4
    )
    own_clip = clip_near[2 : 2 + frames]
    allowed = jnp.stack(
        [
            (clip_near[offset : offset + frames] == own_clip)
            & ((window_mask[0][:, offset] == 1) | (offset == 2))
            for offset in range(WIN)
        ]
    )
    temporal_probs = temporal_weights(temporal_query, temporal_keys, allowed, frames)
    temporal_flat = flat(temporal_mix(temporal_probs, temporal_values, frames).astype(NARROW))
    text_packed = dot(text_rows, keyval_in, 1, 1).astype(NARROW)
    slot_pad = -slots % 128
    slot_index = jnp.arange(slots)
    key_valid = (own_clip[:, None] == (slot_index // text_length)[None, :]) & (
        slot_index % text_length < jnp.repeat(text_counts[0], text_length)
    )[None, :]
    bias = jnp.pad(jnp.where(key_valid, 0.0, NEGATIVE), ((0, 0), (0, slot_pad)), constant_values=NEGATIVE)
    bias = jnp.broadcast_to(bias[:, None], (frames, 8, slots + slot_pad))
    head_mask = (jnp.arange(local) // HD)[None, :] == jnp.arange(local // HD)[:, None]

    def by_head(values):
        padded = jnp.pad(values, ((0, slot_pad), (0, 0)))
        return jnp.where(head_mask[:, None], padded[None], 0).reshape(-1, local)

    def from_heads(values):
        kept = jnp.where(head_mask[:, None], values.reshape(local // HD, -1, local), 0.0)
        return jnp.sum(kept, axis=0)[0:slots]

    (
        base_three, grad_two, grad_temporal_low, grad_cross_low, grad_mlp_low, cross_hidden, mlp_hidden,
        mlp_low, grad_inner, cross_flat, grad_cross_packed, text_grad_keys, text_grad_values, sums_middle,
    ) = call_middle(
        count, frames, dot(temporal_flat, temporal_outproj, 1, 0).astype(NARROW), base_one, cotangent_full,
        rows_of(mods[5], cross_gain.astype(WIDE), 1.0 + mods[7], mods[6], mods[8]), bias,
        by_head(text_packed[:, :local]), by_head(text_packed[:, local:]),
        query_in, cross_outproj, mlp_up, mlp_down,
    )

    inside = can_scatter(groups, frames_axis, features)

    def matrix_grad(first, second):
        return dot(first, second, 0, 0).astype(NARROW)

    mlp_part = dot(mlp_low, mlp_down, 1, 0).astype(NARROW)
    mlp_out = lax.psum_scatter(grid(mlp_part), LINE, scatter_dimension=1, tiled=True).astype(WIDE)
    output = (own(base_three) + mods[8] * mlp_out).astype(NARROW)[None]
    gate_mlp_part = jnp.sum(cotangent[0].astype(WIDE) * mlp_out, axis=(0, 1))
    grad_text_packed = jnp.concatenate(
        [HD ** (-0.5) * from_heads(text_grad_keys), from_heads(text_grad_values)], axis=1
    )
    text_high, text_rest = split_pair(grad_text_packed)
    grad_keyval_part = dot(text_rows, text_high, 0, 0) + dot(text_rows, text_rest, 0, 0)
    text_grad_part = dot(text_high, keyval_in, 1, 0) + dot(text_rest, keyval_in, 1, 0)
    text_grad = lax.psum_scatter(text_grad_part.astype(NARROW), LINE, scatter_dimension=1, tiled=True)
    text_grad_all = lax.all_gather(text_grad, BOTH).reshape(groups, frames_axis, slots, local)
    text_grad_wide = jnp.sum(text_grad_all.astype(WIDE), axis=1).reshape(groups * slots, local)
    text_all_high, text_all_rest = split_pair(text_grad_wide)
    caption_rows = caption_share.reshape(groups * slots, -1)
    grad_caption = dot(caption_rows, text_all_high, 0, 0) + dot(caption_rows, text_all_rest, 0, 0)

    grad_temporal_heads = dot(grad_temporal_low, temporal_outproj, 1, 1).astype(NARROW)
    temporal_grad_query, near_grad_keys, near_grad_values = temporal_backward(
        temporal_query, temporal_keys, temporal_values, temporal_probs, heads(grad_temporal_heads), frames
    )

    def joined(first, last):
        return jnp.concatenate(
            [
                jnp.concatenate([part[cell].reshape(1, patches, local) for cell in range(first, last)], axis=0)
                for part in (near_grad_keys, near_grad_values)
            ],
            axis=2,
        )

    from_next = to_previous(joined(0, 2).astype(NARROW)).astype(WIDE)
    from_previous = to_next(joined(frames + 2, frames + 3).astype(NARROW)).astype(WIDE)
    own_grads = joined(2, 2 + frames)
    own_grads = (
        own_grads
        + jnp.pad(from_next, ((frames - 2, 0), (0, 0), (0, 0)))
        + jnp.pad(from_previous, ((0, frames - 1), (0, 0), (0, 0)))
    )
    grad_temporal_packed = jnp.concatenate(
        [flat(temporal_grad_query).astype(NARROW), flat(own_grads).astype(NARROW)], axis=1
    )
    early = [matrix_grad(mlp_hidden, grad_inner), matrix_grad(grad_mlp_low, mlp_low)]
    found = call_backward(
        count, groups, frames_axis, dot(grad_temporal_packed, temporal_in, 1, 0).astype(NARROW), base_one,
        grad_two, spatial_out, rows_of(1.0 + mods[4], mods[2]), early if inside else [], 2,
    )
    grad_one, grad_spatial_low, sums_temporal = found[:3]
    grad_up, grad_down = found[3:] if inside else sum_matrix_grads(early)

    grad_spatial_heads = dot(grad_spatial_low, spatial_outproj, 1, 1).astype(NARROW)
    spatial_grads = attend_backward(
        spatial_query, spatial_keys, spatial_values, None, spatial_logs, heads(grad_spatial_heads)
    )
    grad_spatial_packed = jnp.concatenate([flat(part) for part in spatial_grads], axis=1).astype(NARROW)
    grad_spatial_part = dot(grad_spatial_packed, spatial_in, 1, 0).astype(NARROW)
    side_row = jnp.pad(jnp.concatenate([cond_row, chosen]), (0, features - local - chosen.shape[0]))
    blank = jnp.zeros((features,), WIDE)
    small = jnp.stack(
        [blank, blank, gate_mlp_part]
        + [blank] * 5
        + [
            sums_temporal[2], sums_temporal[0], sums_temporal[1], sums_middle[3], sums_middle[0],
            sums_middle[1], sums_middle[2], side_row,
        ]
    )
    late = [
        matrix_grad(cross_hidden, grad_cross_packed),
        matrix_grad(grad_cross_low, cross_flat),
        grad_keyval_part.astype(NARROW),
        matrix_grad(temporal_hidden, grad_temporal_packed),
        matrix_grad(grad_temporal_low, temporal_flat),
        matrix_grad(spatial_hidden, grad_spatial_packed),
        matrix_grad(grad_spatial_low, spatial_flat),
    ]
    found = call_closing(
        count, groups, frames_axis, grid(grad_spatial_part), grid(base_zero), grid(grad_one), small,
        rows_of(1.0 + mods[1]), late if inside else [],
    )
    grad_latent, small_all = found[:2]
    late_grads = found[2:] if inside else sum_matrix_grads(late)
    grad_query_cross, grad_outproj_cross, grad_keyval_cross = late_grads[:3]
    grad_inproj_temporal, grad_outproj_temporal, grad_inproj_spatial, grad_outproj_spatial = late_grads[3:]

    small_all = small_all.reshape(groups, frames_axis, 16, features)
    small_sums = jnp.sum(small_all, axis=1)
    modulation_grad = jnp.stack([small_sums[:, i] for i in (0, 1, 8, 9, 10, 11, 12, 13, 2)], axis=1)
    grad_gain = jnp.sum(small_sums[:, 14], axis=0)
    cond_all = small_all[:, 0, 15, 0:local]
    chosen_all = small_all[:, 0, 15, local : local + chosen.shape[0]]
    act_all, swish_pull = jax.vjp(swish_act, cond_all)
    act_all = act_all.astype(NARROW).astype(WIDE)
    column = features // (groups * frames_axis)
    rank = lax.axis_index(BOTH)
    column_grads = lax.dynamic_slice_in_dim(modulation_grad, rank * column, column, axis=2)
    grad_ada = jnp.einsum("gc,gkd->ckd", act_all, column_grads, precision=HIGHEST)
    grad_act = jnp.einsum("ckd,gkd->gc", ada_weight.astype(WIDE), modulation_grad, precision=HIGHEST)
    grad_cond = swish_pull(grad_act)[0]
    grad_table = jnp.einsum("gn,gc->nc", chosen_all, grad_cond, precision=HIGHEST)

    def unpack(values, parts):
        return values.reshape(values.shape[0], parts, -1)

    return (
        output,
        grad_latent[None],
        grad_table,
        grad_ada,
        unpack(grad_inproj_spatial, 3),
        grad_outproj_spatial.T,
        unpack(grad_inproj_temporal, 3),
        grad_outproj_temporal.T,
        grad_caption,
        grad_gain,
        grad_query_cross,
        unpack(grad_keyval_cross, 2),
        grad_outproj_cross.T,
        grad_up,
        grad_down.T,
    )


def solution(mesh):
    tokens = P(GROUP, FRAME, LINE, None)
    packed_in, rows_in, columns_in = P(None, None, LINE), P(LINE, None), P(None, LINE)
    in_specs = (
        tokens, P(GROUP, None, None, None), P(GROUP), P(GROUP, None), P(GROUP, FRAME, None),
        P(GROUP, None), columns_in, P(LINE, None, None), packed_in, rows_in, packed_in, rows_in,
        columns_in, P(), columns_in, packed_in, rows_in, columns_in, rows_in, tokens,
    )
    packed_out, rows_out, columns_out = P(BOTH, None, LINE), P(LINE, BOTH), P(BOTH, LINE)
    out_specs = (
        tokens, tokens, columns_in, P(LINE, None, BOTH), packed_out, rows_out, packed_out, rows_out,
        columns_out, P(), columns_out, packed_out, rows_out, columns_out, rows_out,
    )
    return jax.shard_map(
        per_device, mesh=mesh, in_specs=in_specs, out_specs=out_specs, check_vma=False
    )
```

```python
import functools

import jax
import jax.numpy as jnp
from jax import lax
from jax.experimental import pallas as pl
from jax.experimental.pallas import tpu as pltpu
from jax.sharding import PartitionSpec as P

HD = 72
WIN = 4
EPSILON = 1e-06
HIGHEST = lax.Precision.HIGHEST
NEGATIVE = -1e30
WIDE = jnp.float32
NARROW = jnp.bfloat16
GROUP, FRAME, LINE = "group", "frame", "tensor"
BOTH = (GROUP, FRAME)
MESH = pl.DeviceIdType.MESH
CHUNKS = 16
LAG = 2
VMEM_LIMIT = 48 * 2**20


def swish_act(values):
    return values / (1.0 + jnp.exp(-values))


def gelu_tanh(values):
    return (
        0.5
        * values
        * (1.0 + jnp.tanh(0.7978845608028654 * (values + 0.044715 * values * values * values)))
    )


def dot(first, second, contract_first, contract_second):
    return lax.dot_general(
        first, second, (((contract_first,), (contract_second,)), ((), ())), preferred_element_type=WIDE
    )


def split_heads(values):
    return values.reshape(values.shape[:-1] + (values.shape[-1] // HD, HD))


def split_pair(values):
    high_part = values.astype(NARROW)
    rest_part = (values - high_part.astype(WIDE)).astype(NARROW)
    return (high_part, rest_part)


def norm_parts(values):
    centred = values - jnp.mean(values, axis=-1, keepdims=True)
    spread = lax.rsqrt(jnp.mean(centred * centred, axis=-1, keepdims=True) + EPSILON)
    return centred * spread, spread


def norm_pull(scaled, normal, spread):
    return spread * (
        scaled
        - jnp.mean(scaled, axis=-1, keepdims=True)
        - normal * jnp.mean(scaled * normal, axis=-1, keepdims=True)
    )


def remote(source, target, send_sem, recv_sem, where):
    return pltpu.make_async_remote_copy(
        src_ref=source,
        dst_ref=target,
        send_sem=send_sem,
        recv_sem=recv_sem,
        device_id=where,
        device_id_type=MESH,
    )


def greet_line(place, count, more=0, others=()):
    barrier = pltpu.get_barrier_semaphore()
    for where in others:
        pl.semaphore_signal(barrier, inc=1, device_id=where, device_id_type=MESH)

    @pl.when(place > 0)
    def _():
        pl.semaphore_signal(barrier, inc=1, device_id={LINE: place - 1}, device_id_type=MESH)

    @pl.when(place < count - 1)
    def _():
        pl.semaphore_signal(barrier, inc=1, device_id={LINE: place + 1}, device_id_type=MESH)

    pl.semaphore_wait(
        barrier, (place > 0).astype(jnp.int32) + (place < count - 1).astype(jnp.int32) + len(others) + more
    )


class Scatter:
    def __init__(self, groups, frames_axis, source, scratch):
        self.source = source
        self.inbox, self.stage, self.found, self.kept = scratch[:4]
        self.twin_send, self.twin_recv, self.peer_send, self.peer_recv = scratch[4:8]
        self.groups, self.frames_axis = groups, frames_axis
        self.block = source.shape[0] // (groups * frames_axis)
        self.total = groups // 2 * frames_axis
        group = lax.axis_index(GROUP)
        self.core = lax.rem(group, 2)
        self.me = lax.div(group, 2) * frames_axis + lax.axis_index(FRAME)
        self.twin = {GROUP: group + 1 - 2 * self.core}

    def peer(self, step):
        to = lax.rem(self.me + step, self.total)
        return to, {GROUP: lax.div(to, self.frames_axis) * 2 + self.core, FRAME: lax.rem(to, self.frames_axis)}

    def partners(self):
        return [self.twin] + [self.peer(step)[1] for step in range(1, self.total)]

    def twin_copy(self, high):
        rows = self.block * self.frames_axis
        first = pl.multiple_of((high * 2 + 1 - self.core) * rows, 16)
        return remote(
            self.source.at[pl.ds(first, rows)],
            self.inbox.at[pl.ds(high * rows, rows)],
            self.twin_send.at[high],
            self.twin_recv.at[high],
            self.twin,
        )

    def peer_copy(self, step):
        return remote(
            self.stage.at[step - 1],
            self.found.at[step - 1],
            self.peer_send.at[step],
            self.peer_recv.at[step],
            self.peer(step)[1],
        )

    def start(self):
        for high in range(self.groups // 2):
            self.twin_copy(high).start()

    def fold(self, step):
        if step == self.total - 1:
            for high in range(self.groups // 2):
                self.twin_copy(high).wait_recv()
        to = self.peer(step)[0]
        high, frame = lax.div(to, self.frames_axis), lax.rem(to, self.frames_axis)
        first = ((high * 2 + self.core) * self.frames_axis + frame) * self.block
        mine = self.source[pl.ds(pl.multiple_of(first, 16), self.block)]
        other = self.inbox[pl.ds(pl.multiple_of(to * self.block, 16), self.block)]
        summed = mine.astype(WIDE) + other.astype(WIDE)
        if step == 0:
            self.kept[...] = summed
        else:
            self.stage[step - 1] = summed.astype(NARROW)
            self.peer_copy(step).start()

    def fold_all(self):
        for step in range(self.total - 1, -1, -1):
            self.fold(step)

    def finish(self, results):
        for step in range(1, self.total):
            self.peer_copy(step).wait_recv()
        start = 0
        for result in results:
            span = slice(start, start + result.shape[1])
            summed = self.kept[:, span]
            for step in range(1, self.total):
                summed = summed + self.found[step - 1, :, span].astype(WIDE)
            result[...] = summed
            start += result.shape[1]
        for high in range(self.groups // 2):
            self.twin_copy(high).wait_send()
        for step in range(1, self.total):
            self.peer_copy(step).wait_send()

    @staticmethod
    def scratch(groups, frames_axis, width, columns):
        total, block = groups // 2 * frames_axis, width // (groups * frames_axis)
        dma = pltpu.SemaphoreType.DMA
        return (
            [pltpu.VMEM((width // 2, columns), NARROW)]
            + [pltpu.VMEM((total - 1, block, columns), NARROW)] * 2
            + [pltpu.VMEM((block, columns), WIDE)]
            + [dma((groups // 2,))] * 2
            + [dma((total,))] * 2
        )


def can_scatter(groups, frames_axis, width):
    return groups % 2 == 0 and width % (16 * groups * frames_axis) == 0


class Products:
    def __init__(self, groups, frames_axis, pairs, results, scratch, scattered):
        self.pairs, self.results, self.scattered = pairs, results, scattered
        self.source = scratch[0] if scattered else None
        self.aside = Scatter(groups, frames_axis, self.source, scratch[1:]) if scattered else None

    def product(self, i):
        first, second = self.pairs[i]
        found = dot(first[...], second[...], 0, 0).astype(NARROW)
        if self.scattered:
            start = sum(item.shape[1] for _, item in self.pairs[:i])
            self.source[:, start : start + second.shape[1]] = found
        else:
            self.results[i][...] = found

    def work(self):
        found = [functools.partial(self.product, i) for i in range(len(self.pairs))]
        return found + ([self.aside.start] if self.scattered else [])

    def partners(self):
        return self.aside.partners() if self.scattered else []

    def finish(self):
        if self.scattered:
            self.aside.finish(self.results)

    @staticmethod
    def shapes(groups, frames_axis, columns, features):
        if not can_scatter(groups, frames_axis, features):
            return [jax.ShapeDtypeStruct((features, n), NARROW) for n in columns], []
        block = features // (groups * frames_axis)
        results = [jax.ShapeDtypeStruct((block, n), WIDE) for n in columns]
        source = [pltpu.VMEM((features, sum(columns)), NARROW)]
        return results, source + Scatter.scratch(groups, frames_axis, features, sum(columns))


class GroupExchange:
    def __init__(self, groups, frames_axis, source, every, scratch):
        self.groups, self.frames_axis = groups, frames_axis
        self.source, self.every = source, every
        self.near, self.frame_send, self.frame_recv, self.group_send, self.group_recv = scratch
        self.group, self.frame = lax.axis_index(GROUP), lax.axis_index(FRAME)

    def frame_copy(self, step):
        return remote(
            self.source,
            self.near.at[step - 1],
            self.frame_send.at[step],
            self.frame_recv.at[step],
            {FRAME: lax.rem(self.frame + step, self.frames_axis)},
        )

    def group_copy(self, step):
        own = self.every.at[self.group]
        return remote(
            own,
            own,
            self.group_send.at[step],
            self.group_recv.at[step],
            {GROUP: lax.rem(self.group + step, self.groups)},
        )

    def partners(self):
        return [
            {FRAME: lax.rem(self.frame + step, self.frames_axis)} for step in range(1, self.frames_axis)
        ] + [{GROUP: lax.rem(self.group + step, self.groups)} for step in range(1, self.groups)]

    def start(self):
        for step in range(1, self.frames_axis):
            self.frame_copy(step).start()

    def spread(self):
        for step in range(1, self.frames_axis):
            self.frame_copy(step).wait_recv()
        summed = self.source[...].astype(WIDE)
        for step in range(1, self.frames_axis):
            summed = summed + self.near[step - 1].astype(WIDE)
        self.every[self.group] = summed.astype(NARROW)
        for step in range(1, self.groups):
            self.group_copy(step).start()

    def finish(self):
        for step in range(1, self.frames_axis):
            self.frame_copy(step).wait_send()
        for step in range(1, self.groups):
            self.group_copy(step).wait_recv()
            self.group_copy(step).wait_send()

    @staticmethod
    def scratch(groups, frames_axis, shape):
        dma = pltpu.SemaphoreType.DMA
        return (
            [pltpu.VMEM((max(frames_axis - 1, 1),) + shape, NARROW)]
            + [dma((frames_axis,))] * 2
            + [dma((groups,))] * 2
        )


def grad_tile(first, second, result, start, size):
    result[start : start + size] = dot(first[:, start : start + size], second[...], 0, 0).astype(NARROW)


def can_scatter(groups, frames_axis, width):
    return groups % 2 == 0 and width % (16 * groups * frames_axis) == 0


class LineGather:
    def __init__(self, count, place, slot_of, sems):
        self.count, self.place, self.last, self.slot_of = count, place, count - 1, slot_of
        self.up_send, self.down_send, self.arrived = sems

    def shift(self, owner, up):
        slot = self.slot_of(owner)
        to = self.place + 1 if up else self.place - 1
        sent = (self.up_send if up else self.down_send).at[owner]
        return remote(slot, slot, sent, self.arrived.at[owner], {LINE: to})

    def start(self):
        @pl.when(self.place < self.last)
        def _():
            self.shift(self.place, True).start()

        @pl.when(self.place > 0)
        def _():
            self.shift(self.place, False).start()

    def arrive(self, distance):
        @pl.when(self.place >= distance)
        def _():
            self.shift(self.place - distance, True).wait_recv()

            @pl.when(self.place < self.last)
            def _():
                self.shift(self.place - distance, True).start()

        @pl.when(self.place + distance <= self.last)
        def _():
            self.shift(self.place + distance, False).wait_recv()

            @pl.when(self.place > 0)
            def _():
                self.shift(self.place + distance, False).start()

    def settle(self):
        for owner in range(self.count):

            @pl.when((self.place < self.last) & (owner <= self.place))
            def _():
                self.shift(owner, True).wait_send()

            @pl.when((self.place > 0) & (owner >= self.place))
            def _():
                self.shift(owner, False).wait_send()


class LineScatter:
    def __init__(self, count, place, pieces, value_of, land, stage, sems):
        self.count, self.place, self.last, self.pieces = count, place, count - 1, pieces
        self.value_of, self.land, self.stage = value_of, land, stage
        self.from_left, self.from_right, self.to_left, self.to_right = sems

    def pass_on(self, owner, piece, right):
        side = 0 if right else 1
        return remote(
            self.stage.at[side, owner, piece],
            self.land.at[side, owner, piece],
            (self.to_right if right else self.to_left).at[owner, piece],
            (self.from_left if right else self.from_right).at[owner, piece],
            {LINE: self.place + 1 if right else self.place - 1},
        )

    def relay(self, distance, right, chosen=None):
        owner = self.place + distance if right else self.place - distance
        source = (self.place == 0) if right else (self.place == self.last)
        side = 0 if right else 1

        @pl.when((owner <= self.last) if right else (owner >= 0))
        def _():
            for piece in chosen if chosen is not None else range(self.pieces):

                @pl.when(source)
                def _():
                    self.stage[side, owner, piece] = self.value_of(owner, piece)

                @pl.when(jnp.logical_not(source))
                def _():
                    self.pass_on(owner, piece, right).wait_recv()
                    self.stage[side, owner, piece] = (
                        self.value_of(owner, piece).astype(WIDE) + self.land[side, owner, piece].astype(WIDE)
                    ).astype(NARROW)

                self.pass_on(owner, piece, right).start()

    def relay_both(self, distance, chosen=None):
        self.relay(distance, True, chosen)
        self.relay(distance, False, chosen)

    def total(self, piece):
        place = self.place

        @pl.when(place > 0)
        def _():
            self.pass_on(place, piece, True).wait_recv()

        @pl.when(place < self.last)
        def _():
            self.pass_on(place, piece, False).wait_recv()

        left_part = jnp.where(place > 0, self.land[0, place, piece].astype(WIDE), 0.0)
        right_part = jnp.where(place < self.last, self.land[1, place, piece].astype(WIDE), 0.0)
        return self.value_of(place, piece).astype(WIDE) + left_part + right_part

    def settle(self):
        for owner in range(self.count):
            for piece in range(self.pieces):

                @pl.when(owner > self.place)
                def _():
                    self.pass_on(owner, piece, True).wait_send()

                @pl.when(owner < self.place)
                def _():
                    self.pass_on(owner, piece, False).wait_send()


def gather_sems(count):
    return [pltpu.SemaphoreType.DMA((count,))] * 3


def scatter_sems(count, pieces):
    return [pltpu.SemaphoreType.DMA((count, pieces))] * 4


def line_sum(count, place, part_ref, land, cross, stage, total, sems, consume, early=(), folds=()):
    in_send, land_recv, cross_recv, out_send, out_recv = sems
    depth = part_ref.shape[0] // CHUNKS
    half = count // 2
    left = place < half
    level = jnp.where(left, place, count - 1 - place)
    inner = jnp.where(left, place + 1, place - 1)
    outer = jnp.where(left, place - 1, place + 1)
    is_end, is_middle = level == 0, level == half - 1

    def rows_of(chunk):
        return pl.ds(pl.multiple_of(chunk * depth, depth), depth)

    def inward(chunk):
        rows = rows_of(chunk)
        return remote(stage.at[rows], land.at[rows], in_send.at[chunk], land_recv.at[chunk], {LINE: inner})

    def across(chunk):
        rows = rows_of(chunk)
        return remote(stage.at[rows], cross.at[rows], in_send.at[chunk], cross_recv.at[chunk], {LINE: inner})

    def outward(chunk):
        rows = rows_of(chunk)
        return remote(total.at[rows], total.at[rows], out_send.at[chunk], out_recv.at[chunk], {LINE: outer})

    def send_in(chunk):
        @pl.when(is_middle)
        def _():
            across(chunk).start()

        @pl.when(jnp.logical_not(is_middle))
        def _():
            inward(chunk).start()

    def gather_in(chunk):
        rows = rows_of(chunk)
        inward(chunk).wait_recv()
        stage[rows] = (part_ref[rows].astype(WIDE) + land[rows].astype(WIDE)).astype(NARROW)
        send_in(chunk)

    def finish(chunk):
        rows = rows_of(chunk)

        @pl.when(is_middle)
        def _():
            across(chunk).wait_recv()
            total[rows] = (stage[rows].astype(WIDE) + cross[rows].astype(WIDE)).astype(NARROW)

        @pl.when(jnp.logical_not(is_middle))
        def _():
            outward(chunk).wait_recv()

        @pl.when(jnp.logical_not(is_end))
        def _():
            outward(chunk).start()

        consume(rows)

    def begin(chunk, carry):
        rows = rows_of(chunk)
        stage[rows] = part_ref[rows]
        send_in(chunk)
        return carry

    def step(number, carry):
        for i, work in enumerate(early):

            @pl.when(jnp.logical_not(is_end) & (number == i))
            def _():
                work()

        @pl.when(jnp.logical_not(is_end) & (number < CHUNKS))
        def _():
            gather_in(number)

        @pl.when(number >= LAG)
        def _():
            finish(number - LAG)

        for i, work in enumerate(folds):

            @pl.when(number == len(early) + 1 + i)
            def _():
                work()

        return carry

    @pl.when(is_end)
    def _():
        lax.fori_loop(0, CHUNKS, begin, 0)
        for work in early:
            work()

    lax.fori_loop(0, CHUNKS + LAG, step, 0)

    def settle(chunk, carry):
        @pl.when(is_middle)
        def _():
            across(chunk).wait_send()

        @pl.when(jnp.logical_not(is_middle))
        def _():
            inward(chunk).wait_send()

        @pl.when(jnp.logical_not(is_end))
        def _():
            outward(chunk).wait_send()

        return carry

    lax.fori_loop(0, CHUNKS, settle, 0)


def forward_kernel(
    count, part_ref, base_ref, rows_ref, out_ref, next_ref, normed_ref, land, cross, stage, *sems
):
    place = lax.axis_index(LINE)
    greet_line(place, count)
    gate, gain, shift = (rows_ref[i : i + 1] for i in range(3))

    def consume(rows):
        moved = base_ref[rows] + gate * out_ref[rows].astype(WIDE)
        next_ref[rows] = moved
        normed_ref[rows] = (norm_parts(moved)[0] * gain + shift).astype(NARROW)

    line_sum(count, place, part_ref, land, cross, stage, out_ref, sems, consume)


def fold_works(products):
    aside = products.aside
    return [functools.partial(aside.fold, aside.total - 1 - i) for i in range(aside.total)] if aside else []


def backward_kernel(count, groups, frames_axis, many, scattered, *refs):
    part_ref, base_ref, grad_ref, below_ref, rows_ref, text_ref = refs[:6]
    factors, refs = refs[6 : 6 + 2 * many], refs[6 + 2 * many :]
    moved_ref, low_ref, sums_ref, text_all = refs[:4]
    results, refs = refs[4 : 4 + many], refs[4 + many :]
    total, land, cross, stage, tally = refs[:5]
    sems, exchange_scratch, scratch = refs[5:10], refs[10:15], refs[15:]
    place = lax.axis_index(LINE)
    pairs = list(zip(factors[0::2], factors[1::2]))
    products = Products(groups, frames_axis, pairs, results, scratch, scattered)
    exchange = GroupExchange(groups, frames_axis, text_ref, text_all, exchange_scratch)
    greet_line(place, count, 0, exchange.partners() + products.partners())
    exchange.start()
    gain, gate = (rows_ref[i : i + 1] for i in range(2))
    tally[...] = jnp.zeros_like(tally)

    def consume(rows):
        grads = total[rows].astype(WIDE)
        normal, spread = norm_parts(base_ref[rows])
        moved = grad_ref[rows] + norm_pull(grads * gain, normal, spread)
        moved_ref[rows] = moved
        low_ref[rows] = (gate * moved).astype(NARROW)
        for i, terms in enumerate((grads, grads * normal, moved * below_ref[rows].astype(WIDE))):
            tally[i] += jnp.sum(terms.reshape(-1, 8, terms.shape[-1]), axis=0)

    folds = fold_works(products)
    line_sum(
        count, place, part_ref, land, cross, stage, total, sems, consume,
        products.work(), folds[:1] + [exchange.spread] + folds[1:],
    )
    sums_ref[...] = jnp.zeros_like(sums_ref)
    for i in range(3):
        sums_ref[i : i + 1] = jnp.sum(tally[i], axis=0, keepdims=True)
    products.finish()
    exchange.finish()


def vmem(count):
    return [pl.BlockSpec(memory_space=pltpu.VMEM)] * count


def line_sems():
    return [pltpu.SemaphoreType.DMA((CHUNKS,))] * 5


def call_forward(count, part, base, rows):
    shape = part.shape
    return pl.pallas_call(
        functools.partial(forward_kernel, count),
        out_shape=(
            jax.ShapeDtypeStruct(shape, NARROW),
            jax.ShapeDtypeStruct(shape, WIDE),
            jax.ShapeDtypeStruct(shape, NARROW),
        ),
        in_specs=vmem(3),
        out_specs=tuple(vmem(3)),
        scratch_shapes=[pltpu.VMEM(shape, NARROW)] * 3 + line_sems(),
        compiler_params=pltpu.CompilerParams(
            collective_id=1, has_side_effects=True, vmem_limit_bytes=VMEM_LIMIT
        ),
        name="forward_sum",
    )(part, base, rows)


def call_backward(count, groups, frames_axis, part, base, grad, below, rows, text, pairs):
    shape = part.shape
    columns = [second.shape[1] for _, second in pairs]
    results, scratch = Products.shapes(groups, frames_axis, columns, shape[1])
    return pl.pallas_call(
        functools.partial(backward_kernel, count, groups, frames_axis, len(pairs), bool(scratch)),
        out_shape=(
            jax.ShapeDtypeStruct(shape, WIDE),
            jax.ShapeDtypeStruct(shape, NARROW),
            jax.ShapeDtypeStruct((8, shape[1]), WIDE),
            jax.ShapeDtypeStruct((groups,) + text.shape, NARROW),
            *results,
        ),
        in_specs=vmem(6 + 2 * len(pairs)),
        out_specs=tuple(vmem(4 + len(results))),
        scratch_shapes=[pltpu.VMEM(shape, NARROW)] * 4
        + [pltpu.VMEM((3, 8, shape[1]), WIDE)]
        + line_sems()
        + GroupExchange.scratch(groups, frames_axis, text.shape)
        + scratch,
        compiler_params=pltpu.CompilerParams(
            collective_id=2, has_side_effects=True, vmem_limit_bytes=VMEM_LIMIT
        ),
        name="backward_sum",
    )(part, base, grad, below, rows, text, *(item for pair in pairs for item in pair))


def head_mask(head, shape):
    lane = lax.broadcasted_iota(jnp.int32, shape, len(shape) - 1)
    return (lane >= head * HD) & (lane < (head + 1) * HD)


def spread_heads(values, result):
    rows = values.shape[0]
    for head in range(values.shape[1] // HD):
        kept = jnp.where(head_mask(head, values.shape), values.astype(WIDE), 0.0)
        result[head * rows : (head + 1) * rows] = kept.astype(NARROW)


def collect_heads(values, rows):
    found = jnp.zeros((rows, values.shape[1]), WIDE)
    for head in range(values.shape[0] // rows):
        found = jnp.where(head_mask(head, found.shape), values[head * rows : (head + 1) * rows], found)
    return found


def spatial_backward(given, asked, keys, values, key_rows, value_rows, probs_low, scores_low):
    rows, scale = asked.shape[0], HD ** (-0.5)
    heads = asked.shape[1] // HD
    spread_heads(keys, key_rows)
    spread_heads(values, value_rows)
    for head in range(heads):
        spot = slice(head * rows, (head + 1) * rows)
        scores = scale * dot(asked, key_rows[spot], 1, 1)
        raised = jnp.exp(scores - jnp.max(scores, axis=-1, keepdims=True))
        probs = raised * (1.0 / jnp.sum(raised, axis=-1, keepdims=True))
        pulled = dot(given, value_rows[spot], 1, 1)
        moved = probs * (pulled - jnp.sum(pulled * probs, axis=-1, keepdims=True))
        probs_low[:, spot] = probs.astype(NARROW)
        scores_low[:, spot] = moved.astype(NARROW)
    grad_query = scale * dot(scores_low[...], key_rows[...], 1, 0)
    grad_keys = scale * collect_heads(dot(scores_low[...], asked, 0, 0), rows)
    grad_values = collect_heads(dot(probs_low[...], given, 0, 0), rows)
    return grad_query, grad_keys, grad_values


def closing_kernel(count, groups, frames_axis, frames, scattered, *refs):
    (
        low_ref, base_ref, grad_ref, small_ref, rows_ref, packed_ref, heads_ref, hidden_ref, in_ref, out_ref,
        latent_ref, every_ref, in_result, out_result,
        part_ref, grad_packed, key_rows, value_rows, probs_low, scores_low,
        land, stage, line_rows, own_rows, tally,
    ) = refs[:25]
    line_send, line_recv, all_send, all_recv = refs[29:33]
    place, group, here = (lax.axis_index(axis) for axis in (LINE, GROUP, FRAME))
    last = count - 1
    share = latent_ref.shape[1]
    local = out_ref.shape[0]
    everyone = groups * frames_axis
    rank = group * frames_axis + here
    products = Products(
        groups, frames_axis, [(hidden_ref, grad_packed), (low_ref, heads_ref)], [in_result, out_result],
        refs[33:], scattered,
    )

    def member(ahead):
        to = lax.rem(rank + ahead, everyone)
        return {GROUP: lax.div(to, frames_axis), FRAME: lax.rem(to, frames_axis)}

    def neighbour(ahead):
        return {LINE: lax.rem(place + ahead, count)}

    barrier = pltpu.get_barrier_semaphore()

    def greet(ahead, carry):
        pl.semaphore_signal(barrier, inc=1, device_id=member(ahead), device_id_type=MESH)
        return carry

    for ahead in range(1, count):
        pl.semaphore_signal(barrier, inc=1, device_id=neighbour(ahead), device_id_type=MESH)
    lax.fori_loop(1, everyone, greet, 0)
    pl.semaphore_wait(barrier, last + everyone - 1)

    def rows_of(owner):
        return pl.ds(pl.multiple_of(owner * share, share), share)

    passing = LineScatter(
        count, place, frames, lambda owner, frame: part_ref[frame, rows_of(owner)], land, stage, refs[25:29]
    )
    patches = base_ref.shape[1]
    for frame in range(frames):
        rows = slice(frame * patches, (frame + 1) * patches)
        given = dot(low_ref[rows], out_ref[...], 1, 1).astype(NARROW)
        asked, keys, values = (packed_ref[rows, i * local : (i + 1) * local] for i in range(3))
        parts = jnp.zeros(part_ref.shape[1:], WIDE)
        found = spatial_backward(given, asked, keys, values, key_rows, value_rows, probs_low, scores_low)
        for i, item in enumerate(found):
            low = item.astype(NARROW)
            grad_packed[rows, i * local : (i + 1) * local] = low
            parts = parts + dot(low, in_ref[i * local : (i + 1) * local], 1, 0)
        part_ref[frame] = parts.astype(NARROW)
        passing.relay_both(last, (frame,))
    for work in products.work():
        work()

    tally[...] = jnp.zeros_like(tally)
    depth = 32
    blocks = base_ref.shape[1] // depth

    def add_rows(number, carry):
        frame, rows = lax.div(number, blocks), pl.ds(pl.multiple_of(lax.rem(number, blocks) * depth, depth), depth)
        normal = norm_parts(base_ref[frame, rows])[0]
        grads = part_ref[frame, rows].astype(WIDE)
        for i, terms in enumerate((grads, grads * normal)):
            tally[i] += jnp.sum(terms.reshape(-1, 8, terms.shape[-1]), axis=0)
        return carry

    lax.fori_loop(0, frames * blocks, add_rows, 0)
    line_rows[place] = small_ref[0:8]
    for i in range(2):
        line_rows[place, i : i + 1] = jnp.sum(tally[i], axis=0, keepdims=True)

    def line_copy(ahead):
        return remote(
            line_rows.at[place], line_rows.at[place], line_send.at[ahead], line_recv.at[ahead], neighbour(ahead)
        )

    def all_copy(ahead):
        return remote(
            own_rows, every_ref.at[rank], all_send.at[ahead], all_recv.at[ahead], member(ahead)
        )

    for ahead in range(1, count):
        line_copy(ahead).start()
    for distance in range(last - 1, 0, -1):
        passing.relay_both(distance)
        if scattered and distance == last - 1:
            products.aside.fold_all()
    for ahead in range(1, count):
        line_copy(ahead).wait_recv()
    summed = line_rows[0]
    for i in range(1, count):
        summed = summed + line_rows[i]
    own_rows[0:8] = summed
    own_rows[8:16] = small_ref[8:16]
    every_ref[rank] = own_rows[...]

    def send_rows(ahead, carry):
        all_copy(ahead).start()
        return carry

    lax.fori_loop(1, everyone, send_rows, 0)

    own = rows_of(place)
    for frame in range(frames):
        grads = passing.total(frame)
        normal, spread = norm_parts(base_ref[frame, own])
        latent_ref[frame] = (
            grad_ref[frame, own] + norm_pull(grads * rows_ref[0:1], normal, spread)
        ).astype(NARROW)

    passing.settle()
    for ahead in range(1, count):
        line_copy(ahead).wait_send()

    def settle(ahead, carry):
        all_copy(ahead).wait_recv()
        all_copy(ahead).wait_send()
        return carry

    lax.fori_loop(1, everyone, settle, 0)
    products.finish()


def call_closing(count, groups, frames_axis, low, base, grad, small, rows, packed, heads, hidden, in_w, out_w):
    frames, patches, features = base.shape
    everyone = groups * frames_axis
    share = patches // count
    local = out_w.shape[0]
    results, scratch = Products.shapes(groups, frames_axis, [packed.shape[1], local], features)
    dma = pltpu.SemaphoreType.DMA
    wide_keys = local // HD * patches
    return pl.pallas_call(
        functools.partial(closing_kernel, count, groups, frames_axis, frames, bool(scratch)),
        out_shape=(
            jax.ShapeDtypeStruct((frames, share, features), NARROW),
            jax.ShapeDtypeStruct((everyone, 16, features), WIDE),
            *results,
        ),
        in_specs=vmem(10),
        out_specs=tuple(vmem(4)),
        scratch_shapes=[
            pltpu.VMEM((frames, patches, features), NARROW),
            pltpu.VMEM(packed.shape, NARROW),
            pltpu.VMEM((wide_keys, local), NARROW),
            pltpu.VMEM((wide_keys, local), NARROW),
            pltpu.VMEM((patches, wide_keys), NARROW),
            pltpu.VMEM((patches, wide_keys), NARROW),
            pltpu.VMEM((2, count, frames, share, features), NARROW),
            pltpu.VMEM((2, count, frames, share, features), NARROW),
            pltpu.VMEM((count, 8, features), WIDE),
            pltpu.VMEM((16, features), WIDE),
            pltpu.VMEM((2, 8, features), WIDE),
        ]
        + scatter_sems(count, frames)
        + [dma((count,))] * 2
        + [dma((everyone,))] * 2
        + scratch,
        compiler_params=pltpu.CompilerParams(
            collective_id=4, has_side_effects=True, vmem_limit_bytes=VMEM_LIMIT
        ),
        name="closing",
    )(low, base, grad, small, rows, packed, heads, hidden, in_w, out_w)


def opening_kernel(
    count, groups, frames_axis, latent_ref, act_ref, ada_ref, captions_ref,
    base_ref, normed_ref, mods_ref, spread_ref,
    land, ada, mine, others,
    up_send, down_send, land_recv, ada_sem, mods_send, mods_recv, cap_send, cap_recv, cap_local,
):
    place = lax.axis_index(LINE)
    group = lax.axis_index(GROUP)
    here = lax.axis_index(FRAME)
    last = count - 1
    width = spread_ref.shape[2]
    parts = ada_ref.shape[0]
    share = latent_ref.shape[1]

    loads = [pltpu.make_async_copy(ada_ref.at[k], ada.at[k], ada_sem.at[k]) for k in range(parts)]
    for load in loads:
        load.start()

    barrier = pltpu.get_barrier_semaphore()
    for ahead in range(1, count):
        pl.semaphore_signal(
            barrier, inc=1, device_id={LINE: lax.rem(place + ahead, count)}, device_id_type=MESH
        )
    for ahead in range(1, groups):
        pl.semaphore_signal(
            barrier, inc=1, device_id={GROUP: lax.rem(group + ahead, groups)}, device_id_type=MESH
        )
    pl.semaphore_wait(barrier, count - 1 + groups - 1)

    def shift(owner, up):
        to = place + 1 if up else place - 1
        return remote(
            land.at[owner], land.at[owner], (up_send if up else down_send).at[owner], land_recv.at[owner], {LINE: to}
        )

    land[place] = latent_ref[...]

    @pl.when(place < last)
    def _():
        shift(place, True).start()

    @pl.when(place > 0)
    def _():
        shift(place, False).start()

    def caption_block(to):
        if len(captions_ref.shape) == 3:
            return captions_ref.at[to]
        first = pl.multiple_of((to * frames_axis + here) * width, width)
        return captions_ref.at[:, pl.ds(first, width)]

    def caption_copy(ahead):
        to = lax.rem(group + ahead, groups)
        return remote(
            caption_block(to),
            spread_ref.at[group],
            cap_send.at[ahead],
            cap_recv.at[ahead],
            {GROUP: to},
        )

    own_caption = pltpu.make_async_copy(caption_block(group), spread_ref.at[group], cap_local)
    own_caption.start()
    for ahead in range(1, groups):
        caption_copy(ahead).start()

    def arrive(distance):
        @pl.when(place >= distance)
        def _():
            shift(place - distance, True).wait_recv()

            @pl.when(place < last)
            def _():
                shift(place - distance, True).start()

        @pl.when(place + distance <= last)
        def _():
            shift(place + distance, False).wait_recv()

            @pl.when(place > 0)
            def _():
                shift(place + distance, False).start()

    def weigh(k):
        loads[k].wait()
        product = dot(act_ref[...], ada[k], 1, 0)
        mine[k : k + 1] = product[0:1]

    def mods_copy(ahead):
        return remote(
            mine, others.at[place], mods_send.at[ahead], mods_recv.at[ahead], {LINE: lax.rem(place + ahead, count)}
        )

    mine[...] = jnp.zeros_like(mine)
    cut = parts // 2 + 1
    for k in range(cut):
        weigh(k)
    arrive(1)
    for k in range(cut, parts):
        weigh(k)
    for ahead in range(1, count):
        mods_copy(ahead).start()
    others[place] = mine[...]
    for distance in range(2, count - 1):
        arrive(distance)
    for ahead in range(1, count):
        mods_copy(ahead).wait_recv()
    mods = others[0]
    for i in range(1, count):
        mods = mods + others[i]
    mods_ref[...] = mods
    gain = 1.0 + mods[1:2]
    shift_row = mods[0:1]

    def norm_owner(owner):
        for f in range(latent_ref.shape[0]):
            values = land[owner, f].astype(WIDE)
            rows = pl.ds(pl.multiple_of(owner * share, share), share)
            base_ref[f, rows] = values
            normed_ref[f, rows] = (norm_parts(values)[0] * gain + shift_row).astype(NARROW)

    def near(distance):
        @pl.when(place >= distance)
        def _():
            norm_owner(place - distance)

        @pl.when(place + distance <= last)
        def _():
            norm_owner(place + distance)

    norm_owner(place)
    for distance in range(1, count - 1):
        near(distance)
    if count > 2:
        arrive(count - 1)
    near(count - 1)

    for owner in range(count):

        @pl.when((place < last) & (owner <= place))
        def _():
            shift(owner, True).wait_send()

        @pl.when((place > 0) & (owner >= place))
        def _():
            shift(owner, False).wait_send()

    for ahead in range(1, count):
        mods_copy(ahead).wait_send()
    for ahead in range(1, groups):
        caption_copy(ahead).wait_send()
        caption_copy(ahead).wait_recv()
    own_caption.wait()


def call_opening(count, groups, frames_axis, latent, act, ada, captions):
    frames, share, features = latent.shape
    parts = ada.shape[0]
    length, text_width = captions.shape
    width = text_width // (groups * frames_axis)
    if width % 128:
        blocks = captions.reshape(length, groups, frames_axis, width)
        captions = jnp.transpose(
            lax.dynamic_index_in_dim(blocks, lax.axis_index(FRAME), 2, keepdims=False), (1, 0, 2)
        )
    full = (frames, share * count, features)
    dma = pltpu.SemaphoreType.DMA
    anywhere = pl.BlockSpec(memory_space=pl.ANY)
    return pl.pallas_call(
        functools.partial(opening_kernel, count, groups, frames_axis),
        out_shape=(
            jax.ShapeDtypeStruct(full, WIDE),
            jax.ShapeDtypeStruct(full, NARROW),
            jax.ShapeDtypeStruct((16, features), WIDE),
            jax.ShapeDtypeStruct((groups, length, width), NARROW),
        ),
        in_specs=vmem(2) + [anywhere] * 2,
        out_specs=tuple(vmem(3) + [anywhere]),
        scratch_shapes=[
            pltpu.VMEM((count, frames, share, features), NARROW),
            pltpu.VMEM(ada.shape, NARROW),
            pltpu.VMEM((16, features), WIDE),
            pltpu.VMEM((count, 16, features), WIDE),
            dma((count,)),
            dma((count,)),
            dma((count,)),
            dma((parts,)),
            dma((count,)),
            dma((count,)),
            dma((groups,)),
            dma((groups,)),
            dma,
        ],
        compiler_params=pltpu.CompilerParams(
            collective_id=3, has_side_effects=True, vmem_limit_bytes=VMEM_LIMIT
        ),
        name="opening",
    )(latent, act, ada, captions)


STAGES = 4
MIDDLE_ROWS = 32
MIDDLE_LAG = 3


def gelu_both(values):
    square = values * values
    bent = jnp.tanh(0.7978845608028654 * (values + 0.044715 * values * square))
    slope = 0.5 * (1.0 + bent) + 0.5 * values * (1.0 - bent * bent) * (
        0.7978845608028654 * (1.0 + 3.0 * 0.044715 * square)
    )
    return 0.5 * values * (1.0 + bent), slope


def middle_kernel(count, groups, frames_axis, frames, scattered, *refs):
    (
        first_ref, base_ref, cotangent_ref, rows_ref, bias_ref,
        keys_ref, values_ref, query_w, out_w, up_w, down_w,
        base_three, grad_two, low_two, low_three, normed_three, heads_out, grad_query,
        grad_keys, grad_values, sums_ref, extra_part, up_result, down_result,
        normed_four, low_four, active, grad_inner, base_two, branch_two, query, grad_heads, part, mixed, tally,
        land, stage, total, cross, in_send, land_recv, cross_recv, out_send, out_recv, *scratch,
    ) = refs
    place = lax.axis_index(LINE)
    if scattered:
        up_grad, down_grad, *scratch = scratch
        asides = [
            Scatter(groups, frames_axis, source, scratch[i * 8 : (i + 1) * 8])
            for i, source in enumerate((up_grad, down_grad))
        ]
        greet_line(place, count, 0, asides[0].partners())
    else:
        up_grad, down_grad, asides = up_result, down_result, []
        greet_line(place, count)
    half = count // 2
    left = place < half
    level = jnp.where(left, place, count - 1 - place)
    inner = jnp.where(left, place + 1, place - 1)
    outer = jnp.where(left, place - 1, place + 1)
    is_end, is_middle = level == 0, level == half - 1
    inside = jnp.logical_not(is_end)
    patches = base_ref.shape[0] // frames
    chunks = patches // MIDDLE_ROWS
    slots = STAGES * frames
    scale = HD ** (-0.5)
    width = bias_ref.shape[2]
    local = query_w.shape[0]
    half_heads = local // HD // 2
    tile = up_w.shape[1] // 3
    gate_two, cross_gain, gain_three, shift_three, gate_three = (rows_ref[i : i + 1] for i in range(5))

    def where_of(slot, chunk):
        rows = pl.ds(pl.multiple_of(lax.rem(slot, frames) * patches + chunk * MIDDLE_ROWS, MIDDLE_ROWS), MIDDLE_ROWS)
        return lax.rem(lax.div(slot, frames), 2), rows

    def inward(slot, chunk):
        rows = where_of(slot, chunk)[1]
        return remote(
            stage.at[rows], land.at[rows], in_send.at[slot, chunk], land_recv.at[slot, chunk], {LINE: inner}
        )

    def across(slot, chunk):
        side, rows = where_of(slot, chunk)
        return remote(
            stage.at[rows], cross.at[side, rows], in_send.at[slot, chunk], cross_recv.at[slot, chunk], {LINE: inner}
        )

    def outward(slot, chunk):
        rows = where_of(slot, chunk)[1]
        return remote(
            total.at[rows], total.at[rows], out_send.at[slot, chunk], out_recv.at[slot, chunk], {LINE: outer}
        )

    def own_part(slot, rows):
        return jnp.where(slot < frames, first_ref[rows], part[rows])

    def send_in(slot, chunk):
        @pl.when(is_middle)
        def _():
            across(slot, chunk).start()

        @pl.when(jnp.logical_not(is_middle))
        def _():
            inward(slot, chunk).start()

    def sent(slot, chunk):
        @pl.when(is_middle)
        def _():
            across(slot, chunk).wait_send()

        @pl.when(jnp.logical_not(is_middle))
        def _():
            inward(slot, chunk).wait_send()

        @pl.when(inside)
        def _():
            outward(slot, chunk).wait_send()

    def free(slot, chunk):
        @pl.when(slot >= frames)
        def _():
            sent(slot - frames, chunk)

    def gather_in(slot, chunk):
        rows = where_of(slot, chunk)[1]
        free(slot, chunk)
        inward(slot, chunk).wait_recv()
        stage[rows] = (own_part(slot, rows).astype(WIDE) + land[rows].astype(WIDE)).astype(NARROW)
        send_in(slot, chunk)

    def add_rows(which, terms):
        tally[which] += jnp.sum(terms.reshape(-1, 8, terms.shape[-1]), axis=0)

    def consume(slot, rows, summed):
        number = lax.div(slot, frames)

        @pl.when(number == 0)
        def _():
            branch_two[rows] = summed
            moved = base_ref[rows] + gate_two * summed.astype(WIDE)
            base_two[rows] = moved
            normed_three[rows] = (norm_parts(moved)[0] * cross_gain).astype(NARROW)

        @pl.when(number == 1)
        def _():
            moved = base_two[rows] + summed.astype(WIDE)
            base_three[rows] = moved
            normed_four[rows] = (norm_parts(moved)[0] * gain_three + shift_three).astype(NARROW)
            low_four[rows] = (gate_three * cotangent_ref[rows].astype(WIDE)).astype(NARROW)

        @pl.when(number == 2)
        def _():
            grads = summed.astype(WIDE)
            normal, spread = norm_parts(base_three[rows])
            moved = cotangent_ref[rows].astype(WIDE) + norm_pull(grads * gain_three, normal, spread)
            grad_two[rows] = moved
            low_three[rows] = moved.astype(NARROW)
            add_rows(0, grads)
            add_rows(1, grads * normal)

        @pl.when(number == 3)
        def _():
            grads = summed.astype(WIDE)
            normal, spread = norm_parts(base_two[rows])
            moved = grad_two[rows] + norm_pull(grads * cross_gain, normal, spread)
            grad_two[rows] = moved
            low_two[rows] = (gate_two * moved).astype(NARROW)
            add_rows(2, grads * normal)
            add_rows(3, moved * branch_two[rows].astype(WIDE))

    def finish(slot, chunk):
        side, rows = where_of(slot, chunk)

        @pl.when(is_middle)
        def _():
            across(slot, chunk).wait_recv()
            total[rows] = (stage[rows].astype(WIDE) + cross[side, rows].astype(WIDE)).astype(NARROW)

        @pl.when(jnp.logical_not(is_middle))
        def _():
            outward(slot, chunk).wait_recv()

        @pl.when(inside)
        def _():
            outward(slot, chunk).start()

        consume(slot, rows, total[rows])

    def head_rows(head):
        return pl.ds(head * width, width)

    def probs_of(stream, asked, head):
        scores = scale * dot(asked, keys_ref[head_rows(head)], 1, 1) + bias_ref[stream, 0:1]
        raised = jnp.exp(scores - jnp.max(scores, axis=-1, keepdims=True))
        return raised / jnp.sum(raised, axis=-1, keepdims=True)

    def cross_forward(piece, stream, rows):
        if piece == 0:
            query[rows] = dot(normed_three[rows], query_w[...], 1, 1).astype(NARROW)
        elif piece in (1, 2):
            asked = query[rows]
            found = jnp.zeros((patches, local), WIDE) if piece == 1 else mixed[...]
            for head in range((piece - 1) * half_heads, piece * half_heads):
                probs = probs_of(stream, asked, head).astype(NARROW)
                found = found + dot(probs, values_ref[head_rows(head)], 1, 0)
            if piece == 1:
                mixed[...] = found
            else:
                heads_out[rows] = found.astype(NARROW)
        elif piece == 3:
            part[rows] = dot(heads_out[rows], out_w[...], 1, 0).astype(NARROW)

    def feed_forward(piece, stream, rows):
        if piece < 3:
            span = slice(piece * tile, (piece + 1) * tile)
            inner_values = dot(normed_four[rows], up_w[:, span], 1, 0)
            pulled = dot(low_four[rows], down_w[span], 1, 1)
            raised, slope = gelu_both(inner_values)
            active[rows, span] = raised.astype(NARROW)
            grad_inner[rows, span] = (pulled * slope).astype(NARROW)
        else:
            third = up_w.shape[0] // 3
            span = slice((piece - 3) * third, (piece - 2) * third)
            part[rows, span] = dot(grad_inner[rows], up_w[span], 1, 1).astype(NARROW)

    def cross_backward(piece, stream, rows):
        if piece == 0:
            grad_heads[rows] = dot(low_three[rows], out_w[...], 1, 1).astype(NARROW)
        elif piece in (1, 2):
            asked, given = query[rows], grad_heads[rows]
            found = jnp.zeros((patches, local), WIDE) if piece == 1 else mixed[...]
            for head in range((piece - 1) * half_heads, piece * half_heads):
                spot = head_rows(head)
                probs = probs_of(stream, asked, head)
                pulled = dot(given, values_ref[spot], 1, 1)
                grad_scores = probs * (pulled - jnp.sum(pulled * probs, axis=-1, keepdims=True))
                grad_scores = grad_scores.astype(NARROW)
                found = found + dot(grad_scores, keys_ref[spot], 1, 0)
                grad_keys[spot] += dot(grad_scores, asked, 0, 0)
                grad_values[spot] += dot(probs.astype(NARROW), given, 0, 0)
            if piece == 1:
                mixed[...] = found
            else:
                grad_query[rows] = (scale * found).astype(NARROW)
        elif piece == 3:
            part[rows] = dot(grad_query[rows], query_w[...], 1, 0).astype(NARROW)

    def up_tile(number):
        grad_tile(normed_four, grad_inner, up_grad, number * third, third)

    def down_tile(number):
        grad_tile(low_four, active, down_grad, number * third, third)

    def extra(frame):
        rows = slice(frame * patches, (frame + 1) * patches)
        extra_part[rows] = dot(active[rows], down_w[...], 1, 0).astype(NARROW)

    third = up_w.shape[0] // 3
    late = {}

    def later(slot, chunk, work, *args):
        late.setdefault((slots - 3 + slot, chunk), []).append(functools.partial(work, *args))

    for i, spot in enumerate(((0, 0), (0, 1), (0, 2))):
        later(*spot, up_tile, i)
    for i, spot in enumerate(((0, 7), (1, 0), (1, 1))):
        later(*spot, down_tile, i)
    if asides:
        later(0, 2, asides[0].start)
        later(1, 1, asides[1].start)
        spots = (((1, 2), (1, 7), (2, 0), (2, 1)), ((2, 2), (2, 3), (2, 4), (2, 5)))
        for aside, places in zip(asides, spots):
            for i in range(aside.total):
                later(*places[min(i, 3)], aside.fold, aside.total - 1 - i)
    for frame in range(frames):
        later(2, 6 + min(frame, 1), extra, frame)

    tally[...] = jnp.zeros_like(tally)
    grad_keys[...] = jnp.zeros_like(grad_keys)
    grad_values[...] = jnp.zeros_like(grad_values)

    def step(number, carry):
        slot, chunk = lax.div(number, chunks), lax.rem(number, chunks)
        before = slot - 1

        @pl.when(is_end & (chunk == 0))
        def _():
            @pl.when(slot < slots)
            def _():
                def begin(item, inner_carry):
                    rows = where_of(slot, item)[1]
                    free(slot, item)
                    stage[rows] = own_part(slot, rows)
                    send_in(slot, item)
                    return inner_carry

                lax.fori_loop(0, chunks, begin, 0)

            for late_slot in sorted({spot[0] for spot in late}):

                @pl.when(slot == late_slot)
                def _():
                    for late_chunk in range(MIDDLE_LAG):
                        for work in late.get((late_slot, late_chunk), ()):
                            work()

            @pl.when(slot > 0)
            def _():
                def end(item, inner_carry):
                    finish(before, item)
                    return inner_carry

                lax.fori_loop(0, chunks, end, 0)

        @pl.when(inside & (slot < slots))
        def _():
            gather_in(slot, chunk)

            @pl.when(chunk >= MIDDLE_LAG)
            def _():
                finish(slot, chunk - MIDDLE_LAG)

        @pl.when(inside & (slot > 0) & (chunk < MIDDLE_LAG))
        def _():
            finish(before, chunks - MIDDLE_LAG + chunk)

        stream = lax.rem(jnp.maximum(before, 0), frames)
        rows = pl.ds(pl.multiple_of(stream * patches, patches), patches)
        for which, work in enumerate((cross_forward, feed_forward, cross_backward)):

            @pl.when((slot > 0) & (lax.div(jnp.maximum(before, 0), frames) == which))
            def _():
                for piece in range(6 if which == 1 else 4):

                    @pl.when(chunk == jnp.minimum(MIDDLE_LAG + piece, chunks - 1))
                    def _():
                        work(piece, stream, rows)

        for (late_slot, late_chunk), works in late.items():

            @pl.when((slot == late_slot) & (chunk == late_chunk) & (inside | (late_chunk >= MIDDLE_LAG)))
            def _():
                for work in works:
                    work()

        return carry

    lax.fori_loop(0, slots * chunks + MIDDLE_LAG, step, 0)

    def settle(number, carry):
        sent(lax.div(number, chunks), lax.rem(number, chunks))
        return carry

    lax.fori_loop((slots - frames) * chunks, slots * chunks, settle, 0)
    sums_ref[...] = jnp.zeros_like(sums_ref)
    for i in range(4):
        sums_ref[i : i + 1] = jnp.sum(tally[i], axis=0, keepdims=True)
    for aside, result in zip(asides, (up_result, down_result)):
        aside.finish([result])


def call_middle(
    count, groups, frames_axis, frames, first, base, cotangent, rows, bias, keys, values, query_w, out_w, up_w, down_w
):
    tokens, features = first.shape
    local, hidden = query_w.shape[0], up_w.shape[1]
    chunks = tokens // frames // MIDDLE_ROWS
    scattered = can_scatter(groups, frames_axis, features)

    def wide(*shape):
        return jax.ShapeDtypeStruct(shape, WIDE)

    def narrow(*shape):
        return jax.ShapeDtypeStruct(shape, NARROW)

    found, scratch = Products.shapes(groups, frames_axis, [hidden], features)
    scratch = scratch[:1] * 2 + scratch[1:] * 2
    results = (
        [wide(tokens, features)] * 2
        + [narrow(tokens, features)] * 3
        + [narrow(tokens, local)] * 2
        + [wide(*keys.shape)] * 2
        + [wide(8, features), narrow(tokens, features)]
        + found * 2
    )
    sem = pltpu.SemaphoreType.DMA((STAGES * frames, chunks))
    return pl.pallas_call(
        functools.partial(middle_kernel, count, groups, frames_axis, frames, scattered),
        out_shape=tuple(results),
        in_specs=vmem(11),
        out_specs=tuple(vmem(len(results))),
        scratch_shapes=[pltpu.VMEM((tokens, features), NARROW)] * 2
        + [pltpu.VMEM((tokens, hidden), NARROW)] * 2
        + [
            pltpu.VMEM((tokens, features), WIDE),
            pltpu.VMEM((tokens, features), NARROW),
            pltpu.VMEM((tokens, local), NARROW),
            pltpu.VMEM((tokens, local), NARROW),
            pltpu.VMEM((tokens, features), NARROW),
            pltpu.VMEM((tokens // frames, local), WIDE),
            pltpu.VMEM((4, 8, features), WIDE),
        ]
        + [pltpu.VMEM((tokens, features), NARROW)] * 3
        + [pltpu.VMEM((2, tokens, features), NARROW)]
        + [sem] * 5
        + scratch,
        compiler_params=pltpu.CompilerParams(
            collective_id=7, has_side_effects=True, vmem_limit_bytes=62 * 2**20
        ),
        name="middle",
    )(first, base, cotangent, rows, bias, keys, values, query_w, out_w, up_w, down_w)


def greet_frames(here, frames_axis):
    found = (here > 0).astype(jnp.int32) + (here < frames_axis - 1).astype(jnp.int32)
    barrier = pltpu.get_barrier_semaphore()

    @pl.when(here > 0)
    def _():
        pl.semaphore_signal(barrier, inc=1, device_id={FRAME: here - 1}, device_id_type=MESH)

    @pl.when(here < frames_axis - 1)
    def _():
        pl.semaphore_signal(barrier, inc=1, device_id={FRAME: here + 1}, device_id_type=MESH)

    return found


def head_columns(local):
    feature = lax.broadcasted_iota(jnp.int32, (local, 128), 0)
    first = lax.broadcasted_iota(jnp.int32, (local, 128), 1) * HD
    return jnp.where((feature >= first) & (feature < first + HD), 1.0, 0.0).astype(NARROW)


def per_head(values, columns):
    high, rest = split_pair(values)
    return dot(high, columns, 1, 0) + dot(rest, columns, 1, 0)


def over_features(values, columns):
    high, rest = split_pair(values)
    return dot(high, columns, 1, 1) + dot(rest, columns, 1, 1)


def window_probs(query, keys_of, bias_of, columns):
    scores = [
        HD ** (-0.5) * per_head(query * keys_of(offset), columns) + bias_of(offset) for offset in range(WIN)
    ]
    highest = functools.reduce(jnp.maximum, scores)
    raised = [jnp.exp(item - highest) for item in scores]
    whole = 1.0 / sum(raised[1:], raised[0])
    return [item * whole for item in raised]


def temporal_forward_kernel(
    count, frames_axis, frames, hidden_ref, in_ref, out_ref, bias_ref, cotangent_ref, text_ref,
    query_ref, keys_ref, values_ref, heads_ref, part_ref, cotangent_full, text_full,
    halo_send, halo_recv, *sems,
):
    place, here = lax.axis_index(LINE), lax.axis_index(FRAME)
    patches = hidden_ref.shape[0] // frames
    local = heads_ref.shape[1]
    share = cotangent_ref.shape[1]
    last = count - 1
    greet_line(place, count, greet_frames(here, frames_axis))
    cells = (keys_ref, values_ref)

    def shares(owner):
        return cotangent_full.at[:, pl.ds(pl.multiple_of(owner * share, share), share)]

    moving = [
        LineGather(count, place, shares, sems[0:3]),
        LineGather(count, place, lambda owner: text_full.at[owner], sems[3:6]),
    ]
    cotangent_full[:, pl.ds(pl.multiple_of(place * share, share), share)] = cotangent_ref[...]
    text_full[place] = text_ref[...]
    for item in moving:
        item.start()

    def halo(which, item):
        source = 2 + (frames - 2 + which if which < 2 else 0)
        target = which if which < 2 else frames + 2
        to = here + 1 if which < 2 else here - 1
        ref = cells[item]
        return remote(
            ref.at[source], ref.at[target], halo_send.at[which, item], halo_recv.at[which, item], {FRAME: to}
        )

    has_next, has_previous = here < frames_axis - 1, here > 0

    def frame_rows(frame):
        return slice(frame * patches, (frame + 1) * patches)

    for frame in range(frames):
        for item in range(2):
            rows = slice((1 + item) * local, (2 + item) * local)
            cells[item][2 + frame] = dot(hidden_ref[frame_rows(frame)], in_ref[rows], 1, 1).astype(NARROW)
            for which in range(3):
                if (frames - 2 + which if which < 2 else 0) == frame:

                    @pl.when(has_next if which < 2 else has_previous)
                    def _():
                        halo(which, item).start()

    query_ref[...] = dot(hidden_ref[...], in_ref[0:local], 1, 1).astype(NARROW)
    for distance in range(1, last):
        for item in moving:
            item.arrive(distance)
    for item in range(2):

        @pl.when(has_previous)
        def _():
            halo(0, item).wait_recv()
            halo(1, item).wait_recv()

        @pl.when(jnp.logical_not(has_previous))
        def _():
            cells[item][0:2] = jnp.zeros((2,) + cells[item].shape[1:], NARROW)

        @pl.when(has_next)
        def _():
            halo(2, item).wait_recv()

        @pl.when(jnp.logical_not(has_next))
        def _():
            cells[item][frames + 2] = jnp.zeros(cells[item].shape[1:], NARROW)

    columns = head_columns(local)
    for frame in range(frames):
        probs = window_probs(
            query_ref[frame_rows(frame)].astype(WIDE),
            lambda offset: keys_ref[frame + offset].astype(WIDE),
            lambda offset: bias_ref[frame * WIN + offset : frame * WIN + offset + 1],
            columns,
        )
        mixed = over_features(probs[0], columns) * values_ref[frame].astype(WIDE)
        for offset in range(1, WIN):
            mixed = mixed + over_features(probs[offset], columns) * values_ref[frame + offset].astype(WIDE)
        heads_ref[frame_rows(frame)] = mixed.astype(NARROW)
        part_ref[frame_rows(frame)] = dot(mixed.astype(NARROW), out_ref[...], 1, 0).astype(NARROW)
    for item in moving:
        item.arrive(last)
        item.settle()
    for item in range(2):

        @pl.when(has_next)
        def _():
            halo(0, item).wait_send()
            halo(1, item).wait_send()

        @pl.when(has_previous)
        def _():
            halo(2, item).wait_send()


def call_temporal_forward(count, frames_axis, hidden, in_w, out_w, bias, cotangent, text):
    tokens, features = hidden.shape
    frames, share = cotangent.shape[:2]
    local = out_w.shape[0]
    patches = tokens // frames

    def narrow(*shape):
        return jax.ShapeDtypeStruct(shape, NARROW)

    results = (
        [narrow(tokens, local)]
        + [narrow(frames + 3, patches, local)] * 2
        + [narrow(tokens, local), narrow(tokens, features)]
        + [narrow(frames, share * count, features), narrow(count, *text.shape)]
    )
    return pl.pallas_call(
        functools.partial(temporal_forward_kernel, count, frames_axis, frames),
        out_shape=tuple(results),
        in_specs=vmem(6),
        out_specs=tuple(vmem(len(results))),
        scratch_shapes=[pltpu.SemaphoreType.DMA((3, 2))] * 2 + gather_sems(count) * 2,
        compiler_params=pltpu.CompilerParams(
            collective_id=8, has_side_effects=True, vmem_limit_bytes=VMEM_LIMIT
        ),
        name="temporal_forward",
    )(hidden, in_w, out_w, bias, cotangent, text)


def temporal_backward_kernel(
    count, groups, frames_axis, frames, scattered,
    grad_ref, in_ref, out_ref, bias_ref, query_ref, keys_ref, values_ref,
    extra_ref, text_keys, text_values, text_w, text_rows, cross_hidden, cross_grad, cross_low, cross_heads,
    grad_packed, part_ref, extra_own, text_own, query_result, keyval_result, out_result,
    near_keys, near_values, rim_out, rim_in, halo_send, halo_recv, text_ref, text_low,
    extra_land, extra_stage, text_land, text_stage, *sems,
):
    products = Products(
        groups, frames_axis, [(cross_hidden, cross_grad), (text_rows, text_low), (cross_low, cross_heads)],
        [query_result, keyval_result, out_result], sems[8:], scattered,
    )
    place, here = lax.axis_index(LINE), lax.axis_index(FRAME)
    patches = grad_ref.shape[0] // frames
    local = out_ref.shape[0]
    share = extra_own.shape[1]
    last = count - 1
    greet_line(place, count, greet_frames(here, frames_axis), products.partners())

    def shares(owner, frame):
        return extra_ref[frame, pl.ds(pl.multiple_of(owner * share, share), share)]

    moving = [
        LineScatter(count, place, frames, shares, extra_land, extra_stage, sems[0:4]),
        LineScatter(count, place, 1, lambda owner, piece: text_ref[owner], text_land, text_stage, sems[4:8]),
    ]
    moving[0].relay_both(last)
    near = (near_keys, near_values)
    slots = text_low.shape[0]
    text_parts = jnp.zeros((slots, grad_ref.shape[1]), WIDE)
    for item, (source, factor) in enumerate(((text_keys, HD ** (-0.5)), (text_values, 1.0))):
        low = (factor * collect_heads(source[...], slots)).astype(NARROW)
        text_low[:, item * local : (item + 1) * local] = low
        text_parts = text_parts + dot(low, text_w[item * local : (item + 1) * local], 1, 0)
    text_parts = text_parts.astype(NARROW)
    for owner in range(count):
        text_ref[owner] = text_parts[:, owner * local : (owner + 1) * local]
    moving[1].relay_both(last)


    def halo(which):
        to = here - 1 if which < 2 else here + 1
        return remote(
            rim_out.at[which], rim_in.at[which], halo_send.at[which], halo_recv.at[which], {FRAME: to}
        )

    has_next, has_previous = here < frames_axis - 1, here > 0

    def frame_rows(frame):
        return slice(frame * patches, (frame + 1) * patches)

    columns = head_columns(local)
    seen = set()

    def add(item, cell, terms):
        if (item, cell) in seen:
            near[item][cell] += terms
        else:
            near[item][cell] = terms
        seen.add((item, cell))

    for frame in range(frames):
        given = dot(grad_ref[frame_rows(frame)], out_ref[...], 1, 1).astype(NARROW).astype(WIDE)
        asked = query_ref[frame_rows(frame)].astype(WIDE)
        probs = window_probs(
            asked,
            lambda offset: keys_ref[frame + offset].astype(WIDE),
            lambda offset: bias_ref[frame * WIN + offset : frame * WIN + offset + 1],
            columns,
        )
        pulled = [per_head(given * values_ref[frame + offset].astype(WIDE), columns) for offset in range(WIN)]
        shared = sum((probs[i] * pulled[i] for i in range(1, WIN)), probs[0] * pulled[0])
        found = jnp.zeros((patches, local), WIDE)
        for offset in range(WIN):
            scores = HD ** (-0.5) * over_features(probs[offset] * (pulled[offset] - shared), columns)
            found = found + scores * keys_ref[frame + offset].astype(WIDE)
            add(0, frame + offset, scores * asked)
            add(1, frame + offset, over_features(probs[offset], columns) * given)
        grad_packed[frame_rows(frame), 0:local] = found.astype(NARROW)

    for which in range(3):

        @pl.when(has_previous if which < 2 else has_next)
        def _():
            for item in range(2):
                span = slice(item * local, (item + 1) * local)
                rim_out[which, :, span] = near[item][which if which < 2 else frames + 2].astype(NARROW)
            halo(which).start()

    folds = fold_works(products)
    for work in products.work():
        work()
    for distance in range(last - 1, 0, -1):
        for item in moving:
            item.relay_both(distance)
        for work in folds if distance == last - 1 else ():
            work()

    for which in range(3):

        @pl.when(has_next if which < 2 else has_previous)
        def _():
            halo(which).wait_recv()
            for item in range(2):
                span = slice(item * local, (item + 1) * local)
                near[item][2 + (frames - 2 + which if which < 2 else 0)] += rim_in[which, :, span].astype(WIDE)

    for frame in range(frames):
        rows = frame_rows(frame)
        parts = dot(grad_packed[rows, 0:local], in_ref[0:local], 1, 0)
        for item in range(2):
            values = near[item][2 + frame].astype(NARROW)
            grad_packed[rows, (1 + item) * local : (2 + item) * local] = values
            parts = parts + dot(values, in_ref[(1 + item) * local : (2 + item) * local], 1, 0)
        part_ref[rows] = parts.astype(NARROW)

    for frame in range(frames):
        extra_own[frame] = moving[0].total(frame)
    text_own[...] = moving[1].total(0).astype(NARROW)
    for item in moving:
        item.settle()
    for which in range(3):

        @pl.when(has_previous if which < 2 else has_next)
        def _():
            halo(which).wait_send()

    products.finish()


def call_temporal_backward(
    count, groups, frames_axis, grad, in_w, out_w, bias, query, keys, values, extra, text_keys, text_values, text_w,
    text_rows, *cross_pairs,
):
    tokens, features = grad.shape
    frames, patches = extra.shape[:2]
    local = out_w.shape[0]
    share = patches // count
    slots = text_rows.shape[0]

    def narrow(*shape):
        return jax.ShapeDtypeStruct(shape, NARROW)

    found, scratch = Products.shapes(groups, frames_axis, [local, 2 * local, local], features)
    results = (
        [narrow(tokens, 3 * local)]
        + [narrow(tokens, features), jax.ShapeDtypeStruct((frames, share, features), WIDE)]
        + [narrow(slots, local)]
        + found
    )
    return pl.pallas_call(
        functools.partial(temporal_backward_kernel, count, groups, frames_axis, frames, bool(scratch)),
        out_shape=tuple(results),
        in_specs=vmem(16),
        out_specs=tuple(vmem(len(results))),
        scratch_shapes=[pltpu.VMEM((frames + 3, patches, local), WIDE)] * 2
        + [pltpu.VMEM((3, patches, 2 * local), NARROW)] * 2
        + [pltpu.SemaphoreType.DMA((3,))] * 2
        + [pltpu.VMEM((count, slots, local), NARROW), pltpu.VMEM((slots, 2 * local), NARROW)]
        + [pltpu.VMEM((2, count, frames, share, features), NARROW)] * 2
        + [pltpu.VMEM((2, count, 1, slots, local), NARROW)] * 2
        + scatter_sems(count, frames)
        + scatter_sems(count, 1)
        + scratch,
        compiler_params=pltpu.CompilerParams(
            collective_id=9, has_side_effects=True, vmem_limit_bytes=VMEM_LIMIT
        ),
        name="temporal_backward",
    )(grad, in_w, out_w, bias, query, keys, values, extra, text_keys, text_values, text_w, text_rows, *cross_pairs)


def attend_forward(query, keys, values):
    scores = HD ** (-0.5) * jnp.einsum("fphe,fqhe->fhpq", query, keys, preferred_element_type=WIDE)
    shifted = jnp.exp(scores - jnp.max(scores, axis=-1, keepdims=True))
    probs_low = (shifted / jnp.sum(shifted, axis=-1, keepdims=True)).astype(NARROW)
    heads_out = jnp.einsum("fhpq,fqhe->fphe", probs_low, values, preferred_element_type=WIDE)
    return heads_out.astype(NARROW)


def sum_matrix_grads(pieces):
    if not pieces:
        return []
    packed = jnp.concatenate([piece.astype(NARROW) for piece in pieces], axis=1)
    summed = lax.psum_scatter(packed, BOTH, scatter_dimension=0, tiled=True).astype(WIDE)
    found, start = [], 0
    for piece in pieces:
        found.append(summed[:, start : start + piece.shape[1]])
        start += piece.shape[1]
    return found


def per_device(
    latent, captions, bucket, clip_ids, window_mask, text_counts, time_table, ada_weight,
    spatial_inproj, spatial_outproj, temporal_inproj, temporal_outproj, caption_proj, cross_gain,
    cross_query, cross_keyval, cross_outproj, mlp_up, mlp_down, cotangent,
):
    count, groups, frames_axis = (lax.axis_size(axis) for axis in (LINE, GROUP, FRAME))
    place = lax.axis_index(LINE)
    frames, share, features = latent.shape[1:]
    patches = share * count
    tokens = frames * patches
    local = spatial_outproj.shape[0]
    clip_count, text_length, text_width = captions.shape[1:]
    slots = clip_count * text_length

    def flat(values):
        return values.reshape(tokens, -1)

    def grid(values):
        return values.reshape(frames, patches, -1)

    def heads(values):
        return split_heads(grid(values))

    def own(values):
        return lax.dynamic_slice_in_dim(grid(values), place * share, share, axis=1)

    spatial_in, temporal_in, keyval_in = (
        jnp.transpose(w, (1, 2, 0)).reshape(-1, features)
        for w in (spatial_inproj, temporal_inproj, cross_keyval)
    )
    query_in = cross_query.T

    chosen = (jnp.arange(time_table.shape[0]) == bucket[0]).astype(WIDE)
    cond_row = jnp.sum(chosen[:, None] * time_table.astype(WIDE), axis=0)
    act_low = swish_act(cond_row).astype(NARROW)
    caption_here = captions[0].reshape(slots, text_width)
    base_grid, normed_grid, mods, caption_share = call_opening(
        count, groups, frames_axis, latent[0], jnp.broadcast_to(act_low[None], (16, local)),
        jnp.transpose(ada_weight, (1, 0, 2)), caption_here,
    )
    base_zero, spatial_hidden = flat(base_grid), flat(normed_grid)
    text_part = dot(caption_here, caption_proj, 1, 0).astype(NARROW)

    def rows_of(*rows):
        filled = [jnp.zeros((features,), WIDE)] * (8 - len(rows))
        return jnp.stack(list(rows) + filled)

    spatial_packed = dot(spatial_hidden, spatial_in, 1, 1).astype(NARROW)
    spatial_query, spatial_keys, spatial_values = (
        heads(spatial_packed[:, i * local : (i + 1) * local]) for i in range(3)
    )
    spatial_heads = attend_forward(spatial_query, spatial_keys, spatial_values)
    spatial_flat = flat(spatial_heads)
    spatial_out, base_one, temporal_hidden = call_forward(
        count,
        dot(spatial_flat, spatial_outproj, 1, 0).astype(NARROW),
        base_zero,
        rows_of(mods[2], 1.0 + mods[4], mods[3]),
    )

    first_frame = lax.axis_index(FRAME) * frames
    clip_near = lax.dynamic_slice_in_dim(
        jnp.pad(clip_ids[0], (2, 2), constant_values=-1), first_frame, frames + 4
    )
    own_clip = clip_near[2 : 2 + frames]
    allowed = jnp.stack(
        [
            (clip_near[offset : offset + frames] == own_clip)
            & ((window_mask[0][:, offset] == 1) | (offset == 2))
            for offset in range(WIN)
        ],
        axis=1,
    )
    window_bias = jnp.broadcast_to(jnp.where(allowed, 0.0, NEGATIVE).reshape(-1, 1), (frames * WIN, 128))
    (
        temporal_query, temporal_keys, temporal_values, temporal_flat, temporal_part, cotangent_full, text_full,
    ) = call_temporal_forward(
        count, frames_axis, temporal_hidden, temporal_in, temporal_outproj, window_bias, cotangent[0], text_part
    )
    cotangent_full = flat(cotangent_full)
    text_rows = jnp.transpose(text_full, (1, 0, 2)).reshape(slots, features)

    slot_pad = -slots % 128
    text_rows = jnp.pad(text_rows, ((0, slot_pad), (0, 0)))
    text_packed = dot(text_rows, keyval_in, 1, 1).astype(NARROW)
    slot_index = jnp.arange(slots)
    key_valid = (own_clip[:, None] == (slot_index // text_length)[None, :]) & (
        slot_index % text_length < jnp.repeat(text_counts[0], text_length)
    )[None, :]
    bias = jnp.pad(jnp.where(key_valid, 0.0, NEGATIVE), ((0, 0), (0, slot_pad)), constant_values=NEGATIVE)
    bias = jnp.broadcast_to(bias[:, None], (frames, 8, slots + slot_pad))
    mask_of_head = (jnp.arange(local) // HD)[None, :] == jnp.arange(local // HD)[:, None]

    def by_head(values):
        return jnp.where(mask_of_head[:, None], values[None], 0).reshape(-1, local)

    (
        base_three, grad_two, grad_temporal_low, grad_cross_low, cross_hidden, cross_flat, grad_cross_packed,
        text_grad_keys, text_grad_values, sums_middle, mlp_part, grad_up, grad_down,
    ) = call_middle(
        count, groups, frames_axis, frames, temporal_part, base_one, cotangent_full,
        rows_of(mods[5], cross_gain.astype(WIDE), 1.0 + mods[7], mods[6], mods[8]), bias,
        by_head(text_packed[:, :local]), by_head(text_packed[:, local:]),
        query_in, cross_outproj, mlp_up, mlp_down,
    )

    def summed(found):
        return found if can_scatter(groups, frames_axis, features) else sum_matrix_grads(found)

    grad_up, grad_down = summed([grad_up, grad_down])

    grad_temporal_packed, temporal_grad_part, mlp_out, text_grad, *found = call_temporal_backward(
        count, groups, frames_axis, grad_temporal_low, temporal_in, temporal_outproj, window_bias,
        temporal_query, temporal_keys, temporal_values, grid(mlp_part), text_grad_keys, text_grad_values,
        keyval_in, text_rows, cross_hidden, grad_cross_packed, grad_cross_low, cross_flat,
    )
    grad_query_cross, grad_keyval_cross, grad_outproj_cross = summed(found)
    output = (own(base_three) + mods[8] * mlp_out).astype(NARROW)[None]
    gate_mlp_part = jnp.sum(cotangent[0].astype(WIDE) * mlp_out, axis=(0, 1))
    grad_one, grad_spatial_low, sums_temporal, text_grad_all, *found = call_backward(
        count, groups, frames_axis, temporal_grad_part, base_one, grad_two, spatial_out,
        rows_of(1.0 + mods[4], mods[2]), text_grad,
        [(temporal_hidden, grad_temporal_packed), (grad_temporal_low, temporal_flat)],
    )
    grad_inproj_temporal, grad_outproj_temporal = summed(found)
    caption_rows = caption_share.reshape(groups * slots, -1)
    grad_caption = dot(caption_rows, text_grad_all[:, 0:slots].reshape(groups * slots, local), 0, 0)

    side_row = jnp.pad(jnp.concatenate([cond_row, chosen]), (0, features - local - chosen.shape[0]))
    blank = jnp.zeros((features,), WIDE)
    small = jnp.stack(
        [blank, blank, gate_mlp_part]
        + [blank] * 5
        + [
            sums_temporal[2], sums_temporal[0], sums_temporal[1], sums_middle[3], sums_middle[0],
            sums_middle[1], sums_middle[2], side_row,
        ]
    )
    grad_latent, small_all, *found = call_closing(
        count, groups, frames_axis, grad_spatial_low, grid(base_zero), grid(grad_one), small,
        rows_of(1.0 + mods[1]), spatial_packed, spatial_flat, spatial_hidden, spatial_in, spatial_outproj,
    )
    grad_inproj_spatial, grad_outproj_spatial = summed(found)

    small_all = small_all.reshape(groups, frames_axis, 16, features)
    small_sums = jnp.sum(small_all, axis=1)
    modulation_grad = jnp.stack([small_sums[:, i] for i in (0, 1, 8, 9, 10, 11, 12, 13, 2)], axis=1)
    grad_gain = jnp.sum(small_sums[:, 14], axis=0)
    cond_all = small_all[:, 0, 15, 0:local]
    chosen_all = small_all[:, 0, 15, local : local + chosen.shape[0]]
    act_all, swish_pull = jax.vjp(swish_act, cond_all)
    act_all = act_all.astype(NARROW).astype(WIDE)
    column = features // (groups * frames_axis)
    rank = lax.axis_index(BOTH)
    column_grads = lax.dynamic_slice_in_dim(modulation_grad, rank * column, column, axis=2)
    grad_ada = jnp.einsum("gc,gkd->ckd", act_all, column_grads, precision=HIGHEST)
    grad_act = jnp.einsum("ckd,gkd->gc", ada_weight.astype(WIDE), modulation_grad, precision=HIGHEST)
    grad_cond = swish_pull(grad_act)[0]
    grad_table = jnp.einsum("gn,gc->nc", chosen_all, grad_cond, precision=HIGHEST)

    def unpack(values, parts):
        return values.reshape(values.shape[0], parts, -1)

    return (
        output,
        grad_latent[None],
        grad_table,
        grad_ada,
        unpack(grad_inproj_spatial, 3),
        grad_outproj_spatial.T,
        unpack(grad_inproj_temporal, 3),
        grad_outproj_temporal.T,
        grad_caption,
        grad_gain,
        grad_query_cross,
        unpack(grad_keyval_cross, 2),
        grad_outproj_cross.T,
        grad_up,
        grad_down.T,
    )


def solution(mesh):
    tokens = P(GROUP, FRAME, LINE, None)
    packed_in, rows_in, columns_in = P(None, None, LINE), P(LINE, None), P(None, LINE)
    in_specs = (
        tokens, P(GROUP, None, None, None), P(GROUP), P(GROUP, None), P(GROUP, FRAME, None),
        P(GROUP, None), columns_in, P(LINE, None, None), packed_in, rows_in, packed_in, rows_in,
        columns_in, P(), columns_in, packed_in, rows_in, columns_in, rows_in, tokens,
    )
    packed_out, rows_out, columns_out = P(BOTH, None, LINE), P(LINE, BOTH), P(BOTH, LINE)
    out_specs = (
        tokens, tokens, columns_in, P(LINE, None, BOTH), packed_out, rows_out, packed_out, rows_out,
        columns_out, P(), columns_out, packed_out, rows_out, columns_out, rows_out,
    )
    return jax.shard_map(
        per_device, mesh=mesh, in_specs=in_specs, out_specs=out_specs, check_vma=False
    )
```

```python
import functools

import jax
import jax.numpy as jnp
from jax import lax
from jax.experimental import pallas as pl
from jax.experimental.pallas import tpu as pltpu
from jax.sharding import PartitionSpec as P

HD = 72
WIN = 4
EPSILON = 1e-06
HIGHEST = lax.Precision.HIGHEST
NEGATIVE = -1e30
WIDE = jnp.float32
NARROW = jnp.bfloat16
GROUP, FRAME, LINE = "group", "frame", "tensor"
BOTH = (GROUP, FRAME)
MESH = pl.DeviceIdType.MESH
CHUNKS = 16
LAG = 2
VMEM_LIMIT = 48 * 2**20


def swish_act(values):
    return values / (1.0 + jnp.exp(-values))


def gelu_tanh(values):
    return (
        0.5
        * values
        * (1.0 + jnp.tanh(0.7978845608028654 * (values + 0.044715 * values * values * values)))
    )


def dot(first, second, contract_first, contract_second):
    return lax.dot_general(
        first, second, (((contract_first,), (contract_second,)), ((), ())), preferred_element_type=WIDE
    )


def split_heads(values):
    return values.reshape(values.shape[:-1] + (values.shape[-1] // HD, HD))


def split_pair(values):
    high_part = values.astype(NARROW)
    rest_part = (values - high_part.astype(WIDE)).astype(NARROW)
    return (high_part, rest_part)


def norm_parts(values):
    centred = values - jnp.mean(values, axis=-1, keepdims=True)
    spread = lax.rsqrt(jnp.mean(centred * centred, axis=-1, keepdims=True) + EPSILON)
    return centred * spread, spread


def norm_pull(scaled, normal, spread):
    return spread * (
        scaled
        - jnp.mean(scaled, axis=-1, keepdims=True)
        - normal * jnp.mean(scaled * normal, axis=-1, keepdims=True)
    )


def remote(source, target, send_sem, recv_sem, where):
    return pltpu.make_async_remote_copy(
        src_ref=source,
        dst_ref=target,
        send_sem=send_sem,
        recv_sem=recv_sem,
        device_id=where,
        device_id_type=MESH,
    )


def greet_line(place, count, more=0, others=()):
    barrier = pltpu.get_barrier_semaphore()
    for where in others:
        pl.semaphore_signal(barrier, inc=1, device_id=where, device_id_type=MESH)

    @pl.when(place > 0)
    def _():
        pl.semaphore_signal(barrier, inc=1, device_id={LINE: place - 1}, device_id_type=MESH)

    @pl.when(place < count - 1)
    def _():
        pl.semaphore_signal(barrier, inc=1, device_id={LINE: place + 1}, device_id_type=MESH)

    pl.semaphore_wait(
        barrier, (place > 0).astype(jnp.int32) + (place < count - 1).astype(jnp.int32) + len(others) + more
    )


class Scatter:
    def __init__(self, groups, frames_axis, source, scratch):
        self.source = source
        self.inbox, self.stage, self.found, self.kept = scratch[:4]
        self.twin_send, self.twin_recv, self.peer_send, self.peer_recv = scratch[4:8]
        self.groups, self.frames_axis = groups, frames_axis
        self.block = source.shape[0] // (groups * frames_axis)
        self.total = groups // 2 * frames_axis
        group = lax.axis_index(GROUP)
        self.core = lax.rem(group, 2)
        self.me = lax.div(group, 2) * frames_axis + lax.axis_index(FRAME)
        self.twin = {GROUP: group + 1 - 2 * self.core}

    def peer(self, step):
        to = lax.rem(self.me + step, self.total)
        return to, {GROUP: lax.div(to, self.frames_axis) * 2 + self.core, FRAME: lax.rem(to, self.frames_axis)}

    def partners(self):
        return [self.twin] + [self.peer(step)[1] for step in range(1, self.total)]

    def twin_copy(self, high):
        rows = self.block * self.frames_axis
        first = pl.multiple_of((high * 2 + 1 - self.core) * rows, 16)
        return remote(
            self.source.at[pl.ds(first, rows)],
            self.inbox.at[pl.ds(high * rows, rows)],
            self.twin_send.at[high],
            self.twin_recv.at[high],
            self.twin,
        )

    def peer_copy(self, step):
        return remote(
            self.stage.at[step - 1],
            self.found.at[step - 1],
            self.peer_send.at[step],
            self.peer_recv.at[step],
            self.peer(step)[1],
        )

    def start(self):
        for high in range(self.groups // 2):
            self.twin_copy(high).start()

    def fold(self, step):
        if step == self.total - 1:
            for high in range(self.groups // 2):
                self.twin_copy(high).wait_recv()
        to = self.peer(step)[0]
        high, frame = lax.div(to, self.frames_axis), lax.rem(to, self.frames_axis)
        first = ((high * 2 + self.core) * self.frames_axis + frame) * self.block
        mine = self.source[pl.ds(pl.multiple_of(first, 16), self.block)]
        other = self.inbox[pl.ds(pl.multiple_of(to * self.block, 16), self.block)]
        summed = mine.astype(WIDE) + other.astype(WIDE)
        if step == 0:
            self.kept[...] = summed
        else:
            self.stage[step - 1] = summed.astype(NARROW)
            self.peer_copy(step).start()

    def fold_all(self):
        for step in range(self.total - 1, -1, -1):
            self.fold(step)

    def finish(self, results):
        for step in range(1, self.total):
            self.peer_copy(step).wait_recv()
        start = 0
        for result in results:
            span = slice(start, start + result.shape[1])
            summed = self.kept[:, span]
            for step in range(1, self.total):
                summed = summed + self.found[step - 1, :, span].astype(WIDE)
            result[...] = summed
            start += result.shape[1]
        for high in range(self.groups // 2):
            self.twin_copy(high).wait_send()
        for step in range(1, self.total):
            self.peer_copy(step).wait_send()

    @staticmethod
    def scratch(groups, frames_axis, width, columns):
        total, block = groups // 2 * frames_axis, width // (groups * frames_axis)
        dma = pltpu.SemaphoreType.DMA
        return (
            [pltpu.VMEM((width // 2, columns), NARROW)]
            + [pltpu.VMEM((total - 1, block, columns), NARROW)] * 2
            + [pltpu.VMEM((block, columns), WIDE)]
            + [dma((groups // 2,))] * 2
            + [dma((total,))] * 2
        )


def can_scatter(groups, frames_axis, width):
    return groups % 2 == 0 and width % (16 * groups * frames_axis) == 0


class Products:
    def __init__(self, pairs, result):
        self.pairs, self.result = pairs, result

    def product(self, i):
        first, second = self.pairs[i]
        start = sum(item.shape[1] for _, item in self.pairs[:i])
        self.result[:, start : start + second.shape[1]] = dot(first[...], second[...], 0, 0).astype(NARROW)

    def work(self):
        return [functools.partial(self.product, i) for i in range(len(self.pairs))]


class Scatters:
    def __init__(self, groups, frames_axis, sources, widths, results, scratch):
        self.items, self.results = [], []
        for i, source in enumerate(sources):
            self.items.append(Scatter(groups, frames_axis, source, scratch[8 * i : 8 * i + 8]))
            self.results.append(results[: len(widths[i])])
            results = results[len(widths[i]) :]

    def partners(self):
        return self.items[0].partners()

    def folds(self, i):
        item = self.items[i]
        return [functools.partial(item.fold, item.total - 1 - step) for step in range(item.total)]

    def finish(self):
        for item, results in zip(self.items, self.results):
            item.finish(results)

    @staticmethod
    def shapes(groups, frames_axis, features, widths):
        block = features // (groups * frames_axis)
        results = [jax.ShapeDtypeStruct((block, n), WIDE) for columns in widths for n in columns]
        scratch = [Scatter.scratch(groups, frames_axis, features, sum(columns)) for columns in widths]
        return results, sum(scratch, [])


class GroupExchange:
    def __init__(self, groups, frames_axis, source, every, scratch):
        self.groups, self.frames_axis = groups, frames_axis
        self.source, self.every = source, every
        self.near, self.frame_send, self.frame_recv, self.group_send, self.group_recv = scratch
        self.group, self.frame = lax.axis_index(GROUP), lax.axis_index(FRAME)

    def frame_copy(self, step):
        return remote(
            self.source,
            self.near.at[step - 1],
            self.frame_send.at[step],
            self.frame_recv.at[step],
            {FRAME: lax.rem(self.frame + step, self.frames_axis)},
        )

    def group_copy(self, step):
        own = self.every.at[self.group]
        return remote(
            own,
            own,
            self.group_send.at[step],
            self.group_recv.at[step],
            {GROUP: lax.rem(self.group + step, self.groups)},
        )

    def partners(self):
        return [
            {FRAME: lax.rem(self.frame + step, self.frames_axis)} for step in range(1, self.frames_axis)
        ] + [{GROUP: lax.rem(self.group + step, self.groups)} for step in range(1, self.groups)]

    def start(self):
        for step in range(1, self.frames_axis):
            self.frame_copy(step).start()

    def spread(self):
        for step in range(1, self.frames_axis):
            self.frame_copy(step).wait_recv()
        summed = self.source[...].astype(WIDE)
        for step in range(1, self.frames_axis):
            summed = summed + self.near[step - 1].astype(WIDE)
        self.every[self.group] = summed.astype(NARROW)
        for step in range(1, self.groups):
            self.group_copy(step).start()

    def finish(self):
        for step in range(1, self.frames_axis):
            self.frame_copy(step).wait_send()
        for step in range(1, self.groups):
            self.group_copy(step).wait_recv()
            self.group_copy(step).wait_send()

    @staticmethod
    def scratch(groups, frames_axis, shape):
        dma = pltpu.SemaphoreType.DMA
        return (
            [pltpu.VMEM((max(frames_axis - 1, 1),) + shape, NARROW)]
            + [dma((frames_axis,))] * 2
            + [dma((groups,))] * 2
        )


def grad_tile(first, second, result, start, size):
    result[start : start + size] = dot(first[:, start : start + size], second[...], 0, 0).astype(NARROW)


def can_scatter(groups, frames_axis, width):
    return groups % 2 == 0 and width % (16 * groups * frames_axis) == 0


def vmem(count):
    return [pl.BlockSpec(memory_space=pltpu.VMEM)] * count


class Fetch:
    def __init__(self, sources, held, sems):
        self.copies = [
            pltpu.make_async_copy(source, target, sems.at[i]) for i, (source, target) in enumerate(zip(sources, held))
        ]
        self.waiting = list(range(len(self.copies)))
        for copy in self.copies:
            copy.start()

    def __call__(self, *which):
        for i in which or tuple(self.waiting):
            self.copies[i].wait()
            self.waiting.remove(i)

    def again(self, *which):
        for i in which:
            self.copies[i].wait()


def fetching_call(kernel, operands, out_shape, scratch_shapes, kernel_id, name):
    many = len(operands)

    def body(*refs):
        sources, rest = refs[:many], refs[many : -many - 1]
        held, sems = refs[-many - 1 : -1], refs[-1]
        kernel(Fetch(sources, held, sems), *held, *rest)

    return pl.pallas_call(
        body,
        out_shape=tuple(out_shape),
        in_specs=[pl.BlockSpec(memory_space=pl.ANY)] * many,
        out_specs=tuple(vmem(len(out_shape))),
        scratch_shapes=list(scratch_shapes)
        + [pltpu.VMEM(item.shape, item.dtype) for item in operands]
        + [pltpu.SemaphoreType.DMA((many,))],
        compiler_params=pltpu.CompilerParams(
            collective_id=kernel_id, has_side_effects=True, vmem_limit_bytes=62 * 2**20
        ),
        name=name,
    )(*operands)


class LineGather:
    def __init__(self, count, place, slot_of, sems):
        self.count, self.place, self.last, self.slot_of = count, place, count - 1, slot_of
        self.up_send, self.down_send, self.arrived = sems

    def shift(self, owner, up):
        slot = self.slot_of(owner)
        to = self.place + 1 if up else self.place - 1
        sent = (self.up_send if up else self.down_send).at[owner]
        return remote(slot, slot, sent, self.arrived.at[owner], {LINE: to})

    def start(self):
        @pl.when(self.place < self.last)
        def _():
            self.shift(self.place, True).start()

        @pl.when(self.place > 0)
        def _():
            self.shift(self.place, False).start()

    def arrive(self, distance):
        @pl.when(self.place >= distance)
        def _():
            self.shift(self.place - distance, True).wait_recv()

            @pl.when(self.place < self.last)
            def _():
                self.shift(self.place - distance, True).start()

        @pl.when(self.place + distance <= self.last)
        def _():
            self.shift(self.place + distance, False).wait_recv()

            @pl.when(self.place > 0)
            def _():
                self.shift(self.place + distance, False).start()

    def settle(self):
        for owner in range(self.count):

            @pl.when((self.place < self.last) & (owner <= self.place))
            def _():
                self.shift(owner, True).wait_send()

            @pl.when((self.place > 0) & (owner >= self.place))
            def _():
                self.shift(owner, False).wait_send()


class LineScatter:
    def __init__(self, count, place, pieces, value_of, land, stage, sems):
        self.count, self.place, self.last, self.pieces = count, place, count - 1, pieces
        self.value_of, self.land, self.stage = value_of, land, stage
        self.from_left, self.from_right, self.to_left, self.to_right = sems

    def pass_on(self, owner, piece, right):
        side = 0 if right else 1
        return remote(
            self.stage.at[side, owner, piece],
            self.land.at[side, owner, piece],
            (self.to_right if right else self.to_left).at[owner, piece],
            (self.from_left if right else self.from_right).at[owner, piece],
            {LINE: self.place + 1 if right else self.place - 1},
        )

    def relay(self, distance, right, chosen=None):
        owner = self.place + distance if right else self.place - distance
        source = (self.place == 0) if right else (self.place == self.last)
        side = 0 if right else 1

        @pl.when((owner <= self.last) if right else (owner >= 0))
        def _():
            for piece in chosen if chosen is not None else range(self.pieces):

                @pl.when(source)
                def _():
                    self.stage[side, owner, piece] = self.value_of(owner, piece)

                @pl.when(jnp.logical_not(source))
                def _():
                    self.pass_on(owner, piece, right).wait_recv()
                    self.stage[side, owner, piece] = (
                        self.value_of(owner, piece).astype(WIDE) + self.land[side, owner, piece].astype(WIDE)
                    ).astype(NARROW)

                self.pass_on(owner, piece, right).start()

    def relay_both(self, distance, chosen=None):
        self.relay(distance, True, chosen)
        self.relay(distance, False, chosen)

    def total(self, piece):
        place = self.place

        @pl.when(place > 0)
        def _():
            self.pass_on(place, piece, True).wait_recv()

        @pl.when(place < self.last)
        def _():
            self.pass_on(place, piece, False).wait_recv()

        left_part = jnp.where(place > 0, self.land[0, place, piece].astype(WIDE), 0.0)
        right_part = jnp.where(place < self.last, self.land[1, place, piece].astype(WIDE), 0.0)
        return self.value_of(place, piece).astype(WIDE) + left_part + right_part

    def settle(self):
        for owner in range(self.count):
            for piece in range(self.pieces):

                @pl.when(owner > self.place)
                def _():
                    self.pass_on(owner, piece, True).wait_send()

                @pl.when(owner < self.place)
                def _():
                    self.pass_on(owner, piece, False).wait_send()


def gather_sems(count):
    return [pltpu.SemaphoreType.DMA((count,))] * 3


def scatter_sems(count, pieces):
    return [pltpu.SemaphoreType.DMA((count, pieces))] * 4


def line_sum(count, place, part_ref, land, cross, stage, total, sems, consume, early=(), folds=()):
    in_send, land_recv, cross_recv, out_send, out_recv = sems
    depth = part_ref.shape[0] // CHUNKS
    half = count // 2
    left = place < half
    level = jnp.where(left, place, count - 1 - place)
    inner = jnp.where(left, place + 1, place - 1)
    outer = jnp.where(left, place - 1, place + 1)
    is_end, is_middle = level == 0, level == half - 1

    def rows_of(chunk):
        return pl.ds(pl.multiple_of(chunk * depth, depth), depth)

    def inward(chunk):
        rows = rows_of(chunk)
        return remote(stage.at[rows], land.at[rows], in_send.at[chunk], land_recv.at[chunk], {LINE: inner})

    def across(chunk):
        rows = rows_of(chunk)
        return remote(stage.at[rows], cross.at[rows], in_send.at[chunk], cross_recv.at[chunk], {LINE: inner})

    def outward(chunk):
        rows = rows_of(chunk)
        return remote(total.at[rows], total.at[rows], out_send.at[chunk], out_recv.at[chunk], {LINE: outer})

    def send_in(chunk):
        @pl.when(is_middle)
        def _():
            across(chunk).start()

        @pl.when(jnp.logical_not(is_middle))
        def _():
            inward(chunk).start()

    def gather_in(chunk):
        rows = rows_of(chunk)
        inward(chunk).wait_recv()
        stage[rows] = (part_ref[rows].astype(WIDE) + land[rows].astype(WIDE)).astype(NARROW)
        send_in(chunk)

    def finish(chunk):
        rows = rows_of(chunk)

        @pl.when(is_middle)
        def _():
            across(chunk).wait_recv()
            total[rows] = (stage[rows].astype(WIDE) + cross[rows].astype(WIDE)).astype(NARROW)

        @pl.when(jnp.logical_not(is_middle))
        def _():
            outward(chunk).wait_recv()

        @pl.when(jnp.logical_not(is_end))
        def _():
            outward(chunk).start()

        consume(rows)

    def begin(chunk, carry):
        rows = rows_of(chunk)
        stage[rows] = part_ref[rows]
        send_in(chunk)
        return carry

    def step(number, carry):
        for i, work in enumerate(early):

            @pl.when(jnp.logical_not(is_end) & (number == i))
            def _():
                work()

        @pl.when(jnp.logical_not(is_end) & (number < CHUNKS))
        def _():
            gather_in(number)

        @pl.when(number >= LAG)
        def _():
            finish(number - LAG)

        for i, work in enumerate(folds):

            @pl.when(number == len(early) + 1 + i)
            def _():
                work()

        return carry

    @pl.when(is_end)
    def _():
        lax.fori_loop(0, CHUNKS, begin, 0)
        for work in early:
            work()

    lax.fori_loop(0, CHUNKS + LAG, step, 0)

    def settle(chunk, carry):
        @pl.when(is_middle)
        def _():
            across(chunk).wait_send()

        @pl.when(jnp.logical_not(is_middle))
        def _():
            inward(chunk).wait_send()

        @pl.when(jnp.logical_not(is_end))
        def _():
            outward(chunk).wait_send()

        return carry

    lax.fori_loop(0, CHUNKS, settle, 0)


def forward_kernel(
    count, fetch, part_ref, base_ref, rows_ref, out_ref, next_ref, normed_ref, land, cross, stage, *sems
):
    place = lax.axis_index(LINE)
    greet_line(place, count)
    fetch()
    gate, gain, shift = (rows_ref[i : i + 1] for i in range(3))

    def consume(rows):
        moved = base_ref[rows] + gate * out_ref[rows].astype(WIDE)
        next_ref[rows] = moved
        normed_ref[rows] = (norm_parts(moved)[0] * gain + shift).astype(NARROW)

    line_sum(count, place, part_ref, land, cross, stage, out_ref, sems, consume)


def backward_kernel(count, groups, frames_axis, widths, fetch, *refs):
    part_ref, base_ref, grad_ref, below_ref, rows_ref, *refs = refs
    pairs, refs = [refs[0:2], refs[2:4]], refs[4:]
    sources, refs = refs[: len(widths) - 1], refs[max(len(widths) - 1, 0) :]
    moved_ref, low_ref, sums_ref, *refs = refs
    many = sum(len(columns) for columns in widths)
    results, refs = refs[:many], refs[many:]
    product_ref, total, land, cross, stage, tally, *refs = refs
    sems, scratch = refs[:5], refs[5:]
    place = lax.axis_index(LINE)
    early = Products(pairs, product_ref).work()
    scatters = Scatters(
        groups, frames_axis, [*sources, product_ref] if widths else [], widths, results, scratch
    )
    greet_line(place, count, 0, scatters.partners() if widths else ())
    fetch()
    folds = []
    if widths:
        scatters.items[0].start()
        early = scatters.folds(0) + early + [scatters.items[-1].start]
        folds = scatters.folds(len(widths) - 1)
    gain, gate = (rows_ref[i : i + 1] for i in range(2))
    tally[...] = jnp.zeros_like(tally)

    def consume(rows):
        grads = total[rows].astype(WIDE)
        normal, spread = norm_parts(base_ref[rows])
        moved = grad_ref[rows] + norm_pull(grads * gain, normal, spread)
        moved_ref[rows] = moved
        low_ref[rows] = (gate * moved).astype(NARROW)
        for i, terms in enumerate((grads, grads * normal, moved * below_ref[rows].astype(WIDE))):
            tally[i] += jnp.sum(terms.reshape(-1, 8, terms.shape[-1]), axis=0)

    line_sum(count, place, part_ref, land, cross, stage, total, sems, consume, early, folds)
    sums_ref[...] = jnp.zeros_like(sums_ref)
    for i in range(3):
        sums_ref[i : i + 1] = jnp.sum(tally[i], axis=0, keepdims=True)
    scatters.finish()


def line_sems():
    return [pltpu.SemaphoreType.DMA((CHUNKS,))] * 5


def call_forward(count, part, base, rows):
    shape = part.shape
    return fetching_call(
        functools.partial(forward_kernel, count),
        [part, base, rows],
        (
            jax.ShapeDtypeStruct(shape, NARROW),
            jax.ShapeDtypeStruct(shape, WIDE),
            jax.ShapeDtypeStruct(shape, NARROW),
        ),
        [pltpu.VMEM(shape, NARROW)] * 3 + line_sems(),
        1,
        "forward_sum",
    )


def call_backward(count, groups, frames_axis, part, base, grad, below, rows, pairs, sources, widths):
    shape = part.shape
    results, scratch = Scatters.shapes(groups, frames_axis, shape[1], widths)
    product = (shape[1], sum(second.shape[1] for _, second in pairs))
    if not widths:
        results = [jax.ShapeDtypeStruct(product, NARROW)]
    return fetching_call(
        functools.partial(backward_kernel, count, groups, frames_axis, widths),
        [part, base, grad, below, rows, *(item for pair in pairs for item in pair), *sources],
        (
            jax.ShapeDtypeStruct(shape, WIDE),
            jax.ShapeDtypeStruct(shape, NARROW),
            jax.ShapeDtypeStruct((8, shape[1]), WIDE),
            *results,
        ),
        ([pltpu.VMEM(product, NARROW)] if widths else [])
        + [pltpu.VMEM(shape, NARROW)] * 4
        + [pltpu.VMEM((3, 8, shape[1]), WIDE)]
        + line_sems()
        + scratch,
        2,
        "backward_sum",
    )


def head_mask(head, shape):
    lane = lax.broadcasted_iota(jnp.int32, shape, len(shape) - 1)
    return (lane >= head * HD) & (lane < (head + 1) * HD)


def spread_heads(values, result):
    rows = values.shape[0]
    for head in range(values.shape[1] // HD):
        kept = jnp.where(head_mask(head, values.shape), values.astype(WIDE), 0.0)
        result[head * rows : (head + 1) * rows] = kept.astype(NARROW)


def collect_heads(values, rows):
    found = jnp.zeros((rows, values.shape[1]), WIDE)
    for head in range(values.shape[0] // rows):
        found = jnp.where(head_mask(head, found.shape), values[head * rows : (head + 1) * rows], found)
    return found


def spatial_backward(given, asked, keys, values, key_rows, value_rows, probs_low, scores_low):
    rows, scale = asked.shape[0], HD ** (-0.5)
    heads = asked.shape[1] // HD
    spread_heads(keys, key_rows)
    spread_heads(values, value_rows)
    for head in range(heads):
        spot = slice(head * rows, (head + 1) * rows)
        scores = scale * dot(asked, key_rows[spot], 1, 1)
        raised = jnp.exp(scores - jnp.max(scores, axis=-1, keepdims=True))
        probs = raised * (1.0 / jnp.sum(raised, axis=-1, keepdims=True))
        pulled = dot(given, value_rows[spot], 1, 1)
        moved = probs * (pulled - jnp.sum(pulled * probs, axis=-1, keepdims=True))
        probs_low[:, spot] = probs.astype(NARROW)
        scores_low[:, spot] = moved.astype(NARROW)
    grad_query = scale * dot(scores_low[...], key_rows[...], 1, 0)
    grad_keys = scale * collect_heads(dot(scores_low[...], asked, 0, 0), rows)
    grad_values = collect_heads(dot(probs_low[...], given, 0, 0), rows)
    return grad_query, grad_keys, grad_values


def closing_kernel(count, groups, frames_axis, frames, widths, fetch, *refs):
    (
        low_ref, base_ref, grad_ref, small_ref, rows_ref, packed_ref, heads_ref, hidden_ref, in_ref, out_ref,
        text_ref, *refs,
    ) = refs
    sources, refs = refs[: len(widths) - 1], refs[max(len(widths) - 1, 0) :]
    latent_ref, every_ref, text_all, *refs = refs
    many = sum(len(columns) for columns in widths)
    results, refs = refs[:many], refs[many:]
    (
        product_ref, part_ref, grad_packed, key_rows, value_rows, probs_low, scores_low,
        land, stage, line_rows, own_rows, tally, *refs,
    ) = refs
    line_send, line_recv, all_send, all_recv = refs[4:8]
    place, group, here = (lax.axis_index(axis) for axis in (LINE, GROUP, FRAME))
    last = count - 1
    share = latent_ref.shape[1]
    local = out_ref.shape[0]
    everyone = groups * frames_axis
    rank = group * frames_axis + here
    products = Products([(hidden_ref, grad_packed), (low_ref, heads_ref)], product_ref)
    scatters = Scatters(groups, frames_axis, [*sources, product_ref] if widths else [], widths, results, refs[13:])
    exchange = GroupExchange(groups, frames_axis, text_ref, text_all, refs[8:13])

    def member(ahead):
        to = lax.rem(rank + ahead, everyone)
        return {GROUP: lax.div(to, frames_axis), FRAME: lax.rem(to, frames_axis)}

    def neighbour(ahead):
        return {LINE: lax.rem(place + ahead, count)}

    barrier = pltpu.get_barrier_semaphore()

    def greet(ahead, carry):
        pl.semaphore_signal(barrier, inc=1, device_id=member(ahead), device_id_type=MESH)
        return carry

    for ahead in range(1, count):
        pl.semaphore_signal(barrier, inc=1, device_id=neighbour(ahead), device_id_type=MESH)
    lax.fori_loop(1, everyone, greet, 0)
    pl.semaphore_wait(barrier, last + everyone - 1)
    fetch(0, 5, 8, 9, 10)

    def rows_of(owner):
        return pl.ds(pl.multiple_of(owner * share, share), share)

    passing = LineScatter(
        count, place, frames, lambda owner, frame: part_ref[frame, rows_of(owner)], land, stage, refs[0:4]
    )
    patches = base_ref.shape[1]
    exchange.start()
    for frame in range(frames):
        rows = slice(frame * patches, (frame + 1) * patches)
        given = dot(low_ref[rows], out_ref[...], 1, 1).astype(NARROW)
        asked, keys, values = (packed_ref[rows, i * local : (i + 1) * local] for i in range(3))
        parts = jnp.zeros(part_ref.shape[1:], WIDE)
        found = spatial_backward(given, asked, keys, values, key_rows, value_rows, probs_low, scores_low)
        for i, item in enumerate(found):
            low = item.astype(NARROW)
            grad_packed[rows, i * local : (i + 1) * local] = low
            parts = parts + dot(low, in_ref[i * local : (i + 1) * local], 1, 0)
        part_ref[frame] = parts.astype(NARROW)
        passing.relay_both(last, (frame,))
        if frame == 0:
            exchange.spread()
    if last > 1:
        passing.relay_both(last - 1, (0,))
    fetch()
    for work in products.work():
        work()
    if widths:
        scatters.items[-1].start()
    if last > 1:
        passing.relay_both(last - 1, tuple(range(1, frames)))

    tally[...] = jnp.zeros_like(tally)
    depth = 32
    blocks = base_ref.shape[1] // depth

    def add_rows(number, carry):
        frame, rows = lax.div(number, blocks), pl.ds(pl.multiple_of(lax.rem(number, blocks) * depth, depth), depth)
        normal = norm_parts(base_ref[frame, rows])[0]
        grads = part_ref[frame, rows].astype(WIDE)
        for i, terms in enumerate((grads, grads * normal)):
            tally[i] += jnp.sum(terms.reshape(-1, 8, terms.shape[-1]), axis=0)
        return carry

    lax.fori_loop(0, frames * blocks, add_rows, 0)
    line_rows[place] = small_ref[0:8]
    for i in range(2):
        line_rows[place, i : i + 1] = jnp.sum(tally[i], axis=0, keepdims=True)

    def line_copy(ahead):
        return remote(
            line_rows.at[place], line_rows.at[place], line_send.at[ahead], line_recv.at[ahead], neighbour(ahead)
        )

    def all_copy(ahead):
        return remote(
            own_rows, every_ref.at[rank], all_send.at[ahead], all_recv.at[ahead], member(ahead)
        )

    for ahead in range(1, count):
        line_copy(ahead).start()
    if widths:
        for work in scatters.folds(len(widths) - 1):
            work()
    for distance in range(last - 2, 0, -1):
        passing.relay_both(distance)
    for ahead in range(1, count):
        line_copy(ahead).wait_recv()
    summed = line_rows[0]
    for i in range(1, count):
        summed = summed + line_rows[i]
    own_rows[0:8] = summed
    own_rows[8:16] = small_ref[8:16]
    every_ref[rank] = own_rows[...]

    def send_rows(ahead, carry):
        all_copy(ahead).start()
        return carry

    lax.fori_loop(1, everyone, send_rows, 0)

    own = rows_of(place)
    for frame in range(frames):
        grads = passing.total(frame)
        normal, spread = norm_parts(base_ref[frame, own])
        latent_ref[frame] = (
            grad_ref[frame, own] + norm_pull(grads * rows_ref[0:1], normal, spread)
        ).astype(NARROW)

    passing.settle()
    for ahead in range(1, count):
        line_copy(ahead).wait_send()

    def settle(ahead, carry):
        all_copy(ahead).wait_recv()
        all_copy(ahead).wait_send()
        return carry

    lax.fori_loop(1, everyone, settle, 0)
    exchange.finish()
    scatters.finish()


def call_closing(
    count, groups, frames_axis, low, base, grad, small, rows, packed, heads, hidden, in_w, out_w, text, sources, widths
):
    frames, patches, features = base.shape
    everyone = groups * frames_axis
    share = patches // count
    local = out_w.shape[0]
    results, scratch = Scatters.shapes(groups, frames_axis, features, widths)
    product = (features, packed.shape[1] + local)
    if not widths:
        results = [jax.ShapeDtypeStruct(product, NARROW)]
    dma = pltpu.SemaphoreType.DMA
    wide_keys = local // HD * patches
    return fetching_call(
        functools.partial(closing_kernel, count, groups, frames_axis, frames, widths),
        [low, base, grad, small, rows, packed, heads, hidden, in_w, out_w, text, *sources],
        (
            jax.ShapeDtypeStruct((frames, share, features), NARROW),
            jax.ShapeDtypeStruct((everyone, 16, features), WIDE),
            jax.ShapeDtypeStruct((groups,) + text.shape, NARROW),
            *results,
        ),
        ([pltpu.VMEM(product, NARROW)] if widths else [])
        + [
            pltpu.VMEM((frames, patches, features), NARROW),
            pltpu.VMEM(packed.shape, NARROW),
            pltpu.VMEM((wide_keys, local), NARROW),
            pltpu.VMEM((wide_keys, local), NARROW),
            pltpu.VMEM((patches, wide_keys), NARROW),
            pltpu.VMEM((patches, wide_keys), NARROW),
            pltpu.VMEM((2, count, frames, share, features), NARROW),
            pltpu.VMEM((2, count, frames, share, features), NARROW),
            pltpu.VMEM((count, 8, features), WIDE),
            pltpu.VMEM((16, features), WIDE),
            pltpu.VMEM((2, 8, features), WIDE),
        ]
        + scatter_sems(count, frames)
        + [dma((count,))] * 2
        + [dma((everyone,))] * 2
        + GroupExchange.scratch(groups, frames_axis, text.shape)
        + scratch,
        4,
        "closing",
    )


def finishing_kernel(groups, frames_axis, modulation_rows, layouts, small_ref, ada_ref, text_ref, captions_ref, *refs):
    many = len(layouts)
    sources, refs = refs[:many], refs[many:]
    ada_out, table_out, gain_out, caption_out, *results = refs
    local = table_out.shape[1]
    buckets = table_out.shape[0]
    column = ada_out.shape[1]
    features = small_ref.shape[2]
    rank = lax.axis_index(GROUP) * frames_axis + lax.axis_index(FRAME)

    def over_frames(group, row):
        first = group * frames_axis
        found = small_ref[first, row : row + 1]
        for other in range(1, frames_axis):
            found = found + small_ref[first + other, row : row + 1]
        return found

    gain = over_frames(0, 14)
    for group in range(1, groups):
        gain = gain + over_frames(group, 14)
    gain_out[...] = gain

    side = jnp.concatenate([small_ref[group * frames_axis, 15:16] for group in range(groups)], axis=0)
    cond, chosen = side[:, 0:local], side[:, local : local + buckets]
    below = 1.0 / (1.0 + jnp.exp(-cond))
    act_low = (cond * below).astype(NARROW)
    act_twice = jnp.concatenate([act_low, act_low], axis=0)
    where = lax.broadcasted_iota(jnp.int32, (features, column), 0)
    which = lax.broadcasted_iota(jnp.int32, (features, column), 1) + rank * column
    select = jnp.where(where == which, 1.0, 0.0).astype(NARROW)
    grad_act = jnp.zeros((2 * groups, local), WIDE)
    for k, row in enumerate(modulation_rows):
        rows = jnp.concatenate([over_frames(group, row) for group in range(groups)], axis=0)
        pair = jnp.concatenate(split_pair(rows), axis=0)
        grad_act = grad_act + dot(pair, ada_ref[k], 1, 1)
        columns = dot(pair, select, 1, 0).astype(NARROW)
        ada_out[k] = dot(columns, act_twice, 0, 0)
    slope = below * (1.0 + cond * (1.0 - below))
    grad_cond = (grad_act[0:groups] + grad_act[groups:]) * slope
    spread = jnp.concatenate(split_pair(grad_cond), axis=0)
    chosen = chosen.astype(NARROW)
    table_out[...] = dot(jnp.concatenate([chosen, chosen], axis=0), spread, 0, 0)

    slots = captions_ref.shape[1]
    caption = dot(text_ref[0, 0:slots], captions_ref[0], 0, 0)
    for group in range(1, groups):
        caption = caption + dot(text_ref[group, 0:slots], captions_ref[group], 0, 0)
    caption_out[...] = caption
    for source, result, layout in zip(sources, results, layouts):
        if layout == 0:
            result[...] = source[...]
        else:
            parts = source.shape[1] // local
            for i in range(parts):
                values = source[:, i * local : (i + 1) * local]
                if layout == 1:
                    result[i] = values
                else:
                    result[:, i] = values


def call_finishing(groups, frames_axis, buckets, modulation_rows, layouts, small, ada, text, captions, sources):
    parts, local, features = ada.shape
    block = features // (groups * frames_axis)

    def shape_of(source, layout):
        n = source.shape[1] // local
        return (source.shape, (n, source.shape[0], local), (source.shape[0], n, local))[layout]

    results = [
        jax.ShapeDtypeStruct((parts, block, local), WIDE),
        jax.ShapeDtypeStruct((buckets, local), WIDE),
        jax.ShapeDtypeStruct((1, features), WIDE),
        jax.ShapeDtypeStruct((local, captions.shape[2]), WIDE),
    ]
    results += [
        jax.ShapeDtypeStruct(shape_of(source, layout), source.dtype) for source, layout in zip(sources, layouts)
    ]
    return pl.pallas_call(
        functools.partial(finishing_kernel, groups, frames_axis, modulation_rows, layouts),
        out_shape=tuple(results),
        in_specs=vmem(4 + len(sources)),
        out_specs=tuple(vmem(len(results))),
        compiler_params=pltpu.CompilerParams(vmem_limit_bytes=62 * 2**20),
        name="finishing",
    )(small, ada, text, captions, *sources)


def opening_kernel(
    count, groups, frames_axis, latent_ref, act_ref, ada_ref, captions_ref, caption_full, caption_w,
    base_ref, normed_ref, mods_ref, text_out, spread_ref,
    caption_here, caption_here_w, caption_sem, land, ada, mine, others,
    up_send, down_send, land_recv, ada_sem, mods_send, mods_recv, cap_send, cap_recv, cap_local,
):
    place = lax.axis_index(LINE)
    group = lax.axis_index(GROUP)
    here = lax.axis_index(FRAME)
    last = count - 1
    width = spread_ref.shape[2]
    parts = ada_ref.shape[0]
    share = latent_ref.shape[1]

    loads = [pltpu.make_async_copy(ada_ref.at[k], ada.at[k], ada_sem.at[k]) for k in range(parts)]
    for load in loads:
        load.start()
    text_loads = [
        pltpu.make_async_copy(caption_full, caption_here, caption_sem.at[0]),
        pltpu.make_async_copy(caption_w, caption_here_w, caption_sem.at[1]),
    ]
    for load in text_loads:
        load.start()

    barrier = pltpu.get_barrier_semaphore()
    for ahead in range(1, count):
        pl.semaphore_signal(
            barrier, inc=1, device_id={LINE: lax.rem(place + ahead, count)}, device_id_type=MESH
        )
    for ahead in range(1, groups):
        pl.semaphore_signal(
            barrier, inc=1, device_id={GROUP: lax.rem(group + ahead, groups)}, device_id_type=MESH
        )
    pl.semaphore_wait(barrier, count - 1 + groups - 1)

    def shift(owner, up):
        to = place + 1 if up else place - 1
        return remote(
            land.at[owner], land.at[owner], (up_send if up else down_send).at[owner], land_recv.at[owner], {LINE: to}
        )

    land[place] = latent_ref[...]

    @pl.when(place < last)
    def _():
        shift(place, True).start()

    @pl.when(place > 0)
    def _():
        shift(place, False).start()

    def caption_block(to):
        if len(captions_ref.shape) == 3:
            return captions_ref.at[to]
        first = pl.multiple_of((to * frames_axis + here) * width, width)
        return captions_ref.at[:, pl.ds(first, width)]

    def caption_copy(ahead):
        to = lax.rem(group + ahead, groups)
        return remote(
            caption_block(to),
            spread_ref.at[group],
            cap_send.at[ahead],
            cap_recv.at[ahead],
            {GROUP: to},
        )

    own_caption = pltpu.make_async_copy(caption_block(group), spread_ref.at[group], cap_local)
    own_caption.start()
    for ahead in range(1, groups):
        caption_copy(ahead).start()

    def arrive(distance):
        @pl.when(place >= distance)
        def _():
            shift(place - distance, True).wait_recv()

            @pl.when(place < last)
            def _():
                shift(place - distance, True).start()

        @pl.when(place + distance <= last)
        def _():
            shift(place + distance, False).wait_recv()

            @pl.when(place > 0)
            def _():
                shift(place + distance, False).start()

    def weigh(k):
        loads[k].wait()
        product = dot(act_ref[...], ada[k], 1, 0)
        mine[k : k + 1] = product[0:1]

    def mods_copy(ahead):
        return remote(
            mine, others.at[place], mods_send.at[ahead], mods_recv.at[ahead], {LINE: lax.rem(place + ahead, count)}
        )

    mine[...] = jnp.zeros_like(mine)
    cut = parts // 2 + 1
    for k in range(cut):
        weigh(k)
    arrive(1)
    for k in range(cut, parts):
        weigh(k)
    for ahead in range(1, count):
        mods_copy(ahead).start()
    others[place] = mine[...]
    for load in text_loads:
        load.wait()
    text_out[...] = dot(caption_here[...], caption_here_w[...], 1, 1).astype(NARROW)
    for distance in range(2, count - 1):
        arrive(distance)
    for ahead in range(1, count):
        mods_copy(ahead).wait_recv()
    mods = others[0]
    for i in range(1, count):
        mods = mods + others[i]
    mods_ref[...] = mods
    gain = 1.0 + mods[1:2]
    shift_row = mods[0:1]

    def norm_owner(owner):
        for f in range(latent_ref.shape[0]):
            values = land[owner, f].astype(WIDE)
            rows = pl.ds(pl.multiple_of(owner * share, share), share)
            base_ref[f, rows] = values
            normed_ref[f, rows] = (norm_parts(values)[0] * gain + shift_row).astype(NARROW)

    def near(distance):
        @pl.when(place >= distance)
        def _():
            norm_owner(place - distance)

        @pl.when(place + distance <= last)
        def _():
            norm_owner(place + distance)

    norm_owner(place)
    for distance in range(1, count - 1):
        near(distance)
    if count > 2:
        arrive(count - 1)
    near(count - 1)

    for owner in range(count):

        @pl.when((place < last) & (owner <= place))
        def _():
            shift(owner, True).wait_send()

        @pl.when((place > 0) & (owner >= place))
        def _():
            shift(owner, False).wait_send()

    for ahead in range(1, count):
        mods_copy(ahead).wait_send()
    for ahead in range(1, groups):
        caption_copy(ahead).wait_send()
        caption_copy(ahead).wait_recv()
    own_caption.wait()


def call_opening(count, groups, frames_axis, latent, act, ada, captions, caption_w):
    frames, share, features = latent.shape
    parts = ada.shape[0]
    length, text_width = captions.shape
    width = text_width // (groups * frames_axis)
    caption_full = captions
    if width % 128:
        blocks = captions.reshape(length, groups, frames_axis, width)
        captions = jnp.transpose(
            lax.dynamic_index_in_dim(blocks, lax.axis_index(FRAME), 2, keepdims=False), (1, 0, 2)
        )
    full = (frames, share * count, features)
    dma = pltpu.SemaphoreType.DMA
    anywhere = pl.BlockSpec(memory_space=pl.ANY)
    return pl.pallas_call(
        functools.partial(opening_kernel, count, groups, frames_axis),
        out_shape=(
            jax.ShapeDtypeStruct(full, WIDE),
            jax.ShapeDtypeStruct(full, NARROW),
            jax.ShapeDtypeStruct((16, features), WIDE),
            jax.ShapeDtypeStruct((length, caption_w.shape[0]), NARROW),
            jax.ShapeDtypeStruct((groups, length, width), NARROW),
        ),
        in_specs=vmem(2) + [anywhere] * 4,
        out_specs=tuple(vmem(4) + [anywhere]),
        scratch_shapes=[
            pltpu.VMEM(caption_full.shape, NARROW),
            pltpu.VMEM(caption_w.shape, NARROW),
            dma((2,)),
            pltpu.VMEM((count, frames, share, features), NARROW),
            pltpu.VMEM(ada.shape, NARROW),
            pltpu.VMEM((16, features), WIDE),
            pltpu.VMEM((count, 16, features), WIDE),
            dma((count,)),
            dma((count,)),
            dma((count,)),
            dma((parts,)),
            dma((count,)),
            dma((count,)),
            dma((groups,)),
            dma((groups,)),
            dma,
        ],
        compiler_params=pltpu.CompilerParams(
            collective_id=3, has_side_effects=True, vmem_limit_bytes=62 * 2**20
        ),
        name="opening",
    )(latent, act, ada, captions, caption_full, caption_w)


STAGES = 4
MIDDLE_ROWS = 32
MIDDLE_LAG = 3


def gelu_both(values):
    square = values * values
    bent = jnp.tanh(0.7978845608028654 * (values + 0.044715 * values * square))
    slope = 0.5 * (1.0 + bent) + 0.5 * values * (1.0 - bent * bent) * (
        0.7978845608028654 * (1.0 + 3.0 * 0.044715 * square)
    )
    return 0.5 * values * (1.0 + bent), slope


def middle_kernel(count, groups, frames_axis, frames, scattered, fetch, *refs):
    (
        first_ref, base_ref, cotangent_ref, rows_ref, bias_ref,
        text_ref, text_w, query_w, out_w, up_w, down_w,
        base_three, grad_two, low_two, low_three, normed_three, heads_out, grad_query,
        grad_keys, grad_values, sums_ref, extra_part, text_rows, down_grad, up_result,
        keys_ref, values_ref,
        normed_four, low_four, active, grad_inner, base_two, branch_two, query, grad_heads, part, mixed, tally,
        land, stage, total, cross, in_send, land_recv, cross_recv, out_send, out_recv, *scratch,
    ) = refs
    place = lax.axis_index(LINE)
    if scattered:
        up_grad, *scratch = scratch
        scatters = Scatters(groups, frames_axis, [up_grad], [[up_grad.shape[1]]], [up_result], scratch)
        asides = scatters.items
        greet_line(place, count, 0, asides[0].partners())
    else:
        up_grad, asides = up_result, []
        greet_line(place, count)
    fetch(0, 1, 3)
    half = count // 2
    left = place < half
    level = jnp.where(left, place, count - 1 - place)
    inner = jnp.where(left, place + 1, place - 1)
    outer = jnp.where(left, place - 1, place + 1)
    is_end, is_middle = level == 0, level == half - 1
    inside = jnp.logical_not(is_end)
    patches = base_ref.shape[0] // frames
    chunks = patches // MIDDLE_ROWS
    slots = STAGES * frames
    scale = HD ** (-0.5)
    width = bias_ref.shape[2]
    local = query_w.shape[0]
    half_heads = local // HD // 2
    tile = up_w.shape[1] // 3
    gate_two, cross_gain, gain_three, shift_three, gate_three = (rows_ref[i : i + 1] for i in range(5))

    def where_of(slot, chunk):
        rows = pl.ds(pl.multiple_of(lax.rem(slot, frames) * patches + chunk * MIDDLE_ROWS, MIDDLE_ROWS), MIDDLE_ROWS)
        return lax.rem(lax.div(slot, frames), 2), rows

    def inward(slot, chunk):
        rows = where_of(slot, chunk)[1]
        return remote(
            stage.at[rows], land.at[rows], in_send.at[slot, chunk], land_recv.at[slot, chunk], {LINE: inner}
        )

    def across(slot, chunk):
        side, rows = where_of(slot, chunk)
        return remote(
            stage.at[rows], cross.at[side, rows], in_send.at[slot, chunk], cross_recv.at[slot, chunk], {LINE: inner}
        )

    def outward(slot, chunk):
        rows = where_of(slot, chunk)[1]
        return remote(
            total.at[rows], total.at[rows], out_send.at[slot, chunk], out_recv.at[slot, chunk], {LINE: outer}
        )

    def own_part(slot, rows):
        return jnp.where(slot < frames, first_ref[rows], part[rows])

    def send_in(slot, chunk):
        @pl.when(is_middle)
        def _():
            across(slot, chunk).start()

        @pl.when(jnp.logical_not(is_middle))
        def _():
            inward(slot, chunk).start()

    def sent(slot, chunk):
        @pl.when(is_middle)
        def _():
            across(slot, chunk).wait_send()

        @pl.when(jnp.logical_not(is_middle))
        def _():
            inward(slot, chunk).wait_send()

        @pl.when(inside)
        def _():
            outward(slot, chunk).wait_send()

    def free(slot, chunk):
        @pl.when(slot >= frames)
        def _():
            sent(slot - frames, chunk)

    def gather_in(slot, chunk):
        rows = where_of(slot, chunk)[1]
        free(slot, chunk)
        inward(slot, chunk).wait_recv()
        stage[rows] = (own_part(slot, rows).astype(WIDE) + land[rows].astype(WIDE)).astype(NARROW)
        send_in(slot, chunk)

    def add_rows(which, terms):
        tally[which] += jnp.sum(terms.reshape(-1, 8, terms.shape[-1]), axis=0)

    def consume(slot, rows, summed):
        number = lax.div(slot, frames)

        @pl.when(number == 0)
        def _():
            branch_two[rows] = summed
            moved = base_ref[rows] + gate_two * summed.astype(WIDE)
            base_two[rows] = moved
            normed_three[rows] = (norm_parts(moved)[0] * cross_gain).astype(NARROW)

        @pl.when(number == 1)
        def _():
            moved = base_two[rows] + summed.astype(WIDE)
            base_three[rows] = moved
            normed_four[rows] = (norm_parts(moved)[0] * gain_three + shift_three).astype(NARROW)
            low_four[rows] = (gate_three * cotangent_ref[rows].astype(WIDE)).astype(NARROW)

        @pl.when(number == 2)
        def _():
            grads = summed.astype(WIDE)
            normal, spread = norm_parts(base_three[rows])
            moved = cotangent_ref[rows].astype(WIDE) + norm_pull(grads * gain_three, normal, spread)
            grad_two[rows] = moved
            low_three[rows] = moved.astype(NARROW)
            add_rows(0, grads)
            add_rows(1, grads * normal)

        @pl.when(number == 3)
        def _():
            grads = summed.astype(WIDE)
            normal, spread = norm_parts(base_two[rows])
            moved = grad_two[rows] + norm_pull(grads * cross_gain, normal, spread)
            grad_two[rows] = moved
            low_two[rows] = (gate_two * moved).astype(NARROW)
            add_rows(2, grads * normal)
            add_rows(3, moved * branch_two[rows].astype(WIDE))

    def finish(slot, chunk):
        side, rows = where_of(slot, chunk)

        @pl.when(is_middle)
        def _():
            across(slot, chunk).wait_recv()
            total[rows] = (stage[rows].astype(WIDE) + cross[side, rows].astype(WIDE)).astype(NARROW)

        @pl.when(jnp.logical_not(is_middle))
        def _():
            outward(slot, chunk).wait_recv()

        @pl.when(inside)
        def _():
            outward(slot, chunk).start()

        consume(slot, rows, total[rows])

    def head_rows(head):
        return pl.ds(head * width, width)

    def probs_of(stream, asked, head):
        scores = scale * dot(asked, keys_ref[head_rows(head)], 1, 1) + bias_ref[stream, 0:1]
        raised = jnp.exp(scores - jnp.max(scores, axis=-1, keepdims=True))
        return raised / jnp.sum(raised, axis=-1, keepdims=True)

    def cross_forward(piece, stream, rows):
        if piece == 0:
            query[rows] = dot(normed_three[rows], query_w[...], 1, 1).astype(NARROW)
        elif piece in (1, 2):
            asked = query[rows]
            found = jnp.zeros((patches, local), WIDE) if piece == 1 else mixed[...]
            for head in range((piece - 1) * half_heads, piece * half_heads):
                probs = probs_of(stream, asked, head).astype(NARROW)
                found = found + dot(probs, values_ref[head_rows(head)], 1, 0)
            if piece == 1:
                mixed[...] = found
            else:
                heads_out[rows] = found.astype(NARROW)
        elif piece == 3:
            part[rows] = dot(heads_out[rows], out_w[...], 1, 0).astype(NARROW)

    def feed_forward(piece, stream, rows):
        if piece < 3:
            span = slice(piece * tile, (piece + 1) * tile)
            inner_values = dot(normed_four[rows], up_w[:, span], 1, 0)
            pulled = dot(low_four[rows], down_w[span], 1, 1)
            raised, slope = gelu_both(inner_values)
            active[rows, span] = raised.astype(NARROW)
            grad_inner[rows, span] = (pulled * slope).astype(NARROW)
        else:
            third = up_w.shape[0] // 3
            span = slice((piece - 3) * third, (piece - 2) * third)
            part[rows, span] = dot(grad_inner[rows], up_w[span], 1, 1).astype(NARROW)

    def cross_backward(piece, stream, rows):
        if piece == 0:
            grad_heads[rows] = dot(low_three[rows], out_w[...], 1, 1).astype(NARROW)
        elif piece in (1, 2):
            asked, given = query[rows], grad_heads[rows]
            found = jnp.zeros((patches, local), WIDE) if piece == 1 else mixed[...]
            for head in range((piece - 1) * half_heads, piece * half_heads):
                spot = head_rows(head)
                probs = probs_of(stream, asked, head)
                pulled = dot(given, values_ref[spot], 1, 1)
                grad_scores = probs * (pulled - jnp.sum(pulled * probs, axis=-1, keepdims=True))
                grad_scores = grad_scores.astype(NARROW)
                found = found + dot(grad_scores, keys_ref[spot], 1, 0)
                grad_keys[spot] += dot(grad_scores, asked, 0, 0)
                grad_values[spot] += dot(probs.astype(NARROW), given, 0, 0)
            if piece == 1:
                mixed[...] = found
            else:
                grad_query[rows] = (scale * found).astype(NARROW)
        elif piece == 3:
            part[rows] = dot(grad_query[rows], query_w[...], 1, 0).astype(NARROW)

    def up_tile(number):
        grad_tile(normed_four, grad_inner, up_grad, number * third, third)

    def down_tile(number):
        grad_tile(low_four, active, down_grad, number * third, third)

    def extra(frame):
        rows = slice(frame * patches, (frame + 1) * patches)
        extra_part[rows] = dot(active[rows], down_w[...], 1, 0).astype(NARROW)

    def text_pairs():
        fetch.again(2, 4, 5, 6, 7, 8, 9, 10)
        slots_here = text_ref.shape[1]
        text_rows[slots_here:] = jnp.zeros((width - slots_here, text_rows.shape[1]), NARROW)
        for owner in range(count):
            text_rows[0:slots_here, owner * local : (owner + 1) * local] = text_ref[owner]
        packed = dot(text_rows[...], text_w[...], 1, 1).astype(NARROW)
        spread_heads(packed[:, 0:local], keys_ref)
        spread_heads(packed[:, local:], values_ref)

    third = up_w.shape[0] // 3
    late = {(0, 1): [text_pairs]}

    def later(slot, chunk, work, *args):
        late.setdefault((slots - 3 + slot, chunk), []).append(functools.partial(work, *args))

    for i, spot in enumerate(((0, 0), (0, 1), (0, 2))):
        later(*spot, up_tile, i)
    for i in range(3):
        later(2, 1 + i, down_tile, i)
    if asides:
        later(0, 2, asides[0].start)
        for i, work in enumerate(scatters.folds(0)):
            later(*((1, 0), (1, 1), (1, 2), (1, 7))[min(i, 3)], work)
    for frame in range(frames):
        later(2, 6 + min(frame, 1), extra, frame)

    tally[...] = jnp.zeros_like(tally)
    grad_keys[...] = jnp.zeros_like(grad_keys)
    grad_values[...] = jnp.zeros_like(grad_values)

    def step(number, carry):
        slot, chunk = lax.div(number, chunks), lax.rem(number, chunks)
        before = slot - 1

        @pl.when(is_end & (chunk == 0))
        def _():
            @pl.when(slot < slots)
            def _():
                def begin(item, inner_carry):
                    rows = where_of(slot, item)[1]
                    free(slot, item)
                    stage[rows] = own_part(slot, rows)
                    send_in(slot, item)
                    return inner_carry

                lax.fori_loop(0, chunks, begin, 0)

            for late_slot in sorted({spot[0] for spot in late}):

                @pl.when(slot == late_slot)
                def _():
                    for late_chunk in range(MIDDLE_LAG):
                        for work in late.get((late_slot, late_chunk), ()):
                            work()

            @pl.when(slot > 0)
            def _():
                def end(item, inner_carry):
                    finish(before, item)
                    return inner_carry

                lax.fori_loop(0, chunks, end, 0)

        @pl.when(inside & (slot < slots))
        def _():
            gather_in(slot, chunk)

            @pl.when(chunk >= MIDDLE_LAG)
            def _():
                finish(slot, chunk - MIDDLE_LAG)

        @pl.when(inside & (slot > 0) & (chunk < MIDDLE_LAG))
        def _():
            finish(before, chunks - MIDDLE_LAG + chunk)

        stream = lax.rem(jnp.maximum(before, 0), frames)
        rows = pl.ds(pl.multiple_of(stream * patches, patches), patches)
        for which, work in enumerate((cross_forward, feed_forward, cross_backward)):

            @pl.when((slot > 0) & (lax.div(jnp.maximum(before, 0), frames) == which))
            def _():
                for piece in range(6 if which == 1 else 4):

                    @pl.when(chunk == jnp.minimum(MIDDLE_LAG + piece, chunks - 1))
                    def _():
                        work(piece, stream, rows)

        for (late_slot, late_chunk), works in late.items():

            @pl.when((slot == late_slot) & (chunk == late_chunk) & (inside | (late_chunk >= MIDDLE_LAG)))
            def _():
                for work in works:
                    work()

        return carry

    lax.fori_loop(0, slots * chunks + MIDDLE_LAG, step, 0)

    def settle(number, carry):
        sent(lax.div(number, chunks), lax.rem(number, chunks))
        return carry

    lax.fori_loop((slots - frames) * chunks, slots * chunks, settle, 0)
    sums_ref[...] = jnp.zeros_like(sums_ref)
    for i in range(4):
        sums_ref[i : i + 1] = jnp.sum(tally[i], axis=0, keepdims=True)
    for aside in asides:
        aside.finish([up_result])


def call_middle(
    count, groups, frames_axis, frames, first, base, cotangent, rows, bias, text, text_w, query_w, out_w, up_w, down_w
):
    tokens, features = first.shape
    local, hidden = query_w.shape[0], up_w.shape[1]
    chunks = tokens // frames // MIDDLE_ROWS
    scattered = can_scatter(groups, frames_axis, features)
    keys_shape = (local // HD * bias.shape[2], local)

    def wide(*shape):
        return jax.ShapeDtypeStruct(shape, WIDE)

    def narrow(*shape):
        return jax.ShapeDtypeStruct(shape, NARROW)

    found, scratch = [narrow(features, hidden)], []
    if scattered:
        found, scratch = Scatters.shapes(groups, frames_axis, features, [[hidden]])
        scratch = [pltpu.VMEM((features, hidden), NARROW)] + scratch
    results = (
        [wide(tokens, features)] * 2
        + [narrow(tokens, features)] * 3
        + [narrow(tokens, local)] * 2
        + [wide(*keys_shape)] * 2
        + [wide(8, features), narrow(tokens, features), narrow(bias.shape[2], features), narrow(features, hidden)]
        + found
    )
    sem = pltpu.SemaphoreType.DMA((STAGES * frames, chunks))
    return fetching_call(
        functools.partial(middle_kernel, count, groups, frames_axis, frames, scattered),
        [first, base, cotangent, rows, bias, text, text_w, query_w, out_w, up_w, down_w],
        tuple(results),
        [pltpu.VMEM(keys_shape, NARROW)] * 2
        + [pltpu.VMEM((tokens, features), NARROW)] * 2
        + [pltpu.VMEM((tokens, hidden), NARROW)] * 2
        + [
            pltpu.VMEM((tokens, features), WIDE),
            pltpu.VMEM((tokens, features), NARROW),
            pltpu.VMEM((tokens, local), NARROW),
            pltpu.VMEM((tokens, local), NARROW),
            pltpu.VMEM((tokens, features), NARROW),
            pltpu.VMEM((tokens // frames, local), WIDE),
            pltpu.VMEM((4, 8, features), WIDE),
        ]
        + [pltpu.VMEM((tokens, features), NARROW)] * 3
        + [pltpu.VMEM((2, tokens, features), NARROW)]
        + [sem] * 5
        + scratch,
        7,
        "middle",
    )


def greet_frames(here, frames_axis):
    found = (here > 0).astype(jnp.int32) + (here < frames_axis - 1).astype(jnp.int32)
    barrier = pltpu.get_barrier_semaphore()

    @pl.when(here > 0)
    def _():
        pl.semaphore_signal(barrier, inc=1, device_id={FRAME: here - 1}, device_id_type=MESH)

    @pl.when(here < frames_axis - 1)
    def _():
        pl.semaphore_signal(barrier, inc=1, device_id={FRAME: here + 1}, device_id_type=MESH)

    return found


def head_columns(local):
    feature = lax.broadcasted_iota(jnp.int32, (local, 128), 0)
    first = lax.broadcasted_iota(jnp.int32, (local, 128), 1) * HD
    return jnp.where((feature >= first) & (feature < first + HD), 1.0, 0.0).astype(NARROW)


def per_head(values, columns):
    return dot(values.astype(NARROW), columns, 1, 0)


def over_features(values, columns):
    return dot(values.astype(NARROW), columns, 1, 1)


def window_probs(query, keys_of, bias_of, columns):
    scores = [
        HD ** (-0.5) * per_head(query * keys_of(offset), columns) + bias_of(offset) for offset in range(WIN)
    ]
    highest = functools.reduce(jnp.maximum, scores)
    raised = [jnp.exp(item - highest) for item in scores]
    whole = 1.0 / sum(raised[1:], raised[0])
    return [item * whole for item in raised]


def temporal_forward_kernel(
    count, frames_axis, frames, fetch, hidden_ref, in_ref, out_ref, bias_ref, cotangent_ref, text_ref,
    query_ref, keys_ref, values_ref, heads_ref, part_ref, cotangent_full, text_full,
    halo_send, halo_recv, *sems,
):
    place, here = lax.axis_index(LINE), lax.axis_index(FRAME)
    patches = hidden_ref.shape[0] // frames
    local = heads_ref.shape[1]
    share = cotangent_ref.shape[1]
    last = count - 1
    greet_line(place, count, greet_frames(here, frames_axis))
    fetch()
    cells = (keys_ref, values_ref)

    def shares(owner):
        return cotangent_full.at[:, pl.ds(pl.multiple_of(owner * share, share), share)]

    moving = [
        LineGather(count, place, shares, sems[0:3]),
        LineGather(count, place, lambda owner: text_full.at[owner], sems[3:6]),
    ]
    cotangent_full[:, pl.ds(pl.multiple_of(place * share, share), share)] = cotangent_ref[...]
    text_full[place] = text_ref[...]
    for item in moving:
        item.start()

    def halo(which, item):
        source = 2 + (frames - 2 + which if which < 2 else 0)
        target = which if which < 2 else frames + 2
        to = here + 1 if which < 2 else here - 1
        ref = cells[item]
        return remote(
            ref.at[source], ref.at[target], halo_send.at[which, item], halo_recv.at[which, item], {FRAME: to}
        )

    has_next, has_previous = here < frames_axis - 1, here > 0

    def frame_rows(frame):
        return slice(frame * patches, (frame + 1) * patches)

    for frame in range(frames):
        for item in range(2):
            rows = slice((1 + item) * local, (2 + item) * local)
            cells[item][2 + frame] = dot(hidden_ref[frame_rows(frame)], in_ref[rows], 1, 1).astype(NARROW)
            for which in range(3):
                if (frames - 2 + which if which < 2 else 0) == frame:

                    @pl.when(has_next if which < 2 else has_previous)
                    def _():
                        halo(which, item).start()

    query_ref[...] = dot(hidden_ref[...], in_ref[0:local], 1, 1).astype(NARROW)
    for distance in range(1, last):
        for item in moving:
            item.arrive(distance)
    for item in range(2):

        @pl.when(has_previous)
        def _():
            halo(0, item).wait_recv()
            halo(1, item).wait_recv()

        @pl.when(jnp.logical_not(has_previous))
        def _():
            cells[item][0:2] = jnp.zeros((2,) + cells[item].shape[1:], NARROW)

        @pl.when(has_next)
        def _():
            halo(2, item).wait_recv()

        @pl.when(jnp.logical_not(has_next))
        def _():
            cells[item][frames + 2] = jnp.zeros(cells[item].shape[1:], NARROW)

    columns = head_columns(local)
    for frame in range(frames):
        probs = window_probs(
            query_ref[frame_rows(frame)].astype(WIDE),
            lambda offset: keys_ref[frame + offset].astype(WIDE),
            lambda offset: bias_ref[frame * WIN + offset : frame * WIN + offset + 1],
            columns,
        )
        mixed = over_features(probs[0], columns) * values_ref[frame].astype(WIDE)
        for offset in range(1, WIN):
            mixed = mixed + over_features(probs[offset], columns) * values_ref[frame + offset].astype(WIDE)
        heads_ref[frame_rows(frame)] = mixed.astype(NARROW)
        part_ref[frame_rows(frame)] = dot(mixed.astype(NARROW), out_ref[...], 1, 0).astype(NARROW)
    for item in moving:
        item.arrive(last)
        item.settle()
    for item in range(2):

        @pl.when(has_next)
        def _():
            halo(0, item).wait_send()
            halo(1, item).wait_send()

        @pl.when(has_previous)
        def _():
            halo(2, item).wait_send()


def call_temporal_forward(count, frames_axis, hidden, in_w, out_w, bias, cotangent, text):
    tokens, features = hidden.shape
    frames, share = cotangent.shape[:2]
    local = out_w.shape[0]
    patches = tokens // frames

    def narrow(*shape):
        return jax.ShapeDtypeStruct(shape, NARROW)

    results = (
        [narrow(tokens, local)]
        + [narrow(frames + 3, patches, local)] * 2
        + [narrow(tokens, local), narrow(tokens, features)]
        + [narrow(frames, share * count, features), narrow(count, *text.shape)]
    )
    return fetching_call(
        functools.partial(temporal_forward_kernel, count, frames_axis, frames),
        [hidden, in_w, out_w, bias, cotangent, text],
        tuple(results),
        [pltpu.SemaphoreType.DMA((3, 2))] * 2 + gather_sems(count) * 2,
        8,
        "temporal_forward",
    )


def temporal_backward_kernel(
    count, groups, frames_axis, frames, widths, fetch, *refs
):
    (
        grad_ref, in_ref, out_ref, bias_ref, query_ref, keys_ref, values_ref,
        extra_ref, text_keys, text_values, text_w, text_rows, cross_hidden, cross_grad, cross_low, cross_heads, *refs,
    ) = refs
    sources, refs = refs[: len(widths)], refs[len(widths) :]
    grad_packed, part_ref, extra_own, text_own, product_ref, *refs = refs
    results, refs = refs[: len(widths)], refs[len(widths) :]
    (
        near_keys, near_values, rim_out, rim_in, halo_send, halo_recv, text_ref, text_low,
        extra_land, extra_stage, text_land, text_stage, *sems,
    ) = refs
    scatters = Scatters(groups, frames_axis, sources, widths, results, sems[8:])
    products = Products(
        [(cross_hidden, cross_grad), (text_rows, text_low), (cross_low, cross_heads)], product_ref
    ).work()
    place, here = lax.axis_index(LINE), lax.axis_index(FRAME)
    patches = grad_ref.shape[0] // frames
    local = out_ref.shape[0]
    share = extra_own.shape[1]
    last = count - 1
    greet_line(place, count, greet_frames(here, frames_axis), scatters.partners() if widths else ())
    fetch(7, *range(16, 16 + len(sources)))
    for item in scatters.items:
        item.start()

    def shares(owner, frame):
        return extra_ref[frame, pl.ds(pl.multiple_of(owner * share, share), share)]

    moving = [
        LineScatter(count, place, frames, shares, extra_land, extra_stage, sems[0:4]),
        LineScatter(count, place, 1, lambda owner, piece: text_ref[owner], text_land, text_stage, sems[4:8]),
    ]
    moving[0].relay_both(last)
    near = (near_keys, near_values)
    def halo(which):
        to = here - 1 if which < 2 else here + 1
        return remote(
            rim_out.at[which], rim_in.at[which], halo_send.at[which], halo_recv.at[which], {FRAME: to}
        )

    has_next, has_previous = here < frames_axis - 1, here > 0

    def frame_rows(frame):
        return slice(frame * patches, (frame + 1) * patches)

    fetch(0, 2, 3, 4, 5, 6)
    columns = head_columns(local)
    seen = set()

    def add(item, cell, terms):
        if (item, cell) in seen:
            near[item][cell] += terms
        else:
            near[item][cell] = terms
        seen.add((item, cell))

    for frame in range(frames):
        given = dot(grad_ref[frame_rows(frame)], out_ref[...], 1, 1).astype(NARROW).astype(WIDE)
        asked = query_ref[frame_rows(frame)].astype(WIDE)
        probs = window_probs(
            asked,
            lambda offset: keys_ref[frame + offset].astype(WIDE),
            lambda offset: bias_ref[frame * WIN + offset : frame * WIN + offset + 1],
            columns,
        )
        pulled = [per_head(given * values_ref[frame + offset].astype(WIDE), columns) for offset in range(WIN)]
        shared = sum((probs[i] * pulled[i] for i in range(1, WIN)), probs[0] * pulled[0])
        found = jnp.zeros((patches, local), WIDE)
        for offset in range(WIN):
            scores = HD ** (-0.5) * over_features(probs[offset] * (pulled[offset] - shared), columns)
            found = found + scores * keys_ref[frame + offset].astype(WIDE)
            add(0, frame + offset, scores * asked)
            add(1, frame + offset, over_features(probs[offset], columns) * given)
        grad_packed[frame_rows(frame), 0:local] = found.astype(NARROW)
        if frame == 0:
            for item in scatters.items:
                item.fold_all()
            if last > 1:
                moving[0].relay_both(last - 1)

    for which in range(3):

        @pl.when(has_previous if which < 2 else has_next)
        def _():
            for item in range(2):
                span = slice(item * local, (item + 1) * local)
                rim_out[which, :, span] = near[item][which if which < 2 else frames + 2].astype(NARROW)
            halo(which).start()

    for distance in range(last - 2, 0, -1):
        moving[0].relay_both(distance)
    fetch()
    slots = text_low.shape[0]
    text_parts = jnp.zeros((slots, grad_ref.shape[1]), WIDE)
    for item, (source, factor) in enumerate(((text_keys, HD ** (-0.5)), (text_values, 1.0))):
        low = (factor * collect_heads(source[...], slots)).astype(NARROW)
        text_low[:, item * local : (item + 1) * local] = low
        text_parts = text_parts + dot(low, text_w[item * local : (item + 1) * local], 1, 0)
    text_parts = text_parts.astype(NARROW)
    for owner in range(count):
        text_ref[owner] = text_parts[:, owner * local : (owner + 1) * local]
    moving[1].relay_both(last)
    for i, work in enumerate(products):
        work()
        if last - 1 - i > 0:
            moving[1].relay_both(last - 1 - i)
    for distance in range(last - 1 - len(products), 0, -1):
        moving[1].relay_both(distance)

    for which in range(3):

        @pl.when(has_next if which < 2 else has_previous)
        def _():
            halo(which).wait_recv()
            for item in range(2):
                span = slice(item * local, (item + 1) * local)
                near[item][2 + (frames - 2 + which if which < 2 else 0)] += rim_in[which, :, span].astype(WIDE)

    for frame in range(frames):
        rows = frame_rows(frame)
        parts = dot(grad_packed[rows, 0:local], in_ref[0:local], 1, 0)
        for item in range(2):
            values = near[item][2 + frame].astype(NARROW)
            grad_packed[rows, (1 + item) * local : (2 + item) * local] = values
            parts = parts + dot(values, in_ref[(1 + item) * local : (2 + item) * local], 1, 0)
        part_ref[rows] = parts.astype(NARROW)

    for frame in range(frames):
        extra_own[frame] = moving[0].total(frame)
    text_own[...] = moving[1].total(0).astype(NARROW)
    for item in moving:
        item.settle()
    for which in range(3):

        @pl.when(has_previous if which < 2 else has_next)
        def _():
            halo(which).wait_send()

    scatters.finish()


def call_temporal_backward(
    count, groups, frames_axis, grad, in_w, out_w, bias, query, keys, values, extra, text_keys, text_values, text_w,
    text_rows, cross_pairs, sources, widths,
):
    tokens, features = grad.shape
    frames, patches = extra.shape[:2]
    local = out_w.shape[0]
    share = patches // count
    slots = text_rows.shape[0]

    def narrow(*shape):
        return jax.ShapeDtypeStruct(shape, NARROW)

    results = (
        [narrow(tokens, 3 * local)]
        + [narrow(tokens, features), jax.ShapeDtypeStruct((frames, share, features), WIDE)]
        + [narrow(slots, local), narrow(features, 4 * local)]
    )
    found, scratch = Scatters.shapes(groups, frames_axis, features, widths)
    results = results + found
    return fetching_call(
        functools.partial(temporal_backward_kernel, count, groups, frames_axis, frames, widths),
        [grad, in_w, out_w, bias, query, keys, values, extra, text_keys, text_values, text_w, text_rows,
        *cross_pairs, *sources,],
        tuple(results),
        [pltpu.VMEM((frames + 3, patches, local), WIDE)] * 2
        + [pltpu.VMEM((3, patches, 2 * local), NARROW)] * 2
        + [pltpu.SemaphoreType.DMA((3,))] * 2
        + [pltpu.VMEM((count, slots, local), NARROW), pltpu.VMEM((slots, 2 * local), NARROW)]
        + [pltpu.VMEM((2, count, frames, share, features), NARROW)] * 2
        + [pltpu.VMEM((2, count, 1, slots, local), NARROW)] * 2
        + scatter_sems(count, frames)
        + scatter_sems(count, 1)
        + scratch,
        9,
        "temporal_backward",
    )


def attend_forward(query, keys, values):
    scores = HD ** (-0.5) * jnp.einsum("fphe,fqhe->fhpq", query, keys, preferred_element_type=WIDE)
    shifted = jnp.exp(scores - jnp.max(scores, axis=-1, keepdims=True))
    probs_low = (shifted / jnp.sum(shifted, axis=-1, keepdims=True)).astype(NARROW)
    heads_out = jnp.einsum("fhpq,fqhe->fphe", probs_low, values, preferred_element_type=WIDE)
    return heads_out.astype(NARROW)


def sum_matrix_grads(pieces):
    if not pieces:
        return []
    packed = jnp.concatenate([piece.astype(NARROW) for piece in pieces], axis=1)
    summed = lax.psum_scatter(packed, BOTH, scatter_dimension=0, tiled=True).astype(WIDE)
    found, start = [], 0
    for piece in pieces:
        found.append(summed[:, start : start + piece.shape[1]])
        start += piece.shape[1]
    return found


def per_device(
    latent, captions, bucket, clip_ids, window_mask, text_counts, time_table, ada_weight,
    spatial_inproj, spatial_outproj, temporal_inproj, temporal_outproj, caption_proj, cross_gain,
    cross_query, cross_keyval, cross_outproj, mlp_up, mlp_down, cotangent,
):
    count, groups, frames_axis = (lax.axis_size(axis) for axis in (LINE, GROUP, FRAME))
    place = lax.axis_index(LINE)
    frames, share, features = latent.shape[1:]
    patches = share * count
    tokens = frames * patches
    local = spatial_outproj.shape[0]
    clip_count, text_length, text_width = captions.shape[1:]
    slots = clip_count * text_length

    def flat(values):
        return values.reshape(tokens, -1)

    def grid(values):
        return values.reshape(frames, patches, -1)

    def heads(values):
        return split_heads(grid(values))

    def own(values):
        return lax.dynamic_slice_in_dim(grid(values), place * share, share, axis=1)

    spatial_in, temporal_in, keyval_in = (
        jnp.transpose(w, (1, 2, 0)).reshape(-1, features)
        for w in (spatial_inproj, temporal_inproj, cross_keyval)
    )
    query_in = cross_query.T

    chosen = (jnp.arange(time_table.shape[0]) == bucket[0]).astype(WIDE)
    cond_row = jnp.sum(chosen[:, None] * time_table.astype(WIDE), axis=0)
    act_low = swish_act(cond_row).astype(NARROW)
    caption_here = captions[0].reshape(slots, text_width)
    base_grid, normed_grid, mods, text_part, caption_share = call_opening(
        count, groups, frames_axis, latent[0], jnp.broadcast_to(act_low[None], (16, local)),
        jnp.transpose(ada_weight, (1, 0, 2)), caption_here, caption_proj.T,
    )
    base_zero, spatial_hidden = flat(base_grid), flat(normed_grid)

    def rows_of(*rows):
        filled = [jnp.zeros((features,), WIDE)] * (8 - len(rows))
        return jnp.stack(list(rows) + filled)

    spatial_packed = dot(spatial_hidden, spatial_in, 1, 1).astype(NARROW)
    spatial_query, spatial_keys, spatial_values = (
        heads(spatial_packed[:, i * local : (i + 1) * local]) for i in range(3)
    )
    spatial_heads = attend_forward(spatial_query, spatial_keys, spatial_values)
    spatial_flat = flat(spatial_heads)
    spatial_out, base_one, temporal_hidden = call_forward(
        count,
        dot(spatial_flat, spatial_outproj, 1, 0).astype(NARROW),
        base_zero,
        rows_of(mods[2], 1.0 + mods[4], mods[3]),
    )

    first_frame = lax.axis_index(FRAME) * frames
    clip_near = lax.dynamic_slice_in_dim(
        jnp.pad(clip_ids[0], (2, 2), constant_values=-1), first_frame, frames + 4
    )
    own_clip = clip_near[2 : 2 + frames]
    allowed = jnp.stack(
        [
            (clip_near[offset : offset + frames] == own_clip)
            & ((window_mask[0][:, offset] == 1) | (offset == 2))
            for offset in range(WIN)
        ],
        axis=1,
    )
    window_bias = jnp.broadcast_to(jnp.where(allowed, 0.0, NEGATIVE).reshape(-1, 1), (frames * WIN, 128))
    (
        temporal_query, temporal_keys, temporal_values, temporal_flat, temporal_part, cotangent_full, text_full,
    ) = call_temporal_forward(
        count, frames_axis, temporal_hidden, temporal_in, temporal_outproj, window_bias, cotangent[0], text_part
    )
    cotangent_full = flat(cotangent_full)

    slot_pad = -slots % 128
    slot_index = jnp.arange(slots)
    key_valid = (own_clip[:, None] == (slot_index // text_length)[None, :]) & (
        slot_index % text_length < jnp.repeat(text_counts[0], text_length)
    )[None, :]
    bias = jnp.pad(jnp.where(key_valid, 0.0, NEGATIVE), ((0, 0), (0, slot_pad)), constant_values=NEGATIVE)
    bias = jnp.broadcast_to(bias[:, None], (frames, 8, slots + slot_pad))
    (
        base_three, grad_two, grad_temporal_low, grad_cross_low, cross_hidden, cross_flat, grad_cross_packed,
        text_grad_keys, text_grad_values, sums_middle, mlp_part, text_rows, grad_down, grad_up,
    ) = call_middle(
        count, groups, frames_axis, frames, temporal_part, base_one, cotangent_full,
        rows_of(mods[5], cross_gain.astype(WIDE), 1.0 + mods[7], mods[6], mods[8]), bias,
        text_full, keyval_in, query_in, cross_outproj, mlp_up, mlp_down,
    )

    def outside(packed, widths):
        return sum_matrix_grads(
            [
                item[:, sum(columns[:i]) : sum(columns[: i + 1])]
                for item, columns in zip(packed, widths)
                for i in range(len(columns))
            ]
        )

    if not can_scatter(groups, frames_axis, features):
        (grad_up,) = outside([grad_up], [[grad_up.shape[1]]])

    inside = can_scatter(groups, frames_axis, features)
    down_widths = [[grad_down.shape[1]]]
    grad_temporal_packed, temporal_grad_part, mlp_out, text_grad, grad_cross, *found = call_temporal_backward(
        count, groups, frames_axis, grad_temporal_low, temporal_in, temporal_outproj, window_bias,
        temporal_query, temporal_keys, temporal_values, grid(mlp_part), text_grad_keys, text_grad_values,
        keyval_in, text_rows, [cross_hidden, grad_cross_packed, grad_cross_low, cross_flat],
        [grad_down] if inside else [], down_widths if inside else [],
    )
    (grad_down,) = found if inside else outside([grad_down], down_widths)
    output = (own(base_three) + mods[8] * mlp_out).astype(NARROW)[None]
    gate_mlp_part = jnp.sum(cotangent[0].astype(WIDE) * mlp_out, axis=(0, 1))
    cross_widths, qkv_widths = [local, 2 * local, local], [3 * local, local]
    grad_one, grad_spatial_low, sums_temporal, *found = call_backward(
        count, groups, frames_axis, temporal_grad_part, base_one, grad_two, spatial_out,
        rows_of(1.0 + mods[4], mods[2]),
        [(temporal_hidden, grad_temporal_packed), (grad_temporal_low, temporal_flat)],
        [grad_cross] if inside else [], [cross_widths, qkv_widths] if inside else [],
    )
    if not inside:
        found = outside([grad_cross, found[0]], [cross_widths, qkv_widths])
    (
        grad_query_cross, grad_keyval_cross, grad_outproj_cross, grad_inproj_temporal, grad_outproj_temporal,
    ) = found

    side_row = jnp.pad(jnp.concatenate([cond_row, chosen]), (0, features - local - chosen.shape[0]))
    blank = jnp.zeros((features,), WIDE)
    small = jnp.stack(
        [blank, blank, gate_mlp_part]
        + [blank] * 5
        + [
            sums_temporal[2], sums_temporal[0], sums_temporal[1], sums_middle[3], sums_middle[0],
            sums_middle[1], sums_middle[2], side_row,
        ]
    )
    grad_latent, small_all, text_grad_all, *found = call_closing(
        count, groups, frames_axis, grad_spatial_low, grid(base_zero), grid(grad_one), small,
        rows_of(1.0 + mods[1]), spatial_packed, spatial_flat, spatial_hidden, spatial_in, spatial_outproj,
        text_grad, [], [qkv_widths] if inside else [],
    )
    if not inside:
        found = outside([found[0]], [qkv_widths])
    grad_inproj_spatial, grad_outproj_spatial = found

    grad_ada, grad_table, grad_gain, grad_caption, *found = call_finishing(
        groups, frames_axis, chosen.shape[0], (0, 1, 8, 9, 10, 11, 12, 13, 2), (0, 1, 0, 1, 0, 0, 2, 0, 0, 0),
        small_all, jnp.transpose(ada_weight, (1, 0, 2)), text_grad_all, caption_share,
        [
            grad_latent.reshape(frames * share, features), grad_inproj_spatial, grad_outproj_spatial,
            grad_inproj_temporal, grad_outproj_temporal, grad_query_cross, grad_keyval_cross,
            grad_outproj_cross, grad_up, grad_down,
        ],
    )
    (
        grad_latent, grad_inproj_spatial, grad_outproj_spatial, grad_inproj_temporal, grad_outproj_temporal,
        grad_query_cross, grad_keyval_cross, grad_outproj_cross, grad_up, grad_down,
    ) = found
    return (
        output,
        grad_latent.reshape(1, frames, share, features),
        grad_table,
        jnp.transpose(grad_ada, (2, 0, 1)),
        jnp.transpose(grad_inproj_spatial, (1, 0, 2)),
        grad_outproj_spatial.T,
        jnp.transpose(grad_inproj_temporal, (1, 0, 2)),
        grad_outproj_temporal.T,
        grad_caption.T,
        grad_gain[0],
        grad_query_cross,
        grad_keyval_cross,
        grad_outproj_cross.T,
        grad_up,
        grad_down.T,
    )


def solution(mesh):
    tokens = P(GROUP, FRAME, LINE, None)
    packed_in, rows_in, columns_in = P(None, None, LINE), P(LINE, None), P(None, LINE)
    in_specs = (
        tokens, P(GROUP, None, None, None), P(GROUP), P(GROUP, None), P(GROUP, FRAME, None),
        P(GROUP, None), columns_in, P(LINE, None, None), packed_in, rows_in, packed_in, rows_in,
        columns_in, P(), columns_in, packed_in, rows_in, columns_in, rows_in, tokens,
    )
    packed_out, rows_out, columns_out = P(BOTH, None, LINE), P(LINE, BOTH), P(BOTH, LINE)
    out_specs = (
        tokens, tokens, columns_in, P(LINE, None, BOTH), packed_out, rows_out, packed_out, rows_out,
        columns_out, P(), columns_out, packed_out, rows_out, columns_out, rows_out,
    )
    return jax.shard_map(
        per_device, mesh=mesh, in_specs=in_specs, out_specs=out_specs, check_vma=False
    )
```

```python
import functools

import jax
import jax.numpy as jnp
from jax import lax
from jax.experimental import pallas as pl
from jax.experimental.pallas import tpu as pltpu
from jax.sharding import PartitionSpec as P

HD = 72
WIN = 4
EPSILON = 1e-06
HIGHEST = lax.Precision.HIGHEST
NEGATIVE = -1e30
WIDE = jnp.float32
NARROW = jnp.bfloat16
GROUP, FRAME, LINE = "group", "frame", "tensor"
BOTH = (GROUP, FRAME)
MESH = pl.DeviceIdType.MESH
CHUNKS = 16
LAG = 2
VMEM_LIMIT = 48 * 2**20


def swish_act(values):
    return values / (1.0 + jnp.exp(-values))


def gelu_tanh(values):
    return (
        0.5
        * values
        * (1.0 + jnp.tanh(0.7978845608028654 * (values + 0.044715 * values * values * values)))
    )


def dot(first, second, contract_first, contract_second):
    return lax.dot_general(
        first, second, (((contract_first,), (contract_second,)), ((), ())), preferred_element_type=WIDE
    )


def split_pair(values):
    high_part = values.astype(NARROW)
    rest_part = (values - high_part.astype(WIDE)).astype(NARROW)
    return (high_part, rest_part)


def norm_parts(values):
    centred = values - jnp.mean(values, axis=-1, keepdims=True)
    spread = lax.rsqrt(jnp.mean(centred * centred, axis=-1, keepdims=True) + EPSILON)
    return centred * spread, spread


def norm_pull(scaled, normal, spread):
    return spread * (
        scaled
        - jnp.mean(scaled, axis=-1, keepdims=True)
        - normal * jnp.mean(scaled * normal, axis=-1, keepdims=True)
    )


def remote(source, target, send_sem, recv_sem, where):
    return pltpu.make_async_remote_copy(
        src_ref=source,
        dst_ref=target,
        send_sem=send_sem,
        recv_sem=recv_sem,
        device_id=where,
        device_id_type=MESH,
    )


def greet_line(place, count, more=0, others=()):
    barrier = pltpu.get_barrier_semaphore()
    for where in others:
        pl.semaphore_signal(barrier, inc=1, device_id=where, device_id_type=MESH)

    @pl.when(place > 0)
    def _():
        pl.semaphore_signal(barrier, inc=1, device_id={LINE: place - 1}, device_id_type=MESH)

    @pl.when(place < count - 1)
    def _():
        pl.semaphore_signal(barrier, inc=1, device_id={LINE: place + 1}, device_id_type=MESH)

    pl.semaphore_wait(
        barrier, (place > 0).astype(jnp.int32) + (place < count - 1).astype(jnp.int32) + len(others) + more
    )


class Scatter:
    def __init__(self, groups, frames_axis, source, scratch):
        self.source = source
        self.inbox, self.stage, self.found, self.kept = scratch[:4]
        self.twin_send, self.twin_recv, self.peer_send, self.peer_recv = scratch[4:8]
        self.groups, self.frames_axis = groups, frames_axis
        self.block = source.shape[0] // (groups * frames_axis)
        self.total = groups // 2 * frames_axis
        group = lax.axis_index(GROUP)
        self.core = lax.rem(group, 2)
        self.me = lax.div(group, 2) * frames_axis + lax.axis_index(FRAME)
        self.twin = {GROUP: group + 1 - 2 * self.core}

    def peer(self, step):
        to = lax.rem(self.me + step, self.total)
        return to, {GROUP: lax.div(to, self.frames_axis) * 2 + self.core, FRAME: lax.rem(to, self.frames_axis)}

    def partners(self):
        return [self.twin] + [self.peer(step)[1] for step in range(1, self.total)]

    def twin_copy(self, high):
        rows = self.block * self.frames_axis
        first = pl.multiple_of((high * 2 + 1 - self.core) * rows, 16)
        return remote(
            self.source.at[pl.ds(first, rows)],
            self.inbox.at[pl.ds(high * rows, rows)],
            self.twin_send.at[high],
            self.twin_recv.at[high],
            self.twin,
        )

    def peer_copy(self, step):
        return remote(
            self.stage.at[step - 1],
            self.found.at[step - 1],
            self.peer_send.at[step],
            self.peer_recv.at[step],
            self.peer(step)[1],
        )

    def start(self):
        for high in range(self.groups // 2):
            self.twin_copy(high).start()

    def fold(self, step):
        if step == self.total - 1:
            for high in range(self.groups // 2):
                self.twin_copy(high).wait_recv()
        to = self.peer(step)[0]
        high, frame = lax.div(to, self.frames_axis), lax.rem(to, self.frames_axis)
        first = ((high * 2 + self.core) * self.frames_axis + frame) * self.block
        mine = self.source[pl.ds(pl.multiple_of(first, 16), self.block)]
        other = self.inbox[pl.ds(pl.multiple_of(to * self.block, 16), self.block)]
        summed = mine.astype(WIDE) + other.astype(WIDE)
        if step == 0:
            self.kept[...] = summed
        else:
            self.stage[step - 1] = summed.astype(NARROW)
            self.peer_copy(step).start()

    def fold_all(self):
        for step in range(self.total - 1, -1, -1):
            self.fold(step)

    def finish(self, results):
        for step in range(1, self.total):
            self.peer_copy(step).wait_recv()
        start = 0
        for result in results:
            span = slice(start, start + result.shape[1])
            summed = self.kept[:, span]
            for step in range(1, self.total):
                summed = summed + self.found[step - 1, :, span].astype(WIDE)
            result[...] = summed
            start += result.shape[1]
        for high in range(self.groups // 2):
            self.twin_copy(high).wait_send()
        for step in range(1, self.total):
            self.peer_copy(step).wait_send()

    @staticmethod
    def scratch(groups, frames_axis, width, columns):
        total, block = groups // 2 * frames_axis, width // (groups * frames_axis)
        dma = pltpu.SemaphoreType.DMA
        return (
            [pltpu.VMEM((width // 2, columns), NARROW)]
            + [pltpu.VMEM((total - 1, block, columns), NARROW)] * 2
            + [pltpu.VMEM((block, columns), WIDE)]
            + [dma((groups // 2,))] * 2
            + [dma((total,))] * 2
        )


def can_scatter(groups, frames_axis, width):
    return groups % 2 == 0 and width % (16 * groups * frames_axis) == 0


class Products:
    def __init__(self, pairs, result):
        self.pairs, self.result = pairs, result

    def product(self, i):
        first, second, *side = self.pairs[i]
        found = dot(first[...], second[...], *(side or (0, 0))).astype(NARROW)
        start = sum(pair[1].shape[1 if len(pair) == 2 else 0] for pair in self.pairs[:i])
        self.result[:, start : start + found.shape[1]] = found

    def work(self):
        return [functools.partial(self.product, i) for i in range(len(self.pairs))]


class Scatters:
    def __init__(self, groups, frames_axis, sources, widths, results, scratch):
        self.items, self.results = [], []
        for i, source in enumerate(sources):
            self.items.append(Scatter(groups, frames_axis, source, scratch[8 * i : 8 * i + 8]))
            self.results.append(results[: len(widths[i])])
            results = results[len(widths[i]) :]

    def partners(self):
        return self.items[0].partners()

    def folds(self, i):
        item = self.items[i]
        return [functools.partial(item.fold, item.total - 1 - step) for step in range(item.total)]

    def finish(self):
        for item, results in zip(self.items, self.results):
            item.finish(results)

    @staticmethod
    def shapes(groups, frames_axis, features, widths):
        block = features // (groups * frames_axis)
        results = [jax.ShapeDtypeStruct((block, n), WIDE) for columns in widths for n in columns]
        scratch = [Scatter.scratch(groups, frames_axis, features, sum(columns)) for columns in widths]
        return results, sum(scratch, [])


class GroupExchange:
    def __init__(self, groups, frames_axis, source, every, scratch):
        self.groups, self.frames_axis = groups, frames_axis
        self.source, self.every = source, every
        self.near, self.frame_send, self.frame_recv, self.group_send, self.group_recv = scratch
        self.group, self.frame = lax.axis_index(GROUP), lax.axis_index(FRAME)

    def frame_copy(self, step):
        return remote(
            self.source,
            self.near.at[step - 1],
            self.frame_send.at[step],
            self.frame_recv.at[step],
            {FRAME: lax.rem(self.frame + step, self.frames_axis)},
        )

    def group_copy(self, step):
        own = self.every.at[self.group]
        return remote(
            own,
            own,
            self.group_send.at[step],
            self.group_recv.at[step],
            {GROUP: lax.rem(self.group + step, self.groups)},
        )

    def partners(self):
        return [
            {FRAME: lax.rem(self.frame + step, self.frames_axis)} for step in range(1, self.frames_axis)
        ] + [{GROUP: lax.rem(self.group + step, self.groups)} for step in range(1, self.groups)]

    def start(self):
        for step in range(1, self.frames_axis):
            self.frame_copy(step).start()

    def spread(self):
        for step in range(1, self.frames_axis):
            self.frame_copy(step).wait_recv()
        summed = self.source[...].astype(WIDE)
        for step in range(1, self.frames_axis):
            summed = summed + self.near[step - 1].astype(WIDE)
        self.every[self.group] = summed.astype(NARROW)
        for step in range(1, self.groups):
            self.group_copy(step).start()

    def finish(self):
        for step in range(1, self.frames_axis):
            self.frame_copy(step).wait_send()
        for step in range(1, self.groups):
            self.group_copy(step).wait_recv()
            self.group_copy(step).wait_send()

    @staticmethod
    def scratch(groups, frames_axis, shape):
        dma = pltpu.SemaphoreType.DMA
        return (
            [pltpu.VMEM((max(frames_axis - 1, 1),) + shape, NARROW)]
            + [dma((frames_axis,))] * 2
            + [dma((groups,))] * 2
        )


def grad_tile(first, second, result, start, size):
    result[start : start + size] = dot(first[:, start : start + size], second[...], 0, 0).astype(NARROW)


def can_scatter(groups, frames_axis, width):
    return groups % 2 == 0 and width % (16 * groups * frames_axis) == 0


def vmem(count):
    return [pl.BlockSpec(memory_space=pltpu.VMEM)] * count


class Fetch:
    def __init__(self, sources, held, sems):
        self.copies = [
            pltpu.make_async_copy(source, target, sems.at[i]) for i, (source, target) in enumerate(zip(sources, held))
        ]
        self.waiting = list(range(len(self.copies)))
        for copy in self.copies:
            copy.start()

    def __call__(self, *which):
        for i in which or tuple(self.waiting):
            self.copies[i].wait()
            self.waiting.remove(i)

    def again(self, *which):
        for i in which:
            self.copies[i].wait()


def fetching_call(kernel, operands, out_shape, scratch_shapes, kernel_id, name):
    many = len(operands)

    def body(*refs):
        sources, rest = refs[:many], refs[many : -many - 1]
        held, sems = refs[-many - 1 : -1], refs[-1]
        kernel(Fetch(sources, held, sems), *held, *rest)

    return pl.pallas_call(
        body,
        out_shape=tuple(out_shape),
        in_specs=[pl.BlockSpec(memory_space=pl.ANY)] * many,
        out_specs=tuple(vmem(len(out_shape))),
        scratch_shapes=list(scratch_shapes)
        + [pltpu.VMEM(item.shape, item.dtype) for item in operands]
        + [pltpu.SemaphoreType.DMA((many,))],
        compiler_params=pltpu.CompilerParams(
            collective_id=kernel_id, has_side_effects=True, vmem_limit_bytes=62 * 2**20
        ),
        name=name,
    )(*operands)


class LineGather:
    def __init__(self, count, place, slot_of, sems):
        self.count, self.place, self.last, self.slot_of = count, place, count - 1, slot_of
        self.up_send, self.down_send, self.arrived = sems

    def shift(self, owner, up):
        slot = self.slot_of(owner)
        to = self.place + 1 if up else self.place - 1
        sent = (self.up_send if up else self.down_send).at[owner]
        return remote(slot, slot, sent, self.arrived.at[owner], {LINE: to})

    def start(self):
        @pl.when(self.place < self.last)
        def _():
            self.shift(self.place, True).start()

        @pl.when(self.place > 0)
        def _():
            self.shift(self.place, False).start()

    def arrive(self, distance):
        @pl.when(self.place >= distance)
        def _():
            self.shift(self.place - distance, True).wait_recv()

            @pl.when(self.place < self.last)
            def _():
                self.shift(self.place - distance, True).start()

        @pl.when(self.place + distance <= self.last)
        def _():
            self.shift(self.place + distance, False).wait_recv()

            @pl.when(self.place > 0)
            def _():
                self.shift(self.place + distance, False).start()

    def settle(self):
        for owner in range(self.count):

            @pl.when((self.place < self.last) & (owner <= self.place))
            def _():
                self.shift(owner, True).wait_send()

            @pl.when((self.place > 0) & (owner >= self.place))
            def _():
                self.shift(owner, False).wait_send()


class LineScatter:
    def __init__(self, count, place, pieces, value_of, land, stage, sems):
        self.count, self.place, self.last, self.pieces = count, place, count - 1, pieces
        self.value_of, self.land, self.stage = value_of, land, stage
        self.from_left, self.from_right, self.to_left, self.to_right = sems

    def pass_on(self, owner, piece, right):
        side = 0 if right else 1
        return remote(
            self.stage.at[side, owner, piece],
            self.land.at[side, owner, piece],
            (self.to_right if right else self.to_left).at[owner, piece],
            (self.from_left if right else self.from_right).at[owner, piece],
            {LINE: self.place + 1 if right else self.place - 1},
        )

    def relay(self, distance, right, chosen=None):
        owner = self.place + distance if right else self.place - distance
        source = (self.place == 0) if right else (self.place == self.last)
        side = 0 if right else 1

        @pl.when((owner <= self.last) if right else (owner >= 0))
        def _():
            for piece in chosen if chosen is not None else range(self.pieces):

                @pl.when(source)
                def _():
                    self.stage[side, owner, piece] = self.value_of(owner, piece)

                @pl.when(jnp.logical_not(source))
                def _():
                    self.pass_on(owner, piece, right).wait_recv()
                    self.stage[side, owner, piece] = (
                        self.value_of(owner, piece).astype(WIDE) + self.land[side, owner, piece].astype(WIDE)
                    ).astype(NARROW)

                self.pass_on(owner, piece, right).start()

    def relay_both(self, distance, chosen=None):
        self.relay(distance, True, chosen)
        self.relay(distance, False, chosen)

    def total(self, piece):
        place = self.place

        @pl.when(place > 0)
        def _():
            self.pass_on(place, piece, True).wait_recv()

        @pl.when(place < self.last)
        def _():
            self.pass_on(place, piece, False).wait_recv()

        left_part = jnp.where(place > 0, self.land[0, place, piece].astype(WIDE), 0.0)
        right_part = jnp.where(place < self.last, self.land[1, place, piece].astype(WIDE), 0.0)
        return self.value_of(place, piece).astype(WIDE) + left_part + right_part

    def settle(self):
        for owner in range(self.count):
            for piece in range(self.pieces):

                @pl.when(owner > self.place)
                def _():
                    self.pass_on(owner, piece, True).wait_send()

                @pl.when(owner < self.place)
                def _():
                    self.pass_on(owner, piece, False).wait_send()


def gather_sems(count):
    return [pltpu.SemaphoreType.DMA((count,))] * 3


def scatter_sems(count, pieces):
    return [pltpu.SemaphoreType.DMA((count, pieces))] * 4


def line_sum(count, place, part_ref, land, cross, stage, total, sems, consume, early=(), folds=(), make=None, pieces=1):
    in_send, land_recv, cross_recv, out_send, out_recv = sems
    depth = part_ref.shape[0] // CHUNKS
    half = count // 2
    left = place < half
    level = jnp.where(left, place, count - 1 - place)
    inner = jnp.where(left, place + 1, place - 1)
    outer = jnp.where(left, place - 1, place + 1)
    is_end, is_middle = level == 0, level == half - 1

    def rows_of(chunk):
        return pl.ds(pl.multiple_of(chunk * depth, depth), depth)

    def inward(chunk):
        rows = rows_of(chunk)
        return remote(stage.at[rows], land.at[rows], in_send.at[chunk], land_recv.at[chunk], {LINE: inner})

    def across(chunk):
        rows = rows_of(chunk)
        return remote(stage.at[rows], cross.at[rows], in_send.at[chunk], cross_recv.at[chunk], {LINE: inner})

    def outward(chunk):
        rows = rows_of(chunk)
        return remote(total.at[rows], total.at[rows], out_send.at[chunk], out_recv.at[chunk], {LINE: outer})

    def send_in(chunk):
        @pl.when(is_middle)
        def _():
            across(chunk).start()

        @pl.when(jnp.logical_not(is_middle))
        def _():
            inward(chunk).start()

    def gather_in(chunk):
        rows = rows_of(chunk)
        inward(chunk).wait_recv()
        stage[rows] = (part_ref[rows].astype(WIDE) + land[rows].astype(WIDE)).astype(NARROW)
        send_in(chunk)

    def finish(chunk):
        rows = rows_of(chunk)

        @pl.when(is_middle)
        def _():
            across(chunk).wait_recv()
            total[rows] = (stage[rows].astype(WIDE) + cross[rows].astype(WIDE)).astype(NARROW)

        @pl.when(jnp.logical_not(is_middle))
        def _():
            outward(chunk).wait_recv()

        @pl.when(jnp.logical_not(is_end))
        def _():
            outward(chunk).start()

        consume(rows)

    def begin(chunk, carry):
        rows = rows_of(chunk)
        stage[rows] = part_ref[rows]
        send_in(chunk)
        return carry

    def step(number, carry):
        for i, work in enumerate(early):

            @pl.when(jnp.logical_not(is_end) & (number == i))
            def _():
                work()

        @pl.when(jnp.logical_not(is_end) & (number < CHUNKS))
        def _():
            gather_in(number)

        @pl.when(number >= LAG)
        def _():
            finish(number - LAG)

        for i, work in enumerate(folds):

            @pl.when(number == len(early) + 1 + i)
            def _():
                work()

        return carry

    for piece in range(pieces):
        if make is not None:
            make(piece)

        @pl.when(is_end)
        def _():
            lax.fori_loop(piece * CHUNKS // pieces, (piece + 1) * CHUNKS // pieces, begin, 0)

    @pl.when(is_end)
    def _():
        for work in early:
            work()

    lax.fori_loop(0, CHUNKS + LAG, step, 0)

    def settle(chunk, carry):
        @pl.when(is_middle)
        def _():
            across(chunk).wait_send()

        @pl.when(jnp.logical_not(is_middle))
        def _():
            inward(chunk).wait_send()

        @pl.when(jnp.logical_not(is_end))
        def _():
            outward(chunk).wait_send()

        return carry

    lax.fori_loop(0, CHUNKS, settle, 0)


def forward_kernel(
    count, frames, fetch, hidden_ref, in_ref, base_ref, rows_ref, outproj_ref,
    out_ref, next_ref, normed_ref, packed_ref, heads_ref,
    part_ref, key_rows, value_rows, probs_low, land, cross, stage, *sems
):
    place = lax.axis_index(LINE)
    greet_line(place, count)
    fetch(0, 1, 4)
    patches = hidden_ref.shape[0] // frames
    local = heads_ref.shape[1]

    def make(frame):
        rows = slice(frame * patches, (frame + 1) * patches)
        packed = dot(hidden_ref[rows], in_ref[...], 1, 1).astype(NARROW)
        packed_ref[rows] = packed
        asked, keys, values = (packed[:, i * local : (i + 1) * local] for i in range(3))
        spread_heads(keys, key_rows)
        spread_heads(values, value_rows)
        for head in range(local // HD):
            spot = slice(head * patches, (head + 1) * patches)
            scores = HD ** (-0.5) * dot(asked, key_rows[spot], 1, 1)
            raised = jnp.exp(scores - jnp.max(scores, axis=-1, keepdims=True))
            probs_low[:, spot] = (raised * (1.0 / jnp.sum(raised, axis=-1, keepdims=True))).astype(NARROW)
        found = dot(probs_low[...], value_rows[...], 1, 0).astype(NARROW)
        heads_ref[rows] = found
        part_ref[rows] = dot(found, outproj_ref[...], 1, 0).astype(NARROW)
        if frame == frames - 1:
            fetch()

    def consume(rows):
        gate, gain, shift = (rows_ref[i : i + 1] for i in (2, 10, 3))
        moved = base_ref[rows] + gate * out_ref[rows].astype(WIDE)
        next_ref[rows] = moved
        normed_ref[rows] = (norm_parts(moved)[0] * gain + shift).astype(NARROW)

    line_sum(count, place, part_ref, land, cross, stage, out_ref, sems, consume, make=make, pieces=frames)


def backward_kernel(count, groups, frames_axis, widths, fetch, *refs):
    part_ref, base_ref, grad_ref, below_ref, rows_ref, *refs = refs
    pairs, refs = [refs[0:2], refs[2:4]], refs[4:]
    sources, refs = refs[: len(widths) - 1], refs[max(len(widths) - 1, 0) :]
    moved_ref, low_ref, sums_ref, *refs = refs
    many = sum(len(columns) for columns in widths)
    results, refs = refs[:many], refs[many:]
    product_ref, total, land, cross, stage, tally, *refs = refs
    sems, scratch = refs[:5], refs[5:]
    place = lax.axis_index(LINE)
    early = Products(pairs, product_ref).work()
    scatters = Scatters(
        groups, frames_axis, [*sources, product_ref] if widths else [], widths, results, scratch
    )
    greet_line(place, count, 0, scatters.partners() if widths else ())
    fetch()
    folds = []
    if widths:
        scatters.items[0].start()
        early = scatters.folds(0) + early + [scatters.items[-1].start]
        folds = scatters.folds(len(widths) - 1)
    gain, gate = (rows_ref[i : i + 1] for i in (10, 2))
    tally[...] = jnp.zeros_like(tally)

    def consume(rows):
        grads = total[rows].astype(WIDE)
        normal, spread = norm_parts(base_ref[rows])
        moved = grad_ref[rows] + norm_pull(grads * gain, normal, spread)
        moved_ref[rows] = moved
        low_ref[rows] = (gate * moved).astype(NARROW)
        for i, terms in enumerate((grads, grads * normal, moved * below_ref[rows].astype(WIDE))):
            tally[i] += jnp.sum(terms.reshape(-1, 8, terms.shape[-1]), axis=0)

    line_sum(count, place, part_ref, land, cross, stage, total, sems, consume, early, folds)
    sums_ref[...] = jnp.zeros_like(sums_ref)
    for i in range(3):
        sums_ref[i : i + 1] = jnp.sum(tally[i], axis=0, keepdims=True)
    scatters.finish()


def line_sems():
    return [pltpu.SemaphoreType.DMA((CHUNKS,))] * 5


def call_forward(count, frames, hidden, in_w, base, rows, out_w):
    shape, local = hidden.shape, out_w.shape[0]
    patches = shape[0] // frames
    wide_keys = local // HD * patches
    return fetching_call(
        functools.partial(forward_kernel, count, frames),
        [hidden, in_w, base, rows, out_w],
        (
            jax.ShapeDtypeStruct(shape, NARROW),
            jax.ShapeDtypeStruct(shape, WIDE),
            jax.ShapeDtypeStruct(shape, NARROW),
            jax.ShapeDtypeStruct((shape[0], 3 * local), NARROW),
            jax.ShapeDtypeStruct((shape[0], local), NARROW),
        ),
        [
            pltpu.VMEM(shape, NARROW),
            pltpu.VMEM((wide_keys, local), NARROW),
            pltpu.VMEM((wide_keys, local), NARROW),
            pltpu.VMEM((patches, wide_keys), NARROW),
        ]
        + [pltpu.VMEM(shape, NARROW)] * 3
        + line_sems(),
        1,
        "forward_sum",
    )


def call_backward(count, groups, frames_axis, part, base, grad, below, rows, pairs, sources, widths):
    shape = part.shape
    results, scratch = Scatters.shapes(groups, frames_axis, shape[1], widths)
    product = (shape[1], sum(second.shape[1] for _, second in pairs))
    if not widths:
        results = [jax.ShapeDtypeStruct(product, NARROW)]
    return fetching_call(
        functools.partial(backward_kernel, count, groups, frames_axis, widths),
        [part, base, grad, below, rows, *(item for pair in pairs for item in pair), *sources],
        (
            jax.ShapeDtypeStruct(shape, WIDE),
            jax.ShapeDtypeStruct(shape, NARROW),
            jax.ShapeDtypeStruct((8, shape[1]), WIDE),
            *results,
        ),
        ([pltpu.VMEM(product, NARROW)] if widths else [])
        + [pltpu.VMEM(shape, NARROW)] * 4
        + [pltpu.VMEM((3, 8, shape[1]), WIDE)]
        + line_sems()
        + scratch,
        2,
        "backward_sum",
    )


def head_mask(head, shape):
    lane = lax.broadcasted_iota(jnp.int32, shape, len(shape) - 1)
    return (lane >= head * HD) & (lane < (head + 1) * HD)


def spread_heads(values, result):
    rows = values.shape[0]
    for head in range(values.shape[1] // HD):
        kept = jnp.where(head_mask(head, values.shape), values.astype(WIDE), 0.0)
        result[head * rows : (head + 1) * rows] = kept.astype(NARROW)


def collect_heads(values, rows):
    found = jnp.zeros((rows, values.shape[1]), WIDE)
    for head in range(values.shape[0] // rows):
        found = jnp.where(head_mask(head, found.shape), values[head * rows : (head + 1) * rows], found)
    return found


def spatial_backward(given, asked, keys, values, key_rows, value_rows, probs_low, scores_low):
    rows, scale = asked.shape[0], HD ** (-0.5)
    heads = asked.shape[1] // HD
    spread_heads(keys, key_rows)
    spread_heads(values, value_rows)
    for head in range(heads):
        spot = slice(head * rows, (head + 1) * rows)
        scores = scale * dot(asked, key_rows[spot], 1, 1)
        raised = jnp.exp(scores - jnp.max(scores, axis=-1, keepdims=True))
        probs = raised * (1.0 / jnp.sum(raised, axis=-1, keepdims=True))
        pulled = dot(given, value_rows[spot], 1, 1)
        moved = probs * (pulled - jnp.sum(pulled * probs, axis=-1, keepdims=True))
        probs_low[:, spot] = probs.astype(NARROW)
        scores_low[:, spot] = moved.astype(NARROW)
    grad_query = scale * dot(scores_low[...], key_rows[...], 1, 0)
    grad_keys = scale * collect_heads(dot(scores_low[...], asked, 0, 0), rows)
    grad_values = collect_heads(dot(probs_low[...], given, 0, 0), rows)
    return grad_query, grad_keys, grad_values


def closing_kernel(count, groups, frames_axis, frames, widths, fetch, *refs):
    (
        low_ref, base_ref, grad_ref, gate_part, rows_ref, packed_ref, heads_ref, hidden_ref, in_ref, out_ref,
        text_ref, sums_temporal, sums_middle, side_ref, *refs,
    ) = refs
    sources, refs = refs[: len(widths) - 1], refs[max(len(widths) - 1, 0) :]
    latent_ref, every_ref, text_all, *refs = refs
    many = sum(len(columns) for columns in widths)
    results, refs = refs[:many], refs[many:]
    (
        product_ref, part_ref, grad_packed, key_rows, value_rows, probs_low, scores_low,
        land, stage, line_rows, own_rows, tally, *refs,
    ) = refs
    line_send, line_recv, all_send, all_recv = refs[4:8]
    place, group, here = (lax.axis_index(axis) for axis in (LINE, GROUP, FRAME))
    last = count - 1
    share = latent_ref.shape[1]
    local = out_ref.shape[0]
    everyone = groups * frames_axis
    rank = group * frames_axis + here
    products = Products([(hidden_ref, grad_packed), (low_ref, heads_ref)], product_ref)
    scatters = Scatters(groups, frames_axis, [*sources, product_ref] if widths else [], widths, results, refs[13:])
    exchange = GroupExchange(groups, frames_axis, text_ref, text_all, refs[8:13])

    def member(ahead):
        to = lax.rem(rank + ahead, everyone)
        return {GROUP: lax.div(to, frames_axis), FRAME: lax.rem(to, frames_axis)}

    def neighbour(ahead):
        return {LINE: lax.rem(place + ahead, count)}

    barrier = pltpu.get_barrier_semaphore()

    def greet(ahead, carry):
        pl.semaphore_signal(barrier, inc=1, device_id=member(ahead), device_id_type=MESH)
        return carry

    for ahead in range(1, count):
        pl.semaphore_signal(barrier, inc=1, device_id=neighbour(ahead), device_id_type=MESH)
    lax.fori_loop(1, everyone, greet, 0)
    pl.semaphore_wait(barrier, last + everyone - 1)
    fetch(0, 5, 8, 9, 10)

    def rows_of(owner):
        return pl.ds(pl.multiple_of(owner * share, share), share)

    passing = LineScatter(
        count, place, frames, lambda owner, frame: part_ref[frame, rows_of(owner)], land, stage, refs[0:4]
    )
    patches = base_ref.shape[1]
    exchange.start()
    for frame in range(frames):
        rows = slice(frame * patches, (frame + 1) * patches)
        given = dot(low_ref[rows], out_ref[...], 1, 1).astype(NARROW)
        asked, keys, values = (packed_ref[rows, i * local : (i + 1) * local] for i in range(3))
        parts = jnp.zeros(part_ref.shape[1:], WIDE)
        found = spatial_backward(given, asked, keys, values, key_rows, value_rows, probs_low, scores_low)
        for i, item in enumerate(found):
            low = item.astype(NARROW)
            grad_packed[rows, i * local : (i + 1) * local] = low
            parts = parts + dot(low, in_ref[i * local : (i + 1) * local], 1, 0)
        part_ref[frame] = parts.astype(NARROW)
        passing.relay_both(last, (frame,))
        if frame == 0:
            exchange.spread()
    if last > 1:
        passing.relay_both(last - 1, (0,))
    fetch()
    for work in products.work():
        work()
    if widths:
        scatters.items[-1].start()
    if last > 1:
        passing.relay_both(last - 1, tuple(range(1, frames)))

    tally[...] = jnp.zeros_like(tally)
    depth = 32
    blocks = base_ref.shape[1] // depth

    def add_rows(number, carry):
        frame, rows = lax.div(number, blocks), pl.ds(pl.multiple_of(lax.rem(number, blocks) * depth, depth), depth)
        normal = norm_parts(base_ref[frame, rows])[0]
        grads = part_ref[frame, rows].astype(WIDE)
        for i, terms in enumerate((grads, grads * normal)):
            tally[i] += jnp.sum(terms.reshape(-1, 8, terms.shape[-1]), axis=0)
        return carry

    lax.fori_loop(0, frames * blocks, add_rows, 0)
    line_rows[place] = jnp.zeros(line_rows.shape[1:], WIDE)
    line_rows[place, 2:3] = gate_part[0:1]
    for i in range(2):
        line_rows[place, i : i + 1] = jnp.sum(tally[i], axis=0, keepdims=True)

    def line_copy(ahead):
        return remote(
            line_rows.at[place], line_rows.at[place], line_send.at[ahead], line_recv.at[ahead], neighbour(ahead)
        )

    def all_copy(ahead):
        return remote(
            own_rows, every_ref.at[rank], all_send.at[ahead], all_recv.at[ahead], member(ahead)
        )

    for ahead in range(1, count):
        line_copy(ahead).start()
    if widths:
        for work in scatters.folds(len(widths) - 1):
            work()
    for distance in range(last - 2, 0, -1):
        passing.relay_both(distance)
    for ahead in range(1, count):
        line_copy(ahead).wait_recv()
    summed = line_rows[0]
    for i in range(1, count):
        summed = summed + line_rows[i]
    own_rows[0:8] = summed
    picked = ((sums_temporal, (2, 0, 1)), (sums_middle, (3, 0, 1, 2)), (side_ref, (0,)))
    for i, (source, row) in enumerate((source, row) for source, rows in picked for row in rows):
        own_rows[8 + i : 9 + i] = source[row : row + 1]
    every_ref[rank] = own_rows[...]

    def send_rows(ahead, carry):
        all_copy(ahead).start()
        return carry

    lax.fori_loop(1, everyone, send_rows, 0)

    own = rows_of(place)
    for frame in range(frames):
        grads = passing.total(frame)
        normal, spread = norm_parts(base_ref[frame, own])
        latent_ref[frame] = (
            grad_ref[frame, own] + norm_pull(grads * rows_ref[9:10], normal, spread)
        ).astype(NARROW)

    passing.settle()
    for ahead in range(1, count):
        line_copy(ahead).wait_send()

    def settle(ahead, carry):
        all_copy(ahead).wait_recv()
        all_copy(ahead).wait_send()
        return carry

    lax.fori_loop(1, everyone, settle, 0)
    exchange.finish()
    scatters.finish()


def call_closing(
    count, groups, frames_axis, low, base, grad, gate_part, rows, packed, heads, hidden, in_w, out_w, text, sums, sources,
    widths,
):
    frames, patches, features = base.shape
    everyone = groups * frames_axis
    share = patches // count
    local = out_w.shape[0]
    results, scratch = Scatters.shapes(groups, frames_axis, features, widths)
    product = (features, packed.shape[1] + local)
    if not widths:
        results = [jax.ShapeDtypeStruct(product, NARROW)]
    dma = pltpu.SemaphoreType.DMA
    wide_keys = local // HD * patches
    return fetching_call(
        functools.partial(closing_kernel, count, groups, frames_axis, frames, widths),
        [low, base, grad, gate_part, rows, packed, heads, hidden, in_w, out_w, text, *sums, *sources],
        (
            jax.ShapeDtypeStruct((frames, share, features), NARROW),
            jax.ShapeDtypeStruct((everyone, 16, features), WIDE),
            jax.ShapeDtypeStruct((groups,) + text.shape, NARROW),
            *results,
        ),
        ([pltpu.VMEM(product, NARROW)] if widths else [])
        + [
            pltpu.VMEM((frames, patches, features), NARROW),
            pltpu.VMEM(packed.shape, NARROW),
            pltpu.VMEM((wide_keys, local), NARROW),
            pltpu.VMEM((wide_keys, local), NARROW),
            pltpu.VMEM((patches, wide_keys), NARROW),
            pltpu.VMEM((patches, wide_keys), NARROW),
            pltpu.VMEM((2, count, frames, share, features), NARROW),
            pltpu.VMEM((2, count, frames, share, features), NARROW),
            pltpu.VMEM((count, 8, features), WIDE),
            pltpu.VMEM((16, features), WIDE),
            pltpu.VMEM((2, 8, features), WIDE),
        ]
        + scatter_sems(count, frames)
        + [dma((count,))] * 2
        + [dma((everyone,))] * 2
        + GroupExchange.scratch(groups, frames_axis, text.shape)
        + scratch,
        4,
        "closing",
    )


def finishing_kernel(groups, frames_axis, modulation_rows, layouts, small_ref, ada_ref, text_ref, captions_ref, *refs):
    many = len(layouts)
    sources, refs = refs[:many], refs[many:]
    ada_out, table_out, gain_out, caption_out, *results, sems = refs
    moves = [
        pltpu.make_async_copy(source, result, sems.at[i])
        for i, (source, result, layout) in enumerate(zip(sources, results, layouts))
        if layout == 0
    ]
    for move in moves:
        move.start()
    local = table_out.shape[1]
    buckets = table_out.shape[0]
    column = ada_out.shape[1]
    features = small_ref.shape[2]
    rank = lax.axis_index(GROUP) * frames_axis + lax.axis_index(FRAME)

    def over_frames(group, row):
        first = group * frames_axis
        found = small_ref[first, row : row + 1]
        for other in range(1, frames_axis):
            found = found + small_ref[first + other, row : row + 1]
        return found

    gain = over_frames(0, 14)
    for group in range(1, groups):
        gain = gain + over_frames(group, 14)
    gain_out[...] = gain

    side = jnp.concatenate([small_ref[group * frames_axis, 15:16] for group in range(groups)], axis=0)
    cond, chosen = side[:, 0:local], side[:, local : local + buckets]
    below = 1.0 / (1.0 + jnp.exp(-cond))
    act_low = (cond * below).astype(NARROW)
    act_twice = jnp.concatenate([act_low, act_low], axis=0)
    where = lax.broadcasted_iota(jnp.int32, (features, column), 0)
    which = lax.broadcasted_iota(jnp.int32, (features, column), 1) + rank * column
    select = jnp.where(where == which, 1.0, 0.0).astype(NARROW)
    grad_act = jnp.zeros((2 * groups, local), WIDE)
    for k, row in enumerate(modulation_rows):
        rows = jnp.concatenate([over_frames(group, row) for group in range(groups)], axis=0)
        pair = jnp.concatenate(split_pair(rows), axis=0)
        grad_act = grad_act + dot(pair, ada_ref[k], 1, 1)
        columns = dot(pair, select, 1, 0).astype(NARROW)
        ada_out[k] = dot(columns, act_twice, 0, 0)
    slope = below * (1.0 + cond * (1.0 - below))
    grad_cond = (grad_act[0:groups] + grad_act[groups:]) * slope
    spread = jnp.concatenate(split_pair(grad_cond), axis=0)
    chosen = chosen.astype(NARROW)
    table_out[...] = dot(jnp.concatenate([chosen, chosen], axis=0), spread, 0, 0)

    slots = captions_ref.shape[1]
    caption = dot(text_ref[0, :, 0:slots], captions_ref[0], 1, 0)
    for group in range(1, groups):
        caption = caption + dot(text_ref[group, :, 0:slots], captions_ref[group], 1, 0)
    caption_out[...] = caption
    for source, result, layout in zip(sources, results, layouts):
        if layout > 0:
            parts = source.shape[1] // local
            for i in range(parts):
                values = source[:, i * local : (i + 1) * local]
                if layout == 1:
                    result[i] = values
                else:
                    result[:, i] = values
    for move in moves:
        move.wait()


def call_finishing(groups, frames_axis, buckets, modulation_rows, layouts, small, ada, text, captions, sources):
    parts, local, features = ada.shape
    block = features // (groups * frames_axis)

    def shape_of(source, layout):
        n = source.shape[1] // local
        return (source.shape, (n, source.shape[0], local), (source.shape[0], n, local))[layout]

    results = [
        jax.ShapeDtypeStruct((parts, block, local), WIDE),
        jax.ShapeDtypeStruct((buckets, local), WIDE),
        jax.ShapeDtypeStruct((1, features), WIDE),
        jax.ShapeDtypeStruct((local, captions.shape[2]), WIDE),
    ]
    results += [
        jax.ShapeDtypeStruct(shape_of(source, layout), source.dtype) for source, layout in zip(sources, layouts)
    ]
    places = [pl.BlockSpec(memory_space=pltpu.VMEM if layout else pl.ANY) for layout in layouts]
    return pl.pallas_call(
        functools.partial(finishing_kernel, groups, frames_axis, modulation_rows, layouts),
        out_shape=tuple(results),
        in_specs=vmem(4 + len(sources)),
        out_specs=tuple(vmem(4) + places),
        scratch_shapes=[pltpu.SemaphoreType.DMA((len(sources),))],
        compiler_params=pltpu.CompilerParams(vmem_limit_bytes=62 * 2**20),
        name="finishing",
    )(small, ada, text, captions, *sources)


def opening_kernel(
    count, groups, frames_axis, bucket_ref, clip_ref, window_ref, counts_ref, latent_ref, table_ref, gain_ref,
    ada_ref, captions_ref, caption_full, caption_w,
    base_ref, normed_ref, mods_ref, text_out, side_out, window_out, bias_out, spread_ref,
    caption_here, caption_here_w, caption_sem, land, ada, mine, others,
    up_send, down_send, land_recv, ada_sem, mods_send, mods_recv, cap_send, cap_recv, cap_local,
):
    place = lax.axis_index(LINE)
    group = lax.axis_index(GROUP)
    here = lax.axis_index(FRAME)
    last = count - 1
    width = spread_ref.shape[2]
    parts = ada_ref.shape[0]
    share = latent_ref.shape[1]

    loads = [pltpu.make_async_copy(ada_ref.at[k], ada.at[k], ada_sem.at[k]) for k in range(parts)]
    for load in loads:
        load.start()
    text_loads = [
        pltpu.make_async_copy(caption_full, caption_here, caption_sem.at[0]),
        pltpu.make_async_copy(caption_w, caption_here_w, caption_sem.at[1]),
    ]
    for load in text_loads:
        load.start()

    barrier = pltpu.get_barrier_semaphore()
    for ahead in range(1, count):
        pl.semaphore_signal(
            barrier, inc=1, device_id={LINE: lax.rem(place + ahead, count)}, device_id_type=MESH
        )
    for ahead in range(1, groups):
        pl.semaphore_signal(
            barrier, inc=1, device_id={GROUP: lax.rem(group + ahead, groups)}, device_id_type=MESH
        )
    pl.semaphore_wait(barrier, count - 1 + groups - 1)

    def shift(owner, up):
        to = place + 1 if up else place - 1
        return remote(
            land.at[owner], land.at[owner], (up_send if up else down_send).at[owner], land_recv.at[owner], {LINE: to}
        )

    land[place] = latent_ref[...]

    @pl.when(place < last)
    def _():
        shift(place, True).start()

    @pl.when(place > 0)
    def _():
        shift(place, False).start()

    def caption_block(to):
        if len(captions_ref.shape) == 3:
            return captions_ref.at[to]
        first = pl.multiple_of((to * frames_axis + here) * width, width)
        return captions_ref.at[:, pl.ds(first, width)]

    def caption_copy(ahead):
        to = lax.rem(group + ahead, groups)
        return remote(
            caption_block(to),
            spread_ref.at[group],
            cap_send.at[ahead],
            cap_recv.at[ahead],
            {GROUP: to},
        )

    own_caption = pltpu.make_async_copy(caption_block(group), spread_ref.at[group], cap_local)
    own_caption.start()
    for ahead in range(1, groups):
        caption_copy(ahead).start()

    def arrive(distance):
        @pl.when(place >= distance)
        def _():
            shift(place - distance, True).wait_recv()

            @pl.when(place < last)
            def _():
                shift(place - distance, True).start()

        @pl.when(place + distance <= last)
        def _():
            shift(place + distance, False).wait_recv()

            @pl.when(place > 0)
            def _():
                shift(place + distance, False).start()

    buckets, local = table_ref.shape
    frames = latent_ref.shape[0]
    is_row = lax.broadcasted_iota(jnp.int32, (buckets, local), 0) == bucket_ref[0]
    cond = jnp.sum(jnp.where(is_row, table_ref[...].astype(WIDE), 0.0), axis=0, keepdims=True)
    act = jnp.broadcast_to(swish_act(cond), (16, local)).astype(NARROW)
    side_out[...] = jnp.zeros_like(side_out)
    side_out[0:1, 0:local] = cond
    is_column = lax.broadcasted_iota(jnp.int32, (1, buckets), 1) == bucket_ref[0]
    side_out[0:1, local : local + buckets] = jnp.where(is_column, 1.0, 0.0)
    total = clip_ref.shape[1]
    text_length = caption_full.shape[0] // counts_ref.shape[1]
    lane = lax.broadcasted_iota(jnp.int32, bias_out.shape[1:], 1)
    for frame in range(frames):
        own = here * frames + frame
        for offset in range(WIN):
            other = own + offset - 2
            same = clip_ref[0, jnp.clip(other, 0, total - 1)] == clip_ref[0, own]
            reads = same & (other >= 0) & (other < total)
            if offset != 2:
                reads = reads & (window_ref[0, frame, offset] == 1)
            row = frame * WIN + offset
            window_out[row : row + 1] = jnp.full((1, window_out.shape[1]), jnp.where(reads, 0.0, NEGATIVE))
        bias = jnp.full(bias_out.shape[1:], NEGATIVE)
        for clip in range(counts_ref.shape[1]):
            first = clip * text_length
            end = jnp.where(clip_ref[0, own] == clip, first + counts_ref[0, clip], first)
            bias = jnp.where((lane >= first) & (lane < end), 0.0, bias)
        bias_out[frame] = bias

    def weigh(k):
        loads[k].wait()
        product = dot(act, ada[k], 1, 0)
        mine[k : k + 1] = product[0:1]

    def mods_copy(ahead):
        return remote(
            mine, others.at[place], mods_send.at[ahead], mods_recv.at[ahead], {LINE: lax.rem(place + ahead, count)}
        )

    mine[...] = jnp.zeros_like(mine)
    cut = parts // 2 + 1
    for k in range(cut):
        weigh(k)
    arrive(1)
    for k in range(cut, parts):
        weigh(k)
    for ahead in range(1, count):
        mods_copy(ahead).start()
    others[place] = mine[...]
    for load in text_loads:
        load.wait()
    text_here = dot(caption_here_w[...], caption_here[...], 1, 1).astype(NARROW)
    slots = text_here.shape[1]
    text_out[:, 0:slots] = text_here
    if text_out.shape[1] > slots:
        text_out[:, slots:] = jnp.zeros((text_out.shape[0], text_out.shape[1] - slots), NARROW)
    for distance in range(2, count - 1):
        arrive(distance)
    for ahead in range(1, count):
        mods_copy(ahead).wait_recv()
    mods = others[0]
    for i in range(1, count):
        mods = mods + others[i]
    mods_ref[...] = mods
    for i, row in enumerate((1, 4, 7)):
        mods_ref[9 + i : 10 + i] = 1.0 + mods[row : row + 1]
    mods_ref[12:13] = gain_ref[...].astype(WIDE)
    gain = 1.0 + mods[1:2]
    shift_row = mods[0:1]

    def norm_owner(owner):
        for f in range(latent_ref.shape[0]):
            values = land[owner, f].astype(WIDE)
            rows = pl.ds(pl.multiple_of(owner * share, share), share)
            base_ref[f, rows] = values
            normed_ref[f, rows] = (norm_parts(values)[0] * gain + shift_row).astype(NARROW)

    def near(distance):
        @pl.when(place >= distance)
        def _():
            norm_owner(place - distance)

        @pl.when(place + distance <= last)
        def _():
            norm_owner(place + distance)

    norm_owner(place)
    for distance in range(1, count - 1):
        near(distance)
    if count > 2:
        arrive(count - 1)
    near(count - 1)

    for owner in range(count):

        @pl.when((place < last) & (owner <= place))
        def _():
            shift(owner, True).wait_send()

        @pl.when((place > 0) & (owner >= place))
        def _():
            shift(owner, False).wait_send()

    for ahead in range(1, count):
        mods_copy(ahead).wait_send()
    for ahead in range(1, groups):
        caption_copy(ahead).wait_send()
        caption_copy(ahead).wait_recv()
    own_caption.wait()


def call_opening(count, groups, frames_axis, scalars, latent, table, gain, ada, captions, caption_w):
    frames, share, features = latent.shape
    parts = ada.shape[0]
    length, text_width = captions.shape
    width = text_width // (groups * frames_axis)
    caption_full = captions
    if width % 128:
        blocks = captions.reshape(length, groups, frames_axis, width)
        captions = jnp.transpose(
            lax.dynamic_index_in_dim(blocks, lax.axis_index(FRAME), 2, keepdims=False), (1, 0, 2)
        )
    full = (frames, share * count, features)
    dma = pltpu.SemaphoreType.DMA
    anywhere = pl.BlockSpec(memory_space=pl.ANY)
    return pl.pallas_call(
        functools.partial(opening_kernel, count, groups, frames_axis),
        out_shape=(
            jax.ShapeDtypeStruct(full, WIDE),
            jax.ShapeDtypeStruct(full, NARROW),
            jax.ShapeDtypeStruct((16, features), WIDE),
            jax.ShapeDtypeStruct((caption_w.shape[0], length + -length % 128), NARROW),
            jax.ShapeDtypeStruct((8, features), WIDE),
            jax.ShapeDtypeStruct((frames * WIN, 128), WIDE),
            jax.ShapeDtypeStruct((frames, 8, length + -length % 128), WIDE),
            jax.ShapeDtypeStruct((groups, length, width), NARROW),
        ),
        in_specs=[pl.BlockSpec(memory_space=pltpu.SMEM)] * 4 + vmem(3) + [anywhere] * 4,
        out_specs=tuple(vmem(7) + [anywhere]),
        scratch_shapes=[
            pltpu.VMEM(caption_full.shape, NARROW),
            pltpu.VMEM(caption_w.shape, NARROW),
            dma((2,)),
            pltpu.VMEM((count, frames, share, features), NARROW),
            pltpu.VMEM(ada.shape, NARROW),
            pltpu.VMEM((16, features), WIDE),
            pltpu.VMEM((count, 16, features), WIDE),
            dma((count,)),
            dma((count,)),
            dma((count,)),
            dma((parts,)),
            dma((count,)),
            dma((count,)),
            dma((groups,)),
            dma((groups,)),
            dma,
        ],
        compiler_params=pltpu.CompilerParams(
            collective_id=3, has_side_effects=True, vmem_limit_bytes=62 * 2**20
        ),
        name="opening",
    )(*scalars, latent, table, gain, ada, captions, caption_full, caption_w)


STAGES = 4
MIDDLE_ROWS = 32
MIDDLE_LAG = 3


def gelu_both(values):
    square = values * values
    bent = jnp.tanh(0.7978845608028654 * (values + 0.044715 * values * square))
    slope = 0.5 * (1.0 + bent) + 0.5 * values * (1.0 - bent * bent) * (
        0.7978845608028654 * (1.0 + 3.0 * 0.044715 * square)
    )
    return 0.5 * values * (1.0 + bent), slope


def middle_kernel(count, groups, frames_axis, frames, scattered, fetch, *refs):
    (
        first_ref, base_ref, cotangent_ref, rows_ref, bias_ref,
        text_ref, text_w, query_w, out_w, up_w, down_w,
        base_three, grad_two, low_two, low_three, normed_three, heads_out, grad_query,
        grad_keys, grad_values, sums_ref, extra_part, down_grad, up_result,
        keys_ref, values_ref,
        normed_four, low_four, active, grad_inner, base_two, branch_two, query, grad_heads, part, mixed, tally,
        land, stage, total, cross, in_send, land_recv, cross_recv, out_send, out_recv, *scratch,
    ) = refs
    place = lax.axis_index(LINE)
    if scattered:
        up_grad, *scratch = scratch
        scatters = Scatters(groups, frames_axis, [up_grad], [[up_grad.shape[1]]], [up_result], scratch)
        asides = scatters.items
        greet_line(place, count, 0, asides[0].partners())
    else:
        up_grad, asides = up_result, []
        greet_line(place, count)
    fetch(0, 1, 3)
    half = count // 2
    left = place < half
    level = jnp.where(left, place, count - 1 - place)
    inner = jnp.where(left, place + 1, place - 1)
    outer = jnp.where(left, place - 1, place + 1)
    is_end, is_middle = level == 0, level == half - 1
    inside = jnp.logical_not(is_end)
    patches = base_ref.shape[0] // frames
    chunks = patches // MIDDLE_ROWS
    slots = STAGES * frames
    scale = HD ** (-0.5)
    width = bias_ref.shape[2]
    local = query_w.shape[0]
    half_heads = local // HD // 2
    tile = up_w.shape[1] // 3
    gate_two, cross_gain, gain_three, shift_three, gate_three = (
        rows_ref[i : i + 1] for i in (5, 12, 11, 6, 8)
    )

    def where_of(slot, chunk):
        rows = pl.ds(pl.multiple_of(lax.rem(slot, frames) * patches + chunk * MIDDLE_ROWS, MIDDLE_ROWS), MIDDLE_ROWS)
        return lax.rem(lax.div(slot, frames), 2), rows

    def inward(slot, chunk):
        rows = where_of(slot, chunk)[1]
        return remote(
            stage.at[rows], land.at[rows], in_send.at[slot, chunk], land_recv.at[slot, chunk], {LINE: inner}
        )

    def across(slot, chunk):
        side, rows = where_of(slot, chunk)
        return remote(
            stage.at[rows], cross.at[side, rows], in_send.at[slot, chunk], cross_recv.at[slot, chunk], {LINE: inner}
        )

    def outward(slot, chunk):
        rows = where_of(slot, chunk)[1]
        return remote(
            total.at[rows], total.at[rows], out_send.at[slot, chunk], out_recv.at[slot, chunk], {LINE: outer}
        )

    def own_part(slot, rows):
        return jnp.where(slot < frames, first_ref[rows], part[rows])

    def send_in(slot, chunk):
        @pl.when(is_middle)
        def _():
            across(slot, chunk).start()

        @pl.when(jnp.logical_not(is_middle))
        def _():
            inward(slot, chunk).start()

    def sent(slot, chunk):
        @pl.when(is_middle)
        def _():
            across(slot, chunk).wait_send()

        @pl.when(jnp.logical_not(is_middle))
        def _():
            inward(slot, chunk).wait_send()

        @pl.when(inside)
        def _():
            outward(slot, chunk).wait_send()

    def free(slot, chunk):
        @pl.when(slot >= frames)
        def _():
            sent(slot - frames, chunk)

    def gather_in(slot, chunk):
        rows = where_of(slot, chunk)[1]
        free(slot, chunk)
        inward(slot, chunk).wait_recv()
        stage[rows] = (own_part(slot, rows).astype(WIDE) + land[rows].astype(WIDE)).astype(NARROW)
        send_in(slot, chunk)

    def add_rows(which, terms):
        tally[which] += jnp.sum(terms.reshape(-1, 8, terms.shape[-1]), axis=0)

    def consume(slot, rows, summed):
        number = lax.div(slot, frames)

        @pl.when(number == 0)
        def _():
            branch_two[rows] = summed
            moved = base_ref[rows] + gate_two * summed.astype(WIDE)
            base_two[rows] = moved
            normed_three[rows] = (norm_parts(moved)[0] * cross_gain).astype(NARROW)

        @pl.when(number == 1)
        def _():
            moved = base_two[rows] + summed.astype(WIDE)
            base_three[rows] = moved
            normed_four[rows] = (norm_parts(moved)[0] * gain_three + shift_three).astype(NARROW)
            low_four[rows] = (gate_three * cotangent_ref[rows].astype(WIDE)).astype(NARROW)

        @pl.when(number == 2)
        def _():
            grads = summed.astype(WIDE)
            normal, spread = norm_parts(base_three[rows])
            moved = cotangent_ref[rows].astype(WIDE) + norm_pull(grads * gain_three, normal, spread)
            grad_two[rows] = moved
            low_three[rows] = moved.astype(NARROW)
            add_rows(0, grads)
            add_rows(1, grads * normal)

        @pl.when(number == 3)
        def _():
            grads = summed.astype(WIDE)
            normal, spread = norm_parts(base_two[rows])
            moved = grad_two[rows] + norm_pull(grads * cross_gain, normal, spread)
            grad_two[rows] = moved
            low_two[rows] = (gate_two * moved).astype(NARROW)
            add_rows(2, grads * normal)
            add_rows(3, moved * branch_two[rows].astype(WIDE))

    def finish(slot, chunk):
        side, rows = where_of(slot, chunk)

        @pl.when(is_middle)
        def _():
            across(slot, chunk).wait_recv()
            total[rows] = (stage[rows].astype(WIDE) + cross[side, rows].astype(WIDE)).astype(NARROW)

        @pl.when(jnp.logical_not(is_middle))
        def _():
            outward(slot, chunk).wait_recv()

        @pl.when(inside)
        def _():
            outward(slot, chunk).start()

        consume(slot, rows, total[rows])

    def head_rows(head):
        return pl.ds(head * width, width)

    def probs_of(stream, asked, head):
        scores = scale * dot(asked, keys_ref[head_rows(head)], 1, 1) + bias_ref[stream, 0:1]
        raised = jnp.exp(scores - jnp.max(scores, axis=-1, keepdims=True))
        return raised / jnp.sum(raised, axis=-1, keepdims=True)

    def cross_forward(piece, stream, rows):
        if piece == 0:
            query[rows] = dot(normed_three[rows], query_w[...], 1, 1).astype(NARROW)
        elif piece in (1, 2):
            asked = query[rows]
            found = jnp.zeros((patches, local), WIDE) if piece == 1 else mixed[...]
            for head in range((piece - 1) * half_heads, piece * half_heads):
                probs = probs_of(stream, asked, head).astype(NARROW)
                found = found + dot(probs, values_ref[head_rows(head)], 1, 0)
            if piece == 1:
                mixed[...] = found
            else:
                heads_out[rows] = found.astype(NARROW)
        elif piece == 3:
            part[rows] = dot(heads_out[rows], out_w[...], 1, 0).astype(NARROW)

    def feed_forward(piece, stream, rows):
        if piece < 3:
            span = slice(piece * tile, (piece + 1) * tile)
            inner_values = dot(normed_four[rows], up_w[:, span], 1, 0)
            pulled = dot(low_four[rows], down_w[span], 1, 1)
            raised, slope = gelu_both(inner_values)
            active[rows, span] = raised.astype(NARROW)
            grad_inner[rows, span] = (pulled * slope).astype(NARROW)
        else:
            third = up_w.shape[0] // 3
            span = slice((piece - 3) * third, (piece - 2) * third)
            part[rows, span] = dot(grad_inner[rows], up_w[span], 1, 1).astype(NARROW)

    def cross_backward(piece, stream, rows):
        if piece == 0:
            grad_heads[rows] = dot(low_three[rows], out_w[...], 1, 1).astype(NARROW)
        elif piece in (1, 2):
            asked, given = query[rows], grad_heads[rows]
            found = jnp.zeros((patches, local), WIDE) if piece == 1 else mixed[...]
            for head in range((piece - 1) * half_heads, piece * half_heads):
                spot = head_rows(head)
                probs = probs_of(stream, asked, head)
                pulled = dot(given, values_ref[spot], 1, 1)
                grad_scores = probs * (pulled - jnp.sum(pulled * probs, axis=-1, keepdims=True))
                grad_scores = grad_scores.astype(NARROW)
                found = found + dot(grad_scores, keys_ref[spot], 1, 0)
                grad_keys[spot] += dot(grad_scores, asked, 0, 0)
                grad_values[spot] += dot(probs.astype(NARROW), given, 0, 0)
            if piece == 1:
                mixed[...] = found
            else:
                grad_query[rows] = (scale * found).astype(NARROW)
        elif piece == 3:
            part[rows] = dot(grad_query[rows], query_w[...], 1, 0).astype(NARROW)

    def up_tile(number):
        grad_tile(normed_four, grad_inner, up_grad, number * third, third)

    def down_tile(number):
        grad_tile(low_four, active, down_grad, number * third, third)

    def extra(frame):
        rows = slice(frame * patches, (frame + 1) * patches)
        extra_part[rows] = dot(active[rows], down_w[...], 1, 0).astype(NARROW)

    def text_pairs():
        fetch.again(2, 4, 5, 6, 7, 8, 9, 10)
        packed = dot(text_w[...], text_ref[...], 1, 0).T.astype(NARROW)
        spread_heads(packed[:, 0:local], keys_ref)
        spread_heads(packed[:, local:], values_ref)

    third = up_w.shape[0] // 3
    late = {(0, 1): [text_pairs]}

    def later(slot, chunk, work, *args):
        late.setdefault((slots - 3 + slot, chunk), []).append(functools.partial(work, *args))

    for i, spot in enumerate(((0, 0), (0, 1), (0, 2))):
        later(*spot, up_tile, i)
    for i in range(3):
        later(2, 1 + i, down_tile, i)
    if asides:
        later(0, 2, asides[0].start)
        for i, work in enumerate(scatters.folds(0)):
            later(*((1, 0), (1, 1), (1, 2), (1, 7))[min(i, 3)], work)
    for frame in range(frames):
        later(2, 6 + min(frame, 1), extra, frame)

    tally[...] = jnp.zeros_like(tally)
    grad_keys[...] = jnp.zeros_like(grad_keys)
    grad_values[...] = jnp.zeros_like(grad_values)

    def step(number, carry):
        slot, chunk = lax.div(number, chunks), lax.rem(number, chunks)
        before = slot - 1

        @pl.when(is_end & (chunk == 0))
        def _():
            @pl.when(slot < slots)
            def _():
                def begin(item, inner_carry):
                    rows = where_of(slot, item)[1]
                    free(slot, item)
                    stage[rows] = own_part(slot, rows)
                    send_in(slot, item)
                    return inner_carry

                lax.fori_loop(0, chunks, begin, 0)

            for late_slot in sorted({spot[0] for spot in late}):

                @pl.when(slot == late_slot)
                def _():
                    for late_chunk in range(MIDDLE_LAG):
                        for work in late.get((late_slot, late_chunk), ()):
                            work()

            @pl.when(slot > 0)
            def _():
                def end(item, inner_carry):
                    finish(before, item)
                    return inner_carry

                lax.fori_loop(0, chunks, end, 0)

        @pl.when(inside & (slot < slots))
        def _():
            gather_in(slot, chunk)

            @pl.when(chunk >= MIDDLE_LAG)
            def _():
                finish(slot, chunk - MIDDLE_LAG)

        @pl.when(inside & (slot > 0) & (chunk < MIDDLE_LAG))
        def _():
            finish(before, chunks - MIDDLE_LAG + chunk)

        stream = lax.rem(jnp.maximum(before, 0), frames)
        rows = pl.ds(pl.multiple_of(stream * patches, patches), patches)
        for which, work in enumerate((cross_forward, feed_forward, cross_backward)):

            @pl.when((slot > 0) & (lax.div(jnp.maximum(before, 0), frames) == which))
            def _():
                for piece in range(6 if which == 1 else 4):

                    @pl.when(chunk == jnp.minimum(MIDDLE_LAG + piece, chunks - 1))
                    def _():
                        work(piece, stream, rows)

        for (late_slot, late_chunk), works in late.items():

            @pl.when((slot == late_slot) & (chunk == late_chunk) & (inside | (late_chunk >= MIDDLE_LAG)))
            def _():
                for work in works:
                    work()

        return carry

    lax.fori_loop(0, slots * chunks + MIDDLE_LAG, step, 0)

    def settle(number, carry):
        sent(lax.div(number, chunks), lax.rem(number, chunks))
        return carry

    lax.fori_loop((slots - frames) * chunks, slots * chunks, settle, 0)
    sums_ref[...] = jnp.zeros_like(sums_ref)
    for i in range(4):
        sums_ref[i : i + 1] = jnp.sum(tally[i], axis=0, keepdims=True)
    for aside in asides:
        aside.finish([up_result])


def call_middle(
    count, groups, frames_axis, frames, first, base, cotangent, rows, bias, text, text_w, query_w, out_w, up_w, down_w
):
    tokens, features = first.shape
    local, hidden = query_w.shape[0], up_w.shape[1]
    chunks = tokens // frames // MIDDLE_ROWS
    scattered = can_scatter(groups, frames_axis, features)
    keys_shape = (local // HD * bias.shape[2], local)

    def wide(*shape):
        return jax.ShapeDtypeStruct(shape, WIDE)

    def narrow(*shape):
        return jax.ShapeDtypeStruct(shape, NARROW)

    found, scratch = [narrow(features, hidden)], []
    if scattered:
        found, scratch = Scatters.shapes(groups, frames_axis, features, [[hidden]])
        scratch = [pltpu.VMEM((features, hidden), NARROW)] + scratch
    results = (
        [wide(tokens, features)] * 2
        + [narrow(tokens, features)] * 3
        + [narrow(tokens, local)] * 2
        + [wide(*keys_shape)] * 2
        + [wide(8, features), narrow(tokens, features), narrow(features, hidden)]
        + found
    )
    sem = pltpu.SemaphoreType.DMA((STAGES * frames, chunks))
    return fetching_call(
        functools.partial(middle_kernel, count, groups, frames_axis, frames, scattered),
        [first, base, cotangent, rows, bias, text, text_w, query_w, out_w, up_w, down_w],
        tuple(results),
        [pltpu.VMEM(keys_shape, NARROW)] * 2
        + [pltpu.VMEM((tokens, features), NARROW)] * 2
        + [pltpu.VMEM((tokens, hidden), NARROW)] * 2
        + [
            pltpu.VMEM((tokens, features), WIDE),
            pltpu.VMEM((tokens, features), NARROW),
            pltpu.VMEM((tokens, local), NARROW),
            pltpu.VMEM((tokens, local), NARROW),
            pltpu.VMEM((tokens, features), NARROW),
            pltpu.VMEM((tokens // frames, local), WIDE),
            pltpu.VMEM((4, 8, features), WIDE),
        ]
        + [pltpu.VMEM((tokens, features), NARROW)] * 3
        + [pltpu.VMEM((2, tokens, features), NARROW)]
        + [sem] * 5
        + scratch,
        7,
        "middle",
    )


def greet_frames(here, frames_axis):
    found = (here > 0).astype(jnp.int32) + (here < frames_axis - 1).astype(jnp.int32)
    barrier = pltpu.get_barrier_semaphore()

    @pl.when(here > 0)
    def _():
        pl.semaphore_signal(barrier, inc=1, device_id={FRAME: here - 1}, device_id_type=MESH)

    @pl.when(here < frames_axis - 1)
    def _():
        pl.semaphore_signal(barrier, inc=1, device_id={FRAME: here + 1}, device_id_type=MESH)

    return found


def head_columns(local):
    feature = lax.broadcasted_iota(jnp.int32, (local, 128), 0)
    first = lax.broadcasted_iota(jnp.int32, (local, 128), 1) * HD
    return jnp.where((feature >= first) & (feature < first + HD), 1.0, 0.0).astype(NARROW)


def per_head(values, columns):
    return dot(values.astype(NARROW), columns, 1, 0)


def over_features(values, columns):
    return dot(values.astype(NARROW), columns, 1, 1)


def window_probs(query, keys_of, bias_of, columns):
    scores = [
        HD ** (-0.5) * per_head(query * keys_of(offset), columns) + bias_of(offset) for offset in range(WIN)
    ]
    highest = functools.reduce(jnp.maximum, scores)
    raised = [jnp.exp(item - highest) for item in scores]
    whole = 1.0 / sum(raised[1:], raised[0])
    return [item * whole for item in raised]


def temporal_forward_kernel(
    count, frames_axis, frames, fetch, hidden_ref, in_ref, out_ref, bias_ref, cotangent_ref, text_ref,
    query_ref, keys_ref, values_ref, heads_ref, part_ref, cotangent_full, text_full,
    halo_send, halo_recv, *sems,
):
    place, here = lax.axis_index(LINE), lax.axis_index(FRAME)
    patches = hidden_ref.shape[0] // frames
    local = heads_ref.shape[1]
    share = cotangent_ref.shape[1]
    last = count - 1
    greet_line(place, count, greet_frames(here, frames_axis))
    fetch()
    cells = (keys_ref, values_ref)

    def shares(owner):
        return cotangent_full.at[:, pl.ds(pl.multiple_of(owner * share, share), share)]

    def text_share(owner):
        return text_full.at[pl.ds(pl.multiple_of(owner * local, 16), local)]

    moving = [
        LineGather(count, place, shares, sems[0:3]),
        LineGather(count, place, text_share, sems[3:6]),
    ]
    cotangent_full[:, pl.ds(pl.multiple_of(place * share, share), share)] = cotangent_ref[...]
    text_full[pl.ds(pl.multiple_of(place * local, 16), local)] = text_ref[...]
    for item in moving:
        item.start()

    def halo(which, item):
        source = 2 + (frames - 2 + which if which < 2 else 0)
        target = which if which < 2 else frames + 2
        to = here + 1 if which < 2 else here - 1
        ref = cells[item]
        return remote(
            ref.at[source], ref.at[target], halo_send.at[which, item], halo_recv.at[which, item], {FRAME: to}
        )

    has_next, has_previous = here < frames_axis - 1, here > 0

    def frame_rows(frame):
        return slice(frame * patches, (frame + 1) * patches)

    for frame in range(frames):
        for item in range(2):
            rows = slice((1 + item) * local, (2 + item) * local)
            cells[item][2 + frame] = dot(hidden_ref[frame_rows(frame)], in_ref[rows], 1, 1).astype(NARROW)
            for which in range(3):
                if (frames - 2 + which if which < 2 else 0) == frame:

                    @pl.when(has_next if which < 2 else has_previous)
                    def _():
                        halo(which, item).start()

    query_ref[...] = dot(hidden_ref[...], in_ref[0:local], 1, 1).astype(NARROW)
    for distance in range(1, last):
        for item in moving:
            item.arrive(distance)
    for item in range(2):

        @pl.when(has_previous)
        def _():
            halo(0, item).wait_recv()
            halo(1, item).wait_recv()

        @pl.when(jnp.logical_not(has_previous))
        def _():
            cells[item][0:2] = jnp.zeros((2,) + cells[item].shape[1:], NARROW)

        @pl.when(has_next)
        def _():
            halo(2, item).wait_recv()

        @pl.when(jnp.logical_not(has_next))
        def _():
            cells[item][frames + 2] = jnp.zeros(cells[item].shape[1:], NARROW)

    columns = head_columns(local)
    for frame in range(frames):
        probs = window_probs(
            query_ref[frame_rows(frame)].astype(WIDE),
            lambda offset: keys_ref[frame + offset].astype(WIDE),
            lambda offset: bias_ref[frame * WIN + offset : frame * WIN + offset + 1],
            columns,
        )
        mixed = over_features(probs[0], columns) * values_ref[frame].astype(WIDE)
        for offset in range(1, WIN):
            mixed = mixed + over_features(probs[offset], columns) * values_ref[frame + offset].astype(WIDE)
        heads_ref[frame_rows(frame)] = mixed.astype(NARROW)
        part_ref[frame_rows(frame)] = dot(mixed.astype(NARROW), out_ref[...], 1, 0).astype(NARROW)
    for item in moving:
        item.arrive(last)
        item.settle()
    for item in range(2):

        @pl.when(has_next)
        def _():
            halo(0, item).wait_send()
            halo(1, item).wait_send()

        @pl.when(has_previous)
        def _():
            halo(2, item).wait_send()


def call_temporal_forward(count, frames_axis, hidden, in_w, out_w, bias, cotangent, text):
    tokens, features = hidden.shape
    frames, share = cotangent.shape[:2]
    local = out_w.shape[0]
    patches = tokens // frames

    def narrow(*shape):
        return jax.ShapeDtypeStruct(shape, NARROW)

    results = (
        [narrow(tokens, local)]
        + [narrow(frames + 3, patches, local)] * 2
        + [narrow(tokens, local), narrow(tokens, features)]
        + [narrow(frames, share * count, features), narrow(features, text.shape[1])]
    )
    return fetching_call(
        functools.partial(temporal_forward_kernel, count, frames_axis, frames),
        [hidden, in_w, out_w, bias, cotangent, text],
        tuple(results),
        [pltpu.SemaphoreType.DMA((3, 2))] * 2 + gather_sems(count) * 2,
        8,
        "temporal_forward",
    )


def temporal_backward_kernel(
    count, groups, frames_axis, frames, widths, fetch, *refs
):
    (
        grad_ref, in_ref, out_ref, bias_ref, query_ref, keys_ref, values_ref,
        extra_ref, text_keys, text_values, text_w, text_rows, cross_hidden, cross_grad, cross_low, cross_heads,
        base_three, cotangent_ref, gate_ref, *refs,
    ) = refs
    sources, refs = refs[: len(widths)], refs[len(widths) :]
    grad_packed, part_ref, output_ref, gate_part, text_own, product_ref, *refs = refs
    results, refs = refs[: len(widths)], refs[len(widths) :]
    (
        near_keys, near_values, rim_out, rim_in, halo_send, halo_recv, text_ref, text_low,
        extra_land, extra_stage, text_land, text_stage, *sems,
    ) = refs
    scatters = Scatters(groups, frames_axis, sources, widths, results, sems[8:])
    products = Products(
        [(cross_hidden, cross_grad), (text_rows, text_low, 1, 1), (cross_low, cross_heads)], product_ref
    ).work()
    place, here = lax.axis_index(LINE), lax.axis_index(FRAME)
    patches = grad_ref.shape[0] // frames
    local = out_ref.shape[0]
    share = output_ref.shape[1]
    last = count - 1
    greet_line(place, count, greet_frames(here, frames_axis), scatters.partners() if widths else ())
    fetch(7, *range(19, 19 + len(sources)))
    for item in scatters.items:
        item.start()

    def shares(owner, frame):
        return extra_ref[frame, pl.ds(pl.multiple_of(owner * share, share), share)]

    moving = [
        LineScatter(count, place, frames, shares, extra_land, extra_stage, sems[0:4]),
        LineScatter(count, place, 1, lambda owner, piece: text_ref[owner], text_land, text_stage, sems[4:8]),
    ]
    moving[0].relay_both(last)
    near = (near_keys, near_values)
    def halo(which):
        to = here - 1 if which < 2 else here + 1
        return remote(
            rim_out.at[which], rim_in.at[which], halo_send.at[which], halo_recv.at[which], {FRAME: to}
        )

    has_next, has_previous = here < frames_axis - 1, here > 0

    def frame_rows(frame):
        return slice(frame * patches, (frame + 1) * patches)

    fetch(0, 2, 3, 4, 5, 6)
    columns = head_columns(local)
    seen = set()

    def add(item, cell, terms):
        if (item, cell) in seen:
            near[item][cell] += terms
        else:
            near[item][cell] = terms
        seen.add((item, cell))

    for frame in range(frames):
        given = dot(grad_ref[frame_rows(frame)], out_ref[...], 1, 1).astype(NARROW).astype(WIDE)
        asked = query_ref[frame_rows(frame)].astype(WIDE)
        probs = window_probs(
            asked,
            lambda offset: keys_ref[frame + offset].astype(WIDE),
            lambda offset: bias_ref[frame * WIN + offset : frame * WIN + offset + 1],
            columns,
        )
        pulled = [per_head(given * values_ref[frame + offset].astype(WIDE), columns) for offset in range(WIN)]
        shared = sum((probs[i] * pulled[i] for i in range(1, WIN)), probs[0] * pulled[0])
        found = jnp.zeros((patches, local), WIDE)
        for offset in range(WIN):
            scores = HD ** (-0.5) * over_features(probs[offset] * (pulled[offset] - shared), columns)
            found = found + scores * keys_ref[frame + offset].astype(WIDE)
            add(0, frame + offset, scores * asked)
            add(1, frame + offset, over_features(probs[offset], columns) * given)
        grad_packed[frame_rows(frame), 0:local] = found.astype(NARROW)
        if frame == 0:
            for item in scatters.items:
                item.fold_all()
            if last > 1:
                moving[0].relay_both(last - 1)

    for which in range(3):

        @pl.when(has_previous if which < 2 else has_next)
        def _():
            for item in range(2):
                span = slice(item * local, (item + 1) * local)
                rim_out[which, :, span] = near[item][which if which < 2 else frames + 2].astype(NARROW)
            halo(which).start()

    for distance in range(last - 2, 0, -1):
        moving[0].relay_both(distance)
    fetch()
    fetch()
    slots = text_low.shape[1]
    for item, (source, factor) in enumerate(((text_keys, HD ** (-0.5)), (text_values, 1.0))):
        low = (factor * collect_heads(source[...], slots)).T
        text_low[item * local : (item + 1) * local] = low.astype(NARROW)
    text_parts = dot(text_w[...], text_low[...], 0, 0).astype(NARROW)
    for owner in range(count):
        text_ref[owner] = text_parts[owner * local : (owner + 1) * local]
    moving[1].relay_both(last)
    for i, work in enumerate(products):
        work()
        if last - 1 - i > 0:
            moving[1].relay_both(last - 1 - i)
    for distance in range(last - 1 - len(products), 0, -1):
        moving[1].relay_both(distance)

    for which in range(3):

        @pl.when(has_next if which < 2 else has_previous)
        def _():
            halo(which).wait_recv()
            for item in range(2):
                span = slice(item * local, (item + 1) * local)
                near[item][2 + (frames - 2 + which if which < 2 else 0)] += rim_in[which, :, span].astype(WIDE)

    for frame in range(frames):
        rows = frame_rows(frame)
        parts = dot(grad_packed[rows, 0:local], in_ref[0:local], 1, 0)
        for item in range(2):
            values = near[item][2 + frame].astype(NARROW)
            grad_packed[rows, (1 + item) * local : (2 + item) * local] = values
            parts = parts + dot(values, in_ref[(1 + item) * local : (2 + item) * local], 1, 0)
        part_ref[rows] = parts.astype(NARROW)

    gate_sum = jnp.zeros((1, gate_part.shape[1]), WIDE)
    for frame in range(frames):
        found = moving[0].total(frame)
        rows = pl.ds(pl.multiple_of(frame * patches + place * share, share), share)
        output_ref[frame] = (base_three[rows] + gate_ref[8:9] * found).astype(NARROW)
        gate_sum = gate_sum + jnp.sum(cotangent_ref[frame].astype(WIDE) * found, axis=0, keepdims=True)
    gate_part[...] = jnp.broadcast_to(gate_sum, gate_part.shape)
    text_own[...] = moving[1].total(0).astype(NARROW)
    for item in moving:
        item.settle()
    for which in range(3):

        @pl.when(has_previous if which < 2 else has_next)
        def _():
            halo(which).wait_send()

    scatters.finish()


def call_temporal_backward(
    count, groups, frames_axis, grad, in_w, out_w, bias, query, keys, values, extra, text_keys, text_values, text_w,
    text_rows, cross_pairs, sources, widths,
):
    tokens, features = grad.shape
    frames, patches = extra.shape[:2]
    local = out_w.shape[0]
    share = patches // count
    slots = text_rows.shape[1]

    def narrow(*shape):
        return jax.ShapeDtypeStruct(shape, NARROW)

    results = (
        [narrow(tokens, 3 * local)]
        + [narrow(tokens, features), narrow(frames, share, features)]
        + [jax.ShapeDtypeStruct((8, features), WIDE)]
        + [narrow(local, slots), narrow(features, 4 * local)]
    )
    found, scratch = Scatters.shapes(groups, frames_axis, features, widths)
    results = results + found
    return fetching_call(
        functools.partial(temporal_backward_kernel, count, groups, frames_axis, frames, widths),
        [grad, in_w, out_w, bias, query, keys, values, extra, text_keys, text_values, text_w, text_rows,
        *cross_pairs, *sources,],
        tuple(results),
        [pltpu.VMEM((frames + 3, patches, local), WIDE)] * 2
        + [pltpu.VMEM((3, patches, 2 * local), NARROW)] * 2
        + [pltpu.SemaphoreType.DMA((3,))] * 2
        + [pltpu.VMEM((count, local, slots), NARROW), pltpu.VMEM((2 * local, slots), NARROW)]
        + [pltpu.VMEM((2, count, frames, share, features), NARROW)] * 2
        + [pltpu.VMEM((2, count, 1, local, slots), NARROW)] * 2
        + scatter_sems(count, frames)
        + scatter_sems(count, 1)
        + scratch,
        9,
        "temporal_backward",
    )


def sum_matrix_grads(pieces):
    if not pieces:
        return []
    packed = jnp.concatenate([piece.astype(NARROW) for piece in pieces], axis=1)
    summed = lax.psum_scatter(packed, BOTH, scatter_dimension=0, tiled=True).astype(WIDE)
    found, start = [], 0
    for piece in pieces:
        found.append(summed[:, start : start + piece.shape[1]])
        start += piece.shape[1]
    return found


def per_device(
    latent, captions, bucket, clip_ids, window_mask, text_counts, time_table, ada_weight,
    spatial_inproj, spatial_outproj, temporal_inproj, temporal_outproj, caption_proj, cross_gain,
    cross_query, cross_keyval, cross_outproj, mlp_up, mlp_down, cotangent,
):
    count, groups, frames_axis = (lax.axis_size(axis) for axis in (LINE, GROUP, FRAME))
    place = lax.axis_index(LINE)
    frames, share, features = latent.shape[1:]
    patches = share * count
    tokens = frames * patches
    local = spatial_outproj.shape[0]
    clip_count, text_length, text_width = captions.shape[1:]
    slots = clip_count * text_length

    def flat(values):
        return values.reshape(tokens, -1)

    def grid(values):
        return values.reshape(frames, patches, -1)

    spatial_in, temporal_in, keyval_in = (
        jnp.transpose(w, (1, 2, 0)).reshape(-1, features)
        for w in (spatial_inproj, temporal_inproj, cross_keyval)
    )
    query_in = cross_query.T

    caption_here = captions[0].reshape(slots, text_width)
    base_grid, normed_grid, mods, text_part, side, window_bias, text_bias, caption_share = call_opening(
        count, groups, frames_axis, (bucket, clip_ids, window_mask, text_counts), latent[0], time_table,
        cross_gain.reshape(1, features), jnp.transpose(ada_weight, (1, 0, 2)), caption_here, caption_proj.T,
    )
    base_zero, spatial_hidden = flat(base_grid), flat(normed_grid)

    spatial_out, base_one, temporal_hidden, spatial_packed, spatial_flat = call_forward(
        count, frames, spatial_hidden, spatial_in, base_zero, mods, spatial_outproj,
    )

    (
        temporal_query, temporal_keys, temporal_values, temporal_flat, temporal_part, cotangent_full, text_full,
    ) = call_temporal_forward(
        count, frames_axis, temporal_hidden, temporal_in, temporal_outproj, window_bias, cotangent[0], text_part
    )
    cotangent_full = flat(cotangent_full)

    (
        base_three, grad_two, grad_temporal_low, grad_cross_low, cross_hidden, cross_flat, grad_cross_packed,
        text_grad_keys, text_grad_values, sums_middle, mlp_part, grad_down, grad_up,
    ) = call_middle(
        count, groups, frames_axis, frames, temporal_part, base_one, cotangent_full,
        mods, text_bias,
        text_full, keyval_in, query_in, cross_outproj, mlp_up, mlp_down,
    )

    def outside(packed, widths):
        return sum_matrix_grads(
            [
                item[:, sum(columns[:i]) : sum(columns[: i + 1])]
                for item, columns in zip(packed, widths)
                for i in range(len(columns))
            ]
        )

    if not can_scatter(groups, frames_axis, features):
        (grad_up,) = outside([grad_up], [[grad_up.shape[1]]])

    inside = can_scatter(groups, frames_axis, features)
    down_widths = [[grad_down.shape[1]]]
    grad_temporal_packed, temporal_grad_part, output, gate_part, text_grad, grad_cross, *found = call_temporal_backward(
        count, groups, frames_axis, grad_temporal_low, temporal_in, temporal_outproj, window_bias,
        temporal_query, temporal_keys, temporal_values, grid(mlp_part), text_grad_keys, text_grad_values,
        keyval_in, text_full,
        [cross_hidden, grad_cross_packed, grad_cross_low, cross_flat, base_three, cotangent[0], mods],
        [grad_down] if inside else [], down_widths if inside else [],
    )
    (grad_down,) = found if inside else outside([grad_down], down_widths)
    cross_widths, qkv_widths = [local, 2 * local, local], [3 * local, local]
    grad_one, grad_spatial_low, sums_temporal, *found = call_backward(
        count, groups, frames_axis, temporal_grad_part, base_one, grad_two, spatial_out,
        mods,
        [(temporal_hidden, grad_temporal_packed), (grad_temporal_low, temporal_flat)],
        [grad_cross] if inside else [], [cross_widths, qkv_widths] if inside else [],
    )
    if not inside:
        found = outside([grad_cross, found[0]], [cross_widths, qkv_widths])
    (
        grad_query_cross, grad_keyval_cross, grad_outproj_cross, grad_inproj_temporal, grad_outproj_temporal,
    ) = found

    grad_latent, small_all, text_grad_all, *found = call_closing(
        count, groups, frames_axis, grad_spatial_low, grid(base_zero), grid(grad_one), gate_part,
        mods, spatial_packed, spatial_flat, spatial_hidden, spatial_in, spatial_outproj,
        text_grad, [sums_temporal, sums_middle, side], [], [qkv_widths] if inside else [],
    )
    if not inside:
        found = outside([found[0]], [qkv_widths])
    grad_inproj_spatial, grad_outproj_spatial = found

    grad_ada, grad_table, grad_gain, grad_caption, *found = call_finishing(
        groups, frames_axis, time_table.shape[0], (0, 1, 8, 9, 10, 11, 12, 13, 2), (0, 0, 1, 0, 1, 0, 0, 2, 0, 0, 0),
        small_all, jnp.transpose(ada_weight, (1, 0, 2)), text_grad_all, caption_share,
        [
            output.reshape(frames * share, features), grad_latent.reshape(frames * share, features),
            grad_inproj_spatial, grad_outproj_spatial,
            grad_inproj_temporal, grad_outproj_temporal, grad_query_cross, grad_keyval_cross,
            grad_outproj_cross, grad_up, grad_down,
        ],
    )
    (
        output, grad_latent, grad_inproj_spatial, grad_outproj_spatial, grad_inproj_temporal,
        grad_outproj_temporal, grad_query_cross, grad_keyval_cross, grad_outproj_cross, grad_up, grad_down,
    ) = found
    return (
        output.reshape(1, frames, share, features),
        grad_latent.reshape(1, frames, share, features),
        grad_table,
        jnp.transpose(grad_ada, (2, 0, 1)),
        jnp.transpose(grad_inproj_spatial, (1, 0, 2)),
        grad_outproj_spatial.T,
        jnp.transpose(grad_inproj_temporal, (1, 0, 2)),
        grad_outproj_temporal.T,
        grad_caption.T,
        grad_gain[0],
        grad_query_cross,
        grad_keyval_cross,
        grad_outproj_cross.T,
        grad_up,
        grad_down.T,
    )


def solution(mesh):
    tokens = P(GROUP, FRAME, LINE, None)
    packed_in, rows_in, columns_in = P(None, None, LINE), P(LINE, None), P(None, LINE)
    in_specs = (
        tokens, P(GROUP, None, None, None), P(GROUP), P(GROUP, None), P(GROUP, FRAME, None),
        P(GROUP, None), columns_in, P(LINE, None, None), packed_in, rows_in, packed_in, rows_in,
        columns_in, P(), columns_in, packed_in, rows_in, columns_in, rows_in, tokens,
    )
    packed_out, rows_out, columns_out = P(BOTH, None, LINE), P(LINE, BOTH), P(BOTH, LINE)
    out_specs = (
        tokens, tokens, columns_in, P(LINE, None, BOTH), packed_out, rows_out, packed_out, rows_out,
        columns_out, P(), columns_out, packed_out, rows_out, columns_out, rows_out,
    )
    return jax.shard_map(
        per_device, mesh=mesh, in_specs=in_specs, out_specs=out_specs, check_vma=False
    )
```

```python
import functools

import jax
import jax.numpy as jnp
from jax import lax
from jax.experimental import pallas as pl
from jax.experimental.pallas import tpu as pltpu
from jax.sharding import PartitionSpec as P

HD = 72
WIN = 4
EPSILON = 1e-06
HIGHEST = lax.Precision.HIGHEST
NEGATIVE = -1e30
WIDE = jnp.float32
NARROW = jnp.bfloat16
GROUP, FRAME, LINE = "group", "frame", "tensor"
BOTH = (GROUP, FRAME)
MESH = pl.DeviceIdType.MESH
CHUNKS = 16
LAG = 2
AT_ONCE = 4
VMEM_LIMIT = 48 * 2**20


def swish_act(values):
    return values / (1.0 + jnp.exp(-values))


def gelu_tanh(values):
    return (
        0.5
        * values
        * (1.0 + jnp.tanh(0.7978845608028654 * (values + 0.044715 * values * values * values)))
    )


def dot(first, second, contract_first, contract_second):
    return lax.dot_general(
        first, second, (((contract_first,), (contract_second,)), ((), ())), preferred_element_type=WIDE
    )


def split_pair(values):
    high_part = values.astype(NARROW)
    rest_part = (values - high_part.astype(WIDE)).astype(NARROW)
    return (high_part, rest_part)


def norm_parts(values):
    centred = values - jnp.mean(values, axis=-1, keepdims=True)
    spread = lax.rsqrt(jnp.mean(centred * centred, axis=-1, keepdims=True) + EPSILON)
    return centred * spread, spread


def norm_pull(scaled, normal, spread):
    return spread * (
        scaled
        - jnp.mean(scaled, axis=-1, keepdims=True)
        - normal * jnp.mean(scaled * normal, axis=-1, keepdims=True)
    )


def remote(source, target, send_sem, recv_sem, where):
    return pltpu.make_async_remote_copy(
        src_ref=source,
        dst_ref=target,
        send_sem=send_sem,
        recv_sem=recv_sem,
        device_id=where,
        device_id_type=MESH,
    )


def greet_line(place, count, more=0, others=()):
    barrier = pltpu.get_barrier_semaphore()
    for where in others:
        pl.semaphore_signal(barrier, inc=1, device_id=where, device_id_type=MESH)

    @pl.when(place > 0)
    def _():
        pl.semaphore_signal(barrier, inc=1, device_id={LINE: place - 1}, device_id_type=MESH)

    @pl.when(place < count - 1)
    def _():
        pl.semaphore_signal(barrier, inc=1, device_id={LINE: place + 1}, device_id_type=MESH)

    pl.semaphore_wait(
        barrier, (place > 0).astype(jnp.int32) + (place < count - 1).astype(jnp.int32) + len(others) + more
    )


class Scatter:
    SCRATCH = 20

    def __init__(self, groups, frames_axis, source, scratch):
        self.source, self.columns = source, source.shape[1]
        self.inbox, self.kept = scratch[:2]
        self.stages = scratch[2:6]
        self.lands = scratch[6:10]
        self.sends, self.recvs = scratch[10:14], scratch[14:18]
        self.twin_send, self.twin_recv = scratch[18:20]
        self.frames_axis, self.highs = frames_axis, groups // 2
        self.block = source.shape[0] // (groups * frames_axis)
        self.cut = self.columns // 256 * 128
        group = lax.axis_index(GROUP)
        self.core, self.high, self.frame = lax.rem(group, 2), lax.div(group, 2), lax.axis_index(FRAME)
        self.twin = {GROUP: group + 1 - 2 * self.core}

    def other_high(self, step):
        return lax.rem(self.high + step, self.highs)

    def other_frame(self, step):
        return lax.rem(self.frame + step, self.frames_axis)

    def partner(self, along_group, step):
        if along_group:
            return {GROUP: self.other_high(step) * 2 + self.core}
        return {FRAME: self.other_frame(step)}

    def steps(self, along_group):
        return range(1, self.highs if along_group else self.frames_axis)

    def partners(self):
        return [self.twin] + [self.partner(way, step) for way in (True, False) for step in self.steps(way)]

    def twin_copy(self, high):
        rows = self.block * self.frames_axis
        first = pl.multiple_of((high * 2 + 1 - self.core) * rows, 16)
        return remote(
            self.source.at[pl.ds(first, rows)],
            self.inbox.at[pl.ds(high * rows, rows)],
            self.twin_send.at[high],
            self.twin_recv.at[high],
            self.twin,
        )

    def move(self, which, step):
        return remote(
            self.stages[which].at[step - 1],
            self.lands[which].at[step - 1],
            self.sends[which].at[step],
            self.recvs[which].at[step],
            self.partner(which in (0, 3), step),
        )

    def pair_sum(self, high, frame, span):
        first = ((high * 2 + self.core) * self.frames_axis + frame) * self.block
        other = (high * self.frames_axis + frame) * self.block
        mine = self.source[pl.ds(pl.multiple_of(first, 16), self.block), span]
        return mine.astype(WIDE) + self.inbox[pl.ds(pl.multiple_of(other, 16), self.block), span].astype(WIDE)

    def start(self):
        for high in range(self.highs):
            self.twin_copy(high).start()

    def first_round(self):
        for high in range(self.highs):
            self.twin_copy(high).wait_recv()
        left, right = slice(0, self.cut), slice(self.cut, self.columns)
        for step in self.steps(True):
            for frame in range(self.frames_axis):
                rows = slice(frame * self.block, (frame + 1) * self.block)
                self.stages[0][step - 1, rows] = self.pair_sum(self.other_high(step), frame, left).astype(NARROW)
            self.move(0, step).start()
        for step in self.steps(False):
            for high in range(self.highs):
                rows = slice(high * self.block, (high + 1) * self.block)
                self.stages[1][step - 1, rows] = self.pair_sum(high, self.other_frame(step), right).astype(NARROW)
            self.move(1, step).start()

    def gathered(self, which, high, frame):
        span = slice(0, self.cut) if which == 0 else slice(self.cut, self.columns)
        found = self.pair_sum(high, frame, span)
        rows = pl.ds(pl.multiple_of((frame if which == 0 else high) * self.block, 16), self.block)
        for step in self.steps(which == 0):
            found = found + self.lands[which][step - 1, rows].astype(WIDE)
        return found

    def second_round(self):
        for which in (0, 1):
            for step in self.steps(which == 0):
                self.move(which, step).wait_recv()
        for step in self.steps(False):
            self.stages[2][step - 1] = self.gathered(0, self.high, self.other_frame(step)).astype(NARROW)
            self.move(2, step).start()
        for step in self.steps(True):
            self.stages[3][step - 1] = self.gathered(1, self.other_high(step), self.frame).astype(NARROW)
            self.move(3, step).start()
        self.kept[:, 0 : self.cut] = self.gathered(0, self.high, self.frame)
        self.kept[:, self.cut :] = self.gathered(1, self.high, self.frame)

    def finish(self, results):
        for which in (2, 3):
            for step in self.steps(which == 3):
                self.move(which, step).wait_recv()
        for which, span in ((2, slice(0, self.cut)), (3, slice(self.cut, self.columns))):
            for step in self.steps(which == 3):
                self.kept[:, span] += self.lands[which][step - 1].astype(WIDE)
        start = 0
        for result in results:
            result[...] = self.kept[:, start : start + result.shape[1]]
            start += result.shape[1]
        for high in range(self.highs):
            self.twin_copy(high).wait_send()
        for which in range(4):
            for step in self.steps(which in (0, 3)):
                self.move(which, step).wait_send()

    @staticmethod
    def scratch(groups, frames_axis, width, columns):
        block, highs = width // (groups * frames_axis), groups // 2
        cut = columns // 256 * 128
        across, along = max(highs - 1, 1), max(frames_axis - 1, 1)
        shapes = [
            (across, frames_axis * block, cut),
            (along, highs * block, columns - cut),
            (along, block, cut),
            (across, block, columns - cut),
        ]
        dma = pltpu.SemaphoreType.DMA
        sems = [dma((highs,)), dma((frames_axis,)), dma((frames_axis,)), dma((highs,))]
        return (
            [pltpu.VMEM((width // 2, columns), NARROW), pltpu.VMEM((block, columns), WIDE)]
            + [pltpu.VMEM(shape, NARROW) for shape in shapes] * 2
            + sems * 2
            + [dma((highs,))] * 2
        )


def can_scatter(groups, frames_axis, width):
    return groups % 2 == 0 and width % (16 * groups * frames_axis) == 0


class Products:
    def __init__(self, pairs, result):
        self.pairs, self.result = pairs, result

    def product(self, i):
        first, second, *side = self.pairs[i]
        found = dot(first[...], second[...], *(side or (0, 0))).astype(NARROW)
        start = sum(pair[1].shape[1 if len(pair) == 2 else 0] for pair in self.pairs[:i])
        self.result[:, start : start + found.shape[1]] = found

    def work(self):
        return [functools.partial(self.product, i) for i in range(len(self.pairs))]


class Scatters:
    def __init__(self, groups, frames_axis, sources, widths, results, scratch):
        self.items, self.results = [], []
        for i, source in enumerate(sources):
            self.items.append(Scatter(groups, frames_axis, source, scratch[Scatter.SCRATCH * i : Scatter.SCRATCH * (i + 1)]))
            self.results.append(results[: len(widths[i])])
            results = results[len(widths[i]) :]

    def partners(self):
        return self.items[0].partners()

    def folds(self, i):
        return [self.items[i].first_round, self.items[i].second_round]

    def finish(self):
        for item, results in zip(self.items, self.results):
            item.finish(results)

    @staticmethod
    def shapes(groups, frames_axis, features, widths):
        block = features // (groups * frames_axis)
        results = [jax.ShapeDtypeStruct((block, n), WIDE) for columns in widths for n in columns]
        scratch = [Scatter.scratch(groups, frames_axis, features, sum(columns)) for columns in widths]
        return results, sum(scratch, [])


class GroupExchange:
    def __init__(self, groups, frames_axis, source, every, scratch):
        self.groups, self.frames_axis = groups, frames_axis
        self.source, self.every = source, every
        self.near, self.frame_send, self.frame_recv, self.group_send, self.group_recv = scratch
        self.group, self.frame = lax.axis_index(GROUP), lax.axis_index(FRAME)

    def frame_copy(self, step):
        return remote(
            self.source,
            self.near.at[step - 1],
            self.frame_send.at[step],
            self.frame_recv.at[step],
            {FRAME: lax.rem(self.frame + step, self.frames_axis)},
        )

    def group_copy(self, step):
        own = self.every.at[self.group]
        return remote(
            own,
            own,
            self.group_send.at[step],
            self.group_recv.at[step],
            {GROUP: lax.rem(self.group + step, self.groups)},
        )

    def partners(self):
        return [
            {FRAME: lax.rem(self.frame + step, self.frames_axis)} for step in range(1, self.frames_axis)
        ] + [{GROUP: lax.rem(self.group + step, self.groups)} for step in range(1, self.groups)]

    def start(self):
        for step in range(1, self.frames_axis):
            self.frame_copy(step).start()

    def spread(self):
        for step in range(1, self.frames_axis):
            self.frame_copy(step).wait_recv()
        summed = self.source[...].astype(WIDE)
        for step in range(1, self.frames_axis):
            summed = summed + self.near[step - 1].astype(WIDE)
        self.every[self.group] = summed.astype(NARROW)
        for step in range(1, self.groups):
            self.group_copy(step).start()

    def finish(self):
        for step in range(1, self.frames_axis):
            self.frame_copy(step).wait_send()
        for step in range(1, self.groups):
            self.group_copy(step).wait_recv()
            self.group_copy(step).wait_send()

    @staticmethod
    def scratch(groups, frames_axis, shape):
        dma = pltpu.SemaphoreType.DMA
        return (
            [pltpu.VMEM((max(frames_axis - 1, 1),) + shape, NARROW)]
            + [dma((frames_axis,))] * 2
            + [dma((groups,))] * 2
        )


def grad_tile(first, second, result, start, size):
    result[start : start + size] = dot(first[:, start : start + size], second[...], 0, 0).astype(NARROW)


def can_scatter(groups, frames_axis, width):
    return groups % 2 == 0 and width % (16 * groups * frames_axis) == 0


def vmem(count):
    return [pl.BlockSpec(memory_space=pltpu.VMEM)] * count


class Fetch:
    def __init__(self, sources, held, sems):
        self.copies = [
            pltpu.make_async_copy(source, target, sems.at[i]) for i, (source, target) in enumerate(zip(sources, held))
        ]
        self.waiting = list(range(len(self.copies)))
        for copy in self.copies:
            copy.start()

    def __call__(self, *which):
        for i in which or tuple(self.waiting):
            self.copies[i].wait()
            self.waiting.remove(i)

    def again(self, *which):
        for i in which:
            self.copies[i].wait()

    def keep(self, held, results, sems):
        self.stores = [
            pltpu.make_async_copy(source, target, sems.at[i]) for i, (source, target) in enumerate(zip(held, results))
        ]
        self.started = set()

    def store(self, which):
        self.started.add(which)
        self.stores[which].start()

    def flush(self):
        for i, item in enumerate(self.stores):
            if i not in self.started:
                item.start()
        for item in self.stores:
            item.wait()


def fetching_call(kernel, operands, out_shape, scratch_shapes, kernel_id, name, storing=False):
    many, given = len(operands), len(out_shape)

    def body(*refs):
        sources, results, refs = refs[:many], refs[many : many + given], refs[many + given :]
        if storing:
            out_held, out_sems, refs = refs[-given - 1 : -1], refs[-1], refs[: -given - 1]
        held, sems, rest = refs[-many - 1 : -1], refs[-1], refs[: -many - 1]
        fetch = Fetch(sources, held, sems)
        if storing:
            fetch.keep(out_held, results, out_sems)
            kernel(fetch, *held, *out_held, *rest)
            fetch.flush()
        else:
            kernel(fetch, *held, *results, *rest)

    return pl.pallas_call(
        body,
        out_shape=tuple(out_shape),
        in_specs=[pl.BlockSpec(memory_space=pl.ANY)] * many,
        out_specs=tuple([pl.BlockSpec(memory_space=pl.ANY)] * given if storing else vmem(given)),
        scratch_shapes=list(scratch_shapes)
        + [pltpu.VMEM(item.shape, item.dtype) for item in operands]
        + [pltpu.SemaphoreType.DMA((many,))]
        + ([pltpu.VMEM(item.shape, item.dtype) for item in out_shape] if storing else [])
        + ([pltpu.SemaphoreType.DMA((given,))] if storing else []),
        compiler_params=pltpu.CompilerParams(
            collective_id=kernel_id, has_side_effects=True, vmem_limit_bytes=62 * 2**20
        ),
        name=name,
    )(*operands)


class LineGather:
    def __init__(self, count, place, slot_of, sems):
        self.count, self.place, self.last, self.slot_of = count, place, count - 1, slot_of
        self.up_send, self.down_send, self.arrived = sems

    def shift(self, owner, up):
        slot = self.slot_of(owner)
        to = self.place + 1 if up else self.place - 1
        sent = (self.up_send if up else self.down_send).at[owner]
        return remote(slot, slot, sent, self.arrived.at[owner], {LINE: to})

    def start(self):
        @pl.when(self.place < self.last)
        def _():
            self.shift(self.place, True).start()

        @pl.when(self.place > 0)
        def _():
            self.shift(self.place, False).start()

    def arrive(self, distance):
        @pl.when(self.place >= distance)
        def _():
            self.shift(self.place - distance, True).wait_recv()

            @pl.when(self.place < self.last)
            def _():
                self.shift(self.place - distance, True).start()

        @pl.when(self.place + distance <= self.last)
        def _():
            self.shift(self.place + distance, False).wait_recv()

            @pl.when(self.place > 0)
            def _():
                self.shift(self.place + distance, False).start()

    def settle(self):
        for owner in range(self.count):

            @pl.when((self.place < self.last) & (owner <= self.place))
            def _():
                self.shift(owner, True).wait_send()

            @pl.when((self.place > 0) & (owner >= self.place))
            def _():
                self.shift(owner, False).wait_send()


class LineScatter:
    def __init__(self, count, place, pieces, value_of, land, stage, sems):
        self.count, self.place, self.last, self.pieces = count, place, count - 1, pieces
        self.value_of, self.land, self.stage = value_of, land, stage
        self.from_left, self.from_right, self.to_left, self.to_right = sems

    def pass_on(self, owner, piece, right):
        side = 0 if right else 1
        return remote(
            self.stage.at[side, owner, piece],
            self.land.at[side, owner, piece],
            (self.to_right if right else self.to_left).at[owner, piece],
            (self.from_left if right else self.from_right).at[owner, piece],
            {LINE: self.place + 1 if right else self.place - 1},
        )

    def relay(self, distance, right, chosen=None):
        owner = self.place + distance if right else self.place - distance
        source = (self.place == 0) if right else (self.place == self.last)
        side = 0 if right else 1

        @pl.when((owner <= self.last) if right else (owner >= 0))
        def _():
            for piece in chosen if chosen is not None else range(self.pieces):

                @pl.when(source)
                def _():
                    self.stage[side, owner, piece] = self.value_of(owner, piece)

                @pl.when(jnp.logical_not(source))
                def _():
                    self.pass_on(owner, piece, right).wait_recv()
                    self.stage[side, owner, piece] = (
                        self.value_of(owner, piece).astype(WIDE) + self.land[side, owner, piece].astype(WIDE)
                    ).astype(NARROW)

                self.pass_on(owner, piece, right).start()

    def relay_both(self, distance, chosen=None):
        self.relay(distance, True, chosen)
        self.relay(distance, False, chosen)

    def total(self, piece):
        place = self.place

        @pl.when(place > 0)
        def _():
            self.pass_on(place, piece, True).wait_recv()

        @pl.when(place < self.last)
        def _():
            self.pass_on(place, piece, False).wait_recv()

        left_part = jnp.where(place > 0, self.land[0, place, piece].astype(WIDE), 0.0)
        right_part = jnp.where(place < self.last, self.land[1, place, piece].astype(WIDE), 0.0)
        return self.value_of(place, piece).astype(WIDE) + left_part + right_part

    def settle(self):
        for owner in range(self.count):
            for piece in range(self.pieces):

                @pl.when(owner > self.place)
                def _():
                    self.pass_on(owner, piece, True).wait_send()

                @pl.when(owner < self.place)
                def _():
                    self.pass_on(owner, piece, False).wait_send()


def gather_sems(count):
    return [pltpu.SemaphoreType.DMA((count,))] * 3


def scatter_sems(count, pieces):
    return [pltpu.SemaphoreType.DMA((count, pieces))] * 4


def line_sum(count, place, part_ref, land, cross, stage, total, sems, consume, plan=(), make=None, pieces=1):
    in_send, land_recv, cross_recv, out_send, out_recv = sems
    depth = part_ref.shape[0] // CHUNKS
    half = count // 2
    left = place < half
    level = jnp.where(left, place, count - 1 - place)
    inner = jnp.where(left, place + 1, place - 1)
    outer = jnp.where(left, place - 1, place + 1)
    is_end, is_middle = level == 0, level == half - 1

    def rows_of(chunk):
        return pl.ds(pl.multiple_of(chunk * depth, depth), depth)

    def inward(chunk):
        rows = rows_of(chunk)
        return remote(stage.at[rows], land.at[rows], in_send.at[chunk], land_recv.at[chunk], {LINE: inner})

    def across(chunk):
        rows = rows_of(chunk)
        return remote(stage.at[rows], cross.at[rows], in_send.at[chunk], cross_recv.at[chunk], {LINE: inner})

    def outward(chunk):
        rows = rows_of(chunk)
        return remote(total.at[rows], total.at[rows], out_send.at[chunk], out_recv.at[chunk], {LINE: outer})

    def send_in(chunk):
        @pl.when(is_middle)
        def _():
            across(chunk).start()

        @pl.when(jnp.logical_not(is_middle))
        def _():
            inward(chunk).start()

    def gather_in(chunk):
        rows = rows_of(chunk)
        inward(chunk).wait_recv()
        stage[rows] = (part_ref[rows].astype(WIDE) + land[rows].astype(WIDE)).astype(NARROW)
        send_in(chunk)

    def finish(chunk):
        rows = rows_of(chunk)

        @pl.when(is_middle)
        def _():
            across(chunk).wait_recv()
            total[rows] = (stage[rows].astype(WIDE) + cross[rows].astype(WIDE)).astype(NARROW)

        @pl.when(jnp.logical_not(is_middle))
        def _():
            outward(chunk).wait_recv()

        @pl.when(jnp.logical_not(is_end))
        def _():
            outward(chunk).start()

        consume(rows)

    def begin(chunk, carry):
        rows = rows_of(chunk)
        stage[rows] = part_ref[rows]
        send_in(chunk)
        return carry

    def step(number, carry):
        for when, work in plan:

            @pl.when((number == when) & (jnp.logical_not(is_end) | (when > AT_ONCE)))
            def _():
                work()

        @pl.when(jnp.logical_not(is_end) & (number < CHUNKS))
        def _():
            gather_in(number)

        @pl.when(number >= LAG)
        def _():
            finish(number - LAG)

        return carry

    for piece in range(pieces):
        if make is not None:
            make(piece)

        @pl.when(is_end)
        def _():
            lax.fori_loop(piece * CHUNKS // pieces, (piece + 1) * CHUNKS // pieces, begin, 0)

    @pl.when(is_end)
    def _():
        for when, work in plan:
            if when <= AT_ONCE:
                work()

    lax.fori_loop(0, CHUNKS + LAG, step, 0)

    def settle(chunk, carry):
        @pl.when(is_middle)
        def _():
            across(chunk).wait_send()

        @pl.when(jnp.logical_not(is_middle))
        def _():
            inward(chunk).wait_send()

        @pl.when(jnp.logical_not(is_end))
        def _():
            outward(chunk).wait_send()

        return carry

    lax.fori_loop(0, CHUNKS, settle, 0)


def forward_kernel(
    count, frames, fetch, hidden_ref, in_ref, base_ref, rows_ref, outproj_ref,
    out_ref, next_ref, normed_ref, packed_ref, heads_ref,
    part_ref, key_rows, value_rows, probs_low, land, cross, stage, *sems
):
    place = lax.axis_index(LINE)
    greet_line(place, count)
    fetch(0, 1, 4)
    patches = hidden_ref.shape[0] // frames
    local = heads_ref.shape[1]

    def make(frame):
        rows = slice(frame * patches, (frame + 1) * patches)
        packed = dot(hidden_ref[rows], in_ref[...], 1, 1).astype(NARROW)
        packed_ref[rows] = packed
        asked, keys, values = (packed[:, i * local : (i + 1) * local] for i in range(3))
        spread_heads(keys, key_rows)
        spread_heads(values, value_rows)
        for head in range(local // HD):
            spot = slice(head * patches, (head + 1) * patches)
            scores = HD ** (-0.5) * dot(asked, key_rows[spot], 1, 1)
            raised = jnp.exp(scores - jnp.max(scores, axis=-1, keepdims=True))
            probs_low[:, spot] = (raised * (1.0 / jnp.sum(raised, axis=-1, keepdims=True))).astype(NARROW)
        found = dot(probs_low[...], value_rows[...], 1, 0).astype(NARROW)
        heads_ref[rows] = found
        part_ref[rows] = dot(found, outproj_ref[...], 1, 0).astype(NARROW)
        if frame == frames - 1:
            fetch()

    def consume(rows):
        gate, gain, shift = (rows_ref[i : i + 1] for i in (2, 10, 3))
        moved = base_ref[rows] + gate * out_ref[rows].astype(WIDE)
        next_ref[rows] = moved
        normed_ref[rows] = (norm_parts(moved)[0] * gain + shift).astype(NARROW)

    line_sum(count, place, part_ref, land, cross, stage, out_ref, sems, consume, make=make, pieces=frames)


def backward_kernel(count, groups, frames_axis, widths, fetch, *refs):
    part_ref, base_ref, grad_ref, below_ref, rows_ref, *refs = refs
    pairs, refs = [refs[0:2], refs[2:4]], refs[4:]
    sources, refs = refs[: len(widths) - 1], refs[max(len(widths) - 1, 0) :]
    moved_ref, low_ref, sums_ref, *refs = refs
    many = sum(len(columns) for columns in widths)
    results, refs = refs[:many], refs[many:]
    product_ref, total, land, cross, stage, tally, *refs = refs
    sems, scratch = refs[:5], refs[5:]
    place = lax.axis_index(LINE)
    early = Products(pairs, product_ref).work()
    scatters = Scatters(
        groups, frames_axis, [*sources, product_ref] if widths else [], widths, results, scratch
    )
    greet_line(place, count, 0, scatters.partners() if widths else ())
    fetch()
    plan = [(0, work) for work in early]
    if widths:
        scatters.items[0].start()
        first, last = scatters.folds(0), scatters.folds(len(widths) - 1)
        plan += [(1, scatters.items[-1].start), (2, first[0]), (4, last[0]), (9, first[1]), (14, last[1])]
    gain, gate = (rows_ref[i : i + 1] for i in (10, 2))
    tally[...] = jnp.zeros_like(tally)

    def consume(rows):
        grads = total[rows].astype(WIDE)
        normal, spread = norm_parts(base_ref[rows])
        moved = grad_ref[rows] + norm_pull(grads * gain, normal, spread)
        moved_ref[rows] = moved
        low_ref[rows] = (gate * moved).astype(NARROW)
        for i, terms in enumerate((grads, grads * normal, moved * below_ref[rows].astype(WIDE))):
            tally[i] += jnp.sum(terms.reshape(-1, 8, terms.shape[-1]), axis=0)

    line_sum(count, place, part_ref, land, cross, stage, total, sems, consume, plan)
    sums_ref[...] = jnp.zeros_like(sums_ref)
    for i in range(3):
        sums_ref[i : i + 1] = jnp.sum(tally[i], axis=0, keepdims=True)
    scatters.finish()


def line_sems():
    return [pltpu.SemaphoreType.DMA((CHUNKS,))] * 5


def call_forward(count, frames, hidden, in_w, base, rows, out_w):
    shape, local = hidden.shape, out_w.shape[0]
    patches = shape[0] // frames
    wide_keys = local // HD * patches
    return fetching_call(
        functools.partial(forward_kernel, count, frames),
        [hidden, in_w, base, rows, out_w],
        (
            jax.ShapeDtypeStruct(shape, NARROW),
            jax.ShapeDtypeStruct(shape, WIDE),
            jax.ShapeDtypeStruct(shape, NARROW),
            jax.ShapeDtypeStruct((shape[0], 3 * local), NARROW),
            jax.ShapeDtypeStruct((shape[0], local), NARROW),
        ),
        [
            pltpu.VMEM(shape, NARROW),
            pltpu.VMEM((wide_keys, local), NARROW),
            pltpu.VMEM((wide_keys, local), NARROW),
            pltpu.VMEM((patches, wide_keys), NARROW),
        ]
        + [pltpu.VMEM(shape, NARROW)] * 3
        + line_sems(),
        1,
        "forward_sum",
    )


def call_backward(count, groups, frames_axis, part, base, grad, below, rows, pairs, sources, widths):
    shape = part.shape
    results, scratch = Scatters.shapes(groups, frames_axis, shape[1], widths)
    product = (shape[1], sum(second.shape[1] for _, second in pairs))
    if not widths:
        results = [jax.ShapeDtypeStruct(product, NARROW)]
    return fetching_call(
        functools.partial(backward_kernel, count, groups, frames_axis, widths),
        [part, base, grad, below, rows, *(item for pair in pairs for item in pair), *sources],
        (
            jax.ShapeDtypeStruct(shape, WIDE),
            jax.ShapeDtypeStruct(shape, NARROW),
            jax.ShapeDtypeStruct((8, shape[1]), WIDE),
            *results,
        ),
        ([pltpu.VMEM(product, NARROW)] if widths else [])
        + [pltpu.VMEM(shape, NARROW)] * 4
        + [pltpu.VMEM((3, 8, shape[1]), WIDE)]
        + line_sems()
        + scratch,
        2,
        "backward_sum",
    )


def head_mask(head, shape):
    lane = lax.broadcasted_iota(jnp.int32, shape, len(shape) - 1)
    return (lane >= head * HD) & (lane < (head + 1) * HD)


def spread_heads(values, result):
    rows = values.shape[0]
    for head in range(values.shape[1] // HD):
        kept = jnp.where(head_mask(head, values.shape), values.astype(WIDE), 0.0)
        result[head * rows : (head + 1) * rows] = kept.astype(NARROW)


def collect_heads(values, rows):
    found = jnp.zeros((rows, values.shape[1]), WIDE)
    for head in range(values.shape[0] // rows):
        found = jnp.where(head_mask(head, found.shape), values[head * rows : (head + 1) * rows], found)
    return found


def spatial_backward(given, asked, keys, values, key_rows, value_rows, probs_low, scores_low):
    rows, scale = asked.shape[0], HD ** (-0.5)
    heads = asked.shape[1] // HD
    spread_heads(keys, key_rows)
    spread_heads(values, value_rows)
    for head in range(heads):
        spot = slice(head * rows, (head + 1) * rows)
        scores = scale * dot(asked, key_rows[spot], 1, 1)
        raised = jnp.exp(scores - jnp.max(scores, axis=-1, keepdims=True))
        probs = raised * (1.0 / jnp.sum(raised, axis=-1, keepdims=True))
        pulled = dot(given, value_rows[spot], 1, 1)
        moved = probs * (pulled - jnp.sum(pulled * probs, axis=-1, keepdims=True))
        probs_low[:, spot] = probs.astype(NARROW)
        scores_low[:, spot] = moved.astype(NARROW)
    grad_query = scale * dot(scores_low[...], key_rows[...], 1, 0)
    grad_keys = scale * collect_heads(dot(scores_low[...], asked, 0, 0), rows)
    grad_values = collect_heads(dot(probs_low[...], given, 0, 0), rows)
    return grad_query, grad_keys, grad_values


def closing_kernel(count, groups, frames_axis, frames, widths, fetch, *refs):
    (
        low_ref, base_ref, grad_ref, gate_part, rows_ref, packed_ref, heads_ref, hidden_ref, in_ref, out_ref,
        text_ref, sums_temporal, sums_middle, side_ref, *refs,
    ) = refs
    sources, refs = refs[: len(widths) - 1], refs[max(len(widths) - 1, 0) :]
    latent_ref, every_ref, text_all, *refs = refs
    many = sum(len(columns) for columns in widths)
    results, refs = refs[:many], refs[many:]
    (
        product_ref, part_ref, grad_packed, key_rows, value_rows, probs_low, scores_low,
        land, stage, line_rows, own_rows, tally, *refs,
    ) = refs
    line_send, line_recv, all_send, all_recv = refs[4:8]
    place, group, here = (lax.axis_index(axis) for axis in (LINE, GROUP, FRAME))
    last = count - 1
    share = latent_ref.shape[1]
    local = out_ref.shape[0]
    everyone = groups * frames_axis
    rank = group * frames_axis + here
    products = Products([(hidden_ref, grad_packed), (low_ref, heads_ref)], product_ref)
    scatters = Scatters(groups, frames_axis, [*sources, product_ref] if widths else [], widths, results, refs[13:])
    exchange = GroupExchange(groups, frames_axis, text_ref, text_all, refs[8:13])

    def member(ahead):
        to = lax.rem(rank + ahead, everyone)
        return {GROUP: lax.div(to, frames_axis), FRAME: lax.rem(to, frames_axis)}

    def neighbour(ahead):
        return {LINE: lax.rem(place + ahead, count)}

    barrier = pltpu.get_barrier_semaphore()

    def greet(ahead, carry):
        pl.semaphore_signal(barrier, inc=1, device_id=member(ahead), device_id_type=MESH)
        return carry

    for ahead in range(1, count):
        pl.semaphore_signal(barrier, inc=1, device_id=neighbour(ahead), device_id_type=MESH)
    lax.fori_loop(1, everyone, greet, 0)
    pl.semaphore_wait(barrier, last + everyone - 1)
    fetch(0, 5, 8, 9, 10)

    def rows_of(owner):
        return pl.ds(pl.multiple_of(owner * share, share), share)

    passing = LineScatter(
        count, place, frames, lambda owner, frame: part_ref[frame, rows_of(owner)], land, stage, refs[0:4]
    )
    patches = base_ref.shape[1]
    exchange.start()
    for frame in range(frames):
        rows = slice(frame * patches, (frame + 1) * patches)
        given = dot(low_ref[rows], out_ref[...], 1, 1).astype(NARROW)
        asked, keys, values = (packed_ref[rows, i * local : (i + 1) * local] for i in range(3))
        parts = jnp.zeros(part_ref.shape[1:], WIDE)
        found = spatial_backward(given, asked, keys, values, key_rows, value_rows, probs_low, scores_low)
        for i, item in enumerate(found):
            low = item.astype(NARROW)
            grad_packed[rows, i * local : (i + 1) * local] = low
            parts = parts + dot(low, in_ref[i * local : (i + 1) * local], 1, 0)
        part_ref[frame] = parts.astype(NARROW)
        passing.relay_both(last, (frame,))
        if frame == 0:
            exchange.spread()
    if last > 1:
        passing.relay_both(last - 1, (0,))
    fetch()
    for work in products.work():
        work()
    if widths:
        scatters.items[-1].start()
    if last > 1:
        passing.relay_both(last - 1, tuple(range(1, frames)))

    tally[...] = jnp.zeros_like(tally)
    depth = 32
    blocks = base_ref.shape[1] // depth

    def add_rows(number, carry):
        frame, rows = lax.div(number, blocks), pl.ds(pl.multiple_of(lax.rem(number, blocks) * depth, depth), depth)
        normal = norm_parts(base_ref[frame, rows])[0]
        grads = part_ref[frame, rows].astype(WIDE)
        for i, terms in enumerate((grads, grads * normal)):
            tally[i] += jnp.sum(terms.reshape(-1, 8, terms.shape[-1]), axis=0)
        return carry

    lax.fori_loop(0, frames * blocks, add_rows, 0)
    line_rows[place] = jnp.zeros(line_rows.shape[1:], WIDE)
    line_rows[place, 2:3] = gate_part[0:1]
    for i in range(2):
        line_rows[place, i : i + 1] = jnp.sum(tally[i], axis=0, keepdims=True)

    def line_copy(ahead):
        return remote(
            line_rows.at[place], line_rows.at[place], line_send.at[ahead], line_recv.at[ahead], neighbour(ahead)
        )

    def all_copy(ahead):
        return remote(
            own_rows, every_ref.at[rank], all_send.at[ahead], all_recv.at[ahead], member(ahead)
        )

    for ahead in range(1, count):
        line_copy(ahead).start()
    if widths:
        scatters.items[-1].first_round()
    for distance in range(last - 2, 0, -1):
        passing.relay_both(distance)
    for ahead in range(1, count):
        line_copy(ahead).wait_recv()
    summed = line_rows[0]
    for i in range(1, count):
        summed = summed + line_rows[i]
    own_rows[0:8] = summed
    picked = ((sums_temporal, (2, 0, 1)), (sums_middle, (3, 0, 1, 2)), (side_ref, (0,)))
    for i, (source, row) in enumerate((source, row) for source, rows in picked for row in rows):
        own_rows[8 + i : 9 + i] = source[row : row + 1]
    every_ref[rank] = own_rows[...]

    def send_rows(ahead, carry):
        all_copy(ahead).start()
        return carry

    lax.fori_loop(1, everyone, send_rows, 0)
    if widths:
        scatters.items[-1].second_round()

    own = rows_of(place)
    for frame in range(frames):
        grads = passing.total(frame)
        normal, spread = norm_parts(base_ref[frame, own])
        latent_ref[frame] = (
            grad_ref[frame, own] + norm_pull(grads * rows_ref[9:10], normal, spread)
        ).astype(NARROW)

    passing.settle()
    for ahead in range(1, count):
        line_copy(ahead).wait_send()

    def settle(ahead, carry):
        all_copy(ahead).wait_recv()
        all_copy(ahead).wait_send()
        return carry

    lax.fori_loop(1, everyone, settle, 0)
    exchange.finish()
    scatters.finish()


def call_closing(
    count, groups, frames_axis, low, base, grad, gate_part, rows, packed, heads, hidden, in_w, out_w, text, sums, sources,
    widths,
):
    frames, patches, features = base.shape
    everyone = groups * frames_axis
    share = patches // count
    local = out_w.shape[0]
    results, scratch = Scatters.shapes(groups, frames_axis, features, widths)
    product = (features, packed.shape[1] + local)
    if not widths:
        results = [jax.ShapeDtypeStruct(product, NARROW)]
    dma = pltpu.SemaphoreType.DMA
    wide_keys = local // HD * patches
    return fetching_call(
        functools.partial(closing_kernel, count, groups, frames_axis, frames, widths),
        [low, base, grad, gate_part, rows, packed, heads, hidden, in_w, out_w, text, *sums, *sources],
        (
            jax.ShapeDtypeStruct((frames, share, features), NARROW),
            jax.ShapeDtypeStruct((everyone, 16, features), WIDE),
            jax.ShapeDtypeStruct((groups,) + text.shape, NARROW),
            *results,
        ),
        ([pltpu.VMEM(product, NARROW)] if widths else [])
        + [
            pltpu.VMEM((frames, patches, features), NARROW),
            pltpu.VMEM(packed.shape, NARROW),
            pltpu.VMEM((wide_keys, local), NARROW),
            pltpu.VMEM((wide_keys, local), NARROW),
            pltpu.VMEM((patches, wide_keys), NARROW),
            pltpu.VMEM((patches, wide_keys), NARROW),
            pltpu.VMEM((2, count, frames, share, features), NARROW),
            pltpu.VMEM((2, count, frames, share, features), NARROW),
            pltpu.VMEM((count, 8, features), WIDE),
            pltpu.VMEM((16, features), WIDE),
            pltpu.VMEM((2, 8, features), WIDE),
        ]
        + scatter_sems(count, frames)
        + [dma((count,))] * 2
        + [dma((everyone,))] * 2
        + GroupExchange.scratch(groups, frames_axis, text.shape)
        + scratch,
        4,
        "closing",
    )


def finishing_kernel(groups, frames_axis, modulation_rows, layouts, small_ref, ada_ref, text_ref, captions_ref, *refs):
    many = len(layouts)
    sources, refs = refs[:many], refs[many:]
    ada_out, table_out, gain_out, caption_out, *results, sems = refs
    moves = [
        pltpu.make_async_copy(source, result, sems.at[i])
        for i, (source, result, layout) in enumerate(zip(sources, results, layouts))
        if layout == 0
    ]
    for move in moves:
        move.start()
    local = table_out.shape[1]
    buckets = table_out.shape[0]
    column = ada_out.shape[1]
    features = small_ref.shape[2]
    rank = lax.axis_index(GROUP) * frames_axis + lax.axis_index(FRAME)

    def over_frames(group, row):
        first = group * frames_axis
        found = small_ref[first, row : row + 1]
        for other in range(1, frames_axis):
            found = found + small_ref[first + other, row : row + 1]
        return found

    gain = over_frames(0, 14)
    for group in range(1, groups):
        gain = gain + over_frames(group, 14)
    for i in range(gain_out.shape[0]):
        gain_out[i : i + 1] = gain[:, i * 128 : (i + 1) * 128]

    side = jnp.concatenate([small_ref[group * frames_axis, 15:16] for group in range(groups)], axis=0)
    cond, chosen = side[:, 0:local], side[:, local : local + buckets]
    below = 1.0 / (1.0 + jnp.exp(-cond))
    act_low = (cond * below).astype(NARROW)
    act_twice = jnp.concatenate([act_low, act_low], axis=0)
    where = lax.broadcasted_iota(jnp.int32, (features, column), 0)
    which = lax.broadcasted_iota(jnp.int32, (features, column), 1) + rank * column
    select = jnp.where(where == which, 1.0, 0.0).astype(NARROW)
    grad_act = jnp.zeros((2 * groups, local), WIDE)
    for k, row in enumerate(modulation_rows):
        rows = jnp.concatenate([over_frames(group, row) for group in range(groups)], axis=0)
        pair = jnp.concatenate(split_pair(rows), axis=0)
        grad_act = grad_act + dot(pair, ada_ref[k], 1, 1)
        columns = dot(pair, select, 1, 0).astype(NARROW)
        ada_out[k] = dot(columns, act_twice, 0, 0)
    slope = below * (1.0 + cond * (1.0 - below))
    grad_cond = (grad_act[0:groups] + grad_act[groups:]) * slope
    spread = jnp.concatenate(split_pair(grad_cond), axis=0)
    chosen = chosen.astype(NARROW)
    table_out[...] = dot(jnp.concatenate([chosen, chosen], axis=0), spread, 0, 0)

    slots = captions_ref.shape[1]
    caption = dot(text_ref[0, :, 0:slots], captions_ref[0], 1, 0)
    for group in range(1, groups):
        caption = caption + dot(text_ref[group, :, 0:slots], captions_ref[group], 1, 0)
    caption_out[...] = caption
    for source, result, layout in zip(sources, results, layouts):
        if layout > 0:
            parts = source.shape[1] // local
            for i in range(parts):
                values = source[:, i * local : (i + 1) * local]
                if layout == 1:
                    result[i] = values
                else:
                    result[:, i] = values
    for move in moves:
        move.wait()


def call_finishing(groups, frames_axis, buckets, modulation_rows, layouts, small, ada, text, captions, sources):
    parts, local, features = ada.shape
    block = features // (groups * frames_axis)

    def shape_of(source, layout):
        n = source.shape[1] // local
        return (source.shape, (n, source.shape[0], local), (source.shape[0], n, local))[layout]

    results = [
        jax.ShapeDtypeStruct((parts, block, local), WIDE),
        jax.ShapeDtypeStruct((buckets, local), WIDE),
        jax.ShapeDtypeStruct((features // 128, 128), WIDE),
        jax.ShapeDtypeStruct((local, captions.shape[2]), WIDE),
    ]
    results += [
        jax.ShapeDtypeStruct(shape_of(source, layout), source.dtype) for source, layout in zip(sources, layouts)
    ]
    places = [pl.BlockSpec(memory_space=pltpu.VMEM if layout else pl.ANY) for layout in layouts]
    return pl.pallas_call(
        functools.partial(finishing_kernel, groups, frames_axis, modulation_rows, layouts),
        out_shape=tuple(results),
        in_specs=vmem(4 + len(sources)),
        out_specs=tuple(vmem(4) + places),
        scratch_shapes=[pltpu.SemaphoreType.DMA((len(sources),))],
        compiler_params=pltpu.CompilerParams(vmem_limit_bytes=62 * 2**20),
        name="finishing",
    )(small, ada, text, captions, *sources)


def opening_kernel(
    count, groups, frames_axis, bucket_ref, clip_ref, window_ref, counts_ref, latent_ref, table_ref, gain_ref,
    ada_ref, captions_ref, caption_full, caption_w,
    base_ref, normed_ref, mods_ref, text_out, side_out, window_out, bias_out, spread_ref,
    caption_here, caption_here_w, caption_sem, land, ada, mine, others,
    up_send, down_send, land_recv, ada_sem, mods_send, mods_recv, cap_send, cap_recv, cap_local,
):
    place = lax.axis_index(LINE)
    group = lax.axis_index(GROUP)
    here = lax.axis_index(FRAME)
    last = count - 1
    width = spread_ref.shape[2]
    parts = ada_ref.shape[0]
    share = latent_ref.shape[1]

    loads = [pltpu.make_async_copy(ada_ref.at[k], ada.at[k], ada_sem.at[k]) for k in range(parts)]
    for load in loads:
        load.start()
    text_loads = [
        pltpu.make_async_copy(caption_full, caption_here, caption_sem.at[0]),
        pltpu.make_async_copy(caption_w, caption_here_w, caption_sem.at[1]),
    ]
    for load in text_loads:
        load.start()

    barrier = pltpu.get_barrier_semaphore()
    for ahead in range(1, count):
        pl.semaphore_signal(
            barrier, inc=1, device_id={LINE: lax.rem(place + ahead, count)}, device_id_type=MESH
        )
    for ahead in range(1, groups):
        pl.semaphore_signal(
            barrier, inc=1, device_id={GROUP: lax.rem(group + ahead, groups)}, device_id_type=MESH
        )
    pl.semaphore_wait(barrier, count - 1 + groups - 1)

    def shift(owner, up):
        to = place + 1 if up else place - 1
        return remote(
            land.at[owner], land.at[owner], (up_send if up else down_send).at[owner], land_recv.at[owner], {LINE: to}
        )

    land[place] = latent_ref[...]

    @pl.when(place < last)
    def _():
        shift(place, True).start()

    @pl.when(place > 0)
    def _():
        shift(place, False).start()

    def caption_block(to):
        if len(captions_ref.shape) == 3:
            return captions_ref.at[to]
        first = pl.multiple_of((to * frames_axis + here) * width, width)
        return captions_ref.at[:, pl.ds(first, width)]

    def caption_copy(ahead):
        to = lax.rem(group + ahead, groups)
        return remote(
            caption_block(to),
            spread_ref.at[group],
            cap_send.at[ahead],
            cap_recv.at[ahead],
            {GROUP: to},
        )

    own_caption = pltpu.make_async_copy(caption_block(group), spread_ref.at[group], cap_local)
    own_caption.start()
    for ahead in range(1, groups):
        caption_copy(ahead).start()

    def arrive(distance):
        @pl.when(place >= distance)
        def _():
            shift(place - distance, True).wait_recv()

            @pl.when(place < last)
            def _():
                shift(place - distance, True).start()

        @pl.when(place + distance <= last)
        def _():
            shift(place + distance, False).wait_recv()

            @pl.when(place > 0)
            def _():
                shift(place + distance, False).start()

    buckets, local = table_ref.shape
    frames = latent_ref.shape[0]
    is_row = lax.broadcasted_iota(jnp.int32, (buckets, local), 0) == bucket_ref[0]
    cond = jnp.sum(jnp.where(is_row, table_ref[...].astype(WIDE), 0.0), axis=0, keepdims=True)
    act = jnp.broadcast_to(swish_act(cond), (16, local)).astype(NARROW)
    side_out[...] = jnp.zeros_like(side_out)
    side_out[0:1, 0:local] = cond
    is_column = lax.broadcasted_iota(jnp.int32, (1, buckets), 1) == bucket_ref[0]
    side_out[0:1, local : local + buckets] = jnp.where(is_column, 1.0, 0.0)
    total = clip_ref.shape[1]
    text_length = caption_full.shape[0] // counts_ref.shape[1]
    lane = lax.broadcasted_iota(jnp.int32, bias_out.shape[1:], 1)
    for frame in range(frames):
        own = here * frames + frame
        for offset in range(WIN):
            other = own + offset - 2
            same = clip_ref[0, jnp.clip(other, 0, total - 1)] == clip_ref[0, own]
            reads = same & (other >= 0) & (other < total)
            if offset != 2:
                reads = reads & (window_ref[0, frame, offset] == 1)
            row = frame * WIN + offset
            window_out[row : row + 1] = jnp.full((1, window_out.shape[1]), jnp.where(reads, 0.0, NEGATIVE))
        bias = jnp.full(bias_out.shape[1:], NEGATIVE)
        for clip in range(counts_ref.shape[1]):
            first = clip * text_length
            end = jnp.where(clip_ref[0, own] == clip, first + counts_ref[0, clip], first)
            bias = jnp.where((lane >= first) & (lane < end), 0.0, bias)
        bias_out[frame] = bias

    def weigh(k):
        loads[k].wait()
        product = dot(act, ada[k], 1, 0)
        mine[k : k + 1] = product[0:1]

    def mods_copy(ahead):
        return remote(
            mine, others.at[place], mods_send.at[ahead], mods_recv.at[ahead], {LINE: lax.rem(place + ahead, count)}
        )

    mine[...] = jnp.zeros_like(mine)
    cut = parts // 2 + 1
    for k in range(cut):
        weigh(k)
    arrive(1)
    for k in range(cut, parts):
        weigh(k)
    for ahead in range(1, count):
        mods_copy(ahead).start()
    others[place] = mine[...]
    for load in text_loads:
        load.wait()
    text_here = dot(caption_here_w[...], caption_here[...], 1, 1).astype(NARROW)
    slots = text_here.shape[1]
    text_out[:, 0:slots] = text_here
    if text_out.shape[1] > slots:
        text_out[:, slots:] = jnp.zeros((text_out.shape[0], text_out.shape[1] - slots), NARROW)
    for distance in range(2, count - 1):
        arrive(distance)
    for ahead in range(1, count):
        mods_copy(ahead).wait_recv()
    mods = others[0]
    for i in range(1, count):
        mods = mods + others[i]
    mods_ref[...] = mods
    for i, row in enumerate((1, 4, 7)):
        mods_ref[9 + i : 10 + i] = 1.0 + mods[row : row + 1]
    for i in range(gain_ref.shape[0]):
        mods_ref[12:13, i * 128 : (i + 1) * 128] = gain_ref[i : i + 1].astype(WIDE)
    gain = 1.0 + mods[1:2]
    shift_row = mods[0:1]

    def norm_owner(owner):
        for f in range(latent_ref.shape[0]):
            values = land[owner, f].astype(WIDE)
            rows = pl.ds(pl.multiple_of(owner * share, share), share)
            base_ref[f, rows] = values
            normed_ref[f, rows] = (norm_parts(values)[0] * gain + shift_row).astype(NARROW)

    def near(distance):
        @pl.when(place >= distance)
        def _():
            norm_owner(place - distance)

        @pl.when(place + distance <= last)
        def _():
            norm_owner(place + distance)

    norm_owner(place)
    for distance in range(1, count - 1):
        near(distance)
    if count > 2:
        arrive(count - 1)
    near(count - 1)

    for owner in range(count):

        @pl.when((place < last) & (owner <= place))
        def _():
            shift(owner, True).wait_send()

        @pl.when((place > 0) & (owner >= place))
        def _():
            shift(owner, False).wait_send()

    for ahead in range(1, count):
        mods_copy(ahead).wait_send()
    for ahead in range(1, groups):
        caption_copy(ahead).wait_send()
        caption_copy(ahead).wait_recv()
    own_caption.wait()


def call_opening(count, groups, frames_axis, scalars, latent, table, gain, ada, captions, caption_w):
    frames, share, features = latent.shape
    parts = ada.shape[0]
    length, text_width = captions.shape
    width = text_width // (groups * frames_axis)
    caption_full = captions
    if width % 128:
        blocks = captions.reshape(length, groups, frames_axis, width)
        captions = jnp.transpose(
            lax.dynamic_index_in_dim(blocks, lax.axis_index(FRAME), 2, keepdims=False), (1, 0, 2)
        )
    full = (frames, share * count, features)
    dma = pltpu.SemaphoreType.DMA
    anywhere = pl.BlockSpec(memory_space=pl.ANY)
    return pl.pallas_call(
        functools.partial(opening_kernel, count, groups, frames_axis),
        out_shape=(
            jax.ShapeDtypeStruct(full, WIDE),
            jax.ShapeDtypeStruct(full, NARROW),
            jax.ShapeDtypeStruct((16, features), WIDE),
            jax.ShapeDtypeStruct((caption_w.shape[0], length + -length % 128), NARROW),
            jax.ShapeDtypeStruct((8, features), WIDE),
            jax.ShapeDtypeStruct((frames * WIN, 128), WIDE),
            jax.ShapeDtypeStruct((frames, 8, length + -length % 128), WIDE),
            jax.ShapeDtypeStruct((groups, length, width), NARROW),
        ),
        in_specs=[pl.BlockSpec(memory_space=pltpu.SMEM)] * 4 + vmem(3) + [anywhere] * 4,
        out_specs=tuple(vmem(7) + [anywhere]),
        scratch_shapes=[
            pltpu.VMEM(caption_full.shape, NARROW),
            pltpu.VMEM(caption_w.shape, NARROW),
            dma((2,)),
            pltpu.VMEM((count, frames, share, features), NARROW),
            pltpu.VMEM(ada.shape, NARROW),
            pltpu.VMEM((16, features), WIDE),
            pltpu.VMEM((count, 16, features), WIDE),
            dma((count,)),
            dma((count,)),
            dma((count,)),
            dma((parts,)),
            dma((count,)),
            dma((count,)),
            dma((groups,)),
            dma((groups,)),
            dma,
        ],
        compiler_params=pltpu.CompilerParams(
            collective_id=3, has_side_effects=True, vmem_limit_bytes=62 * 2**20
        ),
        name="opening",
    )(*scalars, latent, table, gain, ada, captions, caption_full, caption_w)


STAGES = 4
MIDDLE_ROWS = 32
MIDDLE_LAG = 3


def gelu_both(values):
    square = values * values
    bent = jnp.tanh(0.7978845608028654 * (values + 0.044715 * values * square))
    slope = 0.5 * (1.0 + bent) + 0.5 * values * (1.0 - bent * bent) * (
        0.7978845608028654 * (1.0 + 3.0 * 0.044715 * square)
    )
    return 0.5 * values * (1.0 + bent), slope


def middle_kernel(count, groups, frames_axis, frames, scattered, fetch, *refs):
    (
        first_ref, base_ref, cotangent_ref, rows_ref, bias_ref,
        text_ref, text_w, query_w, out_w, up_w, down_w,
        base_three, grad_two, low_two, low_three, normed_three, heads_out, grad_query,
        grad_keys, grad_values, sums_ref, extra_part, down_grad, up_result,
        keys_ref, values_ref,
        normed_four, low_four, active, grad_inner, base_two, branch_two, query, grad_heads, part, mixed, tally,
        land, stage, total, cross, in_send, land_recv, cross_recv, out_send, out_recv, *scratch,
    ) = refs
    place = lax.axis_index(LINE)
    if scattered:
        up_grad, *scratch = scratch
        scatters = Scatters(groups, frames_axis, [up_grad], [[up_grad.shape[1]]], [up_result], scratch)
        asides = scatters.items
        greet_line(place, count, 0, asides[0].partners())
    else:
        up_grad, asides = up_result, []
        greet_line(place, count)
    fetch(0, 1, 3)
    half = count // 2
    left = place < half
    level = jnp.where(left, place, count - 1 - place)
    inner = jnp.where(left, place + 1, place - 1)
    outer = jnp.where(left, place - 1, place + 1)
    is_end, is_middle = level == 0, level == half - 1
    inside = jnp.logical_not(is_end)
    patches = base_ref.shape[0] // frames
    chunks = patches // MIDDLE_ROWS
    slots = STAGES * frames
    scale = HD ** (-0.5)
    width = bias_ref.shape[2]
    local = query_w.shape[0]
    half_heads = local // HD // 2
    tile = up_w.shape[1] // 3
    gate_two, cross_gain, gain_three, shift_three, gate_three = (
        rows_ref[i : i + 1] for i in (5, 12, 11, 6, 8)
    )

    def where_of(slot, chunk):
        rows = pl.ds(pl.multiple_of(lax.rem(slot, frames) * patches + chunk * MIDDLE_ROWS, MIDDLE_ROWS), MIDDLE_ROWS)
        return lax.rem(lax.div(slot, frames), 2), rows

    def inward(slot, chunk):
        rows = where_of(slot, chunk)[1]
        return remote(
            stage.at[rows], land.at[rows], in_send.at[slot, chunk], land_recv.at[slot, chunk], {LINE: inner}
        )

    def across(slot, chunk):
        side, rows = where_of(slot, chunk)
        return remote(
            stage.at[rows], cross.at[side, rows], in_send.at[slot, chunk], cross_recv.at[slot, chunk], {LINE: inner}
        )

    def outward(slot, chunk):
        rows = where_of(slot, chunk)[1]
        return remote(
            total.at[rows], total.at[rows], out_send.at[slot, chunk], out_recv.at[slot, chunk], {LINE: outer}
        )

    def own_part(slot, rows):
        return jnp.where(slot < frames, first_ref[rows], part[rows])

    def send_in(slot, chunk):
        @pl.when(is_middle)
        def _():
            across(slot, chunk).start()

        @pl.when(jnp.logical_not(is_middle))
        def _():
            inward(slot, chunk).start()

    def sent(slot, chunk):
        @pl.when(is_middle)
        def _():
            across(slot, chunk).wait_send()

        @pl.when(jnp.logical_not(is_middle))
        def _():
            inward(slot, chunk).wait_send()

        @pl.when(inside)
        def _():
            outward(slot, chunk).wait_send()

    def free(slot, chunk):
        @pl.when(slot >= frames)
        def _():
            sent(slot - frames, chunk)

    def gather_in(slot, chunk):
        rows = where_of(slot, chunk)[1]
        free(slot, chunk)
        inward(slot, chunk).wait_recv()
        stage[rows] = (own_part(slot, rows).astype(WIDE) + land[rows].astype(WIDE)).astype(NARROW)
        send_in(slot, chunk)

    def add_rows(which, terms):
        tally[which] += jnp.sum(terms.reshape(-1, 8, terms.shape[-1]), axis=0)

    def consume(slot, rows, summed):
        number = lax.div(slot, frames)

        @pl.when(number == 0)
        def _():
            branch_two[rows] = summed
            moved = base_ref[rows] + gate_two * summed.astype(WIDE)
            base_two[rows] = moved
            normed_three[rows] = (norm_parts(moved)[0] * cross_gain).astype(NARROW)

        @pl.when(number == 1)
        def _():
            moved = base_two[rows] + summed.astype(WIDE)
            base_three[rows] = moved
            normed_four[rows] = (norm_parts(moved)[0] * gain_three + shift_three).astype(NARROW)
            low_four[rows] = (gate_three * cotangent_ref[rows].astype(WIDE)).astype(NARROW)

        @pl.when(number == 2)
        def _():
            grads = summed.astype(WIDE)
            normal, spread = norm_parts(base_three[rows])
            moved = cotangent_ref[rows].astype(WIDE) + norm_pull(grads * gain_three, normal, spread)
            grad_two[rows] = moved
            low_three[rows] = moved.astype(NARROW)
            add_rows(0, grads)
            add_rows(1, grads * normal)

        @pl.when(number == 3)
        def _():
            grads = summed.astype(WIDE)
            normal, spread = norm_parts(base_two[rows])
            moved = grad_two[rows] + norm_pull(grads * cross_gain, normal, spread)
            grad_two[rows] = moved
            low_two[rows] = (gate_two * moved).astype(NARROW)
            add_rows(2, grads * normal)
            add_rows(3, moved * branch_two[rows].astype(WIDE))

    def finish(slot, chunk):
        side, rows = where_of(slot, chunk)

        @pl.when(is_middle)
        def _():
            across(slot, chunk).wait_recv()
            total[rows] = (stage[rows].astype(WIDE) + cross[side, rows].astype(WIDE)).astype(NARROW)

        @pl.when(jnp.logical_not(is_middle))
        def _():
            outward(slot, chunk).wait_recv()

        @pl.when(inside)
        def _():
            outward(slot, chunk).start()

        consume(slot, rows, total[rows])

    def head_rows(head):
        return pl.ds(head * width, width)

    def probs_of(stream, asked, head):
        scores = scale * dot(asked, keys_ref[head_rows(head)], 1, 1) + bias_ref[stream, 0:1]
        raised = jnp.exp(scores - jnp.max(scores, axis=-1, keepdims=True))
        return raised / jnp.sum(raised, axis=-1, keepdims=True)

    def cross_forward(piece, stream, rows):
        if piece == 0:
            query[rows] = dot(normed_three[rows], query_w[...], 1, 1).astype(NARROW)
        elif piece in (1, 2):
            asked = query[rows]
            found = jnp.zeros((patches, local), WIDE) if piece == 1 else mixed[...]
            for head in range((piece - 1) * half_heads, piece * half_heads):
                probs = probs_of(stream, asked, head).astype(NARROW)
                found = found + dot(probs, values_ref[head_rows(head)], 1, 0)
            if piece == 1:
                mixed[...] = found
            else:
                heads_out[rows] = found.astype(NARROW)
        elif piece == 3:
            part[rows] = dot(heads_out[rows], out_w[...], 1, 0).astype(NARROW)

    def feed_forward(piece, stream, rows):
        if piece < 3:
            span = slice(piece * tile, (piece + 1) * tile)
            inner_values = dot(normed_four[rows], up_w[:, span], 1, 0)
            pulled = dot(low_four[rows], down_w[span], 1, 1)
            raised, slope = gelu_both(inner_values)
            active[rows, span] = raised.astype(NARROW)
            grad_inner[rows, span] = (pulled * slope).astype(NARROW)
        else:
            third = up_w.shape[0] // 3
            span = slice((piece - 3) * third, (piece - 2) * third)
            part[rows, span] = dot(grad_inner[rows], up_w[span], 1, 1).astype(NARROW)

    def cross_backward(piece, stream, rows):
        if piece == 0:
            grad_heads[rows] = dot(low_three[rows], out_w[...], 1, 1).astype(NARROW)
        elif piece in (1, 2):
            asked, given = query[rows], grad_heads[rows]
            found = jnp.zeros((patches, local), WIDE) if piece == 1 else mixed[...]
            for head in range((piece - 1) * half_heads, piece * half_heads):
                spot = head_rows(head)
                probs = probs_of(stream, asked, head)
                pulled = dot(given, values_ref[spot], 1, 1)
                grad_scores = probs * (pulled - jnp.sum(pulled * probs, axis=-1, keepdims=True))
                grad_scores = grad_scores.astype(NARROW)
                found = found + dot(grad_scores, keys_ref[spot], 1, 0)
                grad_keys[spot] += dot(grad_scores, asked, 0, 0)
                grad_values[spot] += dot(probs.astype(NARROW), given, 0, 0)
            if piece == 1:
                mixed[...] = found
            else:
                grad_query[rows] = (scale * found).astype(NARROW)
        elif piece == 3:
            part[rows] = dot(grad_query[rows], query_w[...], 1, 0).astype(NARROW)

    def up_tile(number):
        grad_tile(normed_four, grad_inner, up_grad, number * third, third)

    def down_tile(number):
        grad_tile(low_four, active, down_grad, number * third, third)

    def extra(frame):
        rows = slice(frame * patches, (frame + 1) * patches)
        extra_part[rows] = dot(active[rows], down_w[...], 1, 0).astype(NARROW)

    def text_pairs():
        fetch.again(2, 4, 5, 6, 7, 8, 9, 10)
        packed = dot(text_w[...], text_ref[...], 1, 0).T.astype(NARROW)
        spread_heads(packed[:, 0:local], keys_ref)
        spread_heads(packed[:, local:], values_ref)

    third = up_w.shape[0] // 3
    late = {(0, 1): [text_pairs]}

    def later(slot, chunk, work, *args):
        late.setdefault((slots - 3 + slot, chunk), []).append(functools.partial(work, *args))

    for i, spot in enumerate(((0, 0), (0, 1), (0, 2))):
        later(*spot, up_tile, i)
    for i in range(3):
        later(2, 1 + i, down_tile, i)
    if asides:
        later(0, 2, asides[0].start)
        for i, work in enumerate(scatters.folds(0)):
            later(1, (0, 7)[i], work)
    for frame in range(frames):
        later(2, 6 + min(frame, 1), extra, frame)
    for which, slot, chunk in ((4, -2, 3), (5, -2, 4), (0, 0, 4), (3, 1, 5), (6, 2, 3), (7, 2, 4), (8, 2, 5), (11, 2, 5)):
        later(slot, chunk, fetch.store, which)

    tally[...] = jnp.zeros_like(tally)
    grad_keys[...] = jnp.zeros_like(grad_keys)
    grad_values[...] = jnp.zeros_like(grad_values)

    def step(number, carry):
        slot, chunk = lax.div(number, chunks), lax.rem(number, chunks)
        before = slot - 1

        @pl.when(is_end & (chunk == 0))
        def _():
            @pl.when(slot < slots)
            def _():
                def begin(item, inner_carry):
                    rows = where_of(slot, item)[1]
                    free(slot, item)
                    stage[rows] = own_part(slot, rows)
                    send_in(slot, item)
                    return inner_carry

                lax.fori_loop(0, chunks, begin, 0)

            for late_slot in sorted({spot[0] for spot in late}):

                @pl.when(slot == late_slot)
                def _():
                    for late_chunk in range(MIDDLE_LAG):
                        for work in late.get((late_slot, late_chunk), ()):
                            work()

            @pl.when(slot > 0)
            def _():
                def end(item, inner_carry):
                    finish(before, item)
                    return inner_carry

                lax.fori_loop(0, chunks, end, 0)

        @pl.when(inside & (slot < slots))
        def _():
            gather_in(slot, chunk)

            @pl.when(chunk >= MIDDLE_LAG)
            def _():
                finish(slot, chunk - MIDDLE_LAG)

        @pl.when(inside & (slot > 0) & (chunk < MIDDLE_LAG))
        def _():
            finish(before, chunks - MIDDLE_LAG + chunk)

        stream = lax.rem(jnp.maximum(before, 0), frames)
        rows = pl.ds(pl.multiple_of(stream * patches, patches), patches)
        for which, work in enumerate((cross_forward, feed_forward, cross_backward)):

            @pl.when((slot > 0) & (lax.div(jnp.maximum(before, 0), frames) == which))
            def _():
                for piece in range(6 if which == 1 else 4):

                    @pl.when(chunk == jnp.minimum(MIDDLE_LAG + piece, chunks - 1))
                    def _():
                        work(piece, stream, rows)

        for (late_slot, late_chunk), works in late.items():

            @pl.when((slot == late_slot) & (chunk == late_chunk) & (inside | (late_chunk >= MIDDLE_LAG)))
            def _():
                for work in works:
                    work()

        return carry

    lax.fori_loop(0, slots * chunks + MIDDLE_LAG, step, 0)

    def settle(number, carry):
        sent(lax.div(number, chunks), lax.rem(number, chunks))
        return carry

    lax.fori_loop((slots - frames) * chunks, slots * chunks, settle, 0)
    sums_ref[...] = jnp.zeros_like(sums_ref)
    for i in range(4):
        sums_ref[i : i + 1] = jnp.sum(tally[i], axis=0, keepdims=True)
    for aside in asides:
        aside.finish([up_result])


def call_middle(
    count, groups, frames_axis, frames, first, base, cotangent, rows, bias, text, text_w, query_w, out_w, up_w, down_w
):
    tokens, features = first.shape
    local, hidden = query_w.shape[0], up_w.shape[1]
    chunks = tokens // frames // MIDDLE_ROWS
    scattered = can_scatter(groups, frames_axis, features)
    keys_shape = (local // HD * bias.shape[2], local)

    def wide(*shape):
        return jax.ShapeDtypeStruct(shape, WIDE)

    def narrow(*shape):
        return jax.ShapeDtypeStruct(shape, NARROW)

    found, scratch = [narrow(features, hidden)], []
    if scattered:
        found, scratch = Scatters.shapes(groups, frames_axis, features, [[hidden]])
        scratch = [pltpu.VMEM((features, hidden), NARROW)] + scratch
    results = (
        [wide(tokens, features)] * 2
        + [narrow(tokens, features)] * 3
        + [narrow(tokens, local)] * 2
        + [wide(*keys_shape)] * 2
        + [wide(8, features), narrow(tokens, features), narrow(features, hidden)]
        + found
    )
    sem = pltpu.SemaphoreType.DMA((STAGES * frames, chunks))
    return fetching_call(
        functools.partial(middle_kernel, count, groups, frames_axis, frames, scattered),
        [first, base, cotangent, rows, bias, text, text_w, query_w, out_w, up_w, down_w],
        tuple(results),
        [pltpu.VMEM(keys_shape, NARROW)] * 2
        + [pltpu.VMEM((tokens, features), NARROW)] * 2
        + [pltpu.VMEM((tokens, hidden), NARROW)] * 2
        + [
            pltpu.VMEM((tokens, features), WIDE),
            pltpu.VMEM((tokens, features), NARROW),
            pltpu.VMEM((tokens, local), NARROW),
            pltpu.VMEM((tokens, local), NARROW),
            pltpu.VMEM((tokens, features), NARROW),
            pltpu.VMEM((tokens // frames, local), WIDE),
            pltpu.VMEM((4, 8, features), WIDE),
        ]
        + [pltpu.VMEM((tokens, features), NARROW)] * 3
        + [pltpu.VMEM((2, tokens, features), NARROW)]
        + [sem] * 5
        + scratch,
        7,
        "middle",
        storing=True,
    )


def greet_frames(here, frames_axis):
    found = (here > 0).astype(jnp.int32) + (here < frames_axis - 1).astype(jnp.int32)
    barrier = pltpu.get_barrier_semaphore()

    @pl.when(here > 0)
    def _():
        pl.semaphore_signal(barrier, inc=1, device_id={FRAME: here - 1}, device_id_type=MESH)

    @pl.when(here < frames_axis - 1)
    def _():
        pl.semaphore_signal(barrier, inc=1, device_id={FRAME: here + 1}, device_id_type=MESH)

    return found


def head_columns(local):
    feature = lax.broadcasted_iota(jnp.int32, (local, 128), 0)
    first = lax.broadcasted_iota(jnp.int32, (local, 128), 1) * HD
    return jnp.where((feature >= first) & (feature < first + HD), 1.0, 0.0).astype(NARROW)


def per_head(values, columns):
    return dot(values.astype(NARROW), columns, 1, 0)


def over_features(values, columns):
    return dot(values.astype(NARROW), columns, 1, 1)


def window_probs(query, keys_of, bias_of, columns):
    scores = [
        HD ** (-0.5) * per_head(query * keys_of(offset), columns) + bias_of(offset) for offset in range(WIN)
    ]
    highest = functools.reduce(jnp.maximum, scores)
    raised = [jnp.exp(item - highest) for item in scores]
    whole = 1.0 / sum(raised[1:], raised[0])
    return [item * whole for item in raised]


def temporal_forward_kernel(
    count, frames_axis, frames, fetch, hidden_ref, in_ref, out_ref, bias_ref, cotangent_ref, text_ref,
    query_ref, keys_ref, values_ref, heads_ref, part_ref, cotangent_full, text_full,
    halo_send, halo_recv, *sems,
):
    place, here = lax.axis_index(LINE), lax.axis_index(FRAME)
    patches = hidden_ref.shape[0] // frames
    local = heads_ref.shape[1]
    share = cotangent_ref.shape[1]
    last = count - 1
    greet_line(place, count, greet_frames(here, frames_axis))
    fetch()
    cells = (keys_ref, values_ref)

    def shares(owner):
        return cotangent_full.at[:, pl.ds(pl.multiple_of(owner * share, share), share)]

    def text_share(owner):
        return text_full.at[pl.ds(pl.multiple_of(owner * local, 16), local)]

    moving = [
        LineGather(count, place, shares, sems[0:3]),
        LineGather(count, place, text_share, sems[3:6]),
    ]
    cotangent_full[:, pl.ds(pl.multiple_of(place * share, share), share)] = cotangent_ref[...]
    text_full[pl.ds(pl.multiple_of(place * local, 16), local)] = text_ref[...]
    for item in moving:
        item.start()

    def halo(which, item):
        source = 2 + (frames - 2 + which if which < 2 else 0)
        target = which if which < 2 else frames + 2
        to = here + 1 if which < 2 else here - 1
        ref = cells[item]
        return remote(
            ref.at[source], ref.at[target], halo_send.at[which, item], halo_recv.at[which, item], {FRAME: to}
        )

    has_next, has_previous = here < frames_axis - 1, here > 0

    def frame_rows(frame):
        return slice(frame * patches, (frame + 1) * patches)

    for frame in range(frames):
        for item in range(2):
            rows = slice((1 + item) * local, (2 + item) * local)
            cells[item][2 + frame] = dot(hidden_ref[frame_rows(frame)], in_ref[rows], 1, 1).astype(NARROW)
            for which in range(3):
                if (frames - 2 + which if which < 2 else 0) == frame:

                    @pl.when(has_next if which < 2 else has_previous)
                    def _():
                        halo(which, item).start()

    query_ref[...] = dot(hidden_ref[...], in_ref[0:local], 1, 1).astype(NARROW)
    for distance in range(1, last):
        for item in moving:
            item.arrive(distance)
    for item in range(2):

        @pl.when(has_previous)
        def _():
            halo(0, item).wait_recv()
            halo(1, item).wait_recv()

        @pl.when(jnp.logical_not(has_previous))
        def _():
            cells[item][0:2] = jnp.zeros((2,) + cells[item].shape[1:], NARROW)

        @pl.when(has_next)
        def _():
            halo(2, item).wait_recv()

        @pl.when(jnp.logical_not(has_next))
        def _():
            cells[item][frames + 2] = jnp.zeros(cells[item].shape[1:], NARROW)

    columns = head_columns(local)
    for frame in range(frames):
        probs = window_probs(
            query_ref[frame_rows(frame)].astype(WIDE),
            lambda offset: keys_ref[frame + offset].astype(WIDE),
            lambda offset: bias_ref[frame * WIN + offset : frame * WIN + offset + 1],
            columns,
        )
        mixed = over_features(probs[0], columns) * values_ref[frame].astype(WIDE)
        for offset in range(1, WIN):
            mixed = mixed + over_features(probs[offset], columns) * values_ref[frame + offset].astype(WIDE)
        heads_ref[frame_rows(frame)] = mixed.astype(NARROW)
        part_ref[frame_rows(frame)] = dot(mixed.astype(NARROW), out_ref[...], 1, 0).astype(NARROW)
    for item in moving:
        item.arrive(last)
        item.settle()
    for item in range(2):

        @pl.when(has_next)
        def _():
            halo(0, item).wait_send()
            halo(1, item).wait_send()

        @pl.when(has_previous)
        def _():
            halo(2, item).wait_send()


def call_temporal_forward(count, frames_axis, hidden, in_w, out_w, bias, cotangent, text):
    tokens, features = hidden.shape
    frames, share = cotangent.shape[:2]
    local = out_w.shape[0]
    patches = tokens // frames

    def narrow(*shape):
        return jax.ShapeDtypeStruct(shape, NARROW)

    results = (
        [narrow(tokens, local)]
        + [narrow(frames + 3, patches, local)] * 2
        + [narrow(tokens, local), narrow(tokens, features)]
        + [narrow(frames, share * count, features), narrow(features, text.shape[1])]
    )
    return fetching_call(
        functools.partial(temporal_forward_kernel, count, frames_axis, frames),
        [hidden, in_w, out_w, bias, cotangent, text],
        tuple(results),
        [pltpu.SemaphoreType.DMA((3, 2))] * 2 + gather_sems(count) * 2,
        8,
        "temporal_forward",
    )


def temporal_backward_kernel(
    count, groups, frames_axis, frames, widths, fetch, *refs
):
    (
        grad_ref, in_ref, out_ref, bias_ref, query_ref, keys_ref, values_ref,
        extra_ref, text_keys, text_values, text_w, text_rows, cross_hidden, cross_grad, cross_low, cross_heads,
        base_three, cotangent_ref, gate_ref, *refs,
    ) = refs
    sources, refs = refs[: len(widths)], refs[len(widths) :]
    grad_packed, part_ref, output_ref, gate_part, text_own, product_ref, *refs = refs
    results, refs = refs[: len(widths)], refs[len(widths) :]
    (
        near_keys, near_values, rim_out, rim_in, halo_send, halo_recv, text_ref, text_low,
        extra_land, extra_stage, text_land, text_stage, *sems,
    ) = refs
    scatters = Scatters(groups, frames_axis, sources, widths, results, sems[8:])
    products = Products(
        [(cross_hidden, cross_grad), (text_rows, text_low, 1, 1), (cross_low, cross_heads)], product_ref
    ).work()
    place, here = lax.axis_index(LINE), lax.axis_index(FRAME)
    patches = grad_ref.shape[0] // frames
    local = out_ref.shape[0]
    share = output_ref.shape[1]
    last = count - 1
    greet_line(place, count, greet_frames(here, frames_axis), scatters.partners() if widths else ())
    fetch(7, *range(19, 19 + len(sources)))
    for item in scatters.items:
        item.start()

    def shares(owner, frame):
        return extra_ref[frame, pl.ds(pl.multiple_of(owner * share, share), share)]

    moving = [
        LineScatter(count, place, frames, shares, extra_land, extra_stage, sems[0:4]),
        LineScatter(count, place, 1, lambda owner, piece: text_ref[owner], text_land, text_stage, sems[4:8]),
    ]
    moving[0].relay_both(last)
    near = (near_keys, near_values)
    def halo(which):
        to = here - 1 if which < 2 else here + 1
        return remote(
            rim_out.at[which], rim_in.at[which], halo_send.at[which], halo_recv.at[which], {FRAME: to}
        )

    has_next, has_previous = here < frames_axis - 1, here > 0

    def frame_rows(frame):
        return slice(frame * patches, (frame + 1) * patches)

    fetch(0, 2, 3, 4, 5, 6)
    columns = head_columns(local)
    seen = set()

    def add(item, cell, terms):
        if (item, cell) in seen:
            near[item][cell] += terms
        else:
            near[item][cell] = terms
        seen.add((item, cell))

    for frame in range(frames):
        given = dot(grad_ref[frame_rows(frame)], out_ref[...], 1, 1).astype(NARROW).astype(WIDE)
        asked = query_ref[frame_rows(frame)].astype(WIDE)
        probs = window_probs(
            asked,
            lambda offset: keys_ref[frame + offset].astype(WIDE),
            lambda offset: bias_ref[frame * WIN + offset : frame * WIN + offset + 1],
            columns,
        )
        pulled = [per_head(given * values_ref[frame + offset].astype(WIDE), columns) for offset in range(WIN)]
        shared = sum((probs[i] * pulled[i] for i in range(1, WIN)), probs[0] * pulled[0])
        found = jnp.zeros((patches, local), WIDE)
        for offset in range(WIN):
            scores = HD ** (-0.5) * over_features(probs[offset] * (pulled[offset] - shared), columns)
            found = found + scores * keys_ref[frame + offset].astype(WIDE)
            add(0, frame + offset, scores * asked)
            add(1, frame + offset, over_features(probs[offset], columns) * given)
        grad_packed[frame_rows(frame), 0:local] = found.astype(NARROW)
        if frame == 0:
            for item in scatters.items:
                item.first_round()
            if last > 1:
                moving[0].relay_both(last - 1)

    for which in range(3):

        @pl.when(has_previous if which < 2 else has_next)
        def _():
            for item in range(2):
                span = slice(item * local, (item + 1) * local)
                rim_out[which, :, span] = near[item][which if which < 2 else frames + 2].astype(NARROW)
            halo(which).start()

    for distance in range(last - 2, 0, -1):
        moving[0].relay_both(distance)
    for item in scatters.items:
        item.second_round()
    fetch()
    fetch()
    slots = text_low.shape[1]
    for item, (source, factor) in enumerate(((text_keys, HD ** (-0.5)), (text_values, 1.0))):
        low = (factor * collect_heads(source[...], slots)).T
        text_low[item * local : (item + 1) * local] = low.astype(NARROW)
    text_parts = dot(text_w[...], text_low[...], 0, 0).astype(NARROW)
    for owner in range(count):
        text_ref[owner] = text_parts[owner * local : (owner + 1) * local]
    moving[1].relay_both(last)
    for i, work in enumerate(products):
        work()
        if last - 1 - i > 0:
            moving[1].relay_both(last - 1 - i)
    for distance in range(last - 1 - len(products), 0, -1):
        moving[1].relay_both(distance)

    for which in range(3):

        @pl.when(has_next if which < 2 else has_previous)
        def _():
            halo(which).wait_recv()
            for item in range(2):
                span = slice(item * local, (item + 1) * local)
                near[item][2 + (frames - 2 + which if which < 2 else 0)] += rim_in[which, :, span].astype(WIDE)

    for frame in range(frames):
        rows = frame_rows(frame)
        parts = dot(grad_packed[rows, 0:local], in_ref[0:local], 1, 0)
        for item in range(2):
            values = near[item][2 + frame].astype(NARROW)
            grad_packed[rows, (1 + item) * local : (2 + item) * local] = values
            parts = parts + dot(values, in_ref[(1 + item) * local : (2 + item) * local], 1, 0)
        part_ref[rows] = parts.astype(NARROW)

    gate_sum = jnp.zeros((1, gate_part.shape[1]), WIDE)
    for frame in range(frames):
        found = moving[0].total(frame)
        rows = pl.ds(pl.multiple_of(frame * patches + place * share, share), share)
        output_ref[frame] = (base_three[rows] + gate_ref[8:9] * found).astype(NARROW)
        gate_sum = gate_sum + jnp.sum(cotangent_ref[frame].astype(WIDE) * found, axis=0, keepdims=True)
    gate_part[...] = jnp.broadcast_to(gate_sum, gate_part.shape)
    text_own[...] = moving[1].total(0).astype(NARROW)
    for item in moving:
        item.settle()
    for which in range(3):

        @pl.when(has_previous if which < 2 else has_next)
        def _():
            halo(which).wait_send()

    scatters.finish()


def call_temporal_backward(
    count, groups, frames_axis, grad, in_w, out_w, bias, query, keys, values, extra, text_keys, text_values, text_w,
    text_rows, cross_pairs, sources, widths,
):
    tokens, features = grad.shape
    frames, patches = extra.shape[:2]
    local = out_w.shape[0]
    share = patches // count
    slots = text_rows.shape[1]

    def narrow(*shape):
        return jax.ShapeDtypeStruct(shape, NARROW)

    results = (
        [narrow(tokens, 3 * local)]
        + [narrow(tokens, features), narrow(frames, share, features)]
        + [jax.ShapeDtypeStruct((8, features), WIDE)]
        + [narrow(local, slots), narrow(features, 4 * local)]
    )
    found, scratch = Scatters.shapes(groups, frames_axis, features, widths)
    results = results + found
    return fetching_call(
        functools.partial(temporal_backward_kernel, count, groups, frames_axis, frames, widths),
        [grad, in_w, out_w, bias, query, keys, values, extra, text_keys, text_values, text_w, text_rows,
        *cross_pairs, *sources,],
        tuple(results),
        [pltpu.VMEM((frames + 3, patches, local), WIDE)] * 2
        + [pltpu.VMEM((3, patches, 2 * local), NARROW)] * 2
        + [pltpu.SemaphoreType.DMA((3,))] * 2
        + [pltpu.VMEM((count, local, slots), NARROW), pltpu.VMEM((2 * local, slots), NARROW)]
        + [pltpu.VMEM((2, count, frames, share, features), NARROW)] * 2
        + [pltpu.VMEM((2, count, 1, local, slots), NARROW)] * 2
        + scatter_sems(count, frames)
        + scatter_sems(count, 1)
        + scratch,
        9,
        "temporal_backward",
    )


def sum_matrix_grads(pieces):
    if not pieces:
        return []
    packed = jnp.concatenate([piece.astype(NARROW) for piece in pieces], axis=1)
    summed = lax.psum_scatter(packed, BOTH, scatter_dimension=0, tiled=True).astype(WIDE)
    found, start = [], 0
    for piece in pieces:
        found.append(summed[:, start : start + piece.shape[1]])
        start += piece.shape[1]
    return found


def per_device(
    latent, captions, bucket, clip_ids, window_mask, text_counts, time_table, ada_weight,
    spatial_inproj, spatial_outproj, temporal_inproj, temporal_outproj, caption_proj, cross_gain,
    cross_query, cross_keyval, cross_outproj, mlp_up, mlp_down, cotangent,
):
    count, groups, frames_axis = (lax.axis_size(axis) for axis in (LINE, GROUP, FRAME))
    place = lax.axis_index(LINE)
    frames, share, features = latent.shape[1:]
    patches = share * count
    tokens = frames * patches
    local = spatial_outproj.shape[0]
    clip_count, text_length, text_width = captions.shape[1:]
    slots = clip_count * text_length

    def flat(values):
        return values.reshape(tokens, -1)

    def grid(values):
        return values.reshape(frames, patches, -1)

    spatial_in, temporal_in, keyval_in = (
        jnp.transpose(w, (1, 2, 0)).reshape(-1, features)
        for w in (spatial_inproj, temporal_inproj, cross_keyval)
    )
    query_in = cross_query.T

    caption_here = captions[0].reshape(slots, text_width)
    base_grid, normed_grid, mods, text_part, side, window_bias, text_bias, caption_share = call_opening(
        count, groups, frames_axis, (bucket, clip_ids, window_mask, text_counts), latent[0], time_table,
        cross_gain.reshape(-1, 128), jnp.transpose(ada_weight, (1, 0, 2)), caption_here, caption_proj.T,
    )
    base_zero, spatial_hidden = flat(base_grid), flat(normed_grid)

    spatial_out, base_one, temporal_hidden, spatial_packed, spatial_flat = call_forward(
        count, frames, spatial_hidden, spatial_in, base_zero, mods, spatial_outproj,
    )

    (
        temporal_query, temporal_keys, temporal_values, temporal_flat, temporal_part, cotangent_full, text_full,
    ) = call_temporal_forward(
        count, frames_axis, temporal_hidden, temporal_in, temporal_outproj, window_bias, cotangent[0], text_part
    )
    cotangent_full = flat(cotangent_full)

    (
        base_three, grad_two, grad_temporal_low, grad_cross_low, cross_hidden, cross_flat, grad_cross_packed,
        text_grad_keys, text_grad_values, sums_middle, mlp_part, grad_down, grad_up,
    ) = call_middle(
        count, groups, frames_axis, frames, temporal_part, base_one, cotangent_full,
        mods, text_bias,
        text_full, keyval_in, query_in, cross_outproj, mlp_up, mlp_down,
    )

    def outside(packed, widths):
        return sum_matrix_grads(
            [
                item[:, sum(columns[:i]) : sum(columns[: i + 1])]
                for item, columns in zip(packed, widths)
                for i in range(len(columns))
            ]
        )

    if not can_scatter(groups, frames_axis, features):
        (grad_up,) = outside([grad_up], [[grad_up.shape[1]]])

    inside = can_scatter(groups, frames_axis, features)
    down_widths = [[grad_down.shape[1]]]
    grad_temporal_packed, temporal_grad_part, output, gate_part, text_grad, grad_cross, *found = call_temporal_backward(
        count, groups, frames_axis, grad_temporal_low, temporal_in, temporal_outproj, window_bias,
        temporal_query, temporal_keys, temporal_values, grid(mlp_part), text_grad_keys, text_grad_values,
        keyval_in, text_full,
        [cross_hidden, grad_cross_packed, grad_cross_low, cross_flat, base_three, cotangent[0], mods],
        [grad_down] if inside else [], down_widths if inside else [],
    )
    (grad_down,) = found if inside else outside([grad_down], down_widths)
    cross_widths, qkv_widths = [local, 2 * local, local], [3 * local, local]
    grad_one, grad_spatial_low, sums_temporal, *found = call_backward(
        count, groups, frames_axis, temporal_grad_part, base_one, grad_two, spatial_out,
        mods,
        [(temporal_hidden, grad_temporal_packed), (grad_temporal_low, temporal_flat)],
        [grad_cross] if inside else [], [cross_widths, qkv_widths] if inside else [],
    )
    if not inside:
        found = outside([grad_cross, found[0]], [cross_widths, qkv_widths])
    (
        grad_query_cross, grad_keyval_cross, grad_outproj_cross, grad_inproj_temporal, grad_outproj_temporal,
    ) = found

    grad_latent, small_all, text_grad_all, *found = call_closing(
        count, groups, frames_axis, grad_spatial_low, grid(base_zero), grid(grad_one), gate_part,
        mods, spatial_packed, spatial_flat, spatial_hidden, spatial_in, spatial_outproj,
        text_grad, [sums_temporal, sums_middle, side], [], [qkv_widths] if inside else [],
    )
    if not inside:
        found = outside([found[0]], [qkv_widths])
    grad_inproj_spatial, grad_outproj_spatial = found

    grad_ada, grad_table, grad_gain, grad_caption, *found = call_finishing(
        groups, frames_axis, time_table.shape[0], (0, 1, 8, 9, 10, 11, 12, 13, 2), (0, 0, 1, 0, 1, 0, 0, 2, 0, 0, 0),
        small_all, jnp.transpose(ada_weight, (1, 0, 2)), text_grad_all, caption_share,
        [
            output.reshape(frames * share, features), grad_latent.reshape(frames * share, features),
            grad_inproj_spatial, grad_outproj_spatial,
            grad_inproj_temporal, grad_outproj_temporal, grad_query_cross, grad_keyval_cross,
            grad_outproj_cross, grad_up, grad_down,
        ],
    )
    (
        output, grad_latent, grad_inproj_spatial, grad_outproj_spatial, grad_inproj_temporal,
        grad_outproj_temporal, grad_query_cross, grad_keyval_cross, grad_outproj_cross, grad_up, grad_down,
    ) = found
    return (
        output.reshape(1, frames, share, features),
        grad_latent.reshape(1, frames, share, features),
        grad_table,
        jnp.transpose(grad_ada, (2, 0, 1)),
        jnp.transpose(grad_inproj_spatial, (1, 0, 2)),
        grad_outproj_spatial.T,
        jnp.transpose(grad_inproj_temporal, (1, 0, 2)),
        grad_outproj_temporal.T,
        grad_caption.T,
        grad_gain.reshape(features),
        grad_query_cross,
        grad_keyval_cross,
        grad_outproj_cross.T,
        grad_up,
        grad_down.T,
    )


def solution(mesh):
    tokens = P(GROUP, FRAME, LINE, None)
    packed_in, rows_in, columns_in = P(None, None, LINE), P(LINE, None), P(None, LINE)
    in_specs = (
        tokens, P(GROUP, None, None, None), P(GROUP), P(GROUP, None), P(GROUP, FRAME, None),
        P(GROUP, None), columns_in, P(LINE, None, None), packed_in, rows_in, packed_in, rows_in,
        columns_in, P(), columns_in, packed_in, rows_in, columns_in, rows_in, tokens,
    )
    packed_out, rows_out, columns_out = P(BOTH, None, LINE), P(LINE, BOTH), P(BOTH, LINE)
    out_specs = (
        tokens, tokens, columns_in, P(LINE, None, BOTH), packed_out, rows_out, packed_out, rows_out,
        columns_out, P(), columns_out, packed_out, rows_out, columns_out, rows_out,
    )
    return jax.shard_map(
        per_device, mesh=mesh, in_specs=in_specs, out_specs=out_specs, check_vma=False
    )
```

```python
import functools

import jax
import jax.numpy as jnp
from jax import lax
from jax.experimental import pallas as pl
from jax.experimental.pallas import tpu as pltpu
from jax.sharding import PartitionSpec as P

HD = 72
WIN = 4
EPSILON = 1e-06
HIGHEST = lax.Precision.HIGHEST
NEGATIVE = -1e30
WIDE = jnp.float32
NARROW = jnp.bfloat16
GROUP, FRAME, LINE = "group", "frame", "tensor"
BOTH = (GROUP, FRAME)
MESH = pl.DeviceIdType.MESH
CHUNKS = 16
LAG = 2
AT_ONCE = 4
VMEM_LIMIT = 48 * 2**20


def swish_act(values):
    return values / (1.0 + jnp.exp(-values))


def gelu_tanh(values):
    return (
        0.5
        * values
        * (1.0 + jnp.tanh(0.7978845608028654 * (values + 0.044715 * values * values * values)))
    )


def dot(first, second, contract_first, contract_second):
    return lax.dot_general(
        first, second, (((contract_first,), (contract_second,)), ((), ())), preferred_element_type=WIDE
    )


def split_pair(values):
    high_part = values.astype(NARROW)
    rest_part = (values - high_part.astype(WIDE)).astype(NARROW)
    return (high_part, rest_part)


def norm_parts(values):
    centred = values - jnp.mean(values, axis=-1, keepdims=True)
    spread = lax.rsqrt(jnp.mean(centred * centred, axis=-1, keepdims=True) + EPSILON)
    return centred * spread, spread


def norm_pull(scaled, normal, spread):
    return spread * (
        scaled
        - jnp.mean(scaled, axis=-1, keepdims=True)
        - normal * jnp.mean(scaled * normal, axis=-1, keepdims=True)
    )


def remote(source, target, send_sem, recv_sem, where):
    return pltpu.make_async_remote_copy(
        src_ref=source,
        dst_ref=target,
        send_sem=send_sem,
        recv_sem=recv_sem,
        device_id=where,
        device_id_type=MESH,
    )


def greet_line(place, count, more=0, others=()):
    barrier = pltpu.get_barrier_semaphore()
    for where in others:
        pl.semaphore_signal(barrier, inc=1, device_id=where, device_id_type=MESH)

    @pl.when(place > 0)
    def _():
        pl.semaphore_signal(barrier, inc=1, device_id={LINE: place - 1}, device_id_type=MESH)

    @pl.when(place < count - 1)
    def _():
        pl.semaphore_signal(barrier, inc=1, device_id={LINE: place + 1}, device_id_type=MESH)

    pl.semaphore_wait(
        barrier, (place > 0).astype(jnp.int32) + (place < count - 1).astype(jnp.int32) + len(others) + more
    )


class Scatter:
    SCRATCH = 20

    def __init__(self, groups, frames_axis, source, scratch):
        self.source, self.columns = source, source.shape[1]
        self.inbox, self.kept = scratch[:2]
        self.stages = scratch[2:6]
        self.lands = scratch[6:10]
        self.sends, self.recvs = scratch[10:14], scratch[14:18]
        self.twin_send, self.twin_recv = scratch[18:20]
        self.frames_axis, self.highs = frames_axis, groups // 2
        self.block = source.shape[0] // (groups * frames_axis)
        self.cut = self.columns // 256 * 128
        group = lax.axis_index(GROUP)
        self.core, self.high, self.frame = lax.rem(group, 2), lax.div(group, 2), lax.axis_index(FRAME)
        self.twin = {GROUP: group + 1 - 2 * self.core}

    def other_high(self, step):
        return lax.rem(self.high + step, self.highs)

    def other_frame(self, step):
        return lax.rem(self.frame + step, self.frames_axis)

    def partner(self, along_group, step):
        if along_group:
            return {GROUP: self.other_high(step) * 2 + self.core}
        return {FRAME: self.other_frame(step)}

    def steps(self, along_group):
        return range(1, self.highs if along_group else self.frames_axis)

    def partners(self):
        return [self.twin] + [self.partner(way, step) for way in (True, False) for step in self.steps(way)]

    def twin_copy(self, high):
        rows = self.block * self.frames_axis
        first = pl.multiple_of((high * 2 + 1 - self.core) * rows, 16)
        return remote(
            self.source.at[pl.ds(first, rows)],
            self.inbox.at[pl.ds(high * rows, rows)],
            self.twin_send.at[high],
            self.twin_recv.at[high],
            self.twin,
        )

    def move(self, which, step):
        return remote(
            self.stages[which].at[step - 1],
            self.lands[which].at[step - 1],
            self.sends[which].at[step],
            self.recvs[which].at[step],
            self.partner(which in (0, 3), step),
        )

    def pair_sum(self, high, frame, span):
        first = ((high * 2 + self.core) * self.frames_axis + frame) * self.block
        other = (high * self.frames_axis + frame) * self.block
        mine = self.source[pl.ds(pl.multiple_of(first, 16), self.block), span]
        return mine.astype(WIDE) + self.inbox[pl.ds(pl.multiple_of(other, 16), self.block), span].astype(WIDE)

    def start(self):
        for high in range(self.highs):
            self.twin_copy(high).start()

    def first_round(self):
        for high in range(self.highs):
            self.twin_copy(high).wait_recv()
        left, right = slice(0, self.cut), slice(self.cut, self.columns)
        for step in self.steps(True):
            for frame in range(self.frames_axis):
                rows = slice(frame * self.block, (frame + 1) * self.block)
                self.stages[0][step - 1, rows] = self.pair_sum(self.other_high(step), frame, left).astype(NARROW)
            self.move(0, step).start()
        for step in self.steps(False):
            for high in range(self.highs):
                rows = slice(high * self.block, (high + 1) * self.block)
                self.stages[1][step - 1, rows] = self.pair_sum(high, self.other_frame(step), right).astype(NARROW)
            self.move(1, step).start()

    def gathered(self, which, high, frame):
        span = slice(0, self.cut) if which == 0 else slice(self.cut, self.columns)
        found = self.pair_sum(high, frame, span)
        rows = pl.ds(pl.multiple_of((frame if which == 0 else high) * self.block, 16), self.block)
        for step in self.steps(which == 0):
            found = found + self.lands[which][step - 1, rows].astype(WIDE)
        return found

    def second_round(self):
        for which in (0, 1):
            for step in self.steps(which == 0):
                self.move(which, step).wait_recv()
        for step in self.steps(False):
            self.stages[2][step - 1] = self.gathered(0, self.high, self.other_frame(step)).astype(NARROW)
            self.move(2, step).start()
        for step in self.steps(True):
            self.stages[3][step - 1] = self.gathered(1, self.other_high(step), self.frame).astype(NARROW)
            self.move(3, step).start()
        self.kept[:, 0 : self.cut] = self.gathered(0, self.high, self.frame)
        self.kept[:, self.cut :] = self.gathered(1, self.high, self.frame)

    def finish(self, results):
        for which in (2, 3):
            for step in self.steps(which == 3):
                self.move(which, step).wait_recv()
        for which, span in ((2, slice(0, self.cut)), (3, slice(self.cut, self.columns))):
            for step in self.steps(which == 3):
                self.kept[:, span] += self.lands[which][step - 1].astype(WIDE)
        start = 0
        for result in results:
            result[...] = self.kept[:, start : start + result.shape[1]]
            start += result.shape[1]
        for high in range(self.highs):
            self.twin_copy(high).wait_send()
        for which in range(4):
            for step in self.steps(which in (0, 3)):
                self.move(which, step).wait_send()

    @staticmethod
    def scratch(groups, frames_axis, width, columns):
        block, highs = width // (groups * frames_axis), groups // 2
        cut = columns // 256 * 128
        across, along = max(highs - 1, 1), max(frames_axis - 1, 1)
        shapes = [
            (across, frames_axis * block, cut),
            (along, highs * block, columns - cut),
            (along, block, cut),
            (across, block, columns - cut),
        ]
        dma = pltpu.SemaphoreType.DMA
        sems = [dma((highs,)), dma((frames_axis,)), dma((frames_axis,)), dma((highs,))]
        return (
            [pltpu.VMEM((width // 2, columns), NARROW), pltpu.VMEM((block, columns), WIDE)]
            + [pltpu.VMEM(shape, NARROW) for shape in shapes] * 2
            + sems * 2
            + [dma((highs,))] * 2
        )


def can_scatter(groups, frames_axis, width):
    return groups % 2 == 0 and width % (16 * groups * frames_axis) == 0


class Products:
    def __init__(self, pairs, result):
        self.pairs, self.result = pairs, result

    def product(self, i):
        first, second, *side = self.pairs[i]
        found = dot(first[...], second[...], *(side or (0, 0))).astype(NARROW)
        start = sum(pair[1].shape[1 if len(pair) == 2 else 0] for pair in self.pairs[:i])
        self.result[:, start : start + found.shape[1]] = found

    def work(self):
        return [functools.partial(self.product, i) for i in range(len(self.pairs))]


class Scatters:
    def __init__(self, groups, frames_axis, sources, widths, results, scratch):
        self.items, self.results = [], []
        for i, source in enumerate(sources):
            self.items.append(Scatter(groups, frames_axis, source, scratch[Scatter.SCRATCH * i : Scatter.SCRATCH * (i + 1)]))
            self.results.append(results[: len(widths[i])])
            results = results[len(widths[i]) :]

    def partners(self):
        return self.items[0].partners()

    def folds(self, i):
        return [self.items[i].first_round, self.items[i].second_round]

    def finish(self):
        for item, results in zip(self.items, self.results):
            item.finish(results)

    @staticmethod
    def shapes(groups, frames_axis, features, widths):
        block = features // (groups * frames_axis)
        results = [jax.ShapeDtypeStruct((block, n), WIDE) for columns in widths for n in columns]
        scratch = [Scatter.scratch(groups, frames_axis, features, sum(columns)) for columns in widths]
        return results, sum(scratch, [])


class GroupExchange:
    def __init__(self, groups, frames_axis, source, every, scratch):
        self.groups, self.frames_axis = groups, frames_axis
        self.source, self.every = source, every
        self.near, self.frame_send, self.frame_recv, self.group_send, self.group_recv = scratch
        self.group, self.frame = lax.axis_index(GROUP), lax.axis_index(FRAME)

    def frame_copy(self, step):
        return remote(
            self.source,
            self.near.at[step - 1],
            self.frame_send.at[step],
            self.frame_recv.at[step],
            {FRAME: lax.rem(self.frame + step, self.frames_axis)},
        )

    def group_copy(self, step):
        own = self.every.at[self.group]
        return remote(
            own,
            own,
            self.group_send.at[step],
            self.group_recv.at[step],
            {GROUP: lax.rem(self.group + step, self.groups)},
        )

    def partners(self):
        return [
            {FRAME: lax.rem(self.frame + step, self.frames_axis)} for step in range(1, self.frames_axis)
        ] + [{GROUP: lax.rem(self.group + step, self.groups)} for step in range(1, self.groups)]

    def start(self):
        for step in range(1, self.frames_axis):
            self.frame_copy(step).start()

    def spread(self):
        for step in range(1, self.frames_axis):
            self.frame_copy(step).wait_recv()
        summed = self.source[...].astype(WIDE)
        for step in range(1, self.frames_axis):
            summed = summed + self.near[step - 1].astype(WIDE)
        self.every[self.group] = summed.astype(NARROW)
        for step in range(1, self.groups):
            self.group_copy(step).start()

    def finish(self):
        for step in range(1, self.frames_axis):
            self.frame_copy(step).wait_send()
        for step in range(1, self.groups):
            self.group_copy(step).wait_recv()
            self.group_copy(step).wait_send()

    @staticmethod
    def scratch(groups, frames_axis, shape):
        dma = pltpu.SemaphoreType.DMA
        return (
            [pltpu.VMEM((max(frames_axis - 1, 1),) + shape, NARROW)]
            + [dma((frames_axis,))] * 2
            + [dma((groups,))] * 2
        )


def grad_tile(first, second, result, start, size):
    result[start : start + size] = dot(first[:, start : start + size], second[...], 0, 0).astype(NARROW)


def can_scatter(groups, frames_axis, width):
    return groups % 2 == 0 and width % (16 * groups * frames_axis) == 0


def vmem(count):
    return [pl.BlockSpec(memory_space=pltpu.VMEM)] * count


class Fetch:
    def __init__(self, sources, held, sems):
        self.copies = [
            pltpu.make_async_copy(source, target, sems.at[i]) for i, (source, target) in enumerate(zip(sources, held))
        ]
        self.waiting = list(range(len(self.copies)))
        for copy in self.copies:
            copy.start()

    def __call__(self, *which):
        for i in which or tuple(self.waiting):
            self.copies[i].wait()
            self.waiting.remove(i)

    def again(self, *which):
        for i in which:
            self.copies[i].wait()

    def keep(self, held, results, sems):
        self.stores = [
            pltpu.make_async_copy(source, target, sems.at[i]) for i, (source, target) in enumerate(zip(held, results))
        ]
        self.started = set()

    def store(self, which):
        self.started.add(which)
        self.stores[which].start()

    def flush(self):
        for i, item in enumerate(self.stores):
            if i not in self.started:
                item.start()
        for item in self.stores:
            item.wait()


def fetching_call(kernel, operands, out_shape, scratch_shapes, kernel_id, name, storing=False):
    many, given = len(operands), len(out_shape)

    def body(*refs):
        sources, results, refs = refs[:many], refs[many : many + given], refs[many + given :]
        if storing:
            out_held, out_sems, refs = refs[-given - 1 : -1], refs[-1], refs[: -given - 1]
        held, sems, rest = refs[-many - 1 : -1], refs[-1], refs[: -many - 1]
        fetch = Fetch(sources, held, sems)
        if storing:
            fetch.keep(out_held, results, out_sems)
            kernel(fetch, *held, *out_held, *rest)
            fetch.flush()
        else:
            kernel(fetch, *held, *results, *rest)

    return pl.pallas_call(
        body,
        out_shape=tuple(out_shape),
        in_specs=[pl.BlockSpec(memory_space=pl.ANY)] * many,
        out_specs=tuple([pl.BlockSpec(memory_space=pl.ANY)] * given if storing else vmem(given)),
        scratch_shapes=list(scratch_shapes)
        + [pltpu.VMEM(item.shape, item.dtype) for item in operands]
        + [pltpu.SemaphoreType.DMA((many,))]
        + ([pltpu.VMEM(item.shape, item.dtype) for item in out_shape] if storing else [])
        + ([pltpu.SemaphoreType.DMA((given,))] if storing else []),
        compiler_params=pltpu.CompilerParams(
            collective_id=kernel_id, has_side_effects=True, vmem_limit_bytes=62 * 2**20
        ),
        name=name,
    )(*operands)


class LineGather:
    def __init__(self, count, place, slot_of, sems):
        self.count, self.place, self.last, self.slot_of = count, place, count - 1, slot_of
        self.up_send, self.down_send, self.arrived = sems

    def shift(self, owner, up):
        slot = self.slot_of(owner)
        to = self.place + 1 if up else self.place - 1
        sent = (self.up_send if up else self.down_send).at[owner]
        return remote(slot, slot, sent, self.arrived.at[owner], {LINE: to})

    def start(self):
        @pl.when(self.place < self.last)
        def _():
            self.shift(self.place, True).start()

        @pl.when(self.place > 0)
        def _():
            self.shift(self.place, False).start()

    def arrive(self, distance):
        @pl.when(self.place >= distance)
        def _():
            self.shift(self.place - distance, True).wait_recv()

            @pl.when(self.place < self.last)
            def _():
                self.shift(self.place - distance, True).start()

        @pl.when(self.place + distance <= self.last)
        def _():
            self.shift(self.place + distance, False).wait_recv()

            @pl.when(self.place > 0)
            def _():
                self.shift(self.place + distance, False).start()

    def settle(self):
        for owner in range(self.count):

            @pl.when((self.place < self.last) & (owner <= self.place))
            def _():
                self.shift(owner, True).wait_send()

            @pl.when((self.place > 0) & (owner >= self.place))
            def _():
                self.shift(owner, False).wait_send()


class LineScatter:
    def __init__(self, count, place, pieces, value_of, land, stage, sems):
        self.count, self.place, self.last, self.pieces = count, place, count - 1, pieces
        self.value_of, self.land, self.stage = value_of, land, stage
        self.from_left, self.from_right, self.to_left, self.to_right = sems

    def pass_on(self, owner, piece, right):
        side = 0 if right else 1
        return remote(
            self.stage.at[side, owner, piece],
            self.land.at[side, owner, piece],
            (self.to_right if right else self.to_left).at[owner, piece],
            (self.from_left if right else self.from_right).at[owner, piece],
            {LINE: self.place + 1 if right else self.place - 1},
        )

    def relay(self, distance, right, chosen=None):
        owner = self.place + distance if right else self.place - distance
        source = (self.place == 0) if right else (self.place == self.last)
        side = 0 if right else 1

        @pl.when((owner <= self.last) if right else (owner >= 0))
        def _():
            for piece in chosen if chosen is not None else range(self.pieces):

                @pl.when(source)
                def _():
                    self.stage[side, owner, piece] = self.value_of(owner, piece)

                @pl.when(jnp.logical_not(source))
                def _():
                    self.pass_on(owner, piece, right).wait_recv()
                    self.stage[side, owner, piece] = (
                        self.value_of(owner, piece).astype(WIDE) + self.land[side, owner, piece].astype(WIDE)
                    ).astype(NARROW)

                self.pass_on(owner, piece, right).start()

    def relay_both(self, distance, chosen=None):
        self.relay(distance, True, chosen)
        self.relay(distance, False, chosen)

    def total(self, piece):
        place = self.place

        @pl.when(place > 0)
        def _():
            self.pass_on(place, piece, True).wait_recv()

        @pl.when(place < self.last)
        def _():
            self.pass_on(place, piece, False).wait_recv()

        left_part = jnp.where(place > 0, self.land[0, place, piece].astype(WIDE), 0.0)
        right_part = jnp.where(place < self.last, self.land[1, place, piece].astype(WIDE), 0.0)
        return self.value_of(place, piece).astype(WIDE) + left_part + right_part

    def settle(self):
        for owner in range(self.count):
            for piece in range(self.pieces):

                @pl.when(owner > self.place)
                def _():
                    self.pass_on(owner, piece, True).wait_send()

                @pl.when(owner < self.place)
                def _():
                    self.pass_on(owner, piece, False).wait_send()


def gather_sems(count):
    return [pltpu.SemaphoreType.DMA((count,))] * 3


def scatter_sems(count, pieces):
    return [pltpu.SemaphoreType.DMA((count, pieces))] * 4


def line_sum(count, place, part_ref, land, cross, stage, total, sems, consume, plan=(), make=None, pieces=1):
    in_send, land_recv, cross_recv, out_send, out_recv = sems
    depth = part_ref.shape[0] // CHUNKS
    half = count // 2
    left = place < half
    level = jnp.where(left, place, count - 1 - place)
    inner = jnp.where(left, place + 1, place - 1)
    outer = jnp.where(left, place - 1, place + 1)
    is_end, is_middle = level == 0, level == half - 1

    def rows_of(chunk):
        return pl.ds(pl.multiple_of(chunk * depth, depth), depth)

    def inward(chunk):
        rows = rows_of(chunk)
        return remote(stage.at[rows], land.at[rows], in_send.at[chunk], land_recv.at[chunk], {LINE: inner})

    def across(chunk):
        rows = rows_of(chunk)
        return remote(stage.at[rows], cross.at[rows], in_send.at[chunk], cross_recv.at[chunk], {LINE: inner})

    def outward(chunk):
        rows = rows_of(chunk)
        return remote(total.at[rows], total.at[rows], out_send.at[chunk], out_recv.at[chunk], {LINE: outer})

    def send_in(chunk):
        @pl.when(is_middle)
        def _():
            across(chunk).start()

        @pl.when(jnp.logical_not(is_middle))
        def _():
            inward(chunk).start()

    def gather_in(chunk):
        rows = rows_of(chunk)
        inward(chunk).wait_recv()
        stage[rows] = (part_ref[rows].astype(WIDE) + land[rows].astype(WIDE)).astype(NARROW)
        send_in(chunk)

    def finish(chunk):
        rows = rows_of(chunk)

        @pl.when(is_middle)
        def _():
            across(chunk).wait_recv()
            total[rows] = (stage[rows].astype(WIDE) + cross[rows].astype(WIDE)).astype(NARROW)

        @pl.when(jnp.logical_not(is_middle))
        def _():
            outward(chunk).wait_recv()

        @pl.when(jnp.logical_not(is_end))
        def _():
            outward(chunk).start()

        consume(rows)

    def begin(chunk, carry):
        rows = rows_of(chunk)
        stage[rows] = part_ref[rows]
        send_in(chunk)
        return carry

    def step(number, carry):
        for when, work in plan:

            @pl.when((number == when) & (jnp.logical_not(is_end) | (when > AT_ONCE)))
            def _():
                work()

        @pl.when(jnp.logical_not(is_end) & (number < CHUNKS))
        def _():
            gather_in(number)

        @pl.when(number >= LAG)
        def _():
            finish(number - LAG)

        return carry

    for piece in range(pieces):
        if make is not None:
            make(piece)

        @pl.when(is_end)
        def _():
            lax.fori_loop(piece * CHUNKS // pieces, (piece + 1) * CHUNKS // pieces, begin, 0)

    @pl.when(is_end)
    def _():
        for when, work in plan:
            if when <= AT_ONCE:
                work()

    lax.fori_loop(0, CHUNKS + LAG, step, 0)

    def settle(chunk, carry):
        @pl.when(is_middle)
        def _():
            across(chunk).wait_send()

        @pl.when(jnp.logical_not(is_middle))
        def _():
            inward(chunk).wait_send()

        @pl.when(jnp.logical_not(is_end))
        def _():
            outward(chunk).wait_send()

        return carry

    lax.fori_loop(0, CHUNKS, settle, 0)


def forward_kernel(
    count, frames, fetch, hidden_ref, in_ref, base_ref, rows_ref, outproj_ref,
    out_ref, next_ref, normed_ref, packed_ref, heads_ref,
    part_ref, key_rows, value_rows, probs_low, land, cross, stage, *sems
):
    place = lax.axis_index(LINE)
    greet_line(place, count)
    fetch(0, 1, 4)
    patches = hidden_ref.shape[0] // frames
    local = heads_ref.shape[1]

    def make(frame):
        rows = slice(frame * patches, (frame + 1) * patches)
        packed = dot(hidden_ref[rows], in_ref[...], 1, 1).astype(NARROW)
        packed_ref[rows] = packed
        asked, keys, values = (packed[:, i * local : (i + 1) * local] for i in range(3))
        spread_heads(keys, key_rows)
        spread_heads(values, value_rows)
        for head in range(local // HD):
            spot = slice(head * patches, (head + 1) * patches)
            scores = HD ** (-0.5) * dot(asked, key_rows[spot], 1, 1)
            raised = jnp.exp(scores - jnp.max(scores, axis=-1, keepdims=True))
            probs_low[:, spot] = (raised * (1.0 / jnp.sum(raised, axis=-1, keepdims=True))).astype(NARROW)
        found = dot(probs_low[...], value_rows[...], 1, 0).astype(NARROW)
        heads_ref[rows] = found
        part_ref[rows] = dot(found, outproj_ref[...], 1, 0).astype(NARROW)
        if frame == frames - 1:
            fetch()

    def consume(rows):
        gate, gain, shift = (rows_ref[i : i + 1] for i in (2, 10, 3))
        moved = base_ref[rows] + gate * out_ref[rows].astype(WIDE)
        next_ref[rows] = moved
        normed_ref[rows] = (norm_parts(moved)[0] * gain + shift).astype(NARROW)

    line_sum(count, place, part_ref, land, cross, stage, out_ref, sems, consume, make=make, pieces=frames)


def backward_kernel(count, groups, frames_axis, widths, fetch, *refs):
    part_ref, base_ref, grad_ref, below_ref, rows_ref, *refs = refs
    pairs, refs = [refs[0:2], refs[2:4]], refs[4:]
    sources, refs = refs[: len(widths) - 1], refs[max(len(widths) - 1, 0) :]
    moved_ref, low_ref, sums_ref, *refs = refs
    many = sum(len(columns) for columns in widths)
    results, refs = refs[:many], refs[many:]
    product_ref, total, land, cross, stage, tally, *refs = refs
    sems, scratch = refs[:5], refs[5:]
    place = lax.axis_index(LINE)
    early = Products(pairs, product_ref).work()
    scatters = Scatters(
        groups, frames_axis, [*sources, product_ref] if widths else [], widths, results, scratch
    )
    greet_line(place, count, 0, scatters.partners() if widths else ())
    fetch()
    plan = [(0, work) for work in early]
    if widths:
        scatters.items[0].start()
        first, last = scatters.folds(0), scatters.folds(len(widths) - 1)
        plan += [(1, scatters.items[-1].start), (2, first[0]), (4, last[0]), (9, first[1]), (14, last[1])]
    gain, gate = (rows_ref[i : i + 1] for i in (10, 2))
    tally[...] = jnp.zeros_like(tally)

    def consume(rows):
        grads = total[rows].astype(WIDE)
        normal, spread = norm_parts(base_ref[rows])
        moved = grad_ref[rows] + norm_pull(grads * gain, normal, spread)
        moved_ref[rows] = moved
        low_ref[rows] = (gate * moved).astype(NARROW)
        for i, terms in enumerate((grads, grads * normal, moved * below_ref[rows].astype(WIDE))):
            tally[i] += jnp.sum(terms.reshape(-1, 8, terms.shape[-1]), axis=0)

    line_sum(count, place, part_ref, land, cross, stage, total, sems, consume, plan)
    sums_ref[...] = jnp.zeros_like(sums_ref)
    for i in range(3):
        sums_ref[i : i + 1] = jnp.sum(tally[i], axis=0, keepdims=True)
    scatters.finish()


def line_sems():
    return [pltpu.SemaphoreType.DMA((CHUNKS,))] * 5


def call_forward(count, frames, hidden, in_w, base, rows, out_w):
    shape, local = hidden.shape, out_w.shape[0]
    patches = shape[0] // frames
    wide_keys = local // HD * patches
    return fetching_call(
        functools.partial(forward_kernel, count, frames),
        [hidden, in_w, base, rows, out_w],
        (
            jax.ShapeDtypeStruct(shape, NARROW),
            jax.ShapeDtypeStruct(shape, WIDE),
            jax.ShapeDtypeStruct(shape, NARROW),
            jax.ShapeDtypeStruct((shape[0], 3 * local), NARROW),
            jax.ShapeDtypeStruct((shape[0], local), NARROW),
        ),
        [
            pltpu.VMEM(shape, NARROW),
            pltpu.VMEM((wide_keys, local), NARROW),
            pltpu.VMEM((wide_keys, local), NARROW),
            pltpu.VMEM((patches, wide_keys), NARROW),
        ]
        + [pltpu.VMEM(shape, NARROW)] * 3
        + line_sems(),
        1,
        "forward_sum",
    )


def call_backward(count, groups, frames_axis, part, base, grad, below, rows, pairs, sources, widths):
    shape = part.shape
    results, scratch = Scatters.shapes(groups, frames_axis, shape[1], widths)
    product = (shape[1], sum(second.shape[1] for _, second in pairs))
    if not widths:
        results = [jax.ShapeDtypeStruct(product, NARROW)]
    return fetching_call(
        functools.partial(backward_kernel, count, groups, frames_axis, widths),
        [part, base, grad, below, rows, *(item for pair in pairs for item in pair), *sources],
        (
            jax.ShapeDtypeStruct(shape, WIDE),
            jax.ShapeDtypeStruct(shape, NARROW),
            jax.ShapeDtypeStruct((8, shape[1]), WIDE),
            *results,
        ),
        ([pltpu.VMEM(product, NARROW)] if widths else [])
        + [pltpu.VMEM(shape, NARROW)] * 4
        + [pltpu.VMEM((3, 8, shape[1]), WIDE)]
        + line_sems()
        + scratch,
        2,
        "backward_sum",
    )


def head_mask(head, shape):
    lane = lax.broadcasted_iota(jnp.int32, shape, len(shape) - 1)
    return (lane >= head * HD) & (lane < (head + 1) * HD)


def spread_heads(values, result):
    rows = values.shape[0]
    for head in range(values.shape[1] // HD):
        kept = jnp.where(head_mask(head, values.shape), values.astype(WIDE), 0.0)
        result[head * rows : (head + 1) * rows] = kept.astype(NARROW)


def collect_heads(values, rows):
    found = jnp.zeros((rows, values.shape[1]), WIDE)
    for head in range(values.shape[0] // rows):
        found = jnp.where(head_mask(head, found.shape), values[head * rows : (head + 1) * rows], found)
    return found


def spatial_backward(given, asked, keys, values, key_rows, value_rows, probs_low, scores_low):
    rows, scale = asked.shape[0], HD ** (-0.5)
    heads = asked.shape[1] // HD
    spread_heads(keys, key_rows)
    spread_heads(values, value_rows)
    for head in range(heads):
        spot = slice(head * rows, (head + 1) * rows)
        scores = scale * dot(asked, key_rows[spot], 1, 1)
        raised = jnp.exp(scores - jnp.max(scores, axis=-1, keepdims=True))
        probs = raised * (1.0 / jnp.sum(raised, axis=-1, keepdims=True))
        pulled = dot(given, value_rows[spot], 1, 1)
        moved = probs * (pulled - jnp.sum(pulled * probs, axis=-1, keepdims=True))
        probs_low[:, spot] = probs.astype(NARROW)
        scores_low[:, spot] = moved.astype(NARROW)
    grad_query = scale * dot(scores_low[...], key_rows[...], 1, 0)
    grad_keys = scale * collect_heads(dot(scores_low[...], asked, 0, 0), rows)
    grad_values = collect_heads(dot(probs_low[...], given, 0, 0), rows)
    return grad_query, grad_keys, grad_values


def closing_kernel(count, groups, frames_axis, frames, widths, fetch, *refs):
    (
        low_ref, base_ref, grad_ref, gate_part, rows_ref, packed_ref, heads_ref, hidden_ref, in_ref, out_ref,
        text_ref, sums_temporal, sums_middle, side_ref, *refs,
    ) = refs
    sources, refs = refs[: len(widths) - 1], refs[max(len(widths) - 1, 0) :]
    latent_ref, every_ref, text_all, *refs = refs
    many = sum(len(columns) for columns in widths)
    results, refs = refs[:many], refs[many:]
    (
        product_ref, part_ref, grad_packed, key_rows, value_rows, probs_low, scores_low,
        land, stage, line_rows, own_rows, tally, *refs,
    ) = refs
    line_send, line_recv, all_send, all_recv = refs[4:8]
    place, group, here = (lax.axis_index(axis) for axis in (LINE, GROUP, FRAME))
    last = count - 1
    share = latent_ref.shape[1]
    local = out_ref.shape[0]
    everyone = groups * frames_axis
    rank = group * frames_axis + here
    products = Products([(hidden_ref, grad_packed), (low_ref, heads_ref)], product_ref)
    scatters = Scatters(groups, frames_axis, [*sources, product_ref] if widths else [], widths, results, refs[13:])
    exchange = GroupExchange(groups, frames_axis, text_ref, text_all, refs[8:13])

    def member(ahead):
        to = lax.rem(rank + ahead, everyone)
        return {GROUP: lax.div(to, frames_axis), FRAME: lax.rem(to, frames_axis)}

    def neighbour(ahead):
        return {LINE: lax.rem(place + ahead, count)}

    barrier = pltpu.get_barrier_semaphore()

    def greet(ahead, carry):
        pl.semaphore_signal(barrier, inc=1, device_id=member(ahead), device_id_type=MESH)
        return carry

    for ahead in range(1, count):
        pl.semaphore_signal(barrier, inc=1, device_id=neighbour(ahead), device_id_type=MESH)
    lax.fori_loop(1, everyone, greet, 0)
    pl.semaphore_wait(barrier, last + everyone - 1)
    fetch(0, 5, 8, 9, 10)

    def rows_of(owner):
        return pl.ds(pl.multiple_of(owner * share, share), share)

    passing = LineScatter(
        count, place, frames, lambda owner, frame: part_ref[frame, rows_of(owner)], land, stage, refs[0:4]
    )
    patches = base_ref.shape[1]
    exchange.start()
    for frame in range(frames):
        rows = slice(frame * patches, (frame + 1) * patches)
        given = dot(low_ref[rows], out_ref[...], 1, 1).astype(NARROW)
        asked, keys, values = (packed_ref[rows, i * local : (i + 1) * local] for i in range(3))
        parts = jnp.zeros(part_ref.shape[1:], WIDE)
        found = spatial_backward(given, asked, keys, values, key_rows, value_rows, probs_low, scores_low)
        for i, item in enumerate(found):
            low = item.astype(NARROW)
            grad_packed[rows, i * local : (i + 1) * local] = low
            parts = parts + dot(low, in_ref[i * local : (i + 1) * local], 1, 0)
        part_ref[frame] = parts.astype(NARROW)
        passing.relay_both(last, (frame,))
        if frame == 0:
            exchange.spread()
    if last > 1:
        passing.relay_both(last - 1, (0,))
    fetch()
    for work in products.work():
        work()
    if widths:
        scatters.items[-1].start()
    if last > 1:
        passing.relay_both(last - 1, tuple(range(1, frames)))

    tally[...] = jnp.zeros_like(tally)
    depth = 32
    blocks = base_ref.shape[1] // depth

    def add_rows(number, carry):
        frame, rows = lax.div(number, blocks), pl.ds(pl.multiple_of(lax.rem(number, blocks) * depth, depth), depth)
        normal = norm_parts(base_ref[frame, rows])[0]
        grads = part_ref[frame, rows].astype(WIDE)
        for i, terms in enumerate((grads, grads * normal)):
            tally[i] += jnp.sum(terms.reshape(-1, 8, terms.shape[-1]), axis=0)
        return carry

    lax.fori_loop(0, frames * blocks, add_rows, 0)
    line_rows[place] = jnp.zeros(line_rows.shape[1:], WIDE)
    line_rows[place, 2:3] = gate_part[0:1]
    for i in range(2):
        line_rows[place, i : i + 1] = jnp.sum(tally[i], axis=0, keepdims=True)

    def line_copy(ahead):
        return remote(
            line_rows.at[place], line_rows.at[place], line_send.at[ahead], line_recv.at[ahead], neighbour(ahead)
        )

    def all_copy(ahead):
        return remote(
            own_rows, every_ref.at[rank], all_send.at[ahead], all_recv.at[ahead], member(ahead)
        )

    for ahead in range(1, count):
        line_copy(ahead).start()
    if widths:
        scatters.items[-1].first_round()
    for distance in range(last - 2, 0, -1):
        passing.relay_both(distance)
    for ahead in range(1, count):
        line_copy(ahead).wait_recv()
    summed = line_rows[0]
    for i in range(1, count):
        summed = summed + line_rows[i]
    own_rows[0:8] = summed
    picked = ((sums_temporal, (2, 0, 1)), (sums_middle, (3, 0, 1, 2)), (side_ref, (0,)))
    for i, (source, row) in enumerate((source, row) for source, rows in picked for row in rows):
        own_rows[8 + i : 9 + i] = source[row : row + 1]
    every_ref[rank] = own_rows[...]

    def send_rows(ahead, carry):
        all_copy(ahead).start()
        return carry

    lax.fori_loop(1, everyone, send_rows, 0)
    if widths:
        scatters.items[-1].second_round()

    own = rows_of(place)
    for frame in range(frames):
        grads = passing.total(frame)
        normal, spread = norm_parts(base_ref[frame, own])
        latent_ref[frame] = (
            grad_ref[frame, own] + norm_pull(grads * rows_ref[9:10], normal, spread)
        ).astype(NARROW)

    passing.settle()
    for ahead in range(1, count):
        line_copy(ahead).wait_send()

    def settle(ahead, carry):
        all_copy(ahead).wait_recv()
        all_copy(ahead).wait_send()
        return carry

    lax.fori_loop(1, everyone, settle, 0)
    exchange.finish()
    scatters.finish()


def call_closing(
    count, groups, frames_axis, low, base, grad, gate_part, rows, packed, heads, hidden, in_w, out_w, text, sums, sources,
    widths,
):
    frames, patches, features = base.shape
    everyone = groups * frames_axis
    share = patches // count
    local = out_w.shape[0]
    results, scratch = Scatters.shapes(groups, frames_axis, features, widths)
    product = (features, packed.shape[1] + local)
    if not widths:
        results = [jax.ShapeDtypeStruct(product, NARROW)]
    dma = pltpu.SemaphoreType.DMA
    wide_keys = local // HD * patches
    return fetching_call(
        functools.partial(closing_kernel, count, groups, frames_axis, frames, widths),
        [low, base, grad, gate_part, rows, packed, heads, hidden, in_w, out_w, text, *sums, *sources],
        (
            jax.ShapeDtypeStruct((frames, share, features), NARROW),
            jax.ShapeDtypeStruct((everyone, 16, features), WIDE),
            jax.ShapeDtypeStruct((groups,) + text.shape, NARROW),
            *results,
        ),
        ([pltpu.VMEM(product, NARROW)] if widths else [])
        + [
            pltpu.VMEM((frames, patches, features), NARROW),
            pltpu.VMEM(packed.shape, NARROW),
            pltpu.VMEM((wide_keys, local), NARROW),
            pltpu.VMEM((wide_keys, local), NARROW),
            pltpu.VMEM((patches, wide_keys), NARROW),
            pltpu.VMEM((patches, wide_keys), NARROW),
            pltpu.VMEM((2, count, frames, share, features), NARROW),
            pltpu.VMEM((2, count, frames, share, features), NARROW),
            pltpu.VMEM((count, 8, features), WIDE),
            pltpu.VMEM((16, features), WIDE),
            pltpu.VMEM((2, 8, features), WIDE),
        ]
        + scatter_sems(count, frames)
        + [dma((count,))] * 2
        + [dma((everyone,))] * 2
        + GroupExchange.scratch(groups, frames_axis, text.shape)
        + scratch,
        4,
        "closing",
    )


def finishing_kernel(groups, frames_axis, modulation_rows, layouts, small_ref, ada_ref, text_ref, captions_ref, *refs):
    many = len(layouts)
    sources, refs = refs[:many], refs[many:]
    ada_out, table_out, gain_out, caption_out, *results, sems = refs
    moves = [
        pltpu.make_async_copy(source, result, sems.at[i])
        for i, (source, result, layout) in enumerate(zip(sources, results, layouts))
        if layout == 0
    ]
    for move in moves:
        move.start()
    local = table_out.shape[1]
    buckets = table_out.shape[0]
    column = ada_out.shape[1]
    features = small_ref.shape[2]
    rank = lax.axis_index(GROUP) * frames_axis + lax.axis_index(FRAME)

    def over_frames(group, row):
        first = group * frames_axis
        found = small_ref[first, row : row + 1]
        for other in range(1, frames_axis):
            found = found + small_ref[first + other, row : row + 1]
        return found

    gain = over_frames(0, 14)
    for group in range(1, groups):
        gain = gain + over_frames(group, 14)
    for i in range(gain_out.shape[0]):
        gain_out[i : i + 1] = gain[:, i * 128 : (i + 1) * 128]

    side = jnp.concatenate([small_ref[group * frames_axis, 15:16] for group in range(groups)], axis=0)
    cond, chosen = side[:, 0:local], side[:, local : local + buckets]
    below = 1.0 / (1.0 + jnp.exp(-cond))
    act_low = (cond * below).astype(NARROW)
    act_twice = jnp.concatenate([act_low, act_low], axis=0)
    where = lax.broadcasted_iota(jnp.int32, (features, column), 0)
    which = lax.broadcasted_iota(jnp.int32, (features, column), 1) + rank * column
    select = jnp.where(where == which, 1.0, 0.0).astype(NARROW)
    grad_act = jnp.zeros((2 * groups, local), WIDE)
    pairs = []
    for k, row in enumerate(modulation_rows):
        rows = jnp.concatenate([over_frames(group, row) for group in range(groups)], axis=0)
        high, rest = split_pair(rows)
        pair = jnp.concatenate([high.astype(WIDE), rest.astype(WIDE)], axis=0)
        pairs.append(pair)
        grad_act = grad_act + dot(pair.astype(NARROW), ada_ref[k], 1, 1)
    columns = dot(jnp.concatenate(pairs, axis=0).astype(NARROW), select, 1, 0)
    for k in range(len(modulation_rows)):
        rows = columns[2 * groups * k : 2 * groups * (k + 1)].astype(NARROW)
        ada_out[k] = dot(rows, act_twice, 0, 0)
    slope = below * (1.0 + cond * (1.0 - below))
    grad_cond = (grad_act[0:groups] + grad_act[groups:]) * slope
    spread = jnp.concatenate(split_pair(grad_cond), axis=0)
    chosen = chosen.astype(NARROW)
    table_out[...] = dot(jnp.concatenate([chosen, chosen], axis=0), spread, 0, 0)

    slots = captions_ref.shape[1]
    caption = dot(text_ref[0, :, 0:slots], captions_ref[0], 1, 0)
    for group in range(1, groups):
        caption = caption + dot(text_ref[group, :, 0:slots], captions_ref[group], 1, 0)
    caption_out[...] = caption
    for source, result, layout in zip(sources, results, layouts):
        if layout > 0:
            parts = source.shape[1] // local
            for i in range(parts):
                values = source[:, i * local : (i + 1) * local]
                if layout == 1:
                    result[i] = values
                else:
                    result[:, i] = values
    for move in moves:
        move.wait()


def call_finishing(groups, frames_axis, buckets, modulation_rows, layouts, small, ada, text, captions, sources):
    parts, local, features = ada.shape
    block = features // (groups * frames_axis)

    def shape_of(source, layout):
        n = source.shape[1] // local
        return (source.shape, (n, source.shape[0], local), (source.shape[0], n, local))[layout]

    results = [
        jax.ShapeDtypeStruct((parts, block, local), WIDE),
        jax.ShapeDtypeStruct((buckets, local), WIDE),
        jax.ShapeDtypeStruct((features // 128, 128), WIDE),
        jax.ShapeDtypeStruct((local, captions.shape[2]), WIDE),
    ]
    results += [
        jax.ShapeDtypeStruct(shape_of(source, layout), source.dtype) for source, layout in zip(sources, layouts)
    ]
    places = [pl.BlockSpec(memory_space=pltpu.VMEM if layout else pl.ANY) for layout in layouts]
    return pl.pallas_call(
        functools.partial(finishing_kernel, groups, frames_axis, modulation_rows, layouts),
        out_shape=tuple(results),
        in_specs=vmem(4 + len(sources)),
        out_specs=tuple(vmem(4) + places),
        scratch_shapes=[pltpu.SemaphoreType.DMA((len(sources),))],
        compiler_params=pltpu.CompilerParams(vmem_limit_bytes=62 * 2**20),
        name="finishing",
    )(small, ada, text, captions, *sources)


def opening_kernel(
    count, groups, frames_axis, bucket_ref, clip_ref, window_ref, counts_ref, latent_ref, table_ref, gain_ref,
    ada_ref, captions_ref, caption_full, caption_w,
    base_ref, normed_ref, mods_ref, text_out, side_out, window_out, bias_out, spread_ref,
    caption_here, caption_here_w, caption_sem, land, ada, mine, others,
    up_send, down_send, land_recv, ada_sem, mods_send, mods_recv, cap_send, cap_recv, cap_local,
):
    place = lax.axis_index(LINE)
    group = lax.axis_index(GROUP)
    here = lax.axis_index(FRAME)
    last = count - 1
    width = spread_ref.shape[2]
    parts = ada_ref.shape[0]
    share = latent_ref.shape[1]

    loads = [pltpu.make_async_copy(ada_ref.at[k], ada.at[k], ada_sem.at[k]) for k in range(parts)]
    for load in loads:
        load.start()
    text_loads = [
        pltpu.make_async_copy(caption_full, caption_here, caption_sem.at[0]),
        pltpu.make_async_copy(caption_w, caption_here_w, caption_sem.at[1]),
    ]
    for load in text_loads:
        load.start()

    barrier = pltpu.get_barrier_semaphore()
    for ahead in range(1, count):
        pl.semaphore_signal(
            barrier, inc=1, device_id={LINE: lax.rem(place + ahead, count)}, device_id_type=MESH
        )
    for ahead in range(1, groups):
        pl.semaphore_signal(
            barrier, inc=1, device_id={GROUP: lax.rem(group + ahead, groups)}, device_id_type=MESH
        )
    pl.semaphore_wait(barrier, count - 1 + groups - 1)

    def shift(owner, up):
        to = place + 1 if up else place - 1
        return remote(
            land.at[owner], land.at[owner], (up_send if up else down_send).at[owner], land_recv.at[owner], {LINE: to}
        )

    land[place] = latent_ref[...]

    @pl.when(place < last)
    def _():
        shift(place, True).start()

    @pl.when(place > 0)
    def _():
        shift(place, False).start()

    def caption_block(to):
        if len(captions_ref.shape) == 3:
            return captions_ref.at[to]
        first = pl.multiple_of((to * frames_axis + here) * width, width)
        return captions_ref.at[:, pl.ds(first, width)]

    def caption_copy(ahead):
        to = lax.rem(group + ahead, groups)
        return remote(
            caption_block(to),
            spread_ref.at[group],
            cap_send.at[ahead],
            cap_recv.at[ahead],
            {GROUP: to},
        )

    own_caption = pltpu.make_async_copy(caption_block(group), spread_ref.at[group], cap_local)
    own_caption.start()
    for ahead in range(1, groups):
        caption_copy(ahead).start()

    def arrive(distance):
        @pl.when(place >= distance)
        def _():
            shift(place - distance, True).wait_recv()

            @pl.when(place < last)
            def _():
                shift(place - distance, True).start()

        @pl.when(place + distance <= last)
        def _():
            shift(place + distance, False).wait_recv()

            @pl.when(place > 0)
            def _():
                shift(place + distance, False).start()

    buckets, local = table_ref.shape
    frames = latent_ref.shape[0]
    is_row = lax.broadcasted_iota(jnp.int32, (buckets, local), 0) == bucket_ref[0]
    cond = jnp.sum(jnp.where(is_row, table_ref[...].astype(WIDE), 0.0), axis=0, keepdims=True)
    act = jnp.broadcast_to(swish_act(cond), (16, local)).astype(NARROW)
    side_out[...] = jnp.zeros_like(side_out)
    side_out[0:1, 0:local] = cond
    is_column = lax.broadcasted_iota(jnp.int32, (1, buckets), 1) == bucket_ref[0]
    side_out[0:1, local : local + buckets] = jnp.where(is_column, 1.0, 0.0)
    total = clip_ref.shape[1]
    text_length = caption_full.shape[0] // counts_ref.shape[1]
    lane = lax.broadcasted_iota(jnp.int32, bias_out.shape[1:], 1)
    for frame in range(frames):
        own = here * frames + frame
        for offset in range(WIN):
            other = own + offset - 2
            same = clip_ref[0, jnp.clip(other, 0, total - 1)] == clip_ref[0, own]
            reads = same & (other >= 0) & (other < total)
            if offset != 2:
                reads = reads & (window_ref[0, frame, offset] == 1)
            row = frame * WIN + offset
            window_out[row : row + 1] = jnp.full((1, window_out.shape[1]), jnp.where(reads, 0.0, NEGATIVE))
        bias = jnp.full(bias_out.shape[1:], NEGATIVE)
        for clip in range(counts_ref.shape[1]):
            first = clip * text_length
            end = jnp.where(clip_ref[0, own] == clip, first + counts_ref[0, clip], first)
            bias = jnp.where((lane >= first) & (lane < end), 0.0, bias)
        bias_out[frame] = bias

    def weigh(k):
        loads[k].wait()
        product = dot(act, ada[k], 1, 0)
        mine[k : k + 1] = product[0:1]

    def mods_copy(ahead):
        return remote(
            mine, others.at[place], mods_send.at[ahead], mods_recv.at[ahead], {LINE: lax.rem(place + ahead, count)}
        )

    mine[...] = jnp.zeros_like(mine)
    cut = parts // 2 + 1
    for k in range(cut):
        weigh(k)
    arrive(1)
    for k in range(cut, parts):
        weigh(k)
    for ahead in range(1, count):
        mods_copy(ahead).start()
    others[place] = mine[...]
    for load in text_loads:
        load.wait()
    text_here = dot(caption_here_w[...], caption_here[...], 1, 1).astype(NARROW)
    slots = text_here.shape[1]
    text_out[:, 0:slots] = text_here
    if text_out.shape[1] > slots:
        text_out[:, slots:] = jnp.zeros((text_out.shape[0], text_out.shape[1] - slots), NARROW)
    for distance in range(2, count - 1):
        arrive(distance)
    for ahead in range(1, count):
        mods_copy(ahead).wait_recv()
    mods = others[0]
    for i in range(1, count):
        mods = mods + others[i]
    mods_ref[...] = mods
    for i, row in enumerate((1, 4, 7)):
        mods_ref[9 + i : 10 + i] = 1.0 + mods[row : row + 1]
    for i in range(gain_ref.shape[0]):
        mods_ref[12:13, i * 128 : (i + 1) * 128] = gain_ref[i : i + 1].astype(WIDE)
    gain = 1.0 + mods[1:2]
    shift_row = mods[0:1]

    def norm_owner(owner):
        for f in range(latent_ref.shape[0]):
            values = land[owner, f].astype(WIDE)
            rows = pl.ds(pl.multiple_of(owner * share, share), share)
            base_ref[f, rows] = values
            normed_ref[f, rows] = (norm_parts(values)[0] * gain + shift_row).astype(NARROW)

    def near(distance):
        @pl.when(place >= distance)
        def _():
            norm_owner(place - distance)

        @pl.when(place + distance <= last)
        def _():
            norm_owner(place + distance)

    norm_owner(place)
    for distance in range(1, count - 1):
        near(distance)
    if count > 2:
        arrive(count - 1)
    near(count - 1)

    for owner in range(count):

        @pl.when((place < last) & (owner <= place))
        def _():
            shift(owner, True).wait_send()

        @pl.when((place > 0) & (owner >= place))
        def _():
            shift(owner, False).wait_send()

    for ahead in range(1, count):
        mods_copy(ahead).wait_send()
    for ahead in range(1, groups):
        caption_copy(ahead).wait_send()
        caption_copy(ahead).wait_recv()
    own_caption.wait()


def call_opening(count, groups, frames_axis, scalars, latent, table, gain, ada, captions, caption_w):
    frames, share, features = latent.shape
    parts = ada.shape[0]
    length, text_width = captions.shape
    width = text_width // (groups * frames_axis)
    caption_full = captions
    if width % 128:
        blocks = captions.reshape(length, groups, frames_axis, width)
        captions = jnp.transpose(
            lax.dynamic_index_in_dim(blocks, lax.axis_index(FRAME), 2, keepdims=False), (1, 0, 2)
        )
    full = (frames, share * count, features)
    dma = pltpu.SemaphoreType.DMA
    anywhere = pl.BlockSpec(memory_space=pl.ANY)
    return pl.pallas_call(
        functools.partial(opening_kernel, count, groups, frames_axis),
        out_shape=(
            jax.ShapeDtypeStruct(full, WIDE),
            jax.ShapeDtypeStruct(full, NARROW),
            jax.ShapeDtypeStruct((16, features), WIDE),
            jax.ShapeDtypeStruct((caption_w.shape[0], length + -length % 128), NARROW),
            jax.ShapeDtypeStruct((8, features), WIDE),
            jax.ShapeDtypeStruct((frames * WIN, 128), WIDE),
            jax.ShapeDtypeStruct((frames, 8, length + -length % 128), WIDE),
            jax.ShapeDtypeStruct((groups, length, width), NARROW),
        ),
        in_specs=[pl.BlockSpec(memory_space=pltpu.SMEM)] * 4 + vmem(3) + [anywhere] * 4,
        out_specs=tuple(vmem(7) + [anywhere]),
        scratch_shapes=[
            pltpu.VMEM(caption_full.shape, NARROW),
            pltpu.VMEM(caption_w.shape, NARROW),
            dma((2,)),
            pltpu.VMEM((count, frames, share, features), NARROW),
            pltpu.VMEM(ada.shape, NARROW),
            pltpu.VMEM((16, features), WIDE),
            pltpu.VMEM((count, 16, features), WIDE),
            dma((count,)),
            dma((count,)),
            dma((count,)),
            dma((parts,)),
            dma((count,)),
            dma((count,)),
            dma((groups,)),
            dma((groups,)),
            dma,
        ],
        compiler_params=pltpu.CompilerParams(
            collective_id=3, has_side_effects=True, vmem_limit_bytes=62 * 2**20
        ),
        name="opening",
    )(*scalars, latent, table, gain, ada, captions, caption_full, caption_w)


STAGES = 4
MIDDLE_ROWS = 32
MIDDLE_LAG = 3


def gelu_both(values):
    square = values * values
    bent = jnp.tanh(0.7978845608028654 * (values + 0.044715 * values * square))
    slope = 0.5 * (1.0 + bent) + 0.5 * values * (1.0 - bent * bent) * (
        0.7978845608028654 * (1.0 + 3.0 * 0.044715 * square)
    )
    return 0.5 * values * (1.0 + bent), slope


def middle_kernel(count, groups, frames_axis, frames, scattered, fetch, *refs):
    (
        first_ref, base_ref, cotangent_ref, rows_ref, bias_ref,
        text_ref, text_w, query_w, out_w, up_w, down_w,
        base_three, grad_two, low_two, low_three, normed_three, heads_out, grad_query,
        grad_keys, grad_values, sums_ref, extra_part, down_grad, up_result,
        keys_ref, values_ref,
        normed_four, low_four, active, grad_inner, base_two, branch_two, query, grad_heads, part, mixed, tally,
        land, stage, total, cross, in_send, land_recv, cross_recv, out_send, out_recv, *scratch,
    ) = refs
    place = lax.axis_index(LINE)
    if scattered:
        up_grad, *scratch = scratch
        scatters = Scatters(groups, frames_axis, [up_grad], [[up_grad.shape[1]]], [up_result], scratch)
        asides = scatters.items
        greet_line(place, count, 0, asides[0].partners())
    else:
        up_grad, asides = up_result, []
        greet_line(place, count)
    fetch(0, 1, 3)
    half = count // 2
    left = place < half
    level = jnp.where(left, place, count - 1 - place)
    inner = jnp.where(left, place + 1, place - 1)
    outer = jnp.where(left, place - 1, place + 1)
    is_end, is_middle = level == 0, level == half - 1
    inside = jnp.logical_not(is_end)
    patches = base_ref.shape[0] // frames
    chunks = patches // MIDDLE_ROWS
    slots = STAGES * frames
    scale = HD ** (-0.5)
    width = bias_ref.shape[2]
    local = query_w.shape[0]
    half_heads = local // HD // 2
    tile = up_w.shape[1] // 3
    gate_two, cross_gain, gain_three, shift_three, gate_three = (
        rows_ref[i : i + 1] for i in (5, 12, 11, 6, 8)
    )

    def where_of(slot, chunk):
        rows = pl.ds(pl.multiple_of(lax.rem(slot, frames) * patches + chunk * MIDDLE_ROWS, MIDDLE_ROWS), MIDDLE_ROWS)
        return lax.rem(lax.div(slot, frames), 2), rows

    def inward(slot, chunk):
        rows = where_of(slot, chunk)[1]
        return remote(
            stage.at[rows], land.at[rows], in_send.at[slot, chunk], land_recv.at[slot, chunk], {LINE: inner}
        )

    def across(slot, chunk):
        side, rows = where_of(slot, chunk)
        return remote(
            stage.at[rows], cross.at[side, rows], in_send.at[slot, chunk], cross_recv.at[slot, chunk], {LINE: inner}
        )

    def outward(slot, chunk):
        rows = where_of(slot, chunk)[1]
        return remote(
            total.at[rows], total.at[rows], out_send.at[slot, chunk], out_recv.at[slot, chunk], {LINE: outer}
        )

    def own_part(slot, rows):
        return jnp.where(slot < frames, first_ref[rows], part[rows])

    def send_in(slot, chunk):
        @pl.when(is_middle)
        def _():
            across(slot, chunk).start()

        @pl.when(jnp.logical_not(is_middle))
        def _():
            inward(slot, chunk).start()

    def sent(slot, chunk):
        @pl.when(is_middle)
        def _():
            across(slot, chunk).wait_send()

        @pl.when(jnp.logical_not(is_middle))
        def _():
            inward(slot, chunk).wait_send()

        @pl.when(inside)
        def _():
            outward(slot, chunk).wait_send()

    def free(slot, chunk):
        @pl.when(slot >= frames)
        def _():
            sent(slot - frames, chunk)

    def gather_in(slot, chunk):
        rows = where_of(slot, chunk)[1]
        free(slot, chunk)
        inward(slot, chunk).wait_recv()
        stage[rows] = (own_part(slot, rows).astype(WIDE) + land[rows].astype(WIDE)).astype(NARROW)
        send_in(slot, chunk)

    def add_rows(which, terms):
        tally[which] += jnp.sum(terms.reshape(-1, 8, terms.shape[-1]), axis=0)

    def consume(slot, rows, summed):
        number = lax.div(slot, frames)

        @pl.when(number == 0)
        def _():
            branch_two[rows] = summed
            moved = base_ref[rows] + gate_two * summed.astype(WIDE)
            base_two[rows] = moved
            normed_three[rows] = (norm_parts(moved)[0] * cross_gain).astype(NARROW)

        @pl.when(number == 1)
        def _():
            moved = base_two[rows] + summed.astype(WIDE)
            base_three[rows] = moved
            normed_four[rows] = (norm_parts(moved)[0] * gain_three + shift_three).astype(NARROW)
            low_four[rows] = (gate_three * cotangent_ref[rows].astype(WIDE)).astype(NARROW)

        @pl.when(number == 2)
        def _():
            grads = summed.astype(WIDE)
            normal, spread = norm_parts(base_three[rows])
            moved = cotangent_ref[rows].astype(WIDE) + norm_pull(grads * gain_three, normal, spread)
            grad_two[rows] = moved
            low_three[rows] = moved.astype(NARROW)
            add_rows(0, grads)
            add_rows(1, grads * normal)

        @pl.when(number == 3)
        def _():
            grads = summed.astype(WIDE)
            normal, spread = norm_parts(base_two[rows])
            moved = grad_two[rows] + norm_pull(grads * cross_gain, normal, spread)
            grad_two[rows] = moved
            low_two[rows] = (gate_two * moved).astype(NARROW)
            add_rows(2, grads * normal)
            add_rows(3, moved * branch_two[rows].astype(WIDE))

    def finish(slot, chunk):
        side, rows = where_of(slot, chunk)

        @pl.when(is_middle)
        def _():
            across(slot, chunk).wait_recv()
            total[rows] = (stage[rows].astype(WIDE) + cross[side, rows].astype(WIDE)).astype(NARROW)

        @pl.when(jnp.logical_not(is_middle))
        def _():
            outward(slot, chunk).wait_recv()

        @pl.when(inside)
        def _():
            outward(slot, chunk).start()

        consume(slot, rows, total[rows])

    def head_rows(head):
        return pl.ds(head * width, width)

    def probs_of(stream, asked, head):
        scores = scale * dot(asked, keys_ref[head_rows(head)], 1, 1) + bias_ref[stream, 0:1]
        raised = jnp.exp(scores - jnp.max(scores, axis=-1, keepdims=True))
        return raised / jnp.sum(raised, axis=-1, keepdims=True)

    def cross_forward(piece, stream, rows):
        if piece == 0:
            query[rows] = dot(normed_three[rows], query_w[...], 1, 1).astype(NARROW)
        elif piece in (1, 2):
            asked = query[rows]
            found = jnp.zeros((patches, local), WIDE) if piece == 1 else mixed[...]
            for head in range((piece - 1) * half_heads, piece * half_heads):
                probs = probs_of(stream, asked, head).astype(NARROW)
                found = found + dot(probs, values_ref[head_rows(head)], 1, 0)
            if piece == 1:
                mixed[...] = found
            else:
                heads_out[rows] = found.astype(NARROW)
        elif piece == 3:
            part[rows] = dot(heads_out[rows], out_w[...], 1, 0).astype(NARROW)

    def feed_forward(piece, stream, rows):
        if piece < 3:
            span = slice(piece * tile, (piece + 1) * tile)
            inner_values = dot(normed_four[rows], up_w[:, span], 1, 0)
            pulled = dot(low_four[rows], down_w[span], 1, 1)
            raised, slope = gelu_both(inner_values)
            active[rows, span] = raised.astype(NARROW)
            grad_inner[rows, span] = (pulled * slope).astype(NARROW)
        else:
            third = up_w.shape[0] // 3
            span = slice((piece - 3) * third, (piece - 2) * third)
            part[rows, span] = dot(grad_inner[rows], up_w[span], 1, 1).astype(NARROW)

    def cross_backward(piece, stream, rows):
        if piece == 0:
            grad_heads[rows] = dot(low_three[rows], out_w[...], 1, 1).astype(NARROW)
        elif piece in (1, 2):
            asked, given = query[rows], grad_heads[rows]
            found = jnp.zeros((patches, local), WIDE) if piece == 1 else mixed[...]
            for head in range((piece - 1) * half_heads, piece * half_heads):
                spot = head_rows(head)
                probs = probs_of(stream, asked, head)
                pulled = dot(given, values_ref[spot], 1, 1)
                grad_scores = probs * (pulled - jnp.sum(pulled * probs, axis=-1, keepdims=True))
                grad_scores = grad_scores.astype(NARROW)
                found = found + dot(grad_scores, keys_ref[spot], 1, 0)
                grad_keys[spot] += dot(grad_scores, asked, 0, 0)
                grad_values[spot] += dot(probs.astype(NARROW), given, 0, 0)
            if piece == 1:
                mixed[...] = found
            else:
                grad_query[rows] = (scale * found).astype(NARROW)
        elif piece == 3:
            part[rows] = dot(grad_query[rows], query_w[...], 1, 0).astype(NARROW)

    def up_tile(number):
        grad_tile(normed_four, grad_inner, up_grad, number * third, third)

    def down_tile(number):
        grad_tile(low_four, active, down_grad, number * third, third)

    def extra(frame):
        rows = slice(frame * patches, (frame + 1) * patches)
        extra_part[rows] = dot(active[rows], down_w[...], 1, 0).astype(NARROW)

    def text_pairs():
        fetch.again(2, 4, 5, 6, 7, 8, 9, 10)
        packed = dot(text_w[...], text_ref[...], 1, 0).T.astype(NARROW)
        spread_heads(packed[:, 0:local], keys_ref)
        spread_heads(packed[:, local:], values_ref)

    third = up_w.shape[0] // 3
    late = {(0, 1): [text_pairs]}

    def later(slot, chunk, work, *args):
        late.setdefault((slots - 3 + slot, chunk), []).append(functools.partial(work, *args))

    for i, spot in enumerate(((0, 0), (0, 1), (0, 2))):
        later(*spot, up_tile, i)
    for i in range(3):
        later(2, 1 + i, down_tile, i)
    if asides:
        later(0, 2, asides[0].start)
        for i, work in enumerate(scatters.folds(0)):
            later(1, (0, 7)[i], work)
    for frame in range(frames):
        later(2, 6 + min(frame, 1), extra, frame)
    for which, slot, chunk in ((4, -2, 3), (5, -2, 4), (0, 0, 4), (3, 1, 5), (6, 2, 3), (7, 2, 4), (8, 2, 5), (11, 2, 5)):
        later(slot, chunk, fetch.store, which)

    tally[...] = jnp.zeros_like(tally)
    grad_keys[...] = jnp.zeros_like(grad_keys)
    grad_values[...] = jnp.zeros_like(grad_values)

    def step(number, carry):
        slot, chunk = lax.div(number, chunks), lax.rem(number, chunks)
        before = slot - 1

        @pl.when(is_end & (chunk == 0))
        def _():
            @pl.when(slot < slots)
            def _():
                def begin(item, inner_carry):
                    rows = where_of(slot, item)[1]
                    free(slot, item)
                    stage[rows] = own_part(slot, rows)
                    send_in(slot, item)
                    return inner_carry

                lax.fori_loop(0, chunks, begin, 0)

            for late_slot in sorted({spot[0] for spot in late}):

                @pl.when(slot == late_slot)
                def _():
                    for late_chunk in range(MIDDLE_LAG):
                        for work in late.get((late_slot, late_chunk), ()):
                            work()

            @pl.when(slot > 0)
            def _():
                def end(item, inner_carry):
                    finish(before, item)
                    return inner_carry

                lax.fori_loop(0, chunks, end, 0)

        @pl.when(inside & (slot < slots))
        def _():
            gather_in(slot, chunk)

            @pl.when(chunk >= MIDDLE_LAG)
            def _():
                finish(slot, chunk - MIDDLE_LAG)

        @pl.when(inside & (slot > 0) & (chunk < MIDDLE_LAG))
        def _():
            finish(before, chunks - MIDDLE_LAG + chunk)

        stream = lax.rem(jnp.maximum(before, 0), frames)
        rows = pl.ds(pl.multiple_of(stream * patches, patches), patches)
        for which, work in enumerate((cross_forward, feed_forward, cross_backward)):

            @pl.when((slot > 0) & (lax.div(jnp.maximum(before, 0), frames) == which))
            def _():
                for piece in range(6 if which == 1 else 4):

                    @pl.when(chunk == jnp.minimum(MIDDLE_LAG + piece, chunks - 1))
                    def _():
                        work(piece, stream, rows)

        for (late_slot, late_chunk), works in late.items():

            @pl.when((slot == late_slot) & (chunk == late_chunk) & (inside | (late_chunk >= MIDDLE_LAG)))
            def _():
                for work in works:
                    work()

        return carry

    lax.fori_loop(0, slots * chunks + MIDDLE_LAG, step, 0)

    def settle(number, carry):
        sent(lax.div(number, chunks), lax.rem(number, chunks))
        return carry

    lax.fori_loop((slots - frames) * chunks, slots * chunks, settle, 0)
    sums_ref[...] = jnp.zeros_like(sums_ref)
    for i in range(4):
        sums_ref[i : i + 1] = jnp.sum(tally[i], axis=0, keepdims=True)
    for aside in asides:
        aside.finish([up_result])


def call_middle(
    count, groups, frames_axis, frames, first, base, cotangent, rows, bias, text, text_w, query_w, out_w, up_w, down_w
):
    tokens, features = first.shape
    local, hidden = query_w.shape[0], up_w.shape[1]
    chunks = tokens // frames // MIDDLE_ROWS
    scattered = can_scatter(groups, frames_axis, features)
    keys_shape = (local // HD * bias.shape[2], local)

    def wide(*shape):
        return jax.ShapeDtypeStruct(shape, WIDE)

    def narrow(*shape):
        return jax.ShapeDtypeStruct(shape, NARROW)

    found, scratch = [narrow(features, hidden)], []
    if scattered:
        found, scratch = Scatters.shapes(groups, frames_axis, features, [[hidden]])
        scratch = [pltpu.VMEM((features, hidden), NARROW)] + scratch
    results = (
        [wide(tokens, features)] * 2
        + [narrow(tokens, features)] * 3
        + [narrow(tokens, local)] * 2
        + [wide(*keys_shape)] * 2
        + [wide(8, features), narrow(tokens, features), narrow(features, hidden)]
        + found
    )
    sem = pltpu.SemaphoreType.DMA((STAGES * frames, chunks))
    return fetching_call(
        functools.partial(middle_kernel, count, groups, frames_axis, frames, scattered),
        [first, base, cotangent, rows, bias, text, text_w, query_w, out_w, up_w, down_w],
        tuple(results),
        [pltpu.VMEM(keys_shape, NARROW)] * 2
        + [pltpu.VMEM((tokens, features), NARROW)] * 2
        + [pltpu.VMEM((tokens, hidden), NARROW)] * 2
        + [
            pltpu.VMEM((tokens, features), WIDE),
            pltpu.VMEM((tokens, features), NARROW),
            pltpu.VMEM((tokens, local), NARROW),
            pltpu.VMEM((tokens, local), NARROW),
            pltpu.VMEM((tokens, features), NARROW),
            pltpu.VMEM((tokens // frames, local), WIDE),
            pltpu.VMEM((4, 8, features), WIDE),
        ]
        + [pltpu.VMEM((tokens, features), NARROW)] * 3
        + [pltpu.VMEM((2, tokens, features), NARROW)]
        + [sem] * 5
        + scratch,
        7,
        "middle",
        storing=True,
    )


def greet_frames(here, frames_axis):
    found = (here > 0).astype(jnp.int32) + (here < frames_axis - 1).astype(jnp.int32)
    barrier = pltpu.get_barrier_semaphore()

    @pl.when(here > 0)
    def _():
        pl.semaphore_signal(barrier, inc=1, device_id={FRAME: here - 1}, device_id_type=MESH)

    @pl.when(here < frames_axis - 1)
    def _():
        pl.semaphore_signal(barrier, inc=1, device_id={FRAME: here + 1}, device_id_type=MESH)

    return found


def head_columns(local):
    feature = lax.broadcasted_iota(jnp.int32, (local, 128), 0)
    first = lax.broadcasted_iota(jnp.int32, (local, 128), 1) * HD
    return jnp.where((feature >= first) & (feature < first + HD), 1.0, 0.0).astype(NARROW)


def per_head(values, columns):
    return dot(values.astype(NARROW), columns, 1, 0)


def over_features(values, columns):
    return dot(values.astype(NARROW), columns, 1, 1)


def window_probs(query, keys_of, bias_of, columns):
    scores = [
        HD ** (-0.5) * per_head(query * keys_of(offset), columns) + bias_of(offset) for offset in range(WIN)
    ]
    highest = functools.reduce(jnp.maximum, scores)
    raised = [jnp.exp(item - highest) for item in scores]
    whole = 1.0 / sum(raised[1:], raised[0])
    return [item * whole for item in raised]


def temporal_forward_kernel(
    count, frames_axis, frames, fetch, hidden_ref, in_ref, out_ref, bias_ref, cotangent_ref, text_ref,
    query_ref, keys_ref, values_ref, heads_ref, part_ref, cotangent_full, text_full,
    halo_send, halo_recv, *sems,
):
    place, here = lax.axis_index(LINE), lax.axis_index(FRAME)
    patches = hidden_ref.shape[0] // frames
    local = heads_ref.shape[1]
    share = cotangent_ref.shape[1]
    last = count - 1
    greet_line(place, count, greet_frames(here, frames_axis))
    fetch()
    cells = (keys_ref, values_ref)

    def shares(owner):
        return cotangent_full.at[:, pl.ds(pl.multiple_of(owner * share, share), share)]

    def text_share(owner):
        return text_full.at[pl.ds(pl.multiple_of(owner * local, 16), local)]

    moving = [
        LineGather(count, place, shares, sems[0:3]),
        LineGather(count, place, text_share, sems[3:6]),
    ]
    cotangent_full[:, pl.ds(pl.multiple_of(place * share, share), share)] = cotangent_ref[...]
    text_full[pl.ds(pl.multiple_of(place * local, 16), local)] = text_ref[...]
    for item in moving:
        item.start()

    def halo(which, item):
        source = 2 + (frames - 2 + which if which < 2 else 0)
        target = which if which < 2 else frames + 2
        to = here + 1 if which < 2 else here - 1
        ref = cells[item]
        return remote(
            ref.at[source], ref.at[target], halo_send.at[which, item], halo_recv.at[which, item], {FRAME: to}
        )

    has_next, has_previous = here < frames_axis - 1, here > 0

    def frame_rows(frame):
        return slice(frame * patches, (frame + 1) * patches)

    for frame in range(frames):
        for item in range(2):
            rows = slice((1 + item) * local, (2 + item) * local)
            cells[item][2 + frame] = dot(hidden_ref[frame_rows(frame)], in_ref[rows], 1, 1).astype(NARROW)
            for which in range(3):
                if (frames - 2 + which if which < 2 else 0) == frame:

                    @pl.when(has_next if which < 2 else has_previous)
                    def _():
                        halo(which, item).start()

    query_ref[...] = dot(hidden_ref[...], in_ref[0:local], 1, 1).astype(NARROW)
    for distance in range(1, last):
        for item in moving:
            item.arrive(distance)
    for item in range(2):

        @pl.when(has_previous)
        def _():
            halo(0, item).wait_recv()
            halo(1, item).wait_recv()

        @pl.when(jnp.logical_not(has_previous))
        def _():
            cells[item][0:2] = jnp.zeros((2,) + cells[item].shape[1:], NARROW)

        @pl.when(has_next)
        def _():
            halo(2, item).wait_recv()

        @pl.when(jnp.logical_not(has_next))
        def _():
            cells[item][frames + 2] = jnp.zeros(cells[item].shape[1:], NARROW)

    columns = head_columns(local)
    for frame in range(frames):
        probs = window_probs(
            query_ref[frame_rows(frame)].astype(WIDE),
            lambda offset: keys_ref[frame + offset].astype(WIDE),
            lambda offset: bias_ref[frame * WIN + offset : frame * WIN + offset + 1],
            columns,
        )
        mixed = over_features(probs[0], columns) * values_ref[frame].astype(WIDE)
        for offset in range(1, WIN):
            mixed = mixed + over_features(probs[offset], columns) * values_ref[frame + offset].astype(WIDE)
        heads_ref[frame_rows(frame)] = mixed.astype(NARROW)
        part_ref[frame_rows(frame)] = dot(mixed.astype(NARROW), out_ref[...], 1, 0).astype(NARROW)
    for item in moving:
        item.arrive(last)
        item.settle()
    for item in range(2):

        @pl.when(has_next)
        def _():
            halo(0, item).wait_send()
            halo(1, item).wait_send()

        @pl.when(has_previous)
        def _():
            halo(2, item).wait_send()


def call_temporal_forward(count, frames_axis, hidden, in_w, out_w, bias, cotangent, text):
    tokens, features = hidden.shape
    frames, share = cotangent.shape[:2]
    local = out_w.shape[0]
    patches = tokens // frames

    def narrow(*shape):
        return jax.ShapeDtypeStruct(shape, NARROW)

    results = (
        [narrow(tokens, local)]
        + [narrow(frames + 3, patches, local)] * 2
        + [narrow(tokens, local), narrow(tokens, features)]
        + [narrow(frames, share * count, features), narrow(features, text.shape[1])]
    )
    return fetching_call(
        functools.partial(temporal_forward_kernel, count, frames_axis, frames),
        [hidden, in_w, out_w, bias, cotangent, text],
        tuple(results),
        [pltpu.SemaphoreType.DMA((3, 2))] * 2 + gather_sems(count) * 2,
        8,
        "temporal_forward",
    )


def temporal_backward_kernel(
    count, groups, frames_axis, frames, widths, fetch, *refs
):
    (
        grad_ref, in_ref, out_ref, bias_ref, query_ref, keys_ref, values_ref,
        extra_ref, text_keys, text_values, text_w, text_rows, cross_hidden, cross_grad, cross_low, cross_heads,
        base_three, cotangent_ref, gate_ref, *refs,
    ) = refs
    sources, refs = refs[: len(widths)], refs[len(widths) :]
    grad_packed, part_ref, output_ref, gate_part, text_own, product_ref, *refs = refs
    results, refs = refs[: len(widths)], refs[len(widths) :]
    (
        near_keys, near_values, rim_out, rim_in, halo_send, halo_recv, text_ref, text_low,
        extra_land, extra_stage, text_land, text_stage, *sems,
    ) = refs
    scatters = Scatters(groups, frames_axis, sources, widths, results, sems[8:])
    products = Products(
        [(cross_hidden, cross_grad), (text_rows, text_low, 1, 1), (cross_low, cross_heads)], product_ref
    ).work()
    place, here = lax.axis_index(LINE), lax.axis_index(FRAME)
    patches = grad_ref.shape[0] // frames
    local = out_ref.shape[0]
    share = output_ref.shape[1]
    last = count - 1
    greet_line(place, count, greet_frames(here, frames_axis), scatters.partners() if widths else ())
    fetch(7, *range(19, 19 + len(sources)))
    for item in scatters.items:
        item.start()

    def shares(owner, frame):
        return extra_ref[frame, pl.ds(pl.multiple_of(owner * share, share), share)]

    moving = [
        LineScatter(count, place, frames, shares, extra_land, extra_stage, sems[0:4]),
        LineScatter(count, place, 1, lambda owner, piece: text_ref[owner], text_land, text_stage, sems[4:8]),
    ]
    moving[0].relay_both(last)
    near = (near_keys, near_values)
    def halo(which):
        to = here - 1 if which < 2 else here + 1
        return remote(
            rim_out.at[which], rim_in.at[which], halo_send.at[which], halo_recv.at[which], {FRAME: to}
        )

    has_next, has_previous = here < frames_axis - 1, here > 0

    def frame_rows(frame):
        return slice(frame * patches, (frame + 1) * patches)

    fetch(0, 2, 3, 4, 5, 6)
    columns = head_columns(local)
    seen = set()

    def add(item, cell, terms):
        if (item, cell) in seen:
            near[item][cell] += terms
        else:
            near[item][cell] = terms
        seen.add((item, cell))

    for frame in range(frames):
        given = dot(grad_ref[frame_rows(frame)], out_ref[...], 1, 1).astype(NARROW).astype(WIDE)
        asked = query_ref[frame_rows(frame)].astype(WIDE)
        probs = window_probs(
            asked,
            lambda offset: keys_ref[frame + offset].astype(WIDE),
            lambda offset: bias_ref[frame * WIN + offset : frame * WIN + offset + 1],
            columns,
        )
        pulled = [per_head(given * values_ref[frame + offset].astype(WIDE), columns) for offset in range(WIN)]
        shared = sum((probs[i] * pulled[i] for i in range(1, WIN)), probs[0] * pulled[0])
        found = jnp.zeros((patches, local), WIDE)
        for offset in range(WIN):
            scores = HD ** (-0.5) * over_features(probs[offset] * (pulled[offset] - shared), columns)
            found = found + scores * keys_ref[frame + offset].astype(WIDE)
            add(0, frame + offset, scores * asked)
            add(1, frame + offset, over_features(probs[offset], columns) * given)
        grad_packed[frame_rows(frame), 0:local] = found.astype(NARROW)
        if frame == 0:
            for item in scatters.items:
                item.first_round()
            if last > 1:
                moving[0].relay_both(last - 1)

    for which in range(3):

        @pl.when(has_previous if which < 2 else has_next)
        def _():
            for item in range(2):
                span = slice(item * local, (item + 1) * local)
                rim_out[which, :, span] = near[item][which if which < 2 else frames + 2].astype(NARROW)
            halo(which).start()

    for distance in range(last - 2, 0, -1):
        moving[0].relay_both(distance)
    for item in scatters.items:
        item.second_round()
    fetch()
    fetch()
    slots = text_low.shape[1]
    for item, (source, factor) in enumerate(((text_keys, HD ** (-0.5)), (text_values, 1.0))):
        low = (factor * collect_heads(source[...], slots)).T
        text_low[item * local : (item + 1) * local] = low.astype(NARROW)
    text_parts = dot(text_w[...], text_low[...], 0, 0).astype(NARROW)
    for owner in range(count):
        text_ref[owner] = text_parts[owner * local : (owner + 1) * local]
    moving[1].relay_both(last)
    for i, work in enumerate(products):
        work()
        if last - 1 - i > 0:
            moving[1].relay_both(last - 1 - i)
    for distance in range(last - 1 - len(products), 0, -1):
        moving[1].relay_both(distance)

    for which in range(3):

        @pl.when(has_next if which < 2 else has_previous)
        def _():
            halo(which).wait_recv()
            for item in range(2):
                span = slice(item * local, (item + 1) * local)
                near[item][2 + (frames - 2 + which if which < 2 else 0)] += rim_in[which, :, span].astype(WIDE)

    for frame in range(frames):
        rows = frame_rows(frame)
        parts = dot(grad_packed[rows, 0:local], in_ref[0:local], 1, 0)
        for item in range(2):
            values = near[item][2 + frame].astype(NARROW)
            grad_packed[rows, (1 + item) * local : (2 + item) * local] = values
            parts = parts + dot(values, in_ref[(1 + item) * local : (2 + item) * local], 1, 0)
        part_ref[rows] = parts.astype(NARROW)

    gate_sum = jnp.zeros((1, gate_part.shape[1]), WIDE)
    for frame in range(frames):
        found = moving[0].total(frame)
        rows = pl.ds(pl.multiple_of(frame * patches + place * share, share), share)
        output_ref[frame] = (base_three[rows] + gate_ref[8:9] * found).astype(NARROW)
        gate_sum = gate_sum + jnp.sum(cotangent_ref[frame].astype(WIDE) * found, axis=0, keepdims=True)
    gate_part[...] = jnp.broadcast_to(gate_sum, gate_part.shape)
    text_own[...] = moving[1].total(0).astype(NARROW)
    for item in moving:
        item.settle()
    for which in range(3):

        @pl.when(has_previous if which < 2 else has_next)
        def _():
            halo(which).wait_send()

    scatters.finish()


def call_temporal_backward(
    count, groups, frames_axis, grad, in_w, out_w, bias, query, keys, values, extra, text_keys, text_values, text_w,
    text_rows, cross_pairs, sources, widths,
):
    tokens, features = grad.shape
    frames, patches = extra.shape[:2]
    local = out_w.shape[0]
    share = patches // count
    slots = text_rows.shape[1]

    def narrow(*shape):
        return jax.ShapeDtypeStruct(shape, NARROW)

    results = (
        [narrow(tokens, 3 * local)]
        + [narrow(tokens, features), narrow(frames, share, features)]
        + [jax.ShapeDtypeStruct((8, features), WIDE)]
        + [narrow(local, slots), narrow(features, 4 * local)]
    )
    found, scratch = Scatters.shapes(groups, frames_axis, features, widths)
    results = results + found
    return fetching_call(
        functools.partial(temporal_backward_kernel, count, groups, frames_axis, frames, widths),
        [grad, in_w, out_w, bias, query, keys, values, extra, text_keys, text_values, text_w, text_rows,
        *cross_pairs, *sources,],
        tuple(results),
        [pltpu.VMEM((frames + 3, patches, local), WIDE)] * 2
        + [pltpu.VMEM((3, patches, 2 * local), NARROW)] * 2
        + [pltpu.SemaphoreType.DMA((3,))] * 2
        + [pltpu.VMEM((count, local, slots), NARROW), pltpu.VMEM((2 * local, slots), NARROW)]
        + [pltpu.VMEM((2, count, frames, share, features), NARROW)] * 2
        + [pltpu.VMEM((2, count, 1, local, slots), NARROW)] * 2
        + scatter_sems(count, frames)
        + scatter_sems(count, 1)
        + scratch,
        9,
        "temporal_backward",
    )


def sum_matrix_grads(pieces):
    if not pieces:
        return []
    packed = jnp.concatenate([piece.astype(NARROW) for piece in pieces], axis=1)
    summed = lax.psum_scatter(packed, BOTH, scatter_dimension=0, tiled=True).astype(WIDE)
    found, start = [], 0
    for piece in pieces:
        found.append(summed[:, start : start + piece.shape[1]])
        start += piece.shape[1]
    return found


def per_device(
    latent, captions, bucket, clip_ids, window_mask, text_counts, time_table, ada_weight,
    spatial_inproj, spatial_outproj, temporal_inproj, temporal_outproj, caption_proj, cross_gain,
    cross_query, cross_keyval, cross_outproj, mlp_up, mlp_down, cotangent,
):
    count, groups, frames_axis = (lax.axis_size(axis) for axis in (LINE, GROUP, FRAME))
    place = lax.axis_index(LINE)
    frames, share, features = latent.shape[1:]
    patches = share * count
    tokens = frames * patches
    local = spatial_outproj.shape[0]
    clip_count, text_length, text_width = captions.shape[1:]
    slots = clip_count * text_length

    def flat(values):
        return values.reshape(tokens, -1)

    def grid(values):
        return values.reshape(frames, patches, -1)

    spatial_in, temporal_in, keyval_in = (
        jnp.transpose(w, (1, 2, 0)).reshape(-1, features)
        for w in (spatial_inproj, temporal_inproj, cross_keyval)
    )
    query_in = cross_query.T

    caption_here = captions[0].reshape(slots, text_width)
    base_grid, normed_grid, mods, text_part, side, window_bias, text_bias, caption_share = call_opening(
        count, groups, frames_axis, (bucket, clip_ids, window_mask, text_counts), latent[0], time_table,
        cross_gain.reshape(-1, 128), jnp.transpose(ada_weight, (1, 0, 2)), caption_here, caption_proj.T,
    )
    base_zero, spatial_hidden = flat(base_grid), flat(normed_grid)

    spatial_out, base_one, temporal_hidden, spatial_packed, spatial_flat = call_forward(
        count, frames, spatial_hidden, spatial_in, base_zero, mods, spatial_outproj,
    )

    (
        temporal_query, temporal_keys, temporal_values, temporal_flat, temporal_part, cotangent_full, text_full,
    ) = call_temporal_forward(
        count, frames_axis, temporal_hidden, temporal_in, temporal_outproj, window_bias, cotangent[0], text_part
    )
    cotangent_full = flat(cotangent_full)

    (
        base_three, grad_two, grad_temporal_low, grad_cross_low, cross_hidden, cross_flat, grad_cross_packed,
        text_grad_keys, text_grad_values, sums_middle, mlp_part, grad_down, grad_up,
    ) = call_middle(
        count, groups, frames_axis, frames, temporal_part, base_one, cotangent_full,
        mods, text_bias,
        text_full, keyval_in, query_in, cross_outproj, mlp_up, mlp_down,
    )

    def outside(packed, widths):
        return sum_matrix_grads(
            [
                item[:, sum(columns[:i]) : sum(columns[: i + 1])]
                for item, columns in zip(packed, widths)
                for i in range(len(columns))
            ]
        )

    if not can_scatter(groups, frames_axis, features):
        (grad_up,) = outside([grad_up], [[grad_up.shape[1]]])

    inside = can_scatter(groups, frames_axis, features)
    down_widths = [[grad_down.shape[1]]]
    grad_temporal_packed, temporal_grad_part, output, gate_part, text_grad, grad_cross, *found = call_temporal_backward(
        count, groups, frames_axis, grad_temporal_low, temporal_in, temporal_outproj, window_bias,
        temporal_query, temporal_keys, temporal_values, grid(mlp_part), text_grad_keys, text_grad_values,
        keyval_in, text_full,
        [cross_hidden, grad_cross_packed, grad_cross_low, cross_flat, base_three, cotangent[0], mods],
        [grad_down] if inside else [], down_widths if inside else [],
    )
    (grad_down,) = found if inside else outside([grad_down], down_widths)
    cross_widths, qkv_widths = [local, 2 * local, local], [3 * local, local]
    grad_one, grad_spatial_low, sums_temporal, *found = call_backward(
        count, groups, frames_axis, temporal_grad_part, base_one, grad_two, spatial_out,
        mods,
        [(temporal_hidden, grad_temporal_packed), (grad_temporal_low, temporal_flat)],
        [grad_cross] if inside else [], [cross_widths, qkv_widths] if inside else [],
    )
    if not inside:
        found = outside([grad_cross, found[0]], [cross_widths, qkv_widths])
    (
        grad_query_cross, grad_keyval_cross, grad_outproj_cross, grad_inproj_temporal, grad_outproj_temporal,
    ) = found

    grad_latent, small_all, text_grad_all, *found = call_closing(
        count, groups, frames_axis, grad_spatial_low, grid(base_zero), grid(grad_one), gate_part,
        mods, spatial_packed, spatial_flat, spatial_hidden, spatial_in, spatial_outproj,
        text_grad, [sums_temporal, sums_middle, side], [], [qkv_widths] if inside else [],
    )
    if not inside:
        found = outside([found[0]], [qkv_widths])
    grad_inproj_spatial, grad_outproj_spatial = found

    grad_ada, grad_table, grad_gain, grad_caption, *found = call_finishing(
        groups, frames_axis, time_table.shape[0], (0, 1, 8, 9, 10, 11, 12, 13, 2), (0, 0, 1, 0, 1, 0, 0, 2, 0, 0, 0),
        small_all, jnp.transpose(ada_weight, (1, 0, 2)), text_grad_all, caption_share,
        [
            output.reshape(frames * share, features), grad_latent.reshape(frames * share, features),
            grad_inproj_spatial, grad_outproj_spatial,
            grad_inproj_temporal, grad_outproj_temporal, grad_query_cross, grad_keyval_cross,
            grad_outproj_cross, grad_up, grad_down,
        ],
    )
    (
        output, grad_latent, grad_inproj_spatial, grad_outproj_spatial, grad_inproj_temporal,
        grad_outproj_temporal, grad_query_cross, grad_keyval_cross, grad_outproj_cross, grad_up, grad_down,
    ) = found
    return (
        output.reshape(1, frames, share, features),
        grad_latent.reshape(1, frames, share, features),
        grad_table,
        jnp.transpose(grad_ada, (2, 0, 1)),
        jnp.transpose(grad_inproj_spatial, (1, 0, 2)),
        grad_outproj_spatial.T,
        jnp.transpose(grad_inproj_temporal, (1, 0, 2)),
        grad_outproj_temporal.T,
        grad_caption.T,
        grad_gain.reshape(features),
        grad_query_cross,
        grad_keyval_cross,
        grad_outproj_cross.T,
        grad_up,
        grad_down.T,
    )


def solution(mesh):
    tokens = P(GROUP, FRAME, LINE, None)
    packed_in, rows_in, columns_in = P(None, None, LINE), P(LINE, None), P(None, LINE)
    in_specs = (
        tokens, P(GROUP, None, None, None), P(GROUP), P(GROUP, None), P(GROUP, FRAME, None),
        P(GROUP, None), columns_in, P(LINE, None, None), packed_in, rows_in, packed_in, rows_in,
        columns_in, P(), columns_in, packed_in, rows_in, columns_in, rows_in, tokens,
    )
    packed_out, rows_out, columns_out = P(BOTH, None, LINE), P(LINE, BOTH), P(BOTH, LINE)
    out_specs = (
        tokens, tokens, columns_in, P(LINE, None, BOTH), packed_out, rows_out, packed_out, rows_out,
        columns_out, P(), columns_out, packed_out, rows_out, columns_out, rows_out,
    )
    return jax.shard_map(
        per_device, mesh=mesh, in_specs=in_specs, out_specs=out_specs, check_vma=False
    )
```
